32 devices in a mesh: row: 2 (over core), col: 16 (over z, y, x).
Axes of the slice: x: 2, y: 2, z: 4, core: 2. Of those that a mesh axis runs over, the one named last changes fastest.
Arguments:
- image_tokens: bfloat16 [64, 512, 256], P('row', 'col'), may hold values from -6 to 6
- w_in: bfloat16 [256, 768], replicated, may hold values from -0.375 to 0.375
- conv_kernel: bfloat16 [3, 3, 768], replicated, may hold values from -2 to 2
- conv_bias: float32 [768], replicated, may hold values from -3 to 3
- long_filter: bfloat16 [64, 256], replicated, may hold values from -0.75 to 0.75
- skip_gain: float32 [256], replicated, may hold values from 0.5 to 1.5
- w_out: bfloat16 [256, 256], replicated, may hold values from -0.375 to 0.375
Outputs:
- layer_out: bfloat16 [64, 512, 256], P('row', 'col')
The draws below stay inside these ranges and needn't reach their ends.
All inputs are finite; a program needn't handle non-finite values.
Results may differ from the reference program's by a relative error of at most 0.014.
Values may be sent and summed in bfloat16 or wider, within the bound.
No kernel may reach another device: no remote copies, remote signals or barrier semaphores. Data moves between devices by JAX's collectives and lax.ppermute only.
A program may use at most 64 MiB of HBM per device.

```python
import jax
import jax.numpy as jnp
from jax import lax

C = 256
H = 64
W = 512
N_ROW = 2


def shard_levels(own_key, shape, pieces, low, top_value):
    factor_of = 1.0
    for dim, blocks in pieces:
        steps = jax.random.uniform(jax.random.fold_in(jax.random.fold_in(own_key, 6), dim), (blocks,), jnp.float32, low / len(pieces), top_value / len(pieces))
        factor_of = factor_of * jnp.repeat(jnp.exp(steps), shape[dim] // blocks).reshape((-1,) + (1,) * (len(shape) - 1 - dim))
    return factor_of


def gaussian(rng, extent, spread, bound, split=(), dtype=jnp.bfloat16):
    array = jax.random.normal(rng, extent, jnp.float32) * spread
    if len(split) > 0:
        array = shard_levels(rng, extent, split, -0.22, 0.18) * array
    return jnp.clip(array, min=-bound, max=bound).astype(dtype)


def setup_inputs(seed: int = 0) -> dict:
    key_of = jax.random.split(jax.random.key(seed), 8)
    return {
        "image_tokens": gaussian(key_of[0], (H, W, C), 1.0, 6.0, ((0, 2), (1, 16))),
        "w_in": gaussian(key_of[1], (C, 3 * C), C ** -0.5, 0.375),
        "conv_kernel": gaussian(key_of[2], (3, 3, 3 * C), 9 ** -0.5, 2.0),
        "conv_bias": gaussian(key_of[3], (3 * C,), 0.5, 3.0, (), jnp.float32),
        "long_filter": gaussian(key_of[4], (H, C), H ** -0.5, 0.75),
        "skip_gain": jnp.clip(jax.random.uniform(key_of[5], (C,), jnp.float32, 0.5, 1.5), 0.5, 1.5),
        "w_out": gaussian(key_of[6], (C, C), C ** -0.5, 0.375),
    }


def depthwise(field, kernel, bias):
    height = field.shape[0]
    span = field.shape[1]
    padded = jnp.pad(field, ((1, 1), (1, 1), (0, 0)))
    total = jnp.zeros(field.shape, jnp.float32) + bias.astype(jnp.float32)
    for row_off in range(3):
        for col_off in range(3):
            window = padded[row_off:row_off + height, col_off:col_off + span, :].astype(jnp.float32)
            total = total + window * kernel[row_off, col_off].astype(jnp.float32)
    return total.astype(jnp.bfloat16)


def reference(image_tokens, w_in, conv_kernel, conv_bias, long_filter, skip_gain, w_out):
    group = 32 if C % 32 == 0 else C
    count = C // group
    flat = image_tokens.reshape(H * W, C)
    w_groups = jnp.transpose(w_in.reshape(C, 3, count, group), (2, 0, 1, 3)).reshape(count, C, 3 * group)
    k_groups = jnp.transpose(conv_kernel.reshape(3, 3, 3, count, group), (3, 0, 1, 2, 4)).reshape(count, 3, 3, 3 * group)
    b_groups = jnp.transpose(conv_bias.reshape(3, count, group), (1, 0, 2)).reshape(count, 3 * group)
    f_groups = jnp.transpose(long_filter.reshape(H, count, group), (1, 0, 2))
    s_groups = skip_gain.reshape(count, group)

    def one_group(pack):
        weight, kernel, bias, filt, gain = pack
        proj = jnp.dot(flat, weight, preferred_element_type=jnp.float32).astype(jnp.bfloat16)
        proj = proj.reshape(H, W, 3 * group)
        mixed = depthwise(proj, kernel, bias)
        query = mixed[:, :, :group].astype(jnp.float32)
        key = mixed[:, :, group:2 * group].astype(jnp.float32)
        value = mixed[:, :, 2 * group:].astype(jnp.float32)
        product = (key * value).astype(jnp.bfloat16)
        prod_wide = product.astype(jnp.float32)
        spectrum = jnp.fft.rfft(prod_wide, n=2 * H, axis=0)
        response = jnp.fft.rfft(filt.astype(jnp.float32), n=2 * H, axis=0)
        longconv = jnp.fft.irfft(spectrum * response[:, None, :], n=2 * H, axis=0)[:H]
        return (query * (longconv + gain * prod_wide)).astype(jnp.bfloat16)

    gated = lax.map(one_group, (w_groups, k_groups, b_groups, f_groups, s_groups))
    gated = jnp.transpose(gated, (1, 2, 0, 3)).reshape(N_ROW, (H // N_ROW) * W, C)

    def project(block):
        return jnp.dot(block, w_out, preferred_element_type=jnp.float32).astype(jnp.bfloat16)

    return lax.map(project, gated).reshape(H, W, C)
```

```python
import jax
import jax.numpy as jnp
import numpy as np
from jax import lax
from jax.experimental import pallas as pl
from jax.experimental.pallas import tpu as pltpu
from jax.sharding import PartitionSpec as P

F32 = jnp.float32
BF16 = jnp.bfloat16


def transforms(half, group):
    size = 2 * half
    slot = np.arange(half)[:, None]
    pos = np.arange(half)[None, :]
    angle = 2 * np.pi * slot * pos / size
    real, imag = np.cos(angle), -np.sin(angle)
    imag[0] = (-1.0) ** np.arange(half)
    forward = np.concatenate([real, imag], 0)
    back_real = 2 * np.cos(angle.T) / size
    back_real[:, 0] = 1 / size
    back_imag = -2 * np.sin(angle.T) / size
    back_imag[:, 0] = (-1.0) ** np.arange(half) / size
    backward = np.concatenate([back_real, back_imag], 1)
    lag = np.arange(size)[None, :]
    angle = 2 * np.pi * slot * lag / size
    real, imag = np.cos(angle), -np.sin(angle)
    imag[0] = 0
    real2 = real.copy()
    real2[0] = (-1.0) ** np.arange(size)
    near = (lag < half).astype(np.float64)
    sign = (-1.0) ** slot
    sign2 = sign.copy()
    sign2[0] = 1
    spectra = np.concatenate(
        [real * near, imag * near, real2 * near, real * sign, imag * sign, real2 * sign2], 0
    )
    eye = np.eye(group)
    return np.kron(forward, eye), np.kron(backward, eye), spectra


def pick_column(block, column):
    rows, cols, width = block.shape
    at = lax.broadcasted_iota(jnp.int32, (rows, rows * cols), 1)
    want = lax.broadcasted_iota(jnp.int32, (rows, rows * cols), 0) * cols + column
    chosen = jnp.where(at == want, 1.0, 0.0).astype(BF16)
    return jnp.dot(
        chosen, block.reshape(rows * cols, width), preferred_element_type=F32
    ).astype(BF16)


def strip_kernel(own_ref, other_ref, strip_ref):
    core = lax.axis_index("row")
    rows, cols, _ = own_ref.shape
    part = cols // 2
    start = pl.multiple_of(core * part, part)
    column = core * (part - 1)
    mine = pick_column(own_ref[:, pl.ds(start, part), :], column)
    theirs = pick_column(other_ref[:, pl.ds(start, part), :], column)
    strip_ref[pl.ds(pl.multiple_of(core * rows, rows), rows), :] = mine
    strip_ref[pl.ds(pl.multiple_of((1 - core) * rows, rows), rows), :] = theirs


def main_kernel(
    own_ref, other_ref, halo_ref, w_in_ref, taps_ref, filt_ref, gain_ref, w_out_ref,
    fwd_ref, bwd_ref, spec_ref,
    mine_ref, send_ref,
    x_ref, p_ref, edge_ref, u_ref, q_ref, prod_ref, h_ref, z_ref, out_ref,
):
    core = lax.axis_index("row")
    rows, cols, width = own_ref.shape
    part = cols // 2
    height = 2 * rows
    start = pl.multiple_of(core * part, part)
    far = pl.multiple_of((1 - core) * part, part)
    inner = core * (part - 1)
    own_at = core * rows
    other_at = (1 - core) * rows

    x_ref[pl.ds(own_at, rows)] = own_ref[:, pl.ds(start, part), :]
    x_ref[pl.ds(other_at, rows)] = other_ref[:, pl.ds(start, part), :]

    p_ref[0] = jnp.zeros(p_ref.shape[1:], F32)
    p_ref[height + 1] = jnp.zeros(p_ref.shape[1:], F32)
    for row in range(0, height, rows):
        got = jnp.dot(
            x_ref[row : row + rows].reshape(rows * part, width),
            w_in_ref[...],
            preferred_element_type=F32,
        )
        p_ref[row + 1 : row + rows + 1] = got.reshape(rows, part, 3 * width)

    own_in = pick_column(own_ref[:, pl.ds(far, part), :], inner)
    other_in = pick_column(other_ref[:, pl.ds(far, part), :], inner)
    first = jnp.where(core == 0, own_in, other_in)
    second = jnp.where(core == 0, other_in, own_in)
    within = jnp.concatenate([first, second], 0)
    outside = halo_ref[...]
    for side, tokens in (
        (0, jnp.where(core == 0, outside, within)),
        (1, jnp.where(core == 0, within, outside)),
    ):
        edge_ref[...] = jnp.zeros(edge_ref.shape, F32)
        edge_ref[8 : 8 + height, :] = jnp.dot(tokens, w_in_ref[...], preferred_element_type=F32)
        total = jnp.zeros((height, 3 * width), F32)
        for a in range(3):
            tap = 3 * a + 2 * side
            total = total + edge_ref[7 + a : 7 + a + height, :] * taps_ref[tap : tap + 1, :]
        u_ref[side] = total.reshape(height // 8, 8, 3 * width)

    lanes = 128
    group = 8
    chunk = 8
    n_group = part // group
    sub = lax.broadcasted_iota(jnp.int32, (group, lanes), 0)
    is_first = sub == 0
    is_last = sub == group - 1

    def mix(base, i):
        row0 = i * chunk
        at = slice(base, base + lanes)
        tap = [
            [jnp.broadcast_to(taps_ref[3 * a + b : 3 * a + b + 1, at], (group, lanes)) for b in range(3)]
            for a in range(3)
        ]
        bias = jnp.broadcast_to(taps_ref[9:10, at], (group, lanes))
        loaded = [
            [p_ref[row0 + r, g * group : (g + 1) * group, at] for g in range(n_group)]
            for r in range(chunk + 2)
        ]
        out = []
        for r in range(chunk):
            u = [
                [
                    loaded[r][g] * tap[0][b] + loaded[r + 1][g] * tap[1][b] + loaded[r + 2][g] * tap[2][b]
                    for b in range(3)
                ]
                for g in range(n_group)
            ]
            right_turn = [pltpu.roll(u[g][0], 1, 0) for g in range(n_group)]
            left_turn = [pltpu.roll(u[g][2], group - 1, 0) for g in range(n_group)]
            west = jnp.broadcast_to(u_ref[0, i, r : r + 1, at], (group, lanes))
            east = jnp.broadcast_to(u_ref[1, i, r : r + 1, at], (group, lanes))
            line = []
            for g in range(n_group):
                before = west if g == 0 else right_turn[g - 1]
                after = east if g == n_group - 1 else left_turn[g + 1]
                value = u[g][1] + bias
                value = value + jnp.where(is_first, before, right_turn[g])
                value = value + jnp.where(is_last, after, left_turn[g])
                line.append(value)
            out.append(line)
        return out

    def stage(i, carry):
        row0 = i * chunk
        for base in range(0, width, lanes):
            at = slice(base, base + lanes)
            query = mix(base, i)
            for g in range(n_group):
                for r in range(chunk):
                    q_ref[g, row0 + r, :, at] = query[r][g]
            key = mix(width + base, i)
            value = mix(2 * width + base, i)
            for g in range(n_group):
                for r in range(0, chunk, 2):
                    two = jnp.concatenate(
                        [key[r][g] * value[r][g], key[r + 1][g] * value[r + 1][g]], 0
                    )
                    prod_ref[g, pl.ds(pl.multiple_of((row0 + r) * group, 2 * group), 2 * group), at] = (
                        two.astype(BF16)
                    )
        return carry

    lax.fori_loop(0, height // chunk, stage, 0)

    filt = filt_ref[...]
    h_ref[...] = jnp.dot(spec_ref[0], filt, preferred_element_type=F32) + jnp.dot(
        spec_ref[1], filt, preferred_element_type=F32
    )
    gain = gain_ref[...]
    h_ref[0:rows, :] = h_ref[0:rows, :] + gain
    h_ref[2 * rows : 3 * rows, :] = h_ref[2 * rows : 3 * rows, :] + gain

    block = rows * group
    for g in range(n_group):
        low = jnp.dot(fwd_ref[...], prod_ref[g, :block], preferred_element_type=F32)
        high = jnp.dot(fwd_ref[...], prod_ref[g, block:], preferred_element_type=F32)
        for k in range(0, rows, 2):
            parts = [[], [], [], []]
            for s in (k, k + 1):
                near_r, near_i, near_2, all_r, all_i, all_2 = (
                    jnp.broadcast_to(h_ref[j * rows + s : j * rows + s + 1, :], (group, width))
                    for j in range(6)
                )
                re, im = slice(s * group, (s + 1) * group), slice(block + s * group, block + (s + 1) * group)
                lr, li, hr, hi = low[re], low[im], high[re], high[im]
                parts[0].append(lr * near_r - li * near_i)
                parts[1].append(lr * near_i + li * near_2)
                parts[2].append(lr * all_r - li * all_i + hr * near_r - hi * near_i)
                parts[3].append(lr * all_i + li * all_2 + hr * near_i + hi * near_2)
            for j in range(4):
                at = (j % 2) * block + k * group
                z_ref[j // 2, at : at + 2 * group, :] = jnp.concatenate(parts[j], 0).astype(BF16)
        for h in range(2):
            conv = jnp.dot(bwd_ref[...], z_ref[h], preferred_element_type=F32)
            gated = q_ref[g, h * rows : (h + 1) * rows].reshape(block, width) * conv
            final = jnp.dot(gated.astype(BF16), w_out_ref[...], preferred_element_type=F32)
            out_ref[h * rows : (h + 1) * rows, g * group : (g + 1) * group, :] = final.reshape(
                rows, group, width
            )
    mine_ref[...] = out_ref[pl.ds(own_at, rows)].astype(BF16)
    send_ref[...] = out_ref[pl.ds(other_at, rows)].astype(BF16)


def on_device(image_tokens, w_in, conv_kernel, conv_bias, long_filter, skip_gain, w_out):
    rows, cols, width = image_tokens.shape
    part, group = cols // 2, 8
    height = 2 * rows
    n_col = lax.axis_size("col")
    core = lax.axis_index("row")
    fwd, bwd, spectra = transforms(rows, group)
    spec_hi = spectra.astype(BF16)
    spec_lo = (spectra - spec_hi.astype(np.float64)).astype(BF16)
    spec = np.stack([spec_hi, spec_lo])
    taps = jnp.concatenate(
        [conv_kernel.reshape(9, 3 * width).astype(F32), conv_bias[None], jnp.zeros((6, 3 * width), F32)], 0
    )

    swap = [(0, 1), (1, 0)]
    other = lax.ppermute(image_tokens, "row", swap)
    vmem = pl.BlockSpec(memory_space=pltpu.VMEM)
    strip = pl.pallas_call(
        strip_kernel,
        out_shape=jax.ShapeDtypeStruct((height, width), BF16),
        in_specs=[vmem, vmem],
        out_specs=vmem,
    )(image_tokens, other)
    pairs = []
    for j in range(n_col - 1):
        pairs += [(n_col + j, j + 1), (j + 1, n_col + j)]
    halo = lax.ppermute(strip, ("row", "col"), pairs)
    half_shape = jax.ShapeDtypeStruct((rows, part, width), BF16)
    mine, send = pl.pallas_call(
        main_kernel,
        out_shape=(half_shape, half_shape),
        in_specs=[vmem] * 11,
        out_specs=(vmem, vmem),
        scratch_shapes=[
            pltpu.VMEM((height, part, width), BF16),
            pltpu.VMEM((height + 2, part, 3 * width), F32),
            pltpu.VMEM((height + 16, 3 * width), F32),
            pltpu.VMEM((2, height // 8, 8, 3 * width), F32),
            pltpu.VMEM((part // group, height, group, width), F32),
            pltpu.VMEM((part // group, height * group, width), BF16),
            pltpu.VMEM((6 * rows, width), F32),
            pltpu.VMEM((2, 2 * rows * group, width), BF16),
            pltpu.VMEM((height, part, width), F32),
        ],
        compiler_params=pltpu.CompilerParams(vmem_limit_bytes=32 * 1024 * 1024),
    )(
        image_tokens, other, halo, w_in, taps, long_filter, skip_gain[None], w_out,
        fwd.astype(BF16), bwd.astype(BF16), spec,
    )
    theirs = lax.ppermute(send, "row", swap)
    return jnp.where(
        core == 0,
        jnp.concatenate([mine, theirs], 1),
        jnp.concatenate([theirs, mine], 1),
    )


def solution(mesh):
    in_specs = (P("row", "col", None), P(), P(), P(), P(), P(), P())
    out_specs = P("row", "col", None)
    return jax.shard_map(
        on_device, mesh=mesh, in_specs=in_specs, out_specs=out_specs, check_vma=False
    )
```

```python
import jax
import jax.numpy as jnp
import numpy as np
from jax import lax
from jax.experimental import pallas as pl
from jax.experimental.layout import Layout, with_layout_constraint
from jax.experimental.pallas import tpu as pltpu
from jax.sharding import PartitionSpec as P

F32 = jnp.float32
BF16 = jnp.bfloat16


def transforms(half, group):
    size = 2 * half
    slot = np.arange(half)[:, None]
    pos = np.arange(half)[None, :]
    angle = 2 * np.pi * slot * pos / size
    real, imag = np.cos(angle), -np.sin(angle)
    imag[0] = (-1.0) ** np.arange(half)
    forward = np.concatenate([real, imag], 0)
    back_real = 2 * np.cos(angle.T) / size
    back_real[:, 0] = 1 / size
    back_imag = -2 * np.sin(angle.T) / size
    back_imag[:, 0] = (-1.0) ** np.arange(half) / size
    backward = np.concatenate([back_real, back_imag], 1)
    lag = np.arange(size)[None, :]
    angle = 2 * np.pi * slot * lag / size
    real, imag = np.cos(angle), -np.sin(angle)
    imag[0] = 0
    real2 = real.copy()
    real2[0] = (-1.0) ** np.arange(size)
    near = (lag < half).astype(np.float64)
    sign = (-1.0) ** slot
    sign2 = sign.copy()
    sign2[0] = 1
    spectra = np.concatenate(
        [real * near, imag * near, real2 * near, real * sign, imag * sign, real2 * sign2], 0
    )
    eye = np.eye(group)
    return np.kron(forward, eye), np.kron(backward, eye), spectra


LANES = 128
GROUP = 8
CHUNK = 8


def prep_kernel(
    own_hbm, w_in_hbm, w_out_hbm, fwd_hbm, bwd_hbm, spec_hbm, filt_hbm, gain_hbm, kernel_hbm, bias_hbm,
    own_ref, w_in_ref, w_out_ref, fwd_ref, bwd_ref, taps_ref, h_ref,
    spec_ref, filt_ref, gain_ref, kernel_ref, bias_ref, sems,
):
    rows, part, _ = own_ref.shape
    start = pl.multiple_of(lax.axis_index("row") * part, part)
    moves = [
        (own_hbm.at[:, pl.ds(start, part), :], own_ref),
        (w_in_hbm, w_in_ref),
        (spec_hbm, spec_ref),
        (filt_hbm, filt_ref),
        (gain_hbm, gain_ref),
        (kernel_hbm, kernel_ref),
        (bias_hbm, bias_ref),
        (fwd_hbm, fwd_ref),
        (bwd_hbm, bwd_ref),
        (w_out_hbm, w_out_ref),
    ]
    copies = [pltpu.make_async_copy(src, dst, sems.at[i]) for i, (src, dst) in enumerate(moves)]
    for copy in copies:
        copy.start()
    for copy in copies:
        copy.wait()
    for a in range(3):
        taps_ref[3 * a : 3 * a + 3, :] = kernel_ref[a].astype(F32)
    taps_ref[9:10, :] = bias_ref[...]
    filt = filt_ref[...]
    h_ref[...] = jnp.dot(spec_ref[0], filt, preferred_element_type=F32) + jnp.dot(
        spec_ref[1], filt, preferred_element_type=F32
    )
    gain = gain_ref[...]
    h_ref[0:rows, :] = h_ref[0:rows, :] + gain
    h_ref[2 * rows : 3 * rows, :] = h_ref[2 * rows : 3 * rows, :] + gain


def edge_terms(tokens, taps, w_in_ref, edge_ref):
    height = tokens.shape[0]
    edge_ref[0:8, :] = jnp.zeros((8, edge_ref.shape[1]), F32)
    edge_ref[8 + height : 16 + height, :] = jnp.zeros((8, edge_ref.shape[1]), F32)
    edge_ref[8 : 8 + height, :] = jnp.dot(tokens, w_in_ref[...], preferred_element_type=F32)
    total = edge_ref[7 : 7 + height, :] * taps[0]
    for a in (1, 2):
        total = total + edge_ref[7 + a : 7 + a + height, :] * taps[a]
    return total


def column_group(mixed, fwd_ref, bwd_ref, w_out_ref, h_ref, prod_ref, z_ref, put):
    height_group, width = prod_ref.shape
    height = height_group // GROUP
    rows = height // 2
    block = rows * GROUP
    for row in range(0, height, 2):
        for base in range(0, width, LANES):
            two = [mixed(r, width + base) * mixed(r, 2 * width + base) for r in (row, row + 1)]
            prod_ref[row * GROUP : (row + 2) * GROUP, base : base + LANES] = jnp.concatenate(
                two, 0
            ).astype(BF16)
    low = jnp.dot(fwd_ref[...], prod_ref[:block], preferred_element_type=F32)
    high = jnp.dot(fwd_ref[...], prod_ref[block:], preferred_element_type=F32)
    for k in range(0, rows, 2):
        parts = [[], [], [], []]
        for s in (k, k + 1):
            near_r, near_i, near_2, all_r, all_i, all_2 = (
                jnp.broadcast_to(h_ref[j * rows + s : j * rows + s + 1, :], (GROUP, width))
                for j in range(6)
            )
            re, im = slice(s * GROUP, (s + 1) * GROUP), slice(block + s * GROUP, block + (s + 1) * GROUP)
            lr, li, hr, hi = low[re], low[im], high[re], high[im]
            parts[0].append(lr * near_r - li * near_i)
            parts[1].append(lr * near_i + li * near_2)
            parts[2].append(lr * all_r - li * all_i + hr * near_r - hi * near_i)
            parts[3].append(lr * all_i + li * all_2 + hr * near_i + hi * near_2)
        for j in range(4):
            at = (j % 2) * block + k * GROUP
            z_ref[j // 2, at : at + 2 * GROUP, :] = jnp.concatenate(parts[j], 0).astype(BF16)
    for h in range(2):
        conv = jnp.dot(bwd_ref[...], z_ref[h], preferred_element_type=F32)
        gated = []
        for r in range(rows):
            line = [
                mixed(h * rows + r, base) * conv[r * GROUP : (r + 1) * GROUP, base : base + LANES]
                for base in range(0, width, LANES)
            ]
            gated.append(jnp.concatenate(line, 1))
        final = jnp.dot(
            jnp.concatenate(gated, 0).astype(BF16), w_out_ref[...], preferred_element_type=F32
        )
        put(h, final.reshape(rows, GROUP, width))


def inner_kernel(
    own_ref, other_ref, within_ref, w_in_ref, taps_ref, fwd_ref, bwd_ref, w_out_ref, h_ref,
    mixed_ref, inner_ref,
    p_ref, edge_ref, u_ref, prod_ref, z_ref,
):
    core = lax.axis_index("row")
    rows, part, width = own_ref.shape
    height = 2 * rows
    start = pl.multiple_of(core * part, part)
    n_group = part // GROUP

    p_ref[0] = jnp.zeros(p_ref.shape[1:], F32)
    p_ref[height + 1] = jnp.zeros(p_ref.shape[1:], F32)
    for at, tokens in (
        (core * rows, own_ref[...]),
        ((1 - core) * rows, other_ref[:, pl.ds(start, part), :]),
    ):
        got = jnp.dot(
            tokens.reshape(rows * part, width), w_in_ref[...], preferred_element_type=F32
        )
        p_ref[pl.ds(at + 1, rows)] = got.reshape(rows, part, 3 * width)

    taps = [
        jnp.where(core == 0, taps_ref[3 * a + 2 : 3 * a + 3, :], taps_ref[3 * a : 3 * a + 1, :])
        for a in range(3)
    ]
    total = edge_terms(within_ref[...], taps, w_in_ref, edge_ref)
    u_ref[1 - core] = total.reshape(height // 8, 8, 3 * width)
    u_ref[core] = jnp.zeros(u_ref.shape[1:], F32)

    sub = lax.broadcasted_iota(jnp.int32, (GROUP, LANES), 0)
    is_first = sub == 0
    is_last = sub == GROUP - 1

    def stage(i, carry):
        row0 = i * CHUNK
        for base in range(0, 3 * width, LANES):
            at = slice(base, base + LANES)
            tap = [
                [
                    jnp.broadcast_to(taps_ref[3 * a + b : 3 * a + b + 1, at], (GROUP, LANES))
                    for b in range(3)
                ]
                for a in range(3)
            ]
            bias = jnp.broadcast_to(taps_ref[9:10, at], (GROUP, LANES))
            loaded = [
                [p_ref[row0 + r, g * GROUP : (g + 1) * GROUP, at] for g in range(n_group)]
                for r in range(CHUNK + 2)
            ]
            for r in range(CHUNK):
                u = [
                    [
                        loaded[r][g] * tap[0][b]
                        + loaded[r + 1][g] * tap[1][b]
                        + loaded[r + 2][g] * tap[2][b]
                        for b in range(3)
                    ]
                    for g in range(n_group)
                ]
                right_turn = [pltpu.roll(u[g][0], 1, 0) for g in range(n_group)]
                left_turn = [pltpu.roll(u[g][2], GROUP - 1, 0) for g in range(n_group)]
                west = jnp.broadcast_to(u_ref[0, i, r : r + 1, at], (GROUP, LANES))
                east = jnp.broadcast_to(u_ref[1, i, r : r + 1, at], (GROUP, LANES))
                for g in range(n_group):
                    before = west if g == 0 else right_turn[g - 1]
                    after = east if g == n_group - 1 else left_turn[g + 1]
                    value = u[g][1] + bias
                    value = value + jnp.where(is_first, before, right_turn[g])
                    value = value + jnp.where(is_last, after, left_turn[g])
                    slot = core if g == 0 else 1 - core
                    mixed_ref[slot, row0 + r, :, at] = value
        return carry

    lax.fori_loop(0, height // CHUNK, stage, 0)

    def put(h, final):
        inner_ref[h * rows : (h + 1) * rows] = final

    column_group(
        lambda r, base: mixed_ref[1, r, :, base : base + LANES],
        fwd_ref, bwd_ref, w_out_ref, h_ref, prod_ref, z_ref, put,
    )


def edge_kernel(
    halo_ref, mixed_ref, inner_ref, w_in_ref, taps_ref, fwd_ref, bwd_ref, w_out_ref, h_ref,
    mine_ref, send_ref,
    edge_ref, u_ref, fix_ref, prod_ref, z_ref, out_ref,
):
    core = lax.axis_index("row")
    rows, part, width = mine_ref.shape
    height = 2 * rows
    taps = [
        jnp.where(core == 0, taps_ref[3 * a : 3 * a + 1, :], taps_ref[3 * a + 2 : 3 * a + 3, :])
        for a in range(3)
    ]
    total = edge_terms(halo_ref[...], taps, w_in_ref, edge_ref)
    u_ref[...] = total.reshape(height // 8, 8, 3 * width)
    sub = lax.broadcasted_iota(jnp.int32, (GROUP, LANES), 0)
    at_edge = sub == core * (GROUP - 1)
    for base in range(0, 3 * width, LANES):
        at = slice(base, base + LANES)
        for r in range(height):
            add = jnp.broadcast_to(u_ref[r // 8, r % 8 : r % 8 + 1, at], (GROUP, LANES))
            fix_ref[r, :, at] = mixed_ref[0, r, :, at] + jnp.where(at_edge, add, 0.0)

    def put(h, final):
        out_ref[core, h * rows : (h + 1) * rows] = final

    column_group(
        lambda r, base: fix_ref[r, :, base : base + LANES],
        fwd_ref, bwd_ref, w_out_ref, h_ref, prod_ref, z_ref, put,
    )
    out_ref[1 - core] = inner_ref[...]
    for ref, at in ((mine_ref, core * rows), (send_ref, (1 - core) * rows)):
        ref[...] = jnp.concatenate(
            [out_ref[g, pl.ds(at, rows)] for g in range(part // GROUP)], 1
        ).astype(BF16)


def store_kernel(mine_ref, full_hbm, sem):
    _, part, _ = mine_ref.shape
    start = pl.multiple_of(lax.axis_index("row") * part, part)
    copy = pltpu.make_async_copy(mine_ref, full_hbm.at[:, pl.ds(start, part), :], sem)
    copy.start()
    copy.wait()


def fill_kernel(full_in, theirs_ref, full_hbm, sem):
    _, part, _ = theirs_ref.shape
    start = pl.multiple_of((1 - lax.axis_index("row")) * part, part)
    copy = pltpu.make_async_copy(theirs_ref, full_hbm.at[:, pl.ds(start, part), :], sem)
    copy.start()
    copy.wait()


def on_device(image_tokens, w_in, conv_kernel, conv_bias, long_filter, skip_gain, w_out):
    rows, cols, width = image_tokens.shape
    part = cols // 2
    height = 2 * rows
    n_col = lax.axis_size("col")
    core = lax.axis_index("row")
    fwd, bwd, spectra = transforms(rows, GROUP)
    spec_hi = spectra.astype(BF16)
    spec_lo = (spectra - spec_hi.astype(np.float64)).astype(BF16)
    spec = np.stack([spec_hi, spec_lo])
    vmem = pl.BlockSpec(memory_space=pltpu.VMEM)
    hbm = pl.BlockSpec(memory_space=pltpu.HBM)
    shape = jax.ShapeDtypeStruct
    limit = pltpu.CompilerParams(vmem_limit_bytes=24 * 1024 * 1024)

    swap = [(0, 1), (1, 0)]
    rowmajor = Layout((0, 1, 2))
    image_tokens = with_layout_constraint(image_tokens, rowmajor)
    other = with_layout_constraint(lax.ppermute(image_tokens, "row", swap), rowmajor)

    def keep(array):
        return pltpu.with_memory_space_constraint(array, pltpu.HBM)

    own, w_in_v, w_out_v, fwd_v, bwd_v, taps, spectrum = pl.pallas_call(
        prep_kernel,
        out_shape=(
            shape((rows, part, width), BF16),
            shape(w_in.shape, BF16),
            shape(w_out.shape, BF16),
            shape(fwd.shape, BF16),
            shape(bwd.shape, BF16),
            shape((16, 3 * width), F32),
            shape((6 * rows, width), F32),
        ),
        in_specs=[hbm] * 10,
        out_specs=(vmem,) * 7,
        scratch_shapes=[
            pltpu.VMEM(spec.shape, BF16),
            pltpu.VMEM(long_filter.shape, BF16),
            pltpu.VMEM((1, width), F32),
            pltpu.VMEM(conv_kernel.shape, BF16),
            pltpu.VMEM((1, 3 * width), F32),
            pltpu.SemaphoreType.DMA((10,)),
        ],
        compiler_params=limit,
        cost_estimate=pl.CostEstimate(flops=0, bytes_accessed=3 * 1024 * 1024, transcendentals=0),
    )(
        keep(image_tokens), keep(w_in), keep(w_out), keep(fwd.astype(BF16)), keep(bwd.astype(BF16)),
        keep(spec), keep(long_filter), keep(skip_gain[None]), keep(conv_kernel), keep(conv_bias[None]),
    )

    def by_core(low, high):
        return jnp.where(core == 0, low, high)

    def column(low, high):
        mine = by_core(image_tokens[:, low], image_tokens[:, high])
        theirs = by_core(other[:, low], other[:, high])
        return jnp.concatenate([by_core(mine, theirs), by_core(theirs, mine)], 0)

    pairs = []
    for j in range(n_col - 1):
        pairs += [(n_col + j, j + 1), (j + 1, n_col + j)]
    halo = lax.ppermute(column(0, cols - 1), ("row", "col"), pairs)
    within = column(part, part - 1)
    mixed, inner = pl.pallas_call(
        inner_kernel,
        out_shape=(
            shape((2, height, GROUP, 3 * width), F32),
            shape((height, GROUP, width), F32),
        ),
        in_specs=[vmem] * 9,
        out_specs=(vmem,) * 2,
        scratch_shapes=[
            pltpu.VMEM((height + 2, part, 3 * width), F32),
            pltpu.VMEM((height + 16, 3 * width), F32),
            pltpu.VMEM((2, height // 8, 8, 3 * width), F32),
            pltpu.VMEM((height * GROUP, width), BF16),
            pltpu.VMEM((2, 2 * rows * GROUP, width), BF16),
        ],
        compiler_params=limit,
        cost_estimate=pl.CostEstimate(flops=10**9, bytes_accessed=12 * 1024 * 1024, transcendentals=0),
    )(own, other, within, w_in_v, taps, fwd_v, bwd_v, w_out_v, spectrum)
    half_shape = shape((rows, part, width), BF16)
    mine, send = pl.pallas_call(
        edge_kernel,
        out_shape=(half_shape, half_shape),
        in_specs=[vmem] * 9,
        out_specs=(vmem, vmem),
        scratch_shapes=[
            pltpu.VMEM((height + 16, 3 * width), F32),
            pltpu.VMEM((height // 8, 8, 3 * width), F32),
            pltpu.VMEM((height, GROUP, 3 * width), F32),
            pltpu.VMEM((height * GROUP, width), BF16),
            pltpu.VMEM((2, 2 * rows * GROUP, width), BF16),
            pltpu.VMEM((2, height, GROUP, width), F32),
        ],
        compiler_params=limit,
        cost_estimate=pl.CostEstimate(flops=3 * 10**8, bytes_accessed=4 * 1024 * 1024, transcendentals=0),
    )(halo, mixed, inner, w_in_v, taps, fwd_v, bwd_v, w_out_v, spectrum)
    theirs = lax.ppermute(send, "row", swap)
    full_shape = shape((rows, cols, width), BF16)
    full = pl.pallas_call(
        store_kernel,
        out_shape=full_shape,
        in_specs=[vmem],
        out_specs=hbm,
        scratch_shapes=[pltpu.SemaphoreType.DMA],
        cost_estimate=pl.CostEstimate(flops=0, bytes_accessed=512 * 1024, transcendentals=0),
    )(mine)
    return pl.pallas_call(
        fill_kernel,
        out_shape=full_shape,
        in_specs=[hbm, vmem],
        out_specs=hbm,
        scratch_shapes=[pltpu.SemaphoreType.DMA],
        input_output_aliases={0: 0},
        cost_estimate=pl.CostEstimate(flops=0, bytes_accessed=512 * 1024, transcendentals=0),
    )(full, theirs)


def solution(mesh):
    in_specs = (P("row", "col", None), P(), P(), P(), P(), P(), P())
    out_specs = P("row", "col", None)
    return jax.shard_map(
        on_device, mesh=mesh, in_specs=in_specs, out_specs=out_specs, check_vma=False
    )
```

```python
import jax
import jax.numpy as jnp
import numpy as np
from jax import lax
from jax.experimental import pallas as pl
from jax.experimental.layout import Layout, with_layout_constraint
from jax.experimental.pallas import tpu as pltpu
from jax.sharding import PartitionSpec as P

F32 = jnp.float32
BF16 = jnp.bfloat16


def transforms(half, group):
    size = 2 * half
    slot = np.arange(half)[:, None]
    pos = np.arange(half)[None, :]
    angle = 2 * np.pi * slot * pos / size
    real, imag = np.cos(angle), -np.sin(angle)
    imag[0] = (-1.0) ** np.arange(half)
    forward = np.concatenate([real, imag], 0)
    back_real = 2 * np.cos(angle.T) / size
    back_real[:, 0] = 1 / size
    back_imag = -2 * np.sin(angle.T) / size
    back_imag[:, 0] = (-1.0) ** np.arange(half) / size
    backward = np.concatenate([back_real, back_imag], 1)
    lag = np.arange(size)[None, :]
    angle = 2 * np.pi * slot * lag / size
    real, imag = np.cos(angle), -np.sin(angle)
    imag[0] = 0
    real2 = real.copy()
    real2[0] = (-1.0) ** np.arange(size)
    near = (lag < half).astype(np.float64)
    sign = (-1.0) ** slot
    sign2 = sign.copy()
    sign2[0] = 1
    spectra = np.concatenate(
        [real * near, imag * near, real2 * near, real * sign, imag * sign, real2 * sign2], 0
    )
    eye = np.eye(group)
    return np.kron(forward, eye), np.kron(backward, eye), spectra


LANES = 128
GROUP = 8
CHUNK = 8


def prep_kernel(
    own_hbm, w_in_hbm, w_out_hbm, fwd_hbm, bwd_hbm, spec_hbm, filt_hbm, gain_hbm, kernel_hbm, bias_hbm,
    own_ref, w_in_ref, w_out_ref, fwd_ref, bwd_ref, taps_ref, h_ref,
    spec_ref, filt_ref, gain_ref, kernel_ref, bias_ref, sems,
):
    rows = own_ref.shape[0]
    moves = [
        (own_hbm, own_ref),
        (w_in_hbm, w_in_ref),
        (spec_hbm, spec_ref),
        (filt_hbm, filt_ref),
        (gain_hbm, gain_ref),
        (kernel_hbm, kernel_ref),
        (bias_hbm, bias_ref),
        (fwd_hbm, fwd_ref),
        (bwd_hbm, bwd_ref),
        (w_out_hbm, w_out_ref),
    ]
    copies = [pltpu.make_async_copy(src, dst, sems.at[i]) for i, (src, dst) in enumerate(moves)]
    for copy in copies:
        copy.start()
    for copy in copies:
        copy.wait()
    for a in range(3):
        taps_ref[3 * a : 3 * a + 3, :] = kernel_ref[a].astype(F32)
    taps_ref[9, :] = bias_ref[...]
    filt = filt_ref[...]
    h_ref[...] = jnp.dot(spec_ref[0], filt, preferred_element_type=F32) + jnp.dot(
        spec_ref[1], filt, preferred_element_type=F32
    )
    gain = gain_ref[...]
    h_ref[0:rows, :] = h_ref[0:rows, :] + gain
    h_ref[2 * rows : 3 * rows, :] = h_ref[2 * rows : 3 * rows, :] + gain


def edge_terms(tokens, taps, w_in_ref, edge_ref):
    height = tokens.shape[0]
    edge_ref[0:8, :] = jnp.zeros((8, edge_ref.shape[1]), F32)
    edge_ref[8 + height : 16 + height, :] = jnp.zeros((8, edge_ref.shape[1]), F32)
    edge_ref[8 : 8 + height, :] = jnp.dot(tokens, w_in_ref[...], preferred_element_type=F32)
    total = edge_ref[7 : 7 + height, :] * taps[0]
    for a in (1, 2):
        total = total + edge_ref[7 + a : 7 + a + height, :] * taps[a]
    return total


def column_group(mixed, fwd_ref, bwd_ref, w_out_ref, h_ref, prod_ref, z_ref, put):
    height_group, width = prod_ref.shape
    height = height_group // GROUP
    rows = height // 2
    block = rows * GROUP
    for row in range(0, height, 2):
        for base in range(0, width, LANES):
            two = [mixed(r, width + base) * mixed(r, 2 * width + base) for r in (row, row + 1)]
            prod_ref[row * GROUP : (row + 2) * GROUP, base : base + LANES] = jnp.concatenate(
                two, 0
            ).astype(BF16)
    low = jnp.dot(fwd_ref[...], prod_ref[:block], preferred_element_type=F32)
    high = jnp.dot(fwd_ref[...], prod_ref[block:], preferred_element_type=F32)
    for k in range(0, rows, 2):
        parts = [[], [], [], []]
        for s in (k, k + 1):
            near_r, near_i, near_2, all_r, all_i, all_2 = (
                jnp.broadcast_to(h_ref[j * rows + s : j * rows + s + 1, :], (GROUP, width))
                for j in range(6)
            )
            re, im = slice(s * GROUP, (s + 1) * GROUP), slice(block + s * GROUP, block + (s + 1) * GROUP)
            lr, li, hr, hi = low[re], low[im], high[re], high[im]
            parts[0].append(lr * near_r - li * near_i)
            parts[1].append(lr * near_i + li * near_2)
            parts[2].append(lr * all_r - li * all_i + hr * near_r - hi * near_i)
            parts[3].append(lr * all_i + li * all_2 + hr * near_i + hi * near_2)
        for j in range(4):
            at = (j % 2) * block + k * GROUP
            z_ref[j // 2, at : at + 2 * GROUP, :] = jnp.concatenate(parts[j], 0).astype(BF16)
    for h in range(2):
        conv = jnp.dot(bwd_ref[...], z_ref[h], preferred_element_type=F32)
        gated = []
        for r in range(rows):
            line = [
                mixed(h * rows + r, base) * conv[r * GROUP : (r + 1) * GROUP, base : base + LANES]
                for base in range(0, width, LANES)
            ]
            gated.append(jnp.concatenate(line, 1))
        final = jnp.dot(
            jnp.concatenate(gated, 0).astype(BF16), w_out_ref[...], preferred_element_type=F32
        )
        put(h, final.reshape(rows, GROUP, width))


def inner_kernel(
    own_ref, other_ref, within_ref, w_in_ref, taps_ref, fwd_ref, bwd_ref, w_out_ref, h_ref,
    mixed_ref, inner_ref,
    p_ref, edge_ref, u_ref, prod_ref, z_ref,
):
    core = lax.axis_index("row")
    rows, cols, width = own_ref.shape
    part = cols // 2
    height = 2 * rows
    start = pl.multiple_of(core * part, part)
    n_group = part // GROUP

    p_ref[0] = jnp.zeros(p_ref.shape[1:], F32)
    p_ref[height + 1] = jnp.zeros(p_ref.shape[1:], F32)
    for at, tokens in (
        (core * rows, own_ref[:, pl.ds(start, part), :]),
        ((1 - core) * rows, other_ref[:, pl.ds(start, part), :]),
    ):
        got = jnp.dot(
            tokens.reshape(rows * part, width), w_in_ref[...], preferred_element_type=F32
        )
        p_ref[pl.ds(at + 1, rows)] = got.reshape(rows, part, 3 * width)

    taps = [
        jnp.where(core == 0, taps_ref[3 * a + 2 : 3 * a + 3, :], taps_ref[3 * a : 3 * a + 1, :])
        for a in range(3)
    ]
    total = edge_terms(within_ref[...], taps, w_in_ref, edge_ref)
    u_ref[1 - core] = total.reshape(height // 8, 8, 3 * width)
    u_ref[core] = jnp.zeros(u_ref.shape[1:], F32)

    sub = lax.broadcasted_iota(jnp.int32, (GROUP, LANES), 0)
    is_first = sub == 0
    is_last = sub == GROUP - 1

    def stage(i, carry):
        row0 = i * CHUNK
        for base in range(0, 3 * width, LANES):
            at = slice(base, base + LANES)
            tap = [
                [
                    jnp.broadcast_to(taps_ref[3 * a + b : 3 * a + b + 1, at], (GROUP, LANES))
                    for b in range(3)
                ]
                for a in range(3)
            ]
            bias = jnp.broadcast_to(taps_ref[9:10, at], (GROUP, LANES))
            loaded = [
                [p_ref[row0 + r, g * GROUP : (g + 1) * GROUP, at] for g in range(n_group)]
                for r in range(CHUNK + 2)
            ]
            for r in range(CHUNK):
                u = [
                    [
                        loaded[r][g] * tap[0][b]
                        + loaded[r + 1][g] * tap[1][b]
                        + loaded[r + 2][g] * tap[2][b]
                        for b in range(3)
                    ]
                    for g in range(n_group)
                ]
                right_turn = [pltpu.roll(u[g][0], 1, 0) for g in range(n_group)]
                left_turn = [pltpu.roll(u[g][2], GROUP - 1, 0) for g in range(n_group)]
                west = jnp.broadcast_to(u_ref[0, i, r : r + 1, at], (GROUP, LANES))
                east = jnp.broadcast_to(u_ref[1, i, r : r + 1, at], (GROUP, LANES))
                for g in range(n_group):
                    before = west if g == 0 else right_turn[g - 1]
                    after = east if g == n_group - 1 else left_turn[g + 1]
                    value = u[g][1] + bias
                    value = value + jnp.where(is_first, before, right_turn[g])
                    value = value + jnp.where(is_last, after, left_turn[g])
                    slot = core if g == 0 else 1 - core
                    mixed_ref[slot, row0 + r, :, at] = value
        return carry

    lax.fori_loop(0, height // CHUNK, stage, 0)

    def put(h, final):
        inner_ref[h * rows : (h + 1) * rows] = final

    column_group(
        lambda r, base: mixed_ref[1, r, :, base : base + LANES],
        fwd_ref, bwd_ref, w_out_ref, h_ref, prod_ref, z_ref, put,
    )


def edge_kernel(
    halo_ref, mixed_ref, inner_ref, w_in_ref, taps_ref, fwd_ref, bwd_ref, w_out_ref, h_ref,
    mine_ref, send_ref,
    edge_ref, u_ref, fix_ref, prod_ref, z_ref, out_ref,
):
    core = lax.axis_index("row")
    rows, part, width = mine_ref.shape
    height = 2 * rows
    taps = [
        jnp.where(core == 0, taps_ref[3 * a : 3 * a + 1, :], taps_ref[3 * a + 2 : 3 * a + 3, :])
        for a in range(3)
    ]
    total = edge_terms(halo_ref[...], taps, w_in_ref, edge_ref)
    u_ref[...] = total.reshape(height // 8, 8, 3 * width)
    sub = lax.broadcasted_iota(jnp.int32, (GROUP, LANES), 0)
    at_edge = sub == core * (GROUP - 1)
    for base in range(0, 3 * width, LANES):
        at = slice(base, base + LANES)
        for r in range(height):
            add = jnp.broadcast_to(u_ref[r // 8, r % 8 : r % 8 + 1, at], (GROUP, LANES))
            fix_ref[r, :, at] = mixed_ref[0, r, :, at] + jnp.where(at_edge, add, 0.0)

    def put(h, final):
        out_ref[core, h * rows : (h + 1) * rows] = final

    column_group(
        lambda r, base: fix_ref[r, :, base : base + LANES],
        fwd_ref, bwd_ref, w_out_ref, h_ref, prod_ref, z_ref, put,
    )
    out_ref[1 - core] = inner_ref[...]
    for ref, at in ((mine_ref, core * rows), (send_ref, (1 - core) * rows)):
        ref[...] = jnp.concatenate(
            [out_ref[g, pl.ds(at, rows)] for g in range(part // GROUP)], 1
        ).astype(BF16)


def on_device(image_tokens, w_in, conv_kernel, conv_bias, long_filter, skip_gain, w_out):
    rows, cols, width = image_tokens.shape
    part = cols // 2
    height = 2 * rows
    n_col = lax.axis_size("col")
    core = lax.axis_index("row")
    fwd, bwd, spectra = transforms(rows, GROUP)
    spec_hi = spectra.astype(BF16)
    spec_lo = (spectra - spec_hi.astype(np.float64)).astype(BF16)
    spec = np.stack([spec_hi, spec_lo])
    vmem = pl.BlockSpec(memory_space=pltpu.VMEM)
    hbm = pl.BlockSpec(memory_space=pltpu.HBM)
    shape = jax.ShapeDtypeStruct
    limit = pltpu.CompilerParams(vmem_limit_bytes=24 * 1024 * 1024)

    swap = [(0, 1), (1, 0)]
    rowmajor = Layout((0, 1, 2))
    image_tokens = with_layout_constraint(image_tokens, rowmajor)
    other = with_layout_constraint(lax.ppermute(image_tokens, "row", swap), rowmajor)

    def keep(array):
        return pltpu.with_memory_space_constraint(array, pltpu.HBM)

    block, w_in_v, w_out_v, fwd_v, bwd_v, taps, spectrum = pl.pallas_call(
        prep_kernel,
        out_shape=(
            shape(image_tokens.shape, BF16),
            shape(w_in.shape, BF16),
            shape(w_out.shape, BF16),
            shape(fwd.shape, BF16),
            shape(bwd.shape, BF16),
            shape((16, 3 * width), F32),
            shape((6 * rows, width), F32),
        ),
        in_specs=[hbm] * 10,
        out_specs=(vmem,) * 7,
        scratch_shapes=[
            pltpu.VMEM(spec.shape, BF16),
            pltpu.VMEM(long_filter.shape, BF16),
            pltpu.VMEM((1, width), F32),
            pltpu.VMEM(conv_kernel.shape, BF16),
            pltpu.VMEM(conv_bias.shape, F32),
            pltpu.SemaphoreType.DMA((10,)),
        ],
        compiler_params=limit,
        cost_estimate=pl.CostEstimate(flops=0, bytes_accessed=3 * 1024 * 1024, transcendentals=0),
    )(
        keep(image_tokens), keep(w_in), keep(w_out), keep(fwd.astype(BF16)), keep(bwd.astype(BF16)),
        keep(spec), keep(long_filter), keep(skip_gain[None]), keep(conv_kernel), keep(conv_bias),
    )

    own = with_layout_constraint(block, rowmajor)

    def by_core(low, high):
        return jnp.where(core == 0, low, high)

    def column(low, high):
        mine = by_core(own[:, low], own[:, high])
        theirs = by_core(other[:, low], other[:, high])
        return jnp.concatenate([by_core(mine, theirs), by_core(theirs, mine)], 0)

    pairs = []
    for j in range(n_col - 1):
        pairs += [(n_col + j, j + 1), (j + 1, n_col + j)]
    halo = lax.ppermute(column(0, cols - 1), ("row", "col"), pairs)
    within = column(part, part - 1)
    mixed, inner = pl.pallas_call(
        inner_kernel,
        out_shape=(
            shape((2, height, GROUP, 3 * width), F32),
            shape((height, GROUP, width), F32),
        ),
        in_specs=[vmem] * 9,
        out_specs=(vmem,) * 2,
        scratch_shapes=[
            pltpu.VMEM((height + 2, part, 3 * width), F32),
            pltpu.VMEM((height + 16, 3 * width), F32),
            pltpu.VMEM((2, height // 8, 8, 3 * width), F32),
            pltpu.VMEM((height * GROUP, width), BF16),
            pltpu.VMEM((2, 2 * rows * GROUP, width), BF16),
        ],
        compiler_params=limit,
        cost_estimate=pl.CostEstimate(flops=10**9, bytes_accessed=12 * 1024 * 1024, transcendentals=0),
    )(own, other, within, w_in_v, taps, fwd_v, bwd_v, w_out_v, spectrum)
    half_shape = shape((rows, part, width), BF16)
    mine, send = pl.pallas_call(
        edge_kernel,
        out_shape=(half_shape, half_shape),
        in_specs=[vmem] * 9,
        out_specs=(vmem, vmem),
        scratch_shapes=[
            pltpu.VMEM((height + 16, 3 * width), F32),
            pltpu.VMEM((height // 8, 8, 3 * width), F32),
            pltpu.VMEM((height, GROUP, 3 * width), F32),
            pltpu.VMEM((height * GROUP, width), BF16),
            pltpu.VMEM((2, 2 * rows * GROUP, width), BF16),
            pltpu.VMEM((2, height, GROUP, width), F32),
        ],
        compiler_params=limit,
        cost_estimate=pl.CostEstimate(flops=3 * 10**8, bytes_accessed=4 * 1024 * 1024, transcendentals=0),
    )(halo, mixed, inner, w_in_v, taps, fwd_v, bwd_v, w_out_v, spectrum)
    theirs = lax.ppermute(send, "row", swap)
    return by_core(jnp.concatenate([mine, theirs], 1), jnp.concatenate([theirs, mine], 1))


def solution(mesh):
    in_specs = (P("row", "col", None), P(), P(), P(), P(), P(), P())
    out_specs = P("row", "col", None)
    return jax.shard_map(
        on_device, mesh=mesh, in_specs=in_specs, out_specs=out_specs, check_vma=False
    )
```

```python
import jax
import jax.numpy as jnp
import numpy as np
from jax import lax
from jax.experimental import pallas as pl
from jax.experimental.layout import Layout, with_layout_constraint
from jax.experimental.pallas import tpu as pltpu
from jax.sharding import PartitionSpec as P

F32 = jnp.float32
BF16 = jnp.bfloat16


def transforms(half, group):
    size = 2 * half
    slot = np.arange(half)[:, None]
    pos = np.arange(half)[None, :]
    angle = 2 * np.pi * slot * pos / size
    real, imag = np.cos(angle), -np.sin(angle)
    imag[0] = (-1.0) ** np.arange(half)
    forward = np.concatenate([real, imag], 0)
    back_real = 2 * np.cos(angle.T) / size
    back_real[:, 0] = 1 / size
    back_imag = -2 * np.sin(angle.T) / size
    back_imag[:, 0] = (-1.0) ** np.arange(half) / size
    backward = np.concatenate([back_real, back_imag], 1)
    lag = np.arange(size)[None, :]
    angle = 2 * np.pi * slot * lag / size
    real, imag = np.cos(angle), -np.sin(angle)
    imag[0] = 0
    real2 = real.copy()
    real2[0] = (-1.0) ** np.arange(size)
    near = (lag < half).astype(np.float64)
    sign = (-1.0) ** slot
    sign2 = sign.copy()
    sign2[0] = 1
    spectra = np.concatenate(
        [real * near, imag * near, real2 * near, real * sign, imag * sign, real2 * sign2], 0
    )
    eye = np.eye(group)
    return np.kron(forward, eye), np.kron(backward, eye), spectra


LANES = 128
GROUP = 8
CHUNK = 8


def prep_kernel(
    own_hbm, w_in_hbm, w_out_hbm, fwd_hbm, bwd_hbm, spec_hbm, filt_hbm, gain_hbm, kernel_hbm, bias_hbm,
    own_ref, w_in_ref, w_out_ref, fwd_ref, bwd_ref, taps_ref, h_ref,
    spec_ref, filt_ref, gain_ref, kernel_ref, bias_ref, sems,
):
    rows = own_ref.shape[0]
    moves = [
        (own_hbm, own_ref),
        (w_in_hbm, w_in_ref),
        (spec_hbm, spec_ref),
        (filt_hbm, filt_ref),
        (gain_hbm, gain_ref),
        (kernel_hbm, kernel_ref),
        (bias_hbm, bias_ref),
        (fwd_hbm, fwd_ref),
        (bwd_hbm, bwd_ref),
        (w_out_hbm, w_out_ref),
    ]
    copies = [pltpu.make_async_copy(src, dst, sems.at[i]) for i, (src, dst) in enumerate(moves)]
    for copy in copies:
        copy.start()
    for copy in copies:
        copy.wait()
    for a in range(3):
        taps_ref[3 * a : 3 * a + 3, :] = kernel_ref[a].astype(F32)
    taps_ref[9, :] = bias_ref[...]
    filt = filt_ref[...]
    h_ref[...] = jnp.dot(spec_ref[0], filt, preferred_element_type=F32) + jnp.dot(
        spec_ref[1], filt, preferred_element_type=F32
    )
    gain = gain_ref[...]
    h_ref[0:rows, :] = h_ref[0:rows, :] + gain
    h_ref[2 * rows : 3 * rows, :] = h_ref[2 * rows : 3 * rows, :] + gain


def edge_terms(tokens, taps, w_in_ref, edge_ref):
    height = tokens.shape[0]
    edge_ref[0:8, :] = jnp.zeros((8, edge_ref.shape[1]), F32)
    edge_ref[8 + height : 16 + height, :] = jnp.zeros((8, edge_ref.shape[1]), F32)
    edge_ref[8 : 8 + height, :] = jnp.dot(tokens, w_in_ref[...], preferred_element_type=F32)
    total = edge_ref[7 : 7 + height, :] * taps[0]
    for a in (1, 2):
        total = total + edge_ref[7 + a : 7 + a + height, :] * taps[a]
    return total.reshape(height // 8, 8, edge_ref.shape[1])


def column_taps(taps_ref, core, on_core0):
    first, second = on_core0, 2 - on_core0
    return [
        jnp.where(
            core == 0,
            taps_ref[3 * a + first : 3 * a + first + 1, :],
            taps_ref[3 * a + second : 3 * a + second + 1, :],
        )
        for a in range(3)
    ]


def depthwise_steps(load, side_ref, taps_ref, chunk, store, bases):
    sub = lax.broadcasted_iota(jnp.int32, (GROUP, LANES), 0)
    is_first = sub == 0
    is_last = sub == GROUP - 1
    for base in bases:
        at = slice(base, base + LANES)
        tap = [
            [
                jnp.broadcast_to(taps_ref[3 * a + b : 3 * a + b + 1, at], (GROUP, LANES))
                for b in range(3)
            ]
            for a in range(3)
        ]
        bias = jnp.broadcast_to(taps_ref[9:10, at], (GROUP, LANES))
        loaded = [load(chunk * CHUNK + r, at) for r in range(CHUNK + 2)]
        for r in range(CHUNK):
            u = [
                loaded[r] * tap[0][b] + loaded[r + 1] * tap[1][b] + loaded[r + 2] * tap[2][b]
                for b in range(3)
            ]
            west = jnp.broadcast_to(side_ref[0, chunk, r : r + 1, at], (GROUP, LANES))
            east = jnp.broadcast_to(side_ref[1, chunk, r : r + 1, at], (GROUP, LANES))
            value = u[1] + bias
            value = value + jnp.where(is_first, west, pltpu.roll(u[0], 1, 0))
            value = value + jnp.where(is_last, east, pltpu.roll(u[2], GROUP - 1, 0))
            store(chunk * CHUNK + r, at, value)
        yield


def conv_steps(mixed, fwd_ref, bwd_ref, w_out_ref, h_ref, prod_ref, z_ref, put):
    height_group, width = prod_ref.shape
    height = height_group // GROUP
    rows = height // 2
    block = rows * GROUP
    spectra = []
    for h in range(2):
        for row in range(h * rows, (h + 1) * rows, 2):
            for base in range(0, width, LANES):
                two = [mixed(r, width + base) * mixed(r, 2 * width + base) for r in (row, row + 1)]
                prod_ref[row * GROUP : (row + 2) * GROUP, base : base + LANES] = jnp.concatenate(
                    two, 0
                ).astype(BF16)
            if row % 8 == 6:
                yield
        spectra.append(
            jnp.dot(
                fwd_ref[...], prod_ref[h * block : (h + 1) * block], preferred_element_type=F32
            )
        )
        yield
    low, high = spectra
    for k in range(0, rows, 2):
        parts = [[], [], [], []]
        for s in (k, k + 1):
            near_r, near_i, near_2, all_r, all_i, all_2 = (
                jnp.broadcast_to(h_ref[j * rows + s : j * rows + s + 1, :], (GROUP, width))
                for j in range(6)
            )
            re, im = slice(s * GROUP, (s + 1) * GROUP), slice(block + s * GROUP, block + (s + 1) * GROUP)
            lr, li, hr, hi = low[re], low[im], high[re], high[im]
            parts[0].append(lr * near_r - li * near_i)
            parts[1].append(lr * near_i + li * near_2)
            parts[2].append(lr * all_r - li * all_i + hr * near_r - hi * near_i)
            parts[3].append(lr * all_i + li * all_2 + hr * near_i + hi * near_2)
        for j in range(4):
            at = (j % 2) * block + k * GROUP
            z_ref[j // 2, at : at + 2 * GROUP, :] = jnp.concatenate(parts[j], 0).astype(BF16)
        if k % 4 == 2:
            yield
    convs = []
    for h in range(2):
        convs.append(jnp.dot(bwd_ref[...], z_ref[h], preferred_element_type=F32))
        yield
    for h in range(2):
        gated = []
        for r in range(rows):
            line = [
                mixed(h * rows + r, base) * convs[h][r * GROUP : (r + 1) * GROUP, base : base + LANES]
                for base in range(0, width, LANES)
            ]
            gated.append(jnp.concatenate(line, 1))
        final = jnp.dot(
            jnp.concatenate(gated, 0).astype(BF16), w_out_ref[...], preferred_element_type=F32
        )
        put(h, final.reshape(rows, GROUP, width))
        yield


def split_halves(out_ref, core, mine_ref, send_ref):
    mine_ref[...] = out_ref[core].astype(BF16)
    send_ref[...] = out_ref[1 - core].astype(BF16)


def inner_kernel(
    own_ref, other_ref, near_ref, far_ref, edge_near_ref,
    w_in_ref, taps_ref, fwd_ref, bwd_ref, w_out_ref, h_ref,
    edge_mixed_ref, mine_ref, send_ref,
    p_ref, strip_ref, side_ref, edge_side_ref, mixed_ref, prod_ref, z_ref, out_ref,
):
    core = lax.axis_index("row")
    rows, cols, width = own_ref.shape
    part = cols // 2
    height = 2 * rows
    start = pl.multiple_of(core * part, part)

    for slot in range(2):
        p_ref[slot, 0] = jnp.zeros((GROUP, 3 * width), F32)
        p_ref[slot, height + 1] = jnp.zeros((GROUP, 3 * width), F32)
    for row, ref in ((core * rows, own_ref), ((1 - core) * rows, other_ref)):
        tokens = ref[:, pl.ds(start, part), :].reshape(rows * part, width)
        got = jnp.dot(tokens, w_in_ref[...], preferred_element_type=F32)
        got = got.reshape(rows, part, 3 * width)
        p_ref[core, pl.ds(row + 1, rows)] = got[:, :GROUP]
        p_ref[1 - core, pl.ds(row + 1, rows)] = got[:, GROUP:]

    side_ref[core] = edge_terms(
        near_ref[...], column_taps(taps_ref, core, 0), w_in_ref, strip_ref.at[0]
    )
    side_ref[1 - core] = edge_terms(
        far_ref[...], column_taps(taps_ref, core, 2), w_in_ref, strip_ref.at[1]
    )
    edge_side_ref[1 - core] = edge_terms(
        edge_near_ref[...], column_taps(taps_ref, core, 2), w_in_ref, strip_ref.at[2]
    )
    edge_side_ref[core] = jnp.zeros(edge_side_ref.shape[1:], F32)

    def store_inner(row, at, value):
        mixed_ref[row, :, at] = value

    def inner_chunk(i, carry):
        steps = depthwise_steps(
            lambda row, at: p_ref[1, row, :, at], side_ref, taps_ref, i, store_inner,
            range(0, 3 * width, LANES),
        )
        for _ in steps:
            pass
        return carry

    lax.fori_loop(0, height // CHUNK, inner_chunk, 0)

    def store_edge(row, at, value):
        edge_mixed_ref[row, :, at] = value

    def put(h, final):
        out_ref[h] = final

    edge = [
        depthwise_steps(
            lambda row, at: p_ref[0, row, :, at], edge_side_ref, taps_ref, i, store_edge, [base]
        )
        for i in range(height // CHUNK)
        for base in range(0, 3 * width, LANES)
    ]
    conv = conv_steps(
        lambda r, base: mixed_ref[r, :, base : base + LANES],
        fwd_ref, bwd_ref, w_out_ref, h_ref, prod_ref, z_ref, put,
    )
    done = 0
    for _ in conv:
        for step in edge[done : done + 2]:
            for _ in step:
                pass
        done += 2
    for step in edge[done:]:
        for _ in step:
            pass
    split_halves(out_ref, core, mine_ref, send_ref)


def edge_kernel(
    halo_ref, mixed_ref, w_in_ref, taps_ref, fwd_ref, bwd_ref, w_out_ref, h_ref,
    mine_ref, send_ref,
    strip_ref, side_ref, prod_ref, z_ref, out_ref,
):
    core = lax.axis_index("row")
    side_ref[...] = edge_terms(
        halo_ref[...], column_taps(taps_ref, core, 0), w_in_ref, strip_ref
    )
    sub = lax.broadcasted_iota(jnp.int32, (GROUP, LANES), 0)
    at_edge = sub == core * (GROUP - 1)

    def mixed(r, base):
        at = slice(base, base + LANES)
        add = jnp.broadcast_to(side_ref[r // 8, r % 8 : r % 8 + 1, at], (GROUP, LANES))
        return mixed_ref[r, :, at] + jnp.where(at_edge, add, 0.0)

    def put(h, final):
        out_ref[h] = final

    for _ in conv_steps(
        mixed, fwd_ref, bwd_ref, w_out_ref, h_ref, prod_ref, z_ref, put
    ):
        pass
    split_halves(out_ref, core, mine_ref, send_ref)


def on_device(image_tokens, w_in, conv_kernel, conv_bias, long_filter, skip_gain, w_out):
    rows, cols, width = image_tokens.shape
    part = cols // 2
    height = 2 * rows
    n_col = lax.axis_size("col")
    core = lax.axis_index("row")
    fwd, bwd, spectra = transforms(rows, GROUP)
    spec_hi = spectra.astype(BF16)
    spec_lo = (spectra - spec_hi.astype(np.float64)).astype(BF16)
    spec = np.stack([spec_hi, spec_lo])
    vmem = pl.BlockSpec(memory_space=pltpu.VMEM)
    hbm = pl.BlockSpec(memory_space=pltpu.HBM)
    shape = jax.ShapeDtypeStruct
    limit = pltpu.CompilerParams(vmem_limit_bytes=24 * 1024 * 1024)

    swap = [(0, 1), (1, 0)]
    rowmajor = Layout((0, 1, 2))
    image_tokens = with_layout_constraint(image_tokens, rowmajor)
    other = with_layout_constraint(lax.ppermute(image_tokens, "row", swap), rowmajor)

    def keep(array):
        return pltpu.with_memory_space_constraint(array, pltpu.HBM)

    block, w_in_v, w_out_v, fwd_v, bwd_v, taps, spectrum = pl.pallas_call(
        prep_kernel,
        out_shape=(
            shape(image_tokens.shape, BF16),
            shape(w_in.shape, BF16),
            shape(w_out.shape, BF16),
            shape(fwd.shape, BF16),
            shape(bwd.shape, BF16),
            shape((16, 3 * width), F32),
            shape((6 * rows, width), F32),
        ),
        in_specs=[hbm] * 10,
        out_specs=(vmem,) * 7,
        scratch_shapes=[
            pltpu.VMEM(spec.shape, BF16),
            pltpu.VMEM(long_filter.shape, BF16),
            pltpu.VMEM((1, width), F32),
            pltpu.VMEM(conv_kernel.shape, BF16),
            pltpu.VMEM(conv_bias.shape, F32),
            pltpu.SemaphoreType.DMA((10,)),
        ],
        compiler_params=limit,
        cost_estimate=pl.CostEstimate(flops=0, bytes_accessed=3 * 1024 * 1024, transcendentals=0),
    )(
        keep(image_tokens), keep(w_in), keep(w_out), keep(fwd.astype(BF16)), keep(bwd.astype(BF16)),
        keep(spec), keep(long_filter), keep(skip_gain[None]), keep(conv_kernel), keep(conv_bias),
    )

    own = block

    def by_core(low, high):
        return jnp.where(core == 0, low, high)

    def column(low, high):
        mine = by_core(own[:, low], own[:, high])
        theirs = by_core(other[:, low], other[:, high])
        return jnp.concatenate([by_core(mine, theirs), by_core(theirs, mine)], 0)

    pairs = []
    for j in range(n_col - 1):
        pairs += [(n_col + j, j + 1), (j + 1, n_col + j)]
    halo = lax.ppermute(column(0, cols - 1), ("row", "col"), pairs)
    half_shape = shape((rows, GROUP, width), BF16)
    edge_mixed, mine_in, send_in = pl.pallas_call(
        inner_kernel,
        out_shape=(shape((height, GROUP, 3 * width), F32), half_shape, half_shape),
        in_specs=[vmem] * 11,
        out_specs=(vmem,) * 3,
        scratch_shapes=[
            pltpu.VMEM((2, height + 2, GROUP, 3 * width), F32),
            pltpu.VMEM((3, height + 16, 3 * width), F32),
            pltpu.VMEM((2, height // 8, 8, 3 * width), F32),
            pltpu.VMEM((2, height // 8, 8, 3 * width), F32),
            pltpu.VMEM((height, GROUP, 3 * width), F32),
            pltpu.VMEM((height * GROUP, width), BF16),
            pltpu.VMEM((2, 2 * rows * GROUP, width), BF16),
            pltpu.VMEM((2, rows, GROUP, width), F32),
        ],
        compiler_params=limit,
        cost_estimate=pl.CostEstimate(flops=10**9, bytes_accessed=12 * 1024 * 1024, transcendentals=0),
    )(
        block, other, column(GROUP - 1, cols - GROUP), column(part, part - 1),
        column(GROUP, cols - 1 - GROUP), w_in_v, taps, fwd_v, bwd_v, w_out_v, spectrum,
    )
    theirs_in = lax.ppermute(send_in, "row", swap)
    mine_edge, send_edge = pl.pallas_call(
        edge_kernel,
        out_shape=(half_shape, half_shape),
        in_specs=[vmem] * 8,
        out_specs=(vmem, vmem),
        scratch_shapes=[
            pltpu.VMEM((height + 16, 3 * width), F32),
            pltpu.VMEM((height // 8, 8, 3 * width), F32),
            pltpu.VMEM((height * GROUP, width), BF16),
            pltpu.VMEM((2, 2 * rows * GROUP, width), BF16),
            pltpu.VMEM((2, rows, GROUP, width), F32),
        ],
        compiler_params=limit,
        cost_estimate=pl.CostEstimate(flops=3 * 10**8, bytes_accessed=4 * 1024 * 1024, transcendentals=0),
    )(halo, edge_mixed, w_in_v, taps, fwd_v, bwd_v, w_out_v, spectrum)
    theirs_edge = lax.ppermute(send_edge, "row", swap)
    return by_core(
        jnp.concatenate([mine_edge, mine_in, theirs_in, theirs_edge], 1),
        jnp.concatenate([theirs_edge, theirs_in, mine_in, mine_edge], 1),
    )


def solution(mesh):
    in_specs = (P("row", "col", None), P(), P(), P(), P(), P(), P())
    out_specs = P("row", "col", None)
    return jax.shard_map(
        on_device, mesh=mesh, in_specs=in_specs, out_specs=out_specs, check_vma=False
    )
```

```python
import jax
import jax.numpy as jnp
import numpy as np
from jax import lax
from jax.experimental import pallas as pl
from jax.experimental.layout import Layout, with_layout_constraint
from jax.experimental.pallas import tpu as pltpu
from jax.sharding import PartitionSpec as P

F32 = jnp.float32
BF16 = jnp.bfloat16


def transforms(half, group):
    size = 2 * half
    slot = np.arange(half)[:, None]
    pos = np.arange(half)[None, :]
    angle = 2 * np.pi * slot * pos / size
    real, imag = np.cos(angle), -np.sin(angle)
    imag[0] = (-1.0) ** np.arange(half)
    forward = np.concatenate([real, imag], 0)
    back_real = 2 * np.cos(angle.T) / size
    back_real[:, 0] = 1 / size
    back_imag = -2 * np.sin(angle.T) / size
    back_imag[:, 0] = (-1.0) ** np.arange(half) / size
    backward = np.concatenate([back_real, back_imag], 1)
    lag = np.arange(size)[None, :]
    angle = 2 * np.pi * slot * lag / size
    real, imag = np.cos(angle), -np.sin(angle)
    imag[0] = 0
    real2 = real.copy()
    real2[0] = (-1.0) ** np.arange(size)
    near = (lag < half).astype(np.float64)
    sign = (-1.0) ** slot
    sign2 = sign.copy()
    sign2[0] = 1
    spectra = np.concatenate(
        [real * near, imag * near, real2 * near, real * sign, imag * sign, real2 * sign2], 0
    )
    eye = np.eye(group)
    return np.kron(forward, eye), np.kron(backward, eye), spectra


LANES = 128
GROUP = 8
CHUNK = 8


def pick_columns(block, columns):
    rows, cols, width = block.shape
    shape = (rows, rows * cols)
    place = lax.broadcasted_iota(jnp.int32, shape, 1)
    row = lax.broadcasted_iota(jnp.int32, shape, 0) * cols
    chosen = [jnp.where(place == row + column, 1.0, 0.0).astype(BF16) for column in columns]
    return jnp.dot(
        jnp.concatenate(chosen, 0), block.reshape(rows * cols, width), preferred_element_type=F32
    ).astype(BF16)


def prep_kernel(
    own_hbm, w_in_hbm, w_out_hbm, fwd_hbm, bwd_hbm, spec_hbm, filt_hbm, gain_hbm, kernel_hbm, bias_hbm,
    own_ref, w_in_ref, w_out_ref, fwd_ref, bwd_ref, taps_ref, h_ref, outer_ref, strips_ref,
    spec_ref, filt_ref, gain_ref, kernel_ref, bias_ref, sems,
):
    core = lax.axis_index("row")
    rows, cols, _ = own_ref.shape
    part = cols // 2
    moves = [
        (spec_hbm, spec_ref),
        (filt_hbm, filt_ref),
        (gain_hbm, gain_ref),
        (own_hbm, own_ref),
        (kernel_hbm, kernel_ref),
        (bias_hbm, bias_ref),
        (w_in_hbm, w_in_ref),
        (fwd_hbm, fwd_ref),
        (bwd_hbm, bwd_ref),
        (w_out_hbm, w_out_ref),
    ]
    copies = [pltpu.make_async_copy(src, dst, sems.at[i]) for i, (src, dst) in enumerate(moves)]
    for copy in copies:
        copy.start()
    for copy in copies[:3]:
        copy.wait()
    filt = filt_ref[...]
    h_ref[...] = jnp.dot(spec_ref[0], filt, preferred_element_type=F32) + jnp.dot(
        spec_ref[1], filt, preferred_element_type=F32
    )
    gain = gain_ref[...]
    h_ref[0:rows, :] = h_ref[0:rows, :] + gain
    h_ref[2 * rows : 3 * rows, :] = h_ref[2 * rows : 3 * rows, :] + gain
    copies[3].wait()
    start = pl.multiple_of(core * part, part)
    mine = pick_columns(
        own_ref[:, pl.ds(start, part), :],
        [core * (part - 1), GROUP - 1 + core, GROUP - core],
    )
    outer_ref[...] = mine[:rows]
    strips_ref[: 2 * rows] = mine[rows:]
    start = pl.multiple_of((1 - core) * part, part)
    strips_ref[2 * rows :] = pick_columns(
        own_ref[:, pl.ds(start, part), :], [core * (part - 1)]
    )
    for copy in copies[4:]:
        copy.wait()
    for a in range(3):
        taps_ref[3 * a : 3 * a + 3, :] = kernel_ref[a].astype(F32)
    taps_ref[9, :] = bias_ref[...]


def edge_terms(first, second, core, taps, edge_ref):
    rows, channels = first.shape
    height = 2 * rows
    edge_ref[0:8, :] = jnp.zeros((8, channels), F32)
    edge_ref[8 + height : 16 + height, :] = jnp.zeros((8, channels), F32)
    edge_ref[pl.ds(pl.multiple_of(8 + core * rows, 8), rows), :] = first
    edge_ref[pl.ds(pl.multiple_of(8 + (1 - core) * rows, 8), rows), :] = second
    total = edge_ref[7 : 7 + height, :] * taps[0]
    for a in (1, 2):
        total = total + edge_ref[7 + a : 7 + a + height, :] * taps[a]
    return total.reshape(height // 8, 8, channels)


def column_taps(taps_ref, core, on_core0):
    first, second = on_core0, 2 - on_core0
    return [
        jnp.where(
            core == 0,
            taps_ref[3 * a + first : 3 * a + first + 1, :],
            taps_ref[3 * a + second : 3 * a + second + 1, :],
        )
        for a in range(3)
    ]


def depthwise_steps(load, side_ref, taps_ref, chunk, store, bases):
    sub = lax.broadcasted_iota(jnp.int32, (GROUP, LANES), 0)
    is_first = sub == 0
    is_last = sub == GROUP - 1
    for base in bases:
        at = slice(base, base + LANES)
        tap = [
            [
                jnp.broadcast_to(taps_ref[3 * a + b : 3 * a + b + 1, at], (GROUP, LANES))
                for b in range(3)
            ]
            for a in range(3)
        ]
        bias = jnp.broadcast_to(taps_ref[9:10, at], (GROUP, LANES))
        loaded = [load(chunk * CHUNK + r, at) for r in range(CHUNK + 2)]
        for r in range(CHUNK):
            u = [
                loaded[r] * tap[0][b] + loaded[r + 1] * tap[1][b] + loaded[r + 2] * tap[2][b]
                for b in range(3)
            ]
            west = jnp.broadcast_to(side_ref[0, chunk, r : r + 1, at], (GROUP, LANES))
            east = jnp.broadcast_to(side_ref[1, chunk, r : r + 1, at], (GROUP, LANES))
            value = u[1] + bias
            value = value + jnp.where(is_first, west, pltpu.roll(u[0], 1, 0))
            value = value + jnp.where(is_last, east, pltpu.roll(u[2], GROUP - 1, 0))
            store(chunk * CHUNK + r, at, value)
        yield


def conv_steps(mixed, fwd_ref, bwd_ref, w_out_ref, h_ref, prod_ref, z_ref, put):
    height_group, width = prod_ref.shape
    height = height_group // GROUP
    rows = height // 2
    block = rows * GROUP
    spectra = []
    for h in range(2):
        for row in range(h * rows, (h + 1) * rows, 2):
            for base in range(0, width, LANES):
                two = [mixed(r, width + base) * mixed(r, 2 * width + base) for r in (row, row + 1)]
                prod_ref[row * GROUP : (row + 2) * GROUP, base : base + LANES] = jnp.concatenate(
                    two, 0
                ).astype(BF16)
            if row % 8 == 6:
                yield
        spectra.append(
            jnp.dot(
                fwd_ref[...], prod_ref[h * block : (h + 1) * block], preferred_element_type=F32
            )
        )
        yield
    low, high = spectra
    for k in range(0, rows, 2):
        parts = [[], [], [], []]
        for s in (k, k + 1):
            near_r, near_i, near_2, all_r, all_i, all_2 = (
                jnp.broadcast_to(h_ref[j * rows + s : j * rows + s + 1, :], (GROUP, width))
                for j in range(6)
            )
            re, im = slice(s * GROUP, (s + 1) * GROUP), slice(block + s * GROUP, block + (s + 1) * GROUP)
            lr, li, hr, hi = low[re], low[im], high[re], high[im]
            parts[0].append(lr * near_r - li * near_i)
            parts[1].append(lr * near_i + li * near_2)
            parts[2].append(lr * all_r - li * all_i + hr * near_r - hi * near_i)
            parts[3].append(lr * all_i + li * all_2 + hr * near_i + hi * near_2)
        for j in range(4):
            at = (j % 2) * block + k * GROUP
            z_ref[j // 2, at : at + 2 * GROUP, :] = jnp.concatenate(parts[j], 0).astype(BF16)
        if k % 4 == 2:
            yield
    convs = []
    for h in range(2):
        convs.append(jnp.dot(bwd_ref[...], z_ref[h], preferred_element_type=F32))
        yield
    for h in range(2):
        gated = []
        for r in range(rows):
            line = [
                mixed(h * rows + r, base) * convs[h][r * GROUP : (r + 1) * GROUP, base : base + LANES]
                for base in range(0, width, LANES)
            ]
            gated.append(jnp.concatenate(line, 1))
        final = jnp.dot(
            jnp.concatenate(gated, 0).astype(BF16), w_out_ref[...], preferred_element_type=F32
        )
        put(h, final.reshape(rows, GROUP, width))
        yield


def inner_kernel(
    own_ref, other_ref, strips_ref, other_strips_ref,
    w_in_ref, taps_ref, fwd_ref, bwd_ref, w_out_ref, h_ref,
    edge_mixed_ref, out_ref,
    p_ref, strip_ref, side_ref, edge_side_ref, mixed_ref, prod_ref, z_ref,
):
    core = lax.axis_index("row")
    rows, cols, width = own_ref.shape
    part = cols // 2
    height = 2 * rows
    start = pl.multiple_of(core * part, part)

    for slot in range(2):
        p_ref[slot, 0] = jnp.zeros((GROUP, 3 * width), F32)
        p_ref[slot, height + 1] = jnp.zeros((GROUP, 3 * width), F32)
    strips = []
    for row, ref, strip in (
        (core * rows, own_ref, strips_ref),
        ((1 - core) * rows, other_ref, other_strips_ref),
    ):
        count = rows * part
        tokens = ref[:, pl.ds(start, part), :].reshape(count, width)
        got = jnp.dot(
            jnp.concatenate([tokens, strip[...]], 0), w_in_ref[...], preferred_element_type=F32
        )
        grid = got[:count].reshape(rows, part, 3 * width)
        p_ref[core, pl.ds(row + 1, rows)] = grid[:, :GROUP]
        p_ref[1 - core, pl.ds(row + 1, rows)] = grid[:, GROUP:]
        strips.append(
            [got[count + j * rows : count + (j + 1) * rows] for j in range(3)]
        )

    near, edge_near, far = zip(*strips)
    side_ref[core] = edge_terms(*near, core, column_taps(taps_ref, core, 0), strip_ref.at[0])
    side_ref[1 - core] = edge_terms(*far, core, column_taps(taps_ref, core, 2), strip_ref.at[1])
    edge_side_ref[1 - core] = edge_terms(
        *edge_near, core, column_taps(taps_ref, core, 2), strip_ref.at[2]
    )
    edge_side_ref[core] = jnp.zeros(edge_side_ref.shape[1:], F32)

    def store_inner(row, at, value):
        mixed_ref[row, :, at] = value

    def inner_chunk(i, carry):
        steps = depthwise_steps(
            lambda row, at: p_ref[1, row, :, at], side_ref, taps_ref, i, store_inner,
            range(0, 3 * width, LANES),
        )
        for _ in steps:
            pass
        return carry

    lax.fori_loop(0, height // CHUNK, inner_chunk, 0)

    def store_edge(row, at, value):
        edge_mixed_ref[row, :, at] = value

    def put(h, final):
        out_ref[h] = final

    edge = [
        depthwise_steps(
            lambda row, at: p_ref[0, row, :, at], edge_side_ref, taps_ref, i, store_edge, [base]
        )
        for i in range(height // CHUNK)
        for base in range(0, 3 * width, LANES)
    ]
    conv = conv_steps(
        lambda r, base: mixed_ref[r, :, base : base + LANES],
        fwd_ref, bwd_ref, w_out_ref, h_ref, prod_ref, z_ref, put,
    )
    done = 0
    for _ in conv:
        for step in edge[done : done + 2]:
            for _ in step:
                pass
        done += 2
    for step in edge[done:]:
        for _ in step:
            pass


def edge_kernel(
    halo_ref, mixed_ref, inner_ref, w_in_ref, taps_ref, fwd_ref, bwd_ref, w_out_ref, h_ref,
    mine_ref, send_ref,
    strip_ref, side_ref, prod_ref, z_ref, out_ref,
):
    core = lax.axis_index("row")
    rows, part, width = mine_ref.shape
    got = jnp.dot(halo_ref[...], w_in_ref[...], preferred_element_type=F32)
    side_ref[...] = edge_terms(
        got[:rows], got[rows:], 1 - core, column_taps(taps_ref, core, 0), strip_ref
    )
    sub = lax.broadcasted_iota(jnp.int32, (GROUP, LANES), 0)
    at_edge = sub == core * (GROUP - 1)

    def mixed(r, base):
        at = slice(base, base + LANES)
        add = jnp.broadcast_to(side_ref[r // 8, r % 8 : r % 8 + 1, at], (GROUP, LANES))
        return mixed_ref[r, :, at] + jnp.where(at_edge, add, 0.0)

    def put(h, final):
        out_ref[h] = final

    for _ in conv_steps(
        mixed, fwd_ref, bwd_ref, w_out_ref, h_ref, prod_ref, z_ref, put
    ):
        pass
    for ref, half in ((mine_ref, core), (send_ref, 1 - core)):
        pair = [out_ref[half], inner_ref[half]]
        ref[:, :GROUP] = jnp.where(core == 0, pair[0], pair[1]).astype(BF16)
        ref[:, GROUP:] = jnp.where(core == 0, pair[1], pair[0]).astype(BF16)


def on_device(image_tokens, w_in, conv_kernel, conv_bias, long_filter, skip_gain, w_out):
    rows, cols, width = image_tokens.shape
    part = cols // 2
    height = 2 * rows
    n_col = lax.axis_size("col")
    core = lax.axis_index("row")
    fwd, bwd, spectra = transforms(rows, GROUP)
    spec_hi = spectra.astype(BF16)
    spec_lo = (spectra - spec_hi.astype(np.float64)).astype(BF16)
    spec = np.stack([spec_hi, spec_lo])
    vmem = pl.BlockSpec(memory_space=pltpu.VMEM)
    hbm = pl.BlockSpec(memory_space=pltpu.HBM)
    shape = jax.ShapeDtypeStruct
    limit = pltpu.CompilerParams(vmem_limit_bytes=24 * 1024 * 1024)

    swap = [(0, 1), (1, 0)]
    rowmajor = Layout((0, 1, 2))
    image_tokens = with_layout_constraint(image_tokens, rowmajor)
    other = with_layout_constraint(lax.ppermute(image_tokens, "row", swap), rowmajor)

    def keep(array):
        return pltpu.with_memory_space_constraint(array, pltpu.HBM)

    own, w_in_v, w_out_v, fwd_v, bwd_v, taps, spectrum, outer, strips = pl.pallas_call(
        prep_kernel,
        out_shape=(
            shape(image_tokens.shape, BF16),
            shape(w_in.shape, BF16),
            shape(w_out.shape, BF16),
            shape(fwd.shape, BF16),
            shape(bwd.shape, BF16),
            shape((16, 3 * width), F32),
            shape((6 * rows, width), F32),
            shape((rows, width), BF16),
            shape((3 * rows, width), BF16),
        ),
        in_specs=[hbm] * 10,
        out_specs=(vmem,) * 9,
        scratch_shapes=[
            pltpu.VMEM(spec.shape, BF16),
            pltpu.VMEM(long_filter.shape, BF16),
            pltpu.VMEM((1, width), F32),
            pltpu.VMEM(conv_kernel.shape, BF16),
            pltpu.VMEM(conv_bias.shape, F32),
            pltpu.SemaphoreType.DMA((10,)),
        ],
        compiler_params=limit,
        cost_estimate=pl.CostEstimate(flops=0, bytes_accessed=3 * 1024 * 1024, transcendentals=0),
    )(
        keep(image_tokens), keep(w_in), keep(w_out), keep(fwd.astype(BF16)), keep(bwd.astype(BF16)),
        keep(spec), keep(long_filter), keep(skip_gain[None]), keep(conv_kernel), keep(conv_bias),
    )

    def by_core(low, high):
        return jnp.where(core == 0, low, high)

    def column(low):
        return by_core(other[:, low], other[:, cols - 1 - low])

    pairs = []
    for j in range(n_col - 1):
        pairs += [(n_col + j, j + 1), (j + 1, n_col + j)]
    halo = lax.ppermute(jnp.concatenate([outer, column(0)], 0), ("row", "col"), pairs)
    other_strips = jnp.concatenate([column(GROUP - 1), column(GROUP), column(part)], 0)
    edge_mixed, inner = pl.pallas_call(
        inner_kernel,
        out_shape=(
            shape((height, GROUP, 3 * width), F32),
            shape((2, rows, GROUP, width), F32),
        ),
        in_specs=[vmem] * 10,
        out_specs=(vmem,) * 2,
        scratch_shapes=[
            pltpu.VMEM((2, height + 2, GROUP, 3 * width), F32),
            pltpu.VMEM((3, height + 16, 3 * width), F32),
            pltpu.VMEM((2, height // 8, 8, 3 * width), F32),
            pltpu.VMEM((2, height // 8, 8, 3 * width), F32),
            pltpu.VMEM((height, GROUP, 3 * width), F32),
            pltpu.VMEM((height * GROUP, width), BF16),
            pltpu.VMEM((2, 2 * rows * GROUP, width), BF16),
        ],
        compiler_params=limit,
        cost_estimate=pl.CostEstimate(flops=10**9, bytes_accessed=12 * 1024 * 1024, transcendentals=0),
    )(own, other, strips, other_strips, w_in_v, taps, fwd_v, bwd_v, w_out_v, spectrum)
    half_shape = shape((rows, part, width), BF16)
    mine, send = pl.pallas_call(
        edge_kernel,
        out_shape=(half_shape, half_shape),
        in_specs=[vmem] * 9,
        out_specs=(vmem, vmem),
        scratch_shapes=[
            pltpu.VMEM((height + 16, 3 * width), F32),
            pltpu.VMEM((height // 8, 8, 3 * width), F32),
            pltpu.VMEM((height * GROUP, width), BF16),
            pltpu.VMEM((2, 2 * rows * GROUP, width), BF16),
            pltpu.VMEM((2, rows, GROUP, width), F32),
        ],
        compiler_params=limit,
        cost_estimate=pl.CostEstimate(flops=3 * 10**8, bytes_accessed=4 * 1024 * 1024, transcendentals=0),
    )(halo, edge_mixed, inner, w_in_v, taps, fwd_v, bwd_v, w_out_v, spectrum)
    theirs = lax.ppermute(send, "row", swap)
    both = jnp.concatenate([mine, mine], 1)
    return lax.dynamic_update_slice_in_dim(both, theirs, (1 - core) * part, 1)


def solution(mesh):
    in_specs = (P("row", "col", None), P(), P(), P(), P(), P(), P())
    out_specs = P("row", "col", None)
    return jax.shard_map(
        on_device, mesh=mesh, in_specs=in_specs, out_specs=out_specs, check_vma=False
    )
```

```python
import jax
import jax.numpy as jnp
import numpy as np
from jax import lax
from jax.experimental import pallas as pl
from jax.experimental.layout import Layout, with_layout_constraint
from jax.experimental.pallas import tpu as pltpu
from jax.sharding import PartitionSpec as P

F32 = jnp.float32
BF16 = jnp.bfloat16


def transforms(half, group):
    size = 2 * half
    slot = np.arange(half)[:, None]
    pos = np.arange(half)[None, :]
    angle = 2 * np.pi * slot * pos / size
    real, imag = np.cos(angle), -np.sin(angle)
    imag[0] = (-1.0) ** np.arange(half)
    forward = np.concatenate([real, imag], 0)
    back_real = 2 * np.cos(angle.T) / size
    back_real[:, 0] = 1 / size
    back_imag = -2 * np.sin(angle.T) / size
    back_imag[:, 0] = (-1.0) ** np.arange(half) / size
    backward = np.concatenate([back_real, back_imag], 1)
    lag = np.arange(size)[None, :]
    angle = 2 * np.pi * slot * lag / size
    real, imag = np.cos(angle), -np.sin(angle)
    imag[0] = 0
    real2 = real.copy()
    real2[0] = (-1.0) ** np.arange(size)
    near = (lag < half).astype(np.float64)
    sign = (-1.0) ** slot
    sign2 = sign.copy()
    sign2[0] = 1
    spectra = np.concatenate(
        [real * near, imag * near, real2 * near, real * sign, imag * sign, real2 * sign2], 0
    )
    eye = np.eye(group)
    return np.kron(forward, eye), np.kron(backward, eye), spectra


LANES = 128
GROUP = 8
CHUNK = 8


def pick_columns(block, columns):
    rows, cols, width = block.shape
    shape = (rows, rows * cols)
    place = lax.broadcasted_iota(jnp.int32, shape, 1)
    row = lax.broadcasted_iota(jnp.int32, shape, 0) * cols
    chosen = [jnp.where(place == row + column, 1.0, 0.0).astype(BF16) for column in columns]
    return jnp.dot(
        jnp.concatenate(chosen, 0), block.reshape(rows * cols, width), preferred_element_type=F32
    ).astype(BF16)


def project(tokens, strips, core, row, w_in_ref, p_ref, strips_ref):
    rows, part, width = tokens.shape
    count = rows * part
    got = jnp.dot(
        jnp.concatenate([tokens.reshape(count, width), strips], 0),
        w_in_ref[...],
        preferred_element_type=F32,
    )
    grid = got[:count].reshape(rows, part, 3 * width)
    p_ref[core, pl.ds(row + 1, rows)] = grid[:, :GROUP]
    p_ref[1 - core, pl.ds(row + 1, rows)] = grid[:, GROUP:]
    strips_ref[...] = got[count:]


def prep_kernel(
    own_hbm, w_in_hbm, w_out_hbm, fwd_hbm, bwd_hbm, spec_hbm, filt_hbm, gain_hbm, kernel_hbm, bias_hbm,
    p_ref, strips_ref, w_in_ref, w_out_ref, fwd_ref, bwd_ref, taps_ref, h_ref, outer_ref,
    own_ref, spec_ref, filt_ref, gain_ref, kernel_ref, bias_ref, sems,
):
    core = lax.axis_index("row")
    rows, cols, width = own_ref.shape
    part = cols // 2
    height = 2 * rows
    moves = [
        (spec_hbm, spec_ref),
        (filt_hbm, filt_ref),
        (gain_hbm, gain_ref),
        (own_hbm, own_ref),
        (kernel_hbm, kernel_ref),
        (bias_hbm, bias_ref),
        (w_in_hbm, w_in_ref),
        (fwd_hbm, fwd_ref),
        (bwd_hbm, bwd_ref),
        (w_out_hbm, w_out_ref),
    ]
    copies = [pltpu.make_async_copy(src, dst, sems.at[i]) for i, (src, dst) in enumerate(moves)]
    for copy in copies:
        copy.start()
    for copy in copies[:3]:
        copy.wait()
    filt = filt_ref[...]
    h_ref[...] = jnp.dot(spec_ref[0], filt, preferred_element_type=F32) + jnp.dot(
        spec_ref[1], filt, preferred_element_type=F32
    )
    gain = gain_ref[...]
    h_ref[0:rows, :] = h_ref[0:rows, :] + gain
    h_ref[2 * rows : 3 * rows, :] = h_ref[2 * rows : 3 * rows, :] + gain
    for slot in range(2):
        p_ref[slot, 0] = jnp.zeros((GROUP, 3 * width), F32)
        p_ref[slot, height + 1] = jnp.zeros((GROUP, 3 * width), F32)
    copies[3].wait()
    start = pl.multiple_of(core * part, part)
    mine = pick_columns(
        own_ref[:, pl.ds(start, part), :],
        [core * (part - 1), GROUP - 1 + core, GROUP - core],
    )
    outer_ref[...] = mine[:rows]
    far = pl.multiple_of((1 - core) * part, part)
    theirs = pick_columns(own_ref[:, pl.ds(far, part), :], [core * (part - 1)])
    for copy in copies[4:7]:
        copy.wait()
    project(
        own_ref[:, pl.ds(start, part), :], jnp.concatenate([mine[rows:], theirs], 0),
        core, core * rows, w_in_ref, p_ref, strips_ref,
    )
    for a in range(3):
        taps_ref[3 * a : 3 * a + 3, :] = kernel_ref[a].astype(F32)
    taps_ref[9, :] = bias_ref[...]
    for copy in copies[7:]:
        copy.wait()


def edge_terms(first, second, core, taps, edge_ref):
    rows, channels = first.shape
    height = 2 * rows
    edge_ref[0:8, :] = jnp.zeros((8, channels), F32)
    edge_ref[8 + height : 16 + height, :] = jnp.zeros((8, channels), F32)
    edge_ref[pl.ds(pl.multiple_of(8 + core * rows, 8), rows), :] = first
    edge_ref[pl.ds(pl.multiple_of(8 + (1 - core) * rows, 8), rows), :] = second
    total = edge_ref[7 : 7 + height, :] * taps[0]
    for a in (1, 2):
        total = total + edge_ref[7 + a : 7 + a + height, :] * taps[a]
    return total.reshape(height // 8, 8, channels)


def column_taps(taps_ref, core, on_core0):
    first, second = on_core0, 2 - on_core0
    return [
        jnp.where(
            core == 0,
            taps_ref[3 * a + first : 3 * a + first + 1, :],
            taps_ref[3 * a + second : 3 * a + second + 1, :],
        )
        for a in range(3)
    ]


def depthwise_steps(load, side_ref, taps_ref, chunk, store, bases):
    sub = lax.broadcasted_iota(jnp.int32, (GROUP, LANES), 0)
    is_first = sub == 0
    is_last = sub == GROUP - 1
    for base in bases:
        at = slice(base, base + LANES)
        tap = [
            [
                jnp.broadcast_to(taps_ref[3 * a + b : 3 * a + b + 1, at], (GROUP, LANES))
                for b in range(3)
            ]
            for a in range(3)
        ]
        bias = jnp.broadcast_to(taps_ref[9:10, at], (GROUP, LANES))
        loaded = [load(chunk * CHUNK + r, at) for r in range(CHUNK + 2)]
        for r in range(CHUNK):
            u = [
                loaded[r] * tap[0][b] + loaded[r + 1] * tap[1][b] + loaded[r + 2] * tap[2][b]
                for b in range(3)
            ]
            west = jnp.broadcast_to(side_ref[0, chunk, r : r + 1, at], (GROUP, LANES))
            east = jnp.broadcast_to(side_ref[1, chunk, r : r + 1, at], (GROUP, LANES))
            value = u[1] + bias
            value = value + jnp.where(is_first, west, pltpu.roll(u[0], 1, 0))
            value = value + jnp.where(is_last, east, pltpu.roll(u[2], GROUP - 1, 0))
            store(chunk * CHUNK + r, at, value)
        yield


def conv_steps(mixed, fwd_ref, bwd_ref, w_out_ref, h_ref, prod_ref, z_ref, put):
    block, width = prod_ref.shape[0], prod_ref.shape[1] // 2
    rows = block // GROUP
    for row in range(0, rows, 2):
        for h in range(2):
            for base in range(0, width, LANES):
                two = [
                    mixed(h * rows + r, width + base) * mixed(h * rows + r, 2 * width + base)
                    for r in (row, row + 1)
                ]
                at = h * width + base
                prod_ref[row * GROUP : (row + 2) * GROUP, at : at + LANES] = jnp.concatenate(
                    two, 0
                ).astype(BF16)
        if row % 4 == 2:
            yield
    spectra = jnp.dot(fwd_ref[...], prod_ref[...], preferred_element_type=F32)
    low, high = spectra[:, :width], spectra[:, width:]
    yield
    for k in range(0, rows, 2):
        parts = [[], [], [], []]
        for s in (k, k + 1):
            near_r, near_i, near_2, all_r, all_i, all_2 = (
                jnp.broadcast_to(h_ref[j * rows + s : j * rows + s + 1, :], (GROUP, width))
                for j in range(6)
            )
            re, im = slice(s * GROUP, (s + 1) * GROUP), slice(block + s * GROUP, block + (s + 1) * GROUP)
            lr, li, hr, hi = low[re], low[im], high[re], high[im]
            parts[0].append(lr * near_r - li * near_i)
            parts[1].append(lr * near_i + li * near_2)
            parts[2].append(lr * all_r - li * all_i + hr * near_r - hi * near_i)
            parts[3].append(lr * all_i + li * all_2 + hr * near_i + hi * near_2)
        for j in range(4):
            at, lane = (j % 2) * block + k * GROUP, (j // 2) * width
            z_ref[at : at + 2 * GROUP, lane : lane + width] = jnp.concatenate(parts[j], 0).astype(BF16)
        if k % 4 == 2:
            yield
    conv = jnp.dot(bwd_ref[...], z_ref[...], preferred_element_type=F32)
    yield
    gated = []
    for h in range(2):
        for r in range(rows):
            line = [
                mixed(h * rows + r, base)
                * conv[r * GROUP : (r + 1) * GROUP, h * width + base : h * width + base + LANES]
                for base in range(0, width, LANES)
            ]
            gated.append(jnp.concatenate(line, 1))
        yield
    final = jnp.dot(
        jnp.concatenate(gated, 0).astype(BF16), w_out_ref[...], preferred_element_type=F32
    )
    put(final.reshape(2, rows, GROUP, width))


def inner_kernel(
    _, strips_ref, other_ref, other_strips_ref,
    w_in_ref, taps_ref, fwd_ref, bwd_ref, w_out_ref, h_ref,
    p_ref, edge_mixed_ref, out_ref,
    got_strips_ref, strip_ref, side_ref, edge_side_ref, mixed_ref, prod_ref, z_ref,
):
    core = lax.axis_index("row")
    rows, cols, width = other_ref.shape
    part = cols // 2
    height = 2 * rows
    start = pl.multiple_of(core * part, part)
    project(
        other_ref[:, pl.ds(start, part), :], other_strips_ref[...],
        core, (1 - core) * rows, w_in_ref, p_ref, got_strips_ref,
    )

    near, edge_near, far = (
        [ref[j * rows : (j + 1) * rows, :] for ref in (strips_ref, got_strips_ref)]
        for j in range(3)
    )
    side_ref[core] = edge_terms(*near, core, column_taps(taps_ref, core, 0), strip_ref.at[0])
    side_ref[1 - core] = edge_terms(*far, core, column_taps(taps_ref, core, 2), strip_ref.at[1])
    edge_side_ref[1 - core] = edge_terms(
        *edge_near, core, column_taps(taps_ref, core, 2), strip_ref.at[2]
    )
    edge_side_ref[core] = jnp.zeros(edge_side_ref.shape[1:], F32)

    def store_inner(row, at, value):
        mixed_ref[row, :, at] = value

    def inner_chunk(i, carry):
        steps = depthwise_steps(
            lambda row, at: p_ref[1, row, :, at], side_ref, taps_ref, i, store_inner,
            range(0, 3 * width, LANES),
        )
        for _ in steps:
            pass
        return carry

    lax.fori_loop(0, height // CHUNK, inner_chunk, 0)

    def store_edge(row, at, value):
        edge_mixed_ref[row, :, at] = value

    def put(final):
        out_ref[...] = final

    edge = [
        depthwise_steps(
            lambda row, at: p_ref[0, row, :, at], edge_side_ref, taps_ref, i, store_edge, [base]
        )
        for i in range(height // CHUNK)
        for base in range(0, 3 * width, LANES)
    ]
    conv = conv_steps(
        lambda r, base: mixed_ref[r, :, base : base + LANES],
        fwd_ref, bwd_ref, w_out_ref, h_ref, prod_ref, z_ref, put,
    )
    done = 0
    for _ in conv:
        for step in edge[done : done + 2]:
            for _ in step:
                pass
        done += 2
    for step in edge[done:]:
        for _ in step:
            pass


def edge_kernel(
    halo_ref, mixed_ref, inner_ref, w_in_ref, taps_ref, fwd_ref, bwd_ref, w_out_ref, h_ref,
    mine_ref, send_ref,
    strip_ref, side_ref, prod_ref, z_ref, out_ref,
):
    core = lax.axis_index("row")
    rows, part, width = mine_ref.shape
    got = jnp.dot(halo_ref[...], w_in_ref[...], preferred_element_type=F32)
    side_ref[...] = edge_terms(
        got[:rows], got[rows:], 1 - core, column_taps(taps_ref, core, 0), strip_ref
    )
    sub = lax.broadcasted_iota(jnp.int32, (GROUP, LANES), 0)
    at_edge = sub == core * (GROUP - 1)

    def mixed(r, base):
        at = slice(base, base + LANES)
        add = jnp.broadcast_to(side_ref[r // 8, r % 8 : r % 8 + 1, at], (GROUP, LANES))
        return mixed_ref[r, :, at] + jnp.where(at_edge, add, 0.0)

    def put(final):
        out_ref[...] = final

    for _ in conv_steps(
        mixed, fwd_ref, bwd_ref, w_out_ref, h_ref, prod_ref, z_ref, put
    ):
        pass
    for ref, half in ((mine_ref, core), (send_ref, 1 - core)):
        pair = [out_ref[half], inner_ref[half]]
        ref[:, :GROUP] = jnp.where(core == 0, pair[0], pair[1]).astype(BF16)
        ref[:, GROUP:] = jnp.where(core == 0, pair[1], pair[0]).astype(BF16)


def on_device(image_tokens, w_in, conv_kernel, conv_bias, long_filter, skip_gain, w_out):
    rows, cols, width = image_tokens.shape
    part = cols // 2
    height = 2 * rows
    n_col = lax.axis_size("col")
    core = lax.axis_index("row")
    fwd, bwd, spectra = transforms(rows, GROUP)
    spec_hi = spectra.astype(BF16)
    spec_lo = (spectra - spec_hi.astype(np.float64)).astype(BF16)
    spec = np.stack([spec_hi, spec_lo])
    vmem = pl.BlockSpec(memory_space=pltpu.VMEM)
    hbm = pl.BlockSpec(memory_space=pltpu.HBM)
    shape = jax.ShapeDtypeStruct
    limit = pltpu.CompilerParams(vmem_limit_bytes=24 * 1024 * 1024)

    swap = [(0, 1), (1, 0)]
    rowmajor = Layout((0, 1, 2))
    image_tokens = with_layout_constraint(image_tokens, rowmajor)
    other = with_layout_constraint(lax.ppermute(image_tokens, "row", swap), rowmajor)

    def keep(array):
        return pltpu.with_memory_space_constraint(array, pltpu.HBM)

    projected, strips, w_in_v, w_out_v, fwd_v, bwd_v, taps, spectrum, outer = pl.pallas_call(
        prep_kernel,
        out_shape=(
            shape((2, height + 2, GROUP, 3 * width), F32),
            shape((3 * rows, 3 * width), F32),
            shape(w_in.shape, BF16),
            shape(w_out.shape, BF16),
            shape(fwd.shape, BF16),
            shape(bwd.shape, BF16),
            shape((16, 3 * width), F32),
            shape((6 * rows, width), F32),
            shape((rows, width), BF16),
        ),
        in_specs=[hbm] * 10,
        out_specs=(vmem,) * 9,
        scratch_shapes=[
            pltpu.VMEM(image_tokens.shape, BF16),
            pltpu.VMEM(spec.shape, BF16),
            pltpu.VMEM(long_filter.shape, BF16),
            pltpu.VMEM((1, width), F32),
            pltpu.VMEM(conv_kernel.shape, BF16),
            pltpu.VMEM(conv_bias.shape, F32),
            pltpu.SemaphoreType.DMA((10,)),
        ],
        compiler_params=limit,
        cost_estimate=pl.CostEstimate(flops=0, bytes_accessed=3 * 1024 * 1024, transcendentals=0),
    )(
        keep(image_tokens), keep(w_in), keep(w_out), keep(fwd.astype(BF16)), keep(bwd.astype(BF16)),
        keep(spec), keep(long_filter), keep(skip_gain[None]), keep(conv_kernel), keep(conv_bias),
    )

    def by_core(low, high):
        return jnp.where(core == 0, low, high)

    def column(low):
        return by_core(other[:, low], other[:, cols - 1 - low])

    pairs = []
    for j in range(n_col - 1):
        pairs += [(n_col + j, j + 1), (j + 1, n_col + j)]
    halo = lax.ppermute(jnp.concatenate([outer, column(0)], 0), ("row", "col"), pairs)
    other_strips = jnp.concatenate([column(GROUP - 1), column(GROUP), column(part)], 0)
    _, edge_mixed, inner = pl.pallas_call(
        inner_kernel,
        out_shape=(
            shape((2, height + 2, GROUP, 3 * width), F32),
            shape((height, GROUP, 3 * width), F32),
            shape((2, rows, GROUP, width), F32),
        ),
        in_specs=[vmem] * 10,
        out_specs=(vmem,) * 3,
        input_output_aliases={0: 0},
        scratch_shapes=[
            pltpu.VMEM((3 * rows, 3 * width), F32),
            pltpu.VMEM((3, height + 16, 3 * width), F32),
            pltpu.VMEM((2, height // 8, 8, 3 * width), F32),
            pltpu.VMEM((2, height // 8, 8, 3 * width), F32),
            pltpu.VMEM((height, GROUP, 3 * width), F32),
            pltpu.VMEM((rows * GROUP, 2 * width), BF16),
            pltpu.VMEM((2 * rows * GROUP, 2 * width), BF16),
        ],
        compiler_params=limit,
        cost_estimate=pl.CostEstimate(flops=10**9, bytes_accessed=12 * 1024 * 1024, transcendentals=0),
    )(projected, strips, other, other_strips, w_in_v, taps, fwd_v, bwd_v, w_out_v, spectrum)
    half_shape = shape((rows, part, width), BF16)
    mine, send = pl.pallas_call(
        edge_kernel,
        out_shape=(half_shape, half_shape),
        in_specs=[vmem] * 9,
        out_specs=(vmem, vmem),
        scratch_shapes=[
            pltpu.VMEM((height + 16, 3 * width), F32),
            pltpu.VMEM((height // 8, 8, 3 * width), F32),
            pltpu.VMEM((rows * GROUP, 2 * width), BF16),
            pltpu.VMEM((2 * rows * GROUP, 2 * width), BF16),
            pltpu.VMEM((2, rows, GROUP, width), F32),
        ],
        compiler_params=limit,
        cost_estimate=pl.CostEstimate(flops=3 * 10**8, bytes_accessed=4 * 1024 * 1024, transcendentals=0),
    )(halo, edge_mixed, inner, w_in_v, taps, fwd_v, bwd_v, w_out_v, spectrum)
    theirs = lax.ppermute(send, "row", swap)
    both = jnp.concatenate([mine, mine], 1)
    return lax.dynamic_update_slice_in_dim(both, theirs, (1 - core) * part, 1)


def solution(mesh):
    in_specs = (P("row", "col", None), P(), P(), P(), P(), P(), P())
    out_specs = P("row", "col", None)
    return jax.shard_map(
        on_device, mesh=mesh, in_specs=in_specs, out_specs=out_specs, check_vma=False
    )
```

```python
import jax
import jax.numpy as jnp
import numpy as np
from jax import lax
from jax.experimental import pallas as pl
from jax.experimental.layout import Layout, with_layout_constraint
from jax.experimental.pallas import tpu as pltpu
from jax.sharding import PartitionSpec as P

F32 = jnp.float32
BF16 = jnp.bfloat16


def transforms(half, group):
    size = 2 * half
    slot = np.arange(half)[:, None]
    pos = np.arange(half)[None, :]
    angle = 2 * np.pi * slot * pos / size
    real, imag = np.cos(angle), -np.sin(angle)
    imag[0] = (-1.0) ** np.arange(half)
    forward = np.concatenate([real, imag], 0)
    back_real = 2 * np.cos(angle.T) / size
    back_real[:, 0] = 1 / size
    back_imag = -2 * np.sin(angle.T) / size
    back_imag[:, 0] = (-1.0) ** np.arange(half) / size
    backward = np.concatenate([back_real, back_imag], 1)
    lag = np.arange(size)[None, :]
    angle = 2 * np.pi * slot * lag / size
    real, imag = np.cos(angle), -np.sin(angle)
    imag[0] = 0
    real2 = real.copy()
    real2[0] = (-1.0) ** np.arange(size)
    near = (lag < half).astype(np.float64)
    sign = (-1.0) ** slot
    sign2 = sign.copy()
    sign2[0] = 1
    spectra = np.concatenate(
        [real * near, imag * near, real2 * near, real * sign, imag * sign, real2 * sign2], 0
    )
    eye = np.eye(group)
    return np.kron(forward, eye), np.kron(backward, eye), spectra


LANES = 128
GROUP = 8
CHUNK = 8
PITCH = 24
FIRST = 8


def pick_column(block, column):
    rows, cols, width = block.shape
    shape = (rows, rows * cols)
    place = lax.broadcasted_iota(jnp.int32, shape, 1)
    wanted = lax.broadcasted_iota(jnp.int32, shape, 0) * cols + column
    return jnp.dot(
        jnp.where(place == wanted, 1.0, 0.0).astype(BF16),
        block.reshape(rows * cols, width),
        preferred_element_type=F32,
    ).astype(BF16)


def row_place(row, column):
    return row * PITCH + FIRST + column


def project(tokens, strip, core, row, w_in_ref, p_ref):
    rows, part, width = tokens.shape
    count = rows * part
    got = jnp.dot(
        jnp.concatenate([tokens.reshape(count, width), strip], 0),
        w_in_ref[...],
        preferred_element_type=F32,
    )
    for t in range(3 * width // LANES):
        at = slice(t * LANES, (t + 1) * LANES)
        for r in range(rows):
            place = pl.multiple_of(row_place(row + r + 1, 0), GROUP)
            p_ref[t, pl.ds(place, part), :] = got[r * part : (r + 1) * part, at]
        for r in range(0, rows, GROUP):
            beside = got[count + r : count + r + GROUP, at]
            for column, value in (
                (-1, jnp.where(core == 1, beside, 0.0)),
                (part, jnp.where(core == 0, beside, 0.0)),
            ):
                place = row_place(row + r + 1, column)
                p_ref[t, pl.ds(place, GROUP, stride=PITCH), :] = value


def prep_kernel(
    own_hbm, w_in_hbm, w_out_hbm, fwd_hbm, bwd_hbm, spec_hbm, filt_hbm, gain_hbm, kernel_hbm, bias_hbm,
    p_ref, w_in_ref, w_out_ref, fwd_ref, bwd_ref, taps_ref, h_ref, outer_ref,
    own_ref, spec_ref, filt_ref, gain_ref, kernel_ref, bias_ref, sems,
):
    core = lax.axis_index("row")
    rows, cols, width = own_ref.shape
    part = cols // 2
    height = 2 * rows
    moves = [
        (spec_hbm, spec_ref),
        (filt_hbm, filt_ref),
        (gain_hbm, gain_ref),
        (own_hbm, own_ref),
        (kernel_hbm, kernel_ref),
        (bias_hbm, bias_ref),
        (w_in_hbm, w_in_ref),
        (fwd_hbm, fwd_ref),
        (bwd_hbm, bwd_ref),
        (w_out_hbm, w_out_ref),
    ]
    copies = [pltpu.make_async_copy(src, dst, sems.at[i]) for i, (src, dst) in enumerate(moves)]
    for copy in copies:
        copy.start()
    for copy in copies[:3]:
        copy.wait()
    filt = filt_ref[...]
    h_ref[...] = jnp.dot(spec_ref[0], filt, preferred_element_type=F32) + jnp.dot(
        spec_ref[1], filt, preferred_element_type=F32
    )
    gain = gain_ref[...]
    h_ref[0:rows, :] = h_ref[0:rows, :] + gain
    h_ref[2 * rows : 3 * rows, :] = h_ref[2 * rows : 3 * rows, :] + gain
    for t in range(p_ref.shape[0]):
        for row in (0, height + 1):
            p_ref[t, row * PITCH : row * PITCH + PITCH + GROUP, :] = jnp.zeros((PITCH + GROUP, LANES), F32)
    copies[3].wait()
    start = pl.multiple_of(core * part, part)
    far = pl.multiple_of((1 - core) * part, part)
    inner_edge = core * (part - 1)
    outer_ref[...] = pick_column(own_ref[:, pl.ds(start, part), :], inner_edge)
    beside = pick_column(own_ref[:, pl.ds(far, part), :], inner_edge)
    for copy in copies[4:7]:
        copy.wait()
    project(own_ref[:, pl.ds(start, part), :], beside, core, core * rows, w_in_ref, p_ref)
    for a in range(3):
        taps_ref[3 * a : 3 * a + 3, :] = kernel_ref[a].astype(F32)
    taps_ref[9, :] = bias_ref[...]
    for copy in copies[7:]:
        copy.wait()


def edge_terms(first, second, core, taps, edge_ref):
    rows, channels = first.shape
    height = 2 * rows
    edge_ref[0:8, :] = jnp.zeros((8, channels), F32)
    edge_ref[8 + height : 16 + height, :] = jnp.zeros((8, channels), F32)
    edge_ref[pl.ds(pl.multiple_of(8 + core * rows, 8), rows), :] = first
    edge_ref[pl.ds(pl.multiple_of(8 + (1 - core) * rows, 8), rows), :] = second
    total = edge_ref[7 : 7 + height, :] * taps[0]
    for a in (1, 2):
        total = total + edge_ref[7 + a : 7 + a + height, :] * taps[a]
    return total.reshape(height // 8, 8, channels)


def column_taps(taps_ref, core, on_core0):
    first, second = on_core0, 2 - on_core0
    return [
        jnp.where(
            core == 0,
            taps_ref[3 * a + first : 3 * a + first + 1, :],
            taps_ref[3 * a + second : 3 * a + second + 1, :],
        )
        for a in range(3)
    ]


def depthwise_steps(p_ref, first, taps_ref, chunk, store, bases):
    for base in bases:
        at = slice(base, base + LANES)
        tap = [
            jnp.broadcast_to(taps_ref[k : k + 1, at], (GROUP, LANES)) for k in range(10)
        ]
        loaded = [
            [
                p_ref[
                    base // LANES,
                    pl.ds(row_place(chunk * CHUNK + r, first + b - 1), GROUP, stride=2),
                    :,
                ]
                for b in range(3)
            ]
            for r in range(CHUNK + 2)
        ]
        for r in range(CHUNK):
            value = tap[9]
            for a in range(3):
                row = loaded[r + a]
                value = value + (
                    row[0] * tap[3 * a] + row[1] * tap[3 * a + 1] + row[2] * tap[3 * a + 2]
                )
            store(chunk * CHUNK + r, at, value)
        yield


def interleave(out_ref, final, first):
    _, rows, _, width = final.shape
    for h in range(2):
        for t in range(width // LANES):
            for r in range(rows):
                out_ref[h, t, pl.ds(r * 2 * GROUP + first, GROUP, stride=2), :] = final[
                    h, r, :, t * LANES : (t + 1) * LANES
                ]


def conv_steps(mixed, fwd_ref, bwd_ref, w_out_ref, h_ref, prod_ref, z_ref, put):
    block, width = prod_ref.shape[0], prod_ref.shape[1] // 2
    rows = block // GROUP
    for row in range(0, rows, 2):
        for h in range(2):
            for base in range(0, width, LANES):
                two = [
                    mixed(h * rows + r, width + base) * mixed(h * rows + r, 2 * width + base)
                    for r in (row, row + 1)
                ]
                at = h * width + base
                prod_ref[row * GROUP : (row + 2) * GROUP, at : at + LANES] = jnp.concatenate(
                    two, 0
                ).astype(BF16)
        if row % 4 == 2:
            yield
    spectra = jnp.dot(fwd_ref[...], prod_ref[...], preferred_element_type=F32)
    low, high = spectra[:, :width], spectra[:, width:]
    yield
    for k in range(0, rows, 2):
        parts = [[], [], [], []]
        for s in (k, k + 1):
            near_r, near_i, near_2, all_r, all_i, all_2 = (
                jnp.broadcast_to(h_ref[j * rows + s : j * rows + s + 1, :], (GROUP, width))
                for j in range(6)
            )
            re, im = slice(s * GROUP, (s + 1) * GROUP), slice(block + s * GROUP, block + (s + 1) * GROUP)
            lr, li, hr, hi = low[re], low[im], high[re], high[im]
            parts[0].append(lr * near_r - li * near_i)
            parts[1].append(lr * near_i + li * near_2)
            parts[2].append(lr * all_r - li * all_i + hr * near_r - hi * near_i)
            parts[3].append(lr * all_i + li * all_2 + hr * near_i + hi * near_2)
        for j in range(4):
            at, lane = (j % 2) * block + k * GROUP, (j // 2) * width
            z_ref[at : at + 2 * GROUP, lane : lane + width] = jnp.concatenate(parts[j], 0).astype(BF16)
        if k % 4 == 2:
            yield
    conv = jnp.dot(bwd_ref[...], z_ref[...], preferred_element_type=F32)
    yield
    gated = []
    for h in range(2):
        for r in range(rows):
            line = [
                mixed(h * rows + r, base)
                * conv[r * GROUP : (r + 1) * GROUP, h * width + base : h * width + base + LANES]
                for base in range(0, width, LANES)
            ]
            gated.append(jnp.concatenate(line, 1))
        yield
    final = jnp.dot(
        jnp.concatenate(gated, 0).astype(BF16), w_out_ref[...], preferred_element_type=F32
    )
    put(final.reshape(2, rows, GROUP, width))


def inner_kernel(
    _, other_ref, other_strip_ref,
    w_in_ref, taps_ref, fwd_ref, bwd_ref, w_out_ref, h_ref,
    p_ref, edge_mixed_ref, out_ref,
    mixed_ref, prod_ref, z_ref,
):
    core = lax.axis_index("row")
    rows, cols, width = other_ref.shape
    part = cols // 2
    height = 2 * rows
    start = pl.multiple_of(core * part, part)
    project(
        other_ref[:, pl.ds(start, part), :], other_strip_ref[...],
        core, (1 - core) * rows, w_in_ref, p_ref,
    )

    def store_inner(row, at, value):
        mixed_ref[row, :, at] = value

    def inner_chunk(i, carry):
        steps = depthwise_steps(
            p_ref, 1 - core, taps_ref, i, store_inner, range(0, 3 * width, LANES)
        )
        for _ in steps:
            pass
        return carry

    lax.fori_loop(0, height // CHUNK, inner_chunk, 0)

    def store_edge(row, at, value):
        edge_mixed_ref[row, :, at] = value

    def put(final):
        interleave(out_ref, final, 1 - core)

    edge = [
        depthwise_steps(p_ref, core, taps_ref, i, store_edge, [base])
        for i in range(height // CHUNK)
        for base in range(0, 3 * width, LANES)
    ]
    conv = conv_steps(
        lambda r, base: mixed_ref[r, :, base : base + LANES],
        fwd_ref, bwd_ref, w_out_ref, h_ref, prod_ref, z_ref, put,
    )
    done = 0
    for _ in conv:
        for step in edge[done : done + 2]:
            for _ in step:
                pass
        done += 2
    for step in edge[done:]:
        for _ in step:
            pass


def edge_kernel(
    _, halo_ref, mixed_ref, w_in_ref, taps_ref, fwd_ref, bwd_ref, w_out_ref, h_ref,
    out_ref, mine_ref, send_ref,
    strip_ref, side_ref, prod_ref, z_ref,
):
    core = lax.axis_index("row")
    rows, part, width = mine_ref.shape
    got = jnp.dot(halo_ref[...], w_in_ref[...], preferred_element_type=F32)
    side_ref[...] = edge_terms(
        got[:rows], got[rows:], 1 - core, column_taps(taps_ref, core, 0), strip_ref
    )
    sub = lax.broadcasted_iota(jnp.int32, (GROUP, LANES), 0)
    at_edge = sub == core * (GROUP - 1)

    def mixed(r, base):
        at = slice(base, base + LANES)
        add = jnp.broadcast_to(side_ref[r // 8, r % 8 : r % 8 + 1, at], (GROUP, LANES))
        return mixed_ref[r, :, at] + jnp.where(at_edge, add, 0.0)

    def put(final):
        interleave(out_ref, final, core)

    for _ in conv_steps(
        mixed, fwd_ref, bwd_ref, w_out_ref, h_ref, prod_ref, z_ref, put
    ):
        pass
    for ref, half in ((mine_ref, core), (send_ref, 1 - core)):
        for t in range(width // LANES):
            ref[:, :, t * LANES : (t + 1) * LANES] = (
                out_ref[half, t].reshape(rows, part, LANES).astype(BF16)
            )


def on_device(image_tokens, w_in, conv_kernel, conv_bias, long_filter, skip_gain, w_out):
    rows, cols, width = image_tokens.shape
    part = cols // 2
    height = 2 * rows
    n_col = lax.axis_size("col")
    core = lax.axis_index("row")
    fwd, bwd, spectra = transforms(rows, GROUP)
    spec_hi = spectra.astype(BF16)
    spec_lo = (spectra - spec_hi.astype(np.float64)).astype(BF16)
    spec = np.stack([spec_hi, spec_lo])
    vmem = pl.BlockSpec(memory_space=pltpu.VMEM)
    hbm = pl.BlockSpec(memory_space=pltpu.HBM)
    shape = jax.ShapeDtypeStruct
    limit = pltpu.CompilerParams(vmem_limit_bytes=24 * 1024 * 1024)

    p_shape = shape((3 * width // LANES, (height + 2) * PITCH + GROUP, LANES), F32)
    out_shape = shape((2, width // LANES, rows * part, LANES), F32)

    swap = [(0, 1), (1, 0)]
    rowmajor = Layout((0, 1, 2))
    image_tokens = with_layout_constraint(image_tokens, rowmajor)
    other = with_layout_constraint(lax.ppermute(image_tokens, "row", swap), rowmajor)

    def keep(array):
        return pltpu.with_memory_space_constraint(array, pltpu.HBM)

    projected, w_in_v, w_out_v, fwd_v, bwd_v, taps, spectrum, outer = pl.pallas_call(
        prep_kernel,
        out_shape=(
            p_shape,
            shape(w_in.shape, BF16),
            shape(w_out.shape, BF16),
            shape(fwd.shape, BF16),
            shape(bwd.shape, BF16),
            shape((16, 3 * width), F32),
            shape((6 * rows, width), F32),
            shape((rows, width), BF16),
        ),
        in_specs=[hbm] * 10,
        out_specs=(vmem,) * 8,
        scratch_shapes=[
            pltpu.VMEM(image_tokens.shape, BF16),
            pltpu.VMEM(spec.shape, BF16),
            pltpu.VMEM(long_filter.shape, BF16),
            pltpu.VMEM((1, width), F32),
            pltpu.VMEM(conv_kernel.shape, BF16),
            pltpu.VMEM(conv_bias.shape, F32),
            pltpu.SemaphoreType.DMA((10,)),
        ],
        compiler_params=limit,
        cost_estimate=pl.CostEstimate(flops=0, bytes_accessed=3 * 1024 * 1024, transcendentals=0),
    )(
        keep(image_tokens), keep(w_in), keep(w_out), keep(fwd.astype(BF16)), keep(bwd.astype(BF16)),
        keep(spec), keep(long_filter), keep(skip_gain[None]), keep(conv_kernel), keep(conv_bias),
    )

    def by_core(low, high):
        return jnp.where(core == 0, low, high)

    def column(low):
        return by_core(other[:, low], other[:, cols - 1 - low])

    pairs = []
    for j in range(n_col - 1):
        pairs += [(n_col + j, j + 1), (j + 1, n_col + j)]
    halo = lax.ppermute(jnp.concatenate([outer, column(0)], 0), ("row", "col"), pairs)
    _, edge_mixed, inner = pl.pallas_call(
        inner_kernel,
        out_shape=(p_shape, shape((height, GROUP, 3 * width), F32), out_shape),
        in_specs=[vmem] * 9,
        out_specs=(vmem,) * 3,
        input_output_aliases={0: 0},
        scratch_shapes=[
            pltpu.VMEM((height, GROUP, 3 * width), F32),
            pltpu.VMEM((rows * GROUP, 2 * width), BF16),
            pltpu.VMEM((2 * rows * GROUP, 2 * width), BF16),
        ],
        compiler_params=limit,
        cost_estimate=pl.CostEstimate(flops=10**9, bytes_accessed=12 * 1024 * 1024, transcendentals=0),
    )(projected, other, column(part), w_in_v, taps, fwd_v, bwd_v, w_out_v, spectrum)
    half_shape = shape((rows, part, width), BF16)
    _, mine, send = pl.pallas_call(
        edge_kernel,
        out_shape=(out_shape, half_shape, half_shape),
        in_specs=[vmem] * 9,
        out_specs=(vmem,) * 3,
        input_output_aliases={0: 0},
        scratch_shapes=[
            pltpu.VMEM((height + 16, 3 * width), F32),
            pltpu.VMEM((height // 8, 8, 3 * width), F32),
            pltpu.VMEM((rows * GROUP, 2 * width), BF16),
            pltpu.VMEM((2 * rows * GROUP, 2 * width), BF16),
        ],
        compiler_params=limit,
        cost_estimate=pl.CostEstimate(flops=3 * 10**8, bytes_accessed=4 * 1024 * 1024, transcendentals=0),
    )(inner, halo, edge_mixed, w_in_v, taps, fwd_v, bwd_v, w_out_v, spectrum)
    theirs = lax.ppermute(send, "row", swap)
    both = jnp.concatenate([mine, mine], 1)
    return lax.dynamic_update_slice_in_dim(both, theirs, (1 - core) * part, 1)


def solution(mesh):
    in_specs = (P("row", "col", None), P(), P(), P(), P(), P(), P())
    out_specs = P("row", "col", None)
    return jax.shard_map(
        on_device, mesh=mesh, in_specs=in_specs, out_specs=out_specs, check_vma=False
    )
```

```python
import jax
import jax.numpy as jnp
import numpy as np
from jax import lax
from jax.experimental import pallas as pl
from jax.experimental.layout import Layout, with_layout_constraint
from jax.experimental.pallas import tpu as pltpu
from jax.sharding import PartitionSpec as P

F32 = jnp.float32
BF16 = jnp.bfloat16


def transforms(half, group):
    size = 2 * half
    slot = np.arange(half)[:, None]
    pos = np.arange(half)[None, :]
    angle = 2 * np.pi * slot * pos / size
    real, imag = np.cos(angle), -np.sin(angle)
    imag[0] = (-1.0) ** np.arange(half)
    forward = np.concatenate([real, imag], 0)
    back_real = 2 * np.cos(angle.T) / size
    back_real[:, 0] = 1 / size
    back_imag = -2 * np.sin(angle.T) / size
    back_imag[:, 0] = (-1.0) ** np.arange(half) / size
    backward = np.concatenate([back_real, back_imag], 1)
    lag = np.arange(size)[None, :]
    angle = 2 * np.pi * slot * lag / size
    real, imag = np.cos(angle), -np.sin(angle)
    imag[0] = 0
    real2 = real.copy()
    real2[0] = (-1.0) ** np.arange(size)
    near = (lag < half).astype(np.float64)
    sign = (-1.0) ** slot
    sign2 = sign.copy()
    sign2[0] = 1
    spectra = np.concatenate(
        [real * near, imag * near, real2 * near, real * sign, imag * sign, real2 * sign2], 0
    )
    eye = np.eye(group)
    return np.kron(forward, eye), np.kron(backward, eye), spectra


LANES = 128
GROUP = 8
CHUNK = 8
PITCH = 24
FIRST = 8


def pick_column(block, column):
    rows, cols, width = block.shape
    shape = (rows, rows * cols)
    place = lax.broadcasted_iota(jnp.int32, shape, 1)
    wanted = lax.broadcasted_iota(jnp.int32, shape, 0) * cols + column
    return jnp.dot(
        jnp.where(place == wanted, 1.0, 0.0).astype(BF16),
        block.reshape(rows * cols, width),
        preferred_element_type=F32,
    ).astype(BF16)


def row_place(row, column):
    return row * PITCH + FIRST + column


def project(tokens, strip, core, w_in_ref, p_ref):
    rows, part, width = tokens.shape
    count = rows * part
    got = jnp.dot(
        jnp.concatenate([tokens.reshape(count, width), strip], 0),
        w_in_ref[...],
        preferred_element_type=F32,
    )
    for t in range(3 * width // LANES):
        at = slice(t * LANES, (t + 1) * LANES)
        for row in (0, rows + 1):
            place = row * PITCH
            p_ref[t, place : place + PITCH + GROUP, :] = jnp.zeros((PITCH + GROUP, LANES), F32)
        for r in range(rows):
            place = row_place(r + 1, 0)
            p_ref[t, place : place + part, :] = got[r * part : (r + 1) * part, at]
        for r in range(0, rows, GROUP):
            beside = got[count + r : count + r + GROUP, at]
            for column, value in (
                (-1, jnp.where(core == 1, beside, 0.0)),
                (part, jnp.where(core == 0, beside, 0.0)),
            ):
                place = row_place(r + 1, column)
                p_ref[t, pl.ds(place, GROUP, stride=PITCH), :] = value


def copy_row(from_ref, from_row, to_ref, to_row, part):
    sub = lax.broadcasted_iota(jnp.int32, (GROUP, LANES), 0)
    for t in range(from_ref.shape[0]):
        for place in range(0, FIRST + part + GROUP, GROUP):
            source = pl.ds(pl.multiple_of(from_row * PITCH + place, GROUP), GROUP)
            target = pl.ds(pl.multiple_of(to_row * PITCH + place, GROUP), GROUP)
            value = from_ref[t, source, :]
            if place < FIRST:
                value = jnp.where(sub == GROUP - 1, value, to_ref[t, target, :])
            elif place >= FIRST + part:
                value = jnp.where(sub == 0, value, to_ref[t, target, :])
            to_ref[t, target, :] = value


def prep_kernel(
    own_hbm, w_in_hbm, w_out_hbm, fwd_hbm, bwd_hbm, spec_hbm, filt_hbm, gain_hbm, kernel_hbm, bias_hbm,
    p_ref, w_in_ref, w_out_ref, fwd_ref, bwd_ref, taps_ref, h_ref, outer_ref,
    own_ref, spec_ref, filt_ref, gain_ref, kernel_ref, bias_ref, sems,
):
    core = lax.axis_index("row")
    rows, cols, width = own_ref.shape
    part = cols // 2
    moves = [
        (own_hbm, own_ref),
        (w_in_hbm, w_in_ref),
        (spec_hbm, spec_ref),
        (filt_hbm, filt_ref),
        (gain_hbm, gain_ref),
        (kernel_hbm, kernel_ref),
        (bias_hbm, bias_ref),
        (fwd_hbm, fwd_ref),
        (bwd_hbm, bwd_ref),
        (w_out_hbm, w_out_ref),
    ]
    copies = [pltpu.make_async_copy(src, dst, sems.at[i]) for i, (src, dst) in enumerate(moves)]
    for copy in copies:
        copy.start()
    copies[0].wait()
    start = pl.multiple_of(core * part, part)
    far = pl.multiple_of((1 - core) * part, part)
    inner_edge = core * (part - 1)
    outer_ref[...] = pick_column(own_ref[:, pl.ds(start, part), :], inner_edge)
    beside = pick_column(own_ref[:, pl.ds(far, part), :], inner_edge)
    for copy in copies[1:7]:
        copy.wait()
    project(own_ref[:, pl.ds(start, part), :], beside, core, w_in_ref, p_ref)
    filt = filt_ref[...]
    gain = gain_ref[...]
    spectrum = jnp.dot(spec_ref[0], filt, preferred_element_type=F32) + jnp.dot(
        spec_ref[1], filt, preferred_element_type=F32
    )
    for j in range(6):
        part_j = spectrum[j * rows : (j + 1) * rows]
        h_ref[j * rows : (j + 1) * rows, :] = part_j + gain if j in (0, 2) else part_j
    for a in range(3):
        taps_ref[3 * a : 3 * a + 3, :] = kernel_ref[a].astype(F32)
    taps_ref[9, :] = bias_ref[...]
    for copy in copies[7:]:
        copy.wait()


def edge_terms(first, second, core, taps, edge_ref, side_ref):
    rows, channels = first.shape
    for t in range(channels // LANES):
        at = slice(t * LANES, (t + 1) * LANES)
        edge_ref[t, 0:8, :] = jnp.zeros((8, LANES), F32)
        edge_ref[t, 4 * rows : 4 * rows + 8, :] = jnp.zeros((8, LANES), F32)
        for r in range(0, rows, 8):
            for row, half in ((core * rows, first), ((1 - core) * rows, second)):
                place = pl.ds(2 * (row + r + 1), 8, stride=2)
                edge_ref[t, place, :] = half[r : r + 8, at]
        for r in range(0, 2 * rows, 8):
            total = edge_ref[t, pl.ds(2 * r, 8, stride=2), :] * taps[0][:, at]
            for a in (1, 2):
                total = total + edge_ref[t, pl.ds(2 * (r + a), 8, stride=2), :] * taps[a][:, at]
            side_ref[r // 8, :, at] = total


def column_taps(taps_ref, core, on_core0):
    first, second = on_core0, 2 - on_core0
    return [
        jnp.where(
            core == 0,
            taps_ref[3 * a + first : 3 * a + first + 1, :],
            taps_ref[3 * a + second : 3 * a + second + 1, :],
        )
        for a in range(3)
    ]


def depthwise_steps(p_ref, first, taps_ref, chunk, store, bases):
    for base in bases:
        at = slice(base, base + LANES)
        tap = [
            jnp.broadcast_to(taps_ref[k : k + 1, at], (GROUP, LANES)) for k in range(10)
        ]
        loaded = [
            [
                p_ref[
                    base // LANES,
                    pl.ds(row_place(chunk * CHUNK + r, first + b - 1), GROUP, stride=2),
                    :,
                ]
                for b in range(3)
            ]
            for r in range(CHUNK + 2)
        ]
        for r in range(CHUNK):
            value = tap[9]
            for a in range(3):
                row = loaded[r + a]
                value = value + (
                    row[0] * tap[3 * a] + row[1] * tap[3 * a + 1] + row[2] * tap[3 * a + 2]
                )
            store(chunk * CHUNK + r, at, value)
        yield


def interleave(out_ref, final, first):
    _, rows, _, width = final.shape
    for h in range(2):
        for t in range(width // LANES):
            for r in range(rows):
                out_ref[h, t, pl.ds(r * 2 * GROUP + first, GROUP, stride=2), :] = final[
                    h, r, :, t * LANES : (t + 1) * LANES
                ]


def conv_steps(mixed, fwd_ref, bwd_ref, w_out_ref, h_ref, prod_ref, z_ref, put):
    block, width = prod_ref.shape[0], prod_ref.shape[1] // 2
    rows = block // GROUP
    for row in range(0, rows, 2):
        for h in range(2):
            for base in range(0, width, LANES):
                two = [
                    mixed(h * rows + r, width + base) * mixed(h * rows + r, 2 * width + base)
                    for r in (row, row + 1)
                ]
                at = h * width + base
                prod_ref[row * GROUP : (row + 2) * GROUP, at : at + LANES] = jnp.concatenate(
                    two, 0
                ).astype(BF16)
        if row % 4 == 2:
            yield
    spectra = jnp.dot(fwd_ref[...], prod_ref[...], preferred_element_type=F32)
    low, high = spectra[:, :width], spectra[:, width:]
    yield
    for k in range(0, rows, 2):
        parts = [[], [], [], []]
        for s in (k, k + 1):
            near_r, near_i, near_2, all_r, all_i, all_2 = (
                jnp.broadcast_to(h_ref[j * rows + s : j * rows + s + 1, :], (GROUP, width))
                for j in range(6)
            )
            re, im = slice(s * GROUP, (s + 1) * GROUP), slice(block + s * GROUP, block + (s + 1) * GROUP)
            lr, li, hr, hi = low[re], low[im], high[re], high[im]
            parts[0].append(lr * near_r - li * near_i)
            parts[1].append(lr * near_i + li * near_2)
            parts[2].append(lr * all_r - li * all_i + hr * near_r - hi * near_i)
            parts[3].append(lr * all_i + li * all_2 + hr * near_i + hi * near_2)
        for j in range(4):
            at, lane = (j % 2) * block + k * GROUP, (j // 2) * width
            z_ref[at : at + 2 * GROUP, lane : lane + width] = jnp.concatenate(parts[j], 0).astype(BF16)
        if k % 4 == 2:
            yield
    conv = jnp.dot(bwd_ref[...], z_ref[...], preferred_element_type=F32)
    yield
    gated = []
    for h in range(2):
        for r in range(rows):
            line = [
                mixed(h * rows + r, base)
                * conv[r * GROUP : (r + 1) * GROUP, h * width + base : h * width + base + LANES]
                for base in range(0, width, LANES)
            ]
            gated.append(jnp.concatenate(line, 1))
        yield
    final = jnp.dot(
        jnp.concatenate(gated, 0).astype(BF16), w_out_ref[...], preferred_element_type=F32
    )
    put(final.reshape(2, rows, GROUP, width))


def inner_kernel(
    _, other_ref, other_strip_ref,
    w_in_ref, taps_ref, fwd_ref, bwd_ref, w_out_ref, h_ref,
    p_ref, edge_mixed_ref, out_ref,
    q_ref, mixed_ref, prod_ref, z_ref,
):
    core = lax.axis_index("row")
    rows, cols, width = other_ref.shape
    part = cols // 2
    height = 2 * rows
    start = pl.multiple_of(core * part, part)
    channels = range(0, 3 * width, LANES)
    n_chunk = rows // CHUNK

    def store_in(ref, row0):
        def store(row, at, value):
            ref[row0 + row, :, at] = value

        return store

    own_at, other_at = core * rows, (1 - core) * rows

    def inner(ref, row0, chunk):
        return depthwise_steps(ref, 1 - core, taps_ref, chunk, store_in(mixed_ref, row0), channels)

    def edge(ref, row0, chunk):
        return depthwise_steps(ref, core, taps_ref, chunk, store_in(edge_mixed_ref, row0), channels)

    for i in range(n_chunk - 1):
        for _ in inner(p_ref, own_at, core + i):
            pass
    project(other_ref[:, pl.ds(start, part), :], other_strip_ref[...], core, w_in_ref, q_ref)
    copy_row(q_ref, 1 + core * (rows - 1), p_ref, (1 - core) * (rows + 1), part)
    copy_row(p_ref, rows - core * (rows - 1), q_ref, core * (rows + 1), part)
    for _ in inner(p_ref, own_at, (1 - core) * (n_chunk - 1)):
        pass

    def inner_chunk(i, carry):
        for _ in inner(q_ref, other_at, i):
            pass
        return carry

    lax.fori_loop(0, n_chunk, inner_chunk, 0)

    def put(final):
        interleave(out_ref, final, 1 - core)

    def edge_all():
        for ref, row0 in ((p_ref, own_at), (q_ref, other_at)):
            for i in range(n_chunk):
                yield from edge(ref, row0, i)

    steps = edge_all()
    conv = conv_steps(
        lambda r, base: mixed_ref[r, :, base : base + LANES],
        fwd_ref, bwd_ref, w_out_ref, h_ref, prod_ref, z_ref, put,
    )
    for _ in conv:
        for _ in range(2):
            next(steps, None)
    for _ in steps:
        pass


def edge_kernel(
    _, halo_ref, mixed_ref, w_in_ref, taps_ref, fwd_ref, bwd_ref, w_out_ref, h_ref,
    out_ref, mine_ref, send_ref,
    strip_ref, side_ref, prod_ref, z_ref,
):
    core = lax.axis_index("row")
    rows, part, width = mine_ref.shape
    got = jnp.dot(halo_ref[...], w_in_ref[...], preferred_element_type=F32)
    edge_terms(
        got[:rows], got[rows:], 1 - core, column_taps(taps_ref, core, 0), strip_ref, side_ref
    )
    sub = lax.broadcasted_iota(jnp.int32, (GROUP, LANES), 0)
    at_edge = sub == core * (GROUP - 1)

    def mixed(r, base):
        at = slice(base, base + LANES)
        add = jnp.broadcast_to(side_ref[r // 8, r % 8 : r % 8 + 1, at], (GROUP, LANES))
        return mixed_ref[r, :, at] + jnp.where(at_edge, add, 0.0)

    def put(final):
        interleave(out_ref, final, core)

    for _ in conv_steps(
        mixed, fwd_ref, bwd_ref, w_out_ref, h_ref, prod_ref, z_ref, put
    ):
        pass
    for ref, half in ((mine_ref, core), (send_ref, 1 - core)):
        for t in range(width // LANES):
            ref[:, :, t * LANES : (t + 1) * LANES] = (
                out_ref[half, t].reshape(rows, part, LANES).astype(BF16)
            )


def on_device(image_tokens, w_in, conv_kernel, conv_bias, long_filter, skip_gain, w_out):
    rows, cols, width = image_tokens.shape
    part = cols // 2
    height = 2 * rows
    n_col = lax.axis_size("col")
    core = lax.axis_index("row")
    fwd, bwd, spectra = transforms(rows, GROUP)
    spec_hi = spectra.astype(BF16)
    spec_lo = (spectra - spec_hi.astype(np.float64)).astype(BF16)
    spec = np.stack([spec_hi, spec_lo])
    vmem = pl.BlockSpec(memory_space=pltpu.VMEM)
    hbm = pl.BlockSpec(memory_space=pltpu.HBM)
    shape = jax.ShapeDtypeStruct
    limit = pltpu.CompilerParams(vmem_limit_bytes=24 * 1024 * 1024)

    p_shape = shape((3 * width // LANES, (rows + 2) * PITCH + GROUP, LANES), F32)
    out_shape = shape((2, width // LANES, rows * part, LANES), F32)

    swap = [(0, 1), (1, 0)]
    rowmajor = Layout((0, 1, 2))
    image_tokens = with_layout_constraint(image_tokens, rowmajor)
    other = with_layout_constraint(lax.ppermute(image_tokens, "row", swap), rowmajor)

    def keep(array):
        return pltpu.with_memory_space_constraint(array, pltpu.HBM)

    projected, w_in_v, w_out_v, fwd_v, bwd_v, taps, spectrum, outer = pl.pallas_call(
        prep_kernel,
        out_shape=(
            p_shape,
            shape(w_in.shape, BF16),
            shape(w_out.shape, BF16),
            shape(fwd.shape, BF16),
            shape(bwd.shape, BF16),
            shape((16, 3 * width), F32),
            shape((6 * rows, width), F32),
            shape((rows, width), BF16),
        ),
        in_specs=[hbm] * 10,
        out_specs=(vmem,) * 8,
        scratch_shapes=[
            pltpu.VMEM(image_tokens.shape, BF16),
            pltpu.VMEM(spec.shape, BF16),
            pltpu.VMEM(long_filter.shape, BF16),
            pltpu.VMEM((1, width), F32),
            pltpu.VMEM(conv_kernel.shape, BF16),
            pltpu.VMEM(conv_bias.shape, F32),
            pltpu.SemaphoreType.DMA((10,)),
        ],
        compiler_params=limit,
        cost_estimate=pl.CostEstimate(flops=0, bytes_accessed=3 * 1024 * 1024, transcendentals=0),
    )(
        keep(image_tokens), keep(w_in), keep(w_out), keep(fwd.astype(BF16)), keep(bwd.astype(BF16)),
        keep(spec), keep(long_filter), keep(skip_gain[None]), keep(conv_kernel), keep(conv_bias),
    )

    def by_core(low, high):
        return jnp.where(core == 0, low, high)

    def column(low):
        return by_core(other[:, low], other[:, cols - 1 - low])

    pairs = []
    for j in range(n_col - 1):
        pairs += [(n_col + j, j + 1), (j + 1, n_col + j)]
    halo = lax.ppermute(jnp.concatenate([outer, column(0)], 0), ("row", "col"), pairs)
    _, edge_mixed, inner = pl.pallas_call(
        inner_kernel,
        out_shape=(p_shape, shape((height, GROUP, 3 * width), F32), out_shape),
        in_specs=[vmem] * 9,
        out_specs=(vmem,) * 3,
        input_output_aliases={0: 0},
        scratch_shapes=[
            pltpu.VMEM(p_shape.shape, F32),
            pltpu.VMEM((height, GROUP, 3 * width), F32),
            pltpu.VMEM((rows * GROUP, 2 * width), BF16),
            pltpu.VMEM((2 * rows * GROUP, 2 * width), BF16),
        ],
        compiler_params=limit,
        cost_estimate=pl.CostEstimate(flops=10**9, bytes_accessed=12 * 1024 * 1024, transcendentals=0),
    )(projected, other, column(part), w_in_v, taps, fwd_v, bwd_v, w_out_v, spectrum)
    half_shape = shape((rows, part, width), BF16)
    _, mine, send = pl.pallas_call(
        edge_kernel,
        out_shape=(out_shape, half_shape, half_shape),
        in_specs=[vmem] * 9,
        out_specs=(vmem,) * 3,
        input_output_aliases={0: 0},
        scratch_shapes=[
            pltpu.VMEM((3 * width // LANES, 2 * height + 8, LANES), F32),
            pltpu.VMEM((height // 8, 8, 3 * width), F32),
            pltpu.VMEM((rows * GROUP, 2 * width), BF16),
            pltpu.VMEM((2 * rows * GROUP, 2 * width), BF16),
        ],
        compiler_params=limit,
        cost_estimate=pl.CostEstimate(flops=3 * 10**8, bytes_accessed=4 * 1024 * 1024, transcendentals=0),
    )(inner, halo, edge_mixed, w_in_v, taps, fwd_v, bwd_v, w_out_v, spectrum)
    theirs = lax.ppermute(send, "row", swap)
    both = jnp.concatenate([mine, mine], 1)
    return lax.dynamic_update_slice_in_dim(both, theirs, (1 - core) * part, 1)


def solution(mesh):
    in_specs = (P("row", "col", None), P(), P(), P(), P(), P(), P())
    out_specs = P("row", "col", None)
    return jax.shard_map(
        on_device, mesh=mesh, in_specs=in_specs, out_specs=out_specs, check_vma=False
    )
```

```python
import jax
import jax.numpy as jnp
import numpy as np
from jax import lax
from jax.experimental import pallas as pl
from jax.experimental.layout import Layout, with_layout_constraint
from jax.experimental.pallas import tpu as pltpu
from jax.sharding import PartitionSpec as P

F32 = jnp.float32
BF16 = jnp.bfloat16


def transforms(half, group):
    size = 2 * half
    slot = np.arange(half)[:, None]
    pos = np.arange(half)[None, :]
    angle = 2 * np.pi * slot * pos / size
    real, imag = np.cos(angle), -np.sin(angle)
    imag[0] = (-1.0) ** np.arange(half)
    forward = np.concatenate([real, imag], 0)
    back_real = 2 * np.cos(angle.T) / size
    back_real[:, 0] = 1 / size
    back_imag = -2 * np.sin(angle.T) / size
    back_imag[:, 0] = (-1.0) ** np.arange(half) / size
    backward = np.concatenate([back_real, back_imag], 1)
    lag = np.arange(size)[None, :]
    angle = 2 * np.pi * slot * lag / size
    real, imag = np.cos(angle), -np.sin(angle)
    imag[0] = 0
    real2 = real.copy()
    real2[0] = (-1.0) ** np.arange(size)
    near = (lag < half).astype(np.float64)
    sign = (-1.0) ** slot
    sign2 = sign.copy()
    sign2[0] = 1
    spectra = np.concatenate(
        [real * near, imag * near, real2 * near, real * sign, imag * sign, real2 * sign2], 0
    )
    eye = np.eye(group)
    return np.kron(forward, eye), np.kron(backward, eye), spectra


LANES = 128
GROUP = 8
CHUNK = 16
PITCH = 24
FIRST = 8


def pick_column(block, column):
    rows, cols, width = block.shape
    shape = (rows, rows * cols)
    place = lax.broadcasted_iota(jnp.int32, shape, 1)
    wanted = lax.broadcasted_iota(jnp.int32, shape, 0) * cols + column
    return jnp.dot(
        jnp.where(place == wanted, 1.0, 0.0).astype(BF16),
        block.reshape(rows * cols, width),
        preferred_element_type=F32,
    ).astype(BF16)


def row_place(row, column):
    return row * PITCH + FIRST + column


def project(tokens, strip, core, w_in_ref, p_ref):
    rows, part, width = tokens.shape
    count = rows * part
    got = jnp.dot(tokens.reshape(count, width), w_in_ref[...], preferred_element_type=F32)
    got_strip = jnp.dot(strip, w_in_ref[...], preferred_element_type=F32)
    for t in range(3 * width // LANES):
        at = slice(t * LANES, (t + 1) * LANES)
        for row in (0, rows + 1):
            place = row * PITCH
            p_ref[t, place : place + PITCH + GROUP, :] = jnp.zeros((PITCH + GROUP, LANES), F32)
        for r in range(rows):
            place = row_place(r + 1, 0)
            p_ref[t, place : place + part, :] = got[r * part : (r + 1) * part, at]
        for r in range(0, rows, GROUP):
            beside = got_strip[r : r + GROUP, at]
            for column, value in (
                (-1, jnp.where(core == 1, beside, 0.0)),
                (part, jnp.where(core == 0, beside, 0.0)),
            ):
                place = row_place(r + 1, column)
                p_ref[t, pl.ds(place, GROUP, stride=PITCH), :] = value


def copy_row(from_ref, from_row, to_ref, to_row, part):
    sub = lax.broadcasted_iota(jnp.int32, (GROUP, LANES), 0)
    for t in range(from_ref.shape[0]):
        for place in range(0, FIRST + part + GROUP, GROUP):
            source = pl.ds(pl.multiple_of(from_row * PITCH + place, GROUP), GROUP)
            target = pl.ds(pl.multiple_of(to_row * PITCH + place, GROUP), GROUP)
            value = from_ref[t, source, :]
            if place < FIRST:
                value = jnp.where(sub == GROUP - 1, value, to_ref[t, target, :])
            elif place >= FIRST + part:
                value = jnp.where(sub == 0, value, to_ref[t, target, :])
            to_ref[t, target, :] = value


def prep_kernel(
    own_hbm, w_in_hbm, w_out_hbm, fwd_hbm, bwd_hbm, spec_hbm, filt_hbm, gain_hbm, kernel_hbm, bias_hbm,
    p_ref, w_in_ref, w_out_ref, fwd_ref, bwd_ref, taps_ref, h_ref, outer_ref,
    own_ref, spec_ref, filt_ref, gain_ref, kernel_ref, bias_ref, sems,
):
    core = lax.axis_index("row")
    rows, cols, width = own_ref.shape
    part = cols // 2
    moves = [
        (own_hbm, own_ref),
        (w_in_hbm, w_in_ref),
        (spec_hbm, spec_ref),
        (filt_hbm, filt_ref),
        (gain_hbm, gain_ref),
        (kernel_hbm, kernel_ref),
        (bias_hbm, bias_ref),
        (fwd_hbm, fwd_ref),
        (bwd_hbm, bwd_ref),
        (w_out_hbm, w_out_ref),
    ]
    copies = [pltpu.make_async_copy(src, dst, sems.at[i]) for i, (src, dst) in enumerate(moves)]
    for copy in copies:
        copy.start()
    copies[0].wait()
    start = pl.multiple_of(core * part, part)
    far = pl.multiple_of((1 - core) * part, part)
    inner_edge = core * (part - 1)
    outer_ref[...] = pick_column(own_ref[:, pl.ds(start, part), :], inner_edge)
    beside = pick_column(own_ref[:, pl.ds(far, part), :], inner_edge)
    for copy in copies[1:7]:
        copy.wait()
    project(own_ref[:, pl.ds(start, part), :], beside, core, w_in_ref, p_ref)
    filt = filt_ref[...]
    gain = gain_ref[...]
    spectrum = jnp.dot(spec_ref[0], filt, preferred_element_type=F32) + jnp.dot(
        spec_ref[1], filt, preferred_element_type=F32
    )
    for j in range(6):
        part_j = spectrum[j * rows : (j + 1) * rows]
        h_ref[j * rows : (j + 1) * rows, :] = part_j + gain if j in (0, 2) else part_j
    for a in range(3):
        taps_ref[3 * a : 3 * a + 3, :] = kernel_ref[a].astype(F32)
    taps_ref[9, :] = bias_ref[...]
    for copy in copies[7:]:
        copy.wait()


def edge_terms(first, second, core, taps, edge_ref, side_ref):
    rows, channels = first.shape
    for t in range(channels // LANES):
        at = slice(t * LANES, (t + 1) * LANES)
        edge_ref[t, 0:8, :] = jnp.zeros((8, LANES), F32)
        edge_ref[t, 4 * rows : 4 * rows + 8, :] = jnp.zeros((8, LANES), F32)
        for r in range(0, rows, 8):
            for row, half in ((core * rows, first), ((1 - core) * rows, second)):
                place = pl.ds(2 * (row + r + 1), 8, stride=2)
                edge_ref[t, place, :] = half[r : r + 8, at]
        for r in range(0, 2 * rows, 8):
            total = edge_ref[t, pl.ds(2 * r, 8, stride=2), :] * taps[0][:, at]
            for a in (1, 2):
                total = total + edge_ref[t, pl.ds(2 * (r + a), 8, stride=2), :] * taps[a][:, at]
            side_ref[r // 8, :, at] = total


def column_taps(taps_ref, core, on_core0):
    first, second = on_core0, 2 - on_core0
    return [
        jnp.where(
            core == 0,
            taps_ref[3 * a + first : 3 * a + first + 1, :],
            taps_ref[3 * a + second : 3 * a + second + 1, :],
        )
        for a in range(3)
    ]


def depthwise_steps(p_ref, first, taps_ref, chunk, store, bases):
    for base in bases:
        at = slice(base, base + LANES)
        tap = [
            jnp.broadcast_to(taps_ref[k : k + 1, at], (GROUP, LANES)) for k in range(10)
        ]
        loaded = [
            [
                p_ref[
                    base // LANES,
                    pl.ds(row_place(chunk * CHUNK + r, first + b - 1), GROUP, stride=2),
                    :,
                ]
                for b in range(3)
            ]
            for r in range(CHUNK + 2)
        ]
        for r in range(CHUNK):
            value = tap[9]
            for a in range(3):
                row = loaded[r + a]
                value = value + (
                    row[0] * tap[3 * a] + row[1] * tap[3 * a + 1] + row[2] * tap[3 * a + 2]
                )
            store(chunk * CHUNK + r, at, value)
        yield


def interleave(out_ref, final, first):
    _, rows, _, width = final.shape
    for h in range(2):
        for t in range(width // LANES):
            for r in range(rows):
                out_ref[h, t, pl.ds(r * 2 * GROUP + first, GROUP, stride=2), :] = final[
                    h, r, :, t * LANES : (t + 1) * LANES
                ]


def conv_steps(mixed, fwd_ref, bwd_ref, w_out_ref, h_ref, prod_ref, z_ref, put):
    streams, block, _ = prod_ref.shape
    rows = block // GROUP
    width = streams * LANES

    def products(n):
        base = n * LANES
        for row in range(0, rows, 2):
            for h in range(2):
                two = [
                    mixed(h * rows + r, width + base) * mixed(h * rows + r, 2 * width + base)
                    for r in (row, row + 1)
                ]
                prod_ref[n, row * GROUP : (row + 2) * GROUP, h * LANES : (h + 1) * LANES] = (
                    jnp.concatenate(two, 0).astype(BF16)
                )
        return jnp.dot(fwd_ref[...], prod_ref[n], preferred_element_type=F32)

    def filtered(n, spectra):
        base = n * LANES
        low, high = spectra[:, :LANES], spectra[:, LANES:]
        for k in range(0, rows, 2):
            parts = [[], [], [], []]
            for s in (k, k + 1):
                near_r, near_i, near_2, all_r, all_i, all_2 = (
                    jnp.broadcast_to(
                        h_ref[j * rows + s : j * rows + s + 1, base : base + LANES], (GROUP, LANES)
                    )
                    for j in range(6)
                )
                re = slice(s * GROUP, (s + 1) * GROUP)
                im = slice(block + s * GROUP, block + (s + 1) * GROUP)
                lr, li, hr, hi = low[re], low[im], high[re], high[im]
                parts[0].append(lr * near_r - li * near_i)
                parts[1].append(lr * near_i + li * near_2)
                parts[2].append(lr * all_r - li * all_i + hr * near_r - hi * near_i)
                parts[3].append(lr * all_i + li * all_2 + hr * near_i + hi * near_2)
            for j in range(4):
                at, lane = (j % 2) * block + k * GROUP, (j // 2) * LANES
                z_ref[n, at : at + 2 * GROUP, lane : lane + LANES] = jnp.concatenate(
                    parts[j], 0
                ).astype(BF16)
        return jnp.dot(bwd_ref[...], z_ref[n], preferred_element_type=F32)

    def gated(n, conv):
        line = [
            mixed(h * rows + r, n * LANES)
            * conv[r * GROUP : (r + 1) * GROUP, h * LANES : (h + 1) * LANES]
            for h in range(2)
            for r in range(rows)
        ]
        return jnp.concatenate(line, 0).astype(BF16)

    spectra = []
    for n in range(streams):
        spectra.append(products(n))
        yield
    convs = []
    for n in range(streams):
        convs.append(filtered(n, spectra[n]))
        yield
    final = jnp.dot(
        jnp.concatenate([gated(n, convs[n]) for n in range(streams)], 1),
        w_out_ref[...],
        preferred_element_type=F32,
    )
    yield
    put(final.reshape(2, rows, GROUP, width))


def inner_kernel(
    _, other_ref, other_strip_ref,
    w_in_ref, taps_ref, fwd_ref, bwd_ref, w_out_ref, h_ref,
    p_ref, edge_mixed_ref, out_ref,
    q_ref, mixed_ref, prod_ref, z_ref,
):
    core = lax.axis_index("row")
    rows, cols, width = other_ref.shape
    part = cols // 2
    height = 2 * rows
    start = pl.multiple_of(core * part, part)
    channels = range(0, 3 * width, LANES)
    n_chunk = rows // CHUNK

    def store_in(ref, row0):
        def store(row, at, value):
            ref[row0 + row, :, at] = value

        return store

    own_at, other_at = core * rows, (1 - core) * rows

    def inner(ref, row0, chunk):
        return depthwise_steps(ref, 1 - core, taps_ref, chunk, store_in(mixed_ref, row0), channels)

    def edge(ref, row0, chunk):
        return depthwise_steps(ref, core, taps_ref, chunk, store_in(edge_mixed_ref, row0), channels)

    for i in range(n_chunk - 1):
        for _ in inner(p_ref, own_at, core + i):
            pass
    project(other_ref[:, pl.ds(start, part), :], other_strip_ref[...], core, w_in_ref, q_ref)
    copy_row(q_ref, 1 + core * (rows - 1), p_ref, (1 - core) * (rows + 1), part)
    copy_row(p_ref, rows - core * (rows - 1), q_ref, core * (rows + 1), part)
    for _ in inner(p_ref, own_at, (1 - core) * (n_chunk - 1)):
        pass

    def inner_chunk(i, carry):
        for _ in inner(q_ref, other_at, i):
            pass
        return carry

    lax.fori_loop(0, n_chunk, inner_chunk, 0)

    def put(final):
        interleave(out_ref, final, 1 - core)

    def edge_all():
        for ref, row0 in ((p_ref, own_at), (q_ref, other_at)):
            for i in range(n_chunk):
                yield from edge(ref, row0, i)

    steps = edge_all()
    conv = conv_steps(
        lambda r, base: mixed_ref[r, :, base : base + LANES],
        fwd_ref, bwd_ref, w_out_ref, h_ref, prod_ref, z_ref, put,
    )
    for _ in conv:
        for _ in range(5):
            next(steps, None)
    for _ in steps:
        pass


def edge_kernel(
    _, halo_ref, mixed_ref, w_in_ref, taps_ref, fwd_ref, bwd_ref, w_out_ref, h_ref,
    out_ref, mine_ref, send_ref,
    strip_ref, side_ref, prod_ref, z_ref,
):
    core = lax.axis_index("row")
    rows, part, width = mine_ref.shape
    got = jnp.dot(halo_ref[...], w_in_ref[...], preferred_element_type=F32)
    edge_terms(
        got[:rows], got[rows:], 1 - core, column_taps(taps_ref, core, 0), strip_ref, side_ref
    )
    sub = lax.broadcasted_iota(jnp.int32, (GROUP, LANES), 0)
    at_edge = sub == core * (GROUP - 1)

    def mixed(r, base):
        at = slice(base, base + LANES)
        add = jnp.broadcast_to(side_ref[r // 8, r % 8 : r % 8 + 1, at], (GROUP, LANES))
        return mixed_ref[r, :, at] + jnp.where(at_edge, add, 0.0)

    def put(final):
        interleave(out_ref, final, core)

    for _ in conv_steps(
        mixed, fwd_ref, bwd_ref, w_out_ref, h_ref, prod_ref, z_ref, put
    ):
        pass
    for ref, half in ((mine_ref, core), (send_ref, 1 - core)):
        for t in range(width // LANES):
            ref[:, :, t * LANES : (t + 1) * LANES] = (
                out_ref[half, t].reshape(rows, part, LANES).astype(BF16)
            )


def on_device(image_tokens, w_in, conv_kernel, conv_bias, long_filter, skip_gain, w_out):
    rows, cols, width = image_tokens.shape
    part = cols // 2
    height = 2 * rows
    n_col = lax.axis_size("col")
    core = lax.axis_index("row")
    fwd, bwd, spectra = transforms(rows, GROUP)
    spec_hi = spectra.astype(BF16)
    spec_lo = (spectra - spec_hi.astype(np.float64)).astype(BF16)
    spec = np.stack([spec_hi, spec_lo])
    vmem = pl.BlockSpec(memory_space=pltpu.VMEM)
    hbm = pl.BlockSpec(memory_space=pltpu.HBM)
    shape = jax.ShapeDtypeStruct
    limit = pltpu.CompilerParams(vmem_limit_bytes=24 * 1024 * 1024)

    p_shape = shape((3 * width // LANES, (rows + 2) * PITCH + GROUP, LANES), F32)
    out_shape = shape((2, width // LANES, rows * part, LANES), F32)

    swap = [(0, 1), (1, 0)]
    rowmajor = Layout((0, 1, 2))
    image_tokens = with_layout_constraint(image_tokens, rowmajor)
    other = with_layout_constraint(lax.ppermute(image_tokens, "row", swap), rowmajor)

    def keep(array):
        return pltpu.with_memory_space_constraint(array, pltpu.HBM)

    projected, w_in_v, w_out_v, fwd_v, bwd_v, taps, spectrum, outer = pl.pallas_call(
        prep_kernel,
        out_shape=(
            p_shape,
            shape(w_in.shape, BF16),
            shape(w_out.shape, BF16),
            shape(fwd.shape, BF16),
            shape(bwd.shape, BF16),
            shape((16, 3 * width), F32),
            shape((6 * rows, width), F32),
            shape((rows, width), BF16),
        ),
        in_specs=[hbm] * 10,
        out_specs=(vmem,) * 8,
        scratch_shapes=[
            pltpu.VMEM(image_tokens.shape, BF16),
            pltpu.VMEM(spec.shape, BF16),
            pltpu.VMEM(long_filter.shape, BF16),
            pltpu.VMEM((1, width), F32),
            pltpu.VMEM(conv_kernel.shape, BF16),
            pltpu.VMEM(conv_bias.shape, F32),
            pltpu.SemaphoreType.DMA((10,)),
        ],
        compiler_params=limit,
        cost_estimate=pl.CostEstimate(flops=0, bytes_accessed=3 * 1024 * 1024, transcendentals=0),
    )(
        keep(image_tokens), keep(w_in), keep(w_out), keep(fwd.astype(BF16)), keep(bwd.astype(BF16)),
        keep(spec), keep(long_filter), keep(skip_gain[None]), keep(conv_kernel), keep(conv_bias),
    )

    def by_core(low, high):
        return jnp.where(core == 0, low, high)

    def column(low):
        return by_core(other[:, low], other[:, cols - 1 - low])

    pairs = []
    for j in range(n_col - 1):
        pairs += [(n_col + j, j + 1), (j + 1, n_col + j)]
    halo = lax.ppermute(jnp.concatenate([outer, column(0)], 0), ("row", "col"), pairs)
    _, edge_mixed, inner = pl.pallas_call(
        inner_kernel,
        out_shape=(p_shape, shape((height, GROUP, 3 * width), F32), out_shape),
        in_specs=[vmem] * 9,
        out_specs=(vmem,) * 3,
        input_output_aliases={0: 0},
        scratch_shapes=[
            pltpu.VMEM(p_shape.shape, F32),
            pltpu.VMEM((height, GROUP, 3 * width), F32),
            pltpu.VMEM((width // LANES, rows * GROUP, 2 * LANES), BF16),
            pltpu.VMEM((width // LANES, 2 * rows * GROUP, 2 * LANES), BF16),
        ],
        compiler_params=limit,
        cost_estimate=pl.CostEstimate(flops=10**9, bytes_accessed=12 * 1024 * 1024, transcendentals=0),
    )(projected, other, column(part), w_in_v, taps, fwd_v, bwd_v, w_out_v, spectrum)
    half_shape = shape((rows, part, width), BF16)
    _, mine, send = pl.pallas_call(
        edge_kernel,
        out_shape=(out_shape, half_shape, half_shape),
        in_specs=[vmem] * 9,
        out_specs=(vmem,) * 3,
        input_output_aliases={0: 0},
        scratch_shapes=[
            pltpu.VMEM((3 * width // LANES, 2 * height + 8, LANES), F32),
            pltpu.VMEM((height // 8, 8, 3 * width), F32),
            pltpu.VMEM((width // LANES, rows * GROUP, 2 * LANES), BF16),
            pltpu.VMEM((width // LANES, 2 * rows * GROUP, 2 * LANES), BF16),
        ],
        compiler_params=limit,
        cost_estimate=pl.CostEstimate(flops=3 * 10**8, bytes_accessed=4 * 1024 * 1024, transcendentals=0),
    )(inner, halo, edge_mixed, w_in_v, taps, fwd_v, bwd_v, w_out_v, spectrum)
    theirs = lax.ppermute(send, "row", swap)
    both = jnp.concatenate([mine, mine], 1)
    return lax.dynamic_update_slice_in_dim(both, theirs, (1 - core) * part, 1)


def solution(mesh):
    in_specs = (P("row", "col", None), P(), P(), P(), P(), P(), P())
    out_specs = P("row", "col", None)
    return jax.shard_map(
        on_device, mesh=mesh, in_specs=in_specs, out_specs=out_specs, check_vma=False
    )
```

```python
import jax
import jax.numpy as jnp
import numpy as np
from jax import lax
from jax.experimental import pallas as pl
from jax.experimental.layout import Layout, with_layout_constraint
from jax.experimental.pallas import tpu as pltpu
from jax.sharding import PartitionSpec as P

F32 = jnp.float32
BF16 = jnp.bfloat16


def transforms(half, group):
    size = 2 * half
    slot = np.arange(half)[:, None]
    pos = np.arange(half)[None, :]
    angle = 2 * np.pi * slot * pos / size
    real, imag = np.cos(angle), -np.sin(angle)
    imag[0] = (-1.0) ** np.arange(half)
    forward = np.concatenate([real, imag], 0)
    back_real = 2 * np.cos(angle.T) / size
    back_real[:, 0] = 1 / size
    back_imag = -2 * np.sin(angle.T) / size
    back_imag[:, 0] = (-1.0) ** np.arange(half) / size
    backward = np.concatenate([back_real, back_imag], 1)
    lag = np.arange(size)[None, :]
    angle = 2 * np.pi * slot * lag / size
    real, imag = np.cos(angle), -np.sin(angle)
    imag[0] = 0
    real2 = real.copy()
    real2[0] = (-1.0) ** np.arange(size)
    near = (lag < half).astype(np.float64)
    sign = (-1.0) ** slot
    sign2 = sign.copy()
    sign2[0] = 1
    spectra = np.concatenate(
        [real * near, imag * near, real2 * near, real * sign, imag * sign, real2 * sign2], 0
    )
    eye = np.eye(group)
    return np.kron(forward, eye), np.kron(backward, eye), spectra


LANES = 128
GROUP = 8
CHUNK = 16
PITCH = 24
FIRST = 8


def pick_column(block, column):
    rows, cols, width = block.shape
    shape = (rows, rows * cols)
    place = lax.broadcasted_iota(jnp.int32, shape, 1)
    wanted = lax.broadcasted_iota(jnp.int32, shape, 0) * cols + column
    return jnp.dot(
        jnp.where(place == wanted, 1.0, 0.0).astype(BF16),
        block.reshape(rows * cols, width),
        preferred_element_type=F32,
    ).astype(BF16)


def row_place(row, column):
    return row * PITCH + FIRST + column


def project(tokens, strip, core, w_in_ref, p_ref):
    rows, part, width = tokens.shape
    count = rows * part
    got = jnp.dot(tokens.reshape(count, width), w_in_ref[...], preferred_element_type=F32)
    got_strip = jnp.dot(strip, w_in_ref[...], preferred_element_type=F32)
    for t in range(3 * width // LANES):
        at = slice(t * LANES, (t + 1) * LANES)
        for row in (0, rows + 1):
            place = row * PITCH
            p_ref[t, place : place + PITCH + GROUP, :] = jnp.zeros((PITCH + GROUP, LANES), F32)
        for r in range(rows):
            place = row_place(r + 1, 0)
            p_ref[t, place : place + part, :] = got[r * part : (r + 1) * part, at]
        for r in range(0, rows, GROUP):
            beside = got_strip[r : r + GROUP, at]
            for column, value in (
                (-1, jnp.where(core == 1, beside, 0.0)),
                (part, jnp.where(core == 0, beside, 0.0)),
            ):
                place = row_place(r + 1, column)
                p_ref[t, pl.ds(place, GROUP, stride=PITCH), :] = value


def copy_row(from_ref, from_row, to_ref, to_row, part):
    sub = lax.broadcasted_iota(jnp.int32, (GROUP, LANES), 0)
    for t in range(from_ref.shape[0]):
        for place in range(0, FIRST + part + GROUP, GROUP):
            source = pl.ds(pl.multiple_of(from_row * PITCH + place, GROUP), GROUP)
            target = pl.ds(pl.multiple_of(to_row * PITCH + place, GROUP), GROUP)
            value = from_ref[t, source, :]
            if place < FIRST:
                value = jnp.where(sub == GROUP - 1, value, to_ref[t, target, :])
            elif place >= FIRST + part:
                value = jnp.where(sub == 0, value, to_ref[t, target, :])
            to_ref[t, target, :] = value


def prep_kernel(
    own_hbm, w_in_hbm, w_out_hbm, fwd_hbm, bwd_hbm, spec_hbm, filt_hbm, gain_hbm, kernel_hbm, bias_hbm,
    p_ref, w_in_ref, w_out_ref, fwd_ref, bwd_ref, taps_ref, h_ref, outer_ref,
    own_ref, spec_ref, filt_ref, gain_ref, kernel_ref, bias_ref, sems,
):
    core = lax.axis_index("row")
    rows, cols, width = own_ref.shape
    part = cols // 2
    moves = [
        (own_hbm, own_ref),
        (w_in_hbm, w_in_ref),
        (spec_hbm, spec_ref),
        (filt_hbm, filt_ref),
        (gain_hbm, gain_ref),
        (kernel_hbm, kernel_ref),
        (bias_hbm, bias_ref),
        (fwd_hbm, fwd_ref),
        (bwd_hbm, bwd_ref),
        (w_out_hbm, w_out_ref),
    ]
    copies = [pltpu.make_async_copy(src, dst, sems.at[i]) for i, (src, dst) in enumerate(moves)]
    for copy in copies:
        copy.start()
    copies[0].wait()
    start = pl.multiple_of(core * part, part)
    far = pl.multiple_of((1 - core) * part, part)
    inner_edge = core * (part - 1)
    outer_ref[...] = pick_column(own_ref[:, pl.ds(start, part), :], inner_edge)
    beside = pick_column(own_ref[:, pl.ds(far, part), :], inner_edge)
    for copy in copies[1:7]:
        copy.wait()
    project(own_ref[:, pl.ds(start, part), :], beside, core, w_in_ref, p_ref)
    filt = filt_ref[...]
    gain = gain_ref[...]
    spectrum = jnp.dot(spec_ref[0], filt, preferred_element_type=F32) + jnp.dot(
        spec_ref[1], filt, preferred_element_type=F32
    )
    for j in range(6):
        part_j = spectrum[j * rows : (j + 1) * rows]
        h_ref[j * rows : (j + 1) * rows, :] = part_j + gain if j in (0, 2) else part_j
    for a in range(3):
        taps_ref[3 * a : 3 * a + 3, :] = kernel_ref[a].astype(F32)
    taps_ref[9, :] = bias_ref[...]
    for copy in copies[7:]:
        copy.wait()


def add_edge_terms(first, second, core, taps, edge_ref, mixed_ref, column):
    rows, channels = first.shape
    for t in range(channels // LANES):
        at = slice(t * LANES, (t + 1) * LANES)
        edge_ref[t, 0:8, :] = jnp.zeros((8, LANES), F32)
        edge_ref[t, 4 * rows : 4 * rows + 8, :] = jnp.zeros((8, LANES), F32)
        for r in range(0, rows, 8):
            for row, half in ((core * rows, first), ((1 - core) * rows, second)):
                place = pl.ds(2 * (row + r + 1), 8, stride=2)
                edge_ref[t, place, :] = half[r : r + 8, at]
        for r in range(0, 2 * rows, 8):
            place = pl.ds(r * GROUP + column, 8, stride=GROUP)
            total = mixed_ref[t, place, :]
            for a in range(3):
                total = total + edge_ref[t, pl.ds(2 * (r + a), 8, stride=2), :] * taps[a][:, at]
            mixed_ref[t, place, :] = total


def column_taps(taps_ref, core, on_core0):
    first, second = on_core0, 2 - on_core0
    return [
        jnp.where(
            core == 0,
            taps_ref[3 * a + first : 3 * a + first + 1, :],
            taps_ref[3 * a + second : 3 * a + second + 1, :],
        )
        for a in range(3)
    ]


def depthwise_steps(p_ref, first, taps_ref, chunk, store, bases):
    for base in bases:
        at = slice(base, base + LANES)
        tap = [
            jnp.broadcast_to(taps_ref[k : k + 1, at], (GROUP, LANES)) for k in range(10)
        ]
        loaded = [
            [
                p_ref[
                    base // LANES,
                    pl.ds(row_place(chunk * CHUNK + r, first + b - 1), GROUP, stride=2),
                    :,
                ]
                for b in range(3)
            ]
            for r in range(CHUNK + 2)
        ]
        for r in range(CHUNK):
            value = tap[9]
            for a in range(3):
                row = loaded[r + a]
                value = value + (
                    row[0] * tap[3 * a] + row[1] * tap[3 * a + 1] + row[2] * tap[3 * a + 2]
                )
            store(chunk * CHUNK + r, at, value)
        yield


def interleave(out_ref, final, first):
    _, rows, _, width = final.shape
    for h in range(2):
        for t in range(width // LANES):
            for r in range(rows):
                out_ref[h, t, pl.ds(r * 2 * GROUP + first, GROUP, stride=2), :] = final[
                    h, r, :, t * LANES : (t + 1) * LANES
                ]


def conv_steps(mixed, fwd_ref, bwd_ref, w_out_ref, h_ref, prod_ref, z_ref, put):
    streams, block, lanes = prod_ref.shape
    lanes = lanes // 2
    rows = block // GROUP
    width = streams * lanes

    def products(n):
        for row in range(0, rows, 2):
            for h in range(2):
                for base in range(n * lanes, (n + 1) * lanes, LANES):
                    two = [
                        mixed(h * rows + r, width + base) * mixed(h * rows + r, 2 * width + base)
                        for r in (row, row + 1)
                    ]
                    at = h * lanes + base - n * lanes
                    prod_ref[n, row * GROUP : (row + 2) * GROUP, at : at + LANES] = (
                        jnp.concatenate(two, 0).astype(BF16)
                    )
        return jnp.dot(fwd_ref[...], prod_ref[n], preferred_element_type=F32)

    def filtered(n, spectra):
        channels = slice(n * lanes, (n + 1) * lanes)
        low, high = spectra[:, :lanes], spectra[:, lanes:]

        def response(j, s):
            place = j * rows + s
            return jnp.broadcast_to(h_ref[place : place + 1, channels], (GROUP, lanes))

        for k in range(0, rows, 2):
            parts = [[], [], [], []]
            for s in (k, k + 1):
                near_r, near_i = response(0, s), response(1, s)
                all_r, all_i = response(3, s), response(4, s)
                near_2, all_2 = (response(2, s), response(5, s)) if s == 0 else (near_r, all_r)
                re = slice(s * GROUP, (s + 1) * GROUP)
                im = slice(block + s * GROUP, block + (s + 1) * GROUP)
                lr, li, hr, hi = low[re], low[im], high[re], high[im]
                parts[0].append(lr * near_r - li * near_i)
                parts[1].append(lr * near_i + li * near_2)
                parts[2].append(lr * all_r - li * all_i + hr * near_r - hi * near_i)
                parts[3].append(lr * all_i + li * all_2 + hr * near_i + hi * near_2)
            for j in range(4):
                at, lane = (j % 2) * block + k * GROUP, (j // 2) * lanes
                z_ref[n, at : at + 2 * GROUP, lane : lane + lanes] = jnp.concatenate(
                    parts[j], 0
                ).astype(BF16)
        return jnp.dot(bwd_ref[...], z_ref[n], preferred_element_type=F32)

    def gated(n, conv):
        columns = []
        for base in range(0, lanes, LANES):
            line = [
                mixed(h * rows + r, n * lanes + base)
                * conv[r * GROUP : (r + 1) * GROUP, h * lanes + base : h * lanes + base + LANES]
                for h in range(2)
                for r in range(rows)
            ]
            columns.append(jnp.concatenate(line, 0).astype(BF16))
        return columns

    spectra = []
    for n in range(streams):
        spectra.append(products(n))
        yield
    convs = []
    for n in range(streams):
        convs.append(filtered(n, spectra[n]))
        yield
    final = jnp.dot(
        jnp.concatenate([c for n in range(streams) for c in gated(n, convs[n])], 1),
        w_out_ref[...],
        preferred_element_type=F32,
    )
    yield
    put(final.reshape(2, rows, GROUP, width))


def inner_kernel(
    _, other_ref, other_strip_ref,
    w_in_ref, taps_ref, fwd_ref, bwd_ref, w_out_ref, h_ref,
    p_ref, edge_mixed_ref, out_ref,
    q_ref, mixed_ref, prod_ref, z_ref,
):
    core = lax.axis_index("row")
    rows, cols, width = other_ref.shape
    part = cols // 2
    height = 2 * rows
    start = pl.multiple_of(core * part, part)
    channels = range(0, 3 * width, LANES)
    n_chunk = rows // CHUNK

    def store_in(ref, row0):
        def store(row, at, value):
            place = pl.ds(pl.multiple_of((row0 + row) * GROUP, GROUP), GROUP)
            ref[at.start // LANES, place, :] = value

        return store

    own_at, other_at = core * rows, (1 - core) * rows

    def inner(ref, row0, chunk):
        return depthwise_steps(ref, 1 - core, taps_ref, chunk, store_in(mixed_ref, row0), channels)

    def edge(ref, row0, chunk):
        return depthwise_steps(ref, core, taps_ref, chunk, store_in(edge_mixed_ref, row0), channels)

    for i in range(n_chunk - 1):
        for _ in inner(p_ref, own_at, core + i):
            pass
    project(other_ref[:, pl.ds(start, part), :], other_strip_ref[...], core, w_in_ref, q_ref)
    copy_row(q_ref, 1 + core * (rows - 1), p_ref, (1 - core) * (rows + 1), part)
    copy_row(p_ref, rows - core * (rows - 1), q_ref, core * (rows + 1), part)
    for _ in inner(p_ref, own_at, (1 - core) * (n_chunk - 1)):
        pass

    def inner_chunk(i, carry):
        for _ in inner(q_ref, other_at, i):
            pass
        return carry

    lax.fori_loop(0, n_chunk, inner_chunk, 0)

    def put(final):
        interleave(out_ref, final, 1 - core)

    def edge_all():
        for ref, row0 in ((p_ref, own_at), (q_ref, other_at)):
            for i in range(n_chunk):
                yield from edge(ref, row0, i)

    steps = edge_all()
    conv = conv_steps(
        lambda r, base: mixed_ref[base // LANES, r * GROUP : (r + 1) * GROUP, :],
        fwd_ref, bwd_ref, w_out_ref, h_ref, prod_ref, z_ref, put,
    )
    for _ in conv:
        for _ in range(5):
            next(steps, None)
    for _ in steps:
        pass


def edge_kernel(
    _, __, halo_ref, w_in_ref, taps_ref, fwd_ref, bwd_ref, w_out_ref, h_ref,
    out_ref, mixed_ref, mine_ref, send_ref,
    strip_ref, prod_ref, z_ref,
):
    core = lax.axis_index("row")
    rows, part, width = mine_ref.shape
    got = jnp.dot(halo_ref[...], w_in_ref[...], preferred_element_type=F32)
    add_edge_terms(
        got[:rows], got[rows:], 1 - core, column_taps(taps_ref, core, 0), strip_ref,
        mixed_ref, core * (GROUP - 1),
    )

    def mixed(r, base):
        return mixed_ref[base // LANES, r * GROUP : (r + 1) * GROUP, :]

    def put(final):
        interleave(out_ref, final, core)

    for _ in conv_steps(
        mixed, fwd_ref, bwd_ref, w_out_ref, h_ref, prod_ref, z_ref, put
    ):
        pass
    for ref, half in ((mine_ref, core), (send_ref, 1 - core)):
        for t in range(width // LANES):
            ref[:, :, t * LANES : (t + 1) * LANES] = (
                out_ref[half, t].reshape(rows, part, LANES).astype(BF16)
            )


def on_device(image_tokens, w_in, conv_kernel, conv_bias, long_filter, skip_gain, w_out):
    rows, cols, width = image_tokens.shape
    part = cols // 2
    height = 2 * rows
    n_col = lax.axis_size("col")
    core = lax.axis_index("row")
    fwd, bwd, spectra = transforms(rows, GROUP)
    spec_hi = spectra.astype(BF16)
    spec_lo = (spectra - spec_hi.astype(np.float64)).astype(BF16)
    spec = np.stack([spec_hi, spec_lo])
    vmem = pl.BlockSpec(memory_space=pltpu.VMEM)
    hbm = pl.BlockSpec(memory_space=pltpu.HBM)
    shape = jax.ShapeDtypeStruct
    limit = pltpu.CompilerParams(vmem_limit_bytes=24 * 1024 * 1024)

    p_shape = shape((3 * width // LANES, (rows + 2) * PITCH + GROUP, LANES), F32)
    out_shape = shape((2, width // LANES, rows * part, LANES), F32)
    mixed_shape = shape((3 * width // LANES, height * GROUP, LANES), F32)

    swap = [(0, 1), (1, 0)]
    rowmajor = Layout((0, 1, 2))
    image_tokens = with_layout_constraint(image_tokens, rowmajor)
    other = with_layout_constraint(lax.ppermute(image_tokens, "row", swap), rowmajor)

    def keep(array):
        return pltpu.with_memory_space_constraint(array, pltpu.HBM)

    projected, w_in_v, w_out_v, fwd_v, bwd_v, taps, spectrum, outer = pl.pallas_call(
        prep_kernel,
        out_shape=(
            p_shape,
            shape(w_in.shape, BF16),
            shape(w_out.shape, BF16),
            shape(fwd.shape, BF16),
            shape(bwd.shape, BF16),
            shape((16, 3 * width), F32),
            shape((6 * rows, width), F32),
            shape((rows, width), BF16),
        ),
        in_specs=[hbm] * 10,
        out_specs=(vmem,) * 8,
        scratch_shapes=[
            pltpu.VMEM(image_tokens.shape, BF16),
            pltpu.VMEM(spec.shape, BF16),
            pltpu.VMEM(long_filter.shape, BF16),
            pltpu.VMEM((1, width), F32),
            pltpu.VMEM(conv_kernel.shape, BF16),
            pltpu.VMEM(conv_bias.shape, F32),
            pltpu.SemaphoreType.DMA((10,)),
        ],
        compiler_params=limit,
        cost_estimate=pl.CostEstimate(flops=0, bytes_accessed=3 * 1024 * 1024, transcendentals=0),
    )(
        keep(image_tokens), keep(w_in), keep(w_out), keep(fwd.astype(BF16)), keep(bwd.astype(BF16)),
        keep(spec), keep(long_filter), keep(skip_gain[None]), keep(conv_kernel), keep(conv_bias),
    )

    def by_core(low, high):
        return jnp.where(core == 0, low, high)

    def column(low):
        return by_core(other[:, low], other[:, cols - 1 - low])

    pairs = []
    for j in range(n_col - 1):
        pairs += [(n_col + j, j + 1), (j + 1, n_col + j)]
    halo = lax.ppermute(jnp.concatenate([outer, column(0)], 0), ("row", "col"), pairs)
    _, edge_mixed, inner = pl.pallas_call(
        inner_kernel,
        out_shape=(p_shape, mixed_shape, out_shape),
        in_specs=[vmem] * 9,
        out_specs=(vmem,) * 3,
        input_output_aliases={0: 0},
        scratch_shapes=[
            pltpu.VMEM(p_shape.shape, F32),
            pltpu.VMEM(mixed_shape.shape, F32),
            pltpu.VMEM((width // LANES, rows * GROUP, 2 * LANES), BF16),
            pltpu.VMEM((width // LANES, 2 * rows * GROUP, 2 * LANES), BF16),
        ],
        compiler_params=limit,
        cost_estimate=pl.CostEstimate(flops=10**9, bytes_accessed=12 * 1024 * 1024, transcendentals=0),
    )(projected, other, column(part), w_in_v, taps, fwd_v, bwd_v, w_out_v, spectrum)
    half_shape = shape((rows, part, width), BF16)
    _, _, mine, send = pl.pallas_call(
        edge_kernel,
        out_shape=(out_shape, mixed_shape, half_shape, half_shape),
        in_specs=[vmem] * 9,
        out_specs=(vmem,) * 4,
        input_output_aliases={0: 0, 1: 1},
        scratch_shapes=[
            pltpu.VMEM((3 * width // LANES, 2 * height + 8, LANES), F32),
            pltpu.VMEM((1, rows * GROUP, 2 * width), BF16),
            pltpu.VMEM((1, 2 * rows * GROUP, 2 * width), BF16),
        ],
        compiler_params=limit,
        cost_estimate=pl.CostEstimate(flops=3 * 10**8, bytes_accessed=4 * 1024 * 1024, transcendentals=0),
    )(inner, edge_mixed, halo, w_in_v, taps, fwd_v, bwd_v, w_out_v, spectrum)
    theirs = lax.ppermute(send, "row", swap)
    both = jnp.concatenate([mine, mine], 1)
    return lax.dynamic_update_slice_in_dim(both, theirs, (1 - core) * part, 1)


def solution(mesh):
    in_specs = (P("row", "col", None), P(), P(), P(), P(), P(), P())
    out_specs = P("row", "col", None)
    return jax.shard_map(
        on_device, mesh=mesh, in_specs=in_specs, out_specs=out_specs, check_vma=False
    )
```

```python
import jax
import jax.numpy as jnp
import numpy as np
from jax import lax
from jax.experimental import pallas as pl
from jax.experimental.layout import Layout, with_layout_constraint
from jax.experimental.pallas import tpu as pltpu
from jax.sharding import PartitionSpec as P

F32 = jnp.float32
BF16 = jnp.bfloat16


def transforms(half, group):
    size = 2 * half
    slot = np.arange(half)[:, None]
    pos = np.arange(half)[None, :]
    angle = 2 * np.pi * slot * pos / size
    real, imag = np.cos(angle), -np.sin(angle)
    imag[0] = (-1.0) ** np.arange(half)
    forward = np.concatenate([real, imag], 0)
    back_real = 2 * np.cos(angle.T) / size
    back_real[:, 0] = 1 / size
    back_imag = -2 * np.sin(angle.T) / size
    back_imag[:, 0] = (-1.0) ** np.arange(half) / size
    backward = np.concatenate([back_real, back_imag], 1)
    lag = np.arange(size)[None, :]
    angle = 2 * np.pi * slot * lag / size
    real, imag = np.cos(angle), -np.sin(angle)
    imag[0] = 0
    real2 = real.copy()
    real2[0] = (-1.0) ** np.arange(size)
    near = (lag < half).astype(np.float64)
    sign = (-1.0) ** slot
    sign2 = sign.copy()
    sign2[0] = 1
    spectra = np.concatenate(
        [real * near, imag * near, real2 * near, real * sign, imag * sign, real2 * sign2], 0
    )
    eye = np.eye(group)
    return np.kron(forward, eye), np.kron(backward, eye), spectra


LANES = 128
GROUP = 8
CHUNK = 16
PITCH = 24
FIRST = 8


def pick_column(block, column):
    rows, cols, width = block.shape
    shape = (rows, rows * cols)
    place = lax.broadcasted_iota(jnp.int32, shape, 1)
    wanted = lax.broadcasted_iota(jnp.int32, shape, 0) * cols + column
    return jnp.dot(
        jnp.where(place == wanted, 1.0, 0.0).astype(BF16),
        block.reshape(rows * cols, width),
        preferred_element_type=F32,
    ).astype(BF16)


def row_place(row, column):
    return row * PITCH + FIRST + column


def project(tokens, strip, core, w_in_ref, p_ref):
    rows, part, width = tokens.shape
    count = rows * part
    got = jnp.dot(tokens.reshape(count, width), w_in_ref[...], preferred_element_type=F32)
    got_strip = jnp.dot(strip, w_in_ref[...], preferred_element_type=F32)
    for t in range(3 * width // LANES):
        at = slice(t * LANES, (t + 1) * LANES)
        for row in (0, rows + 1):
            place = row * PITCH
            p_ref[t, place : place + PITCH + GROUP, :] = jnp.zeros((PITCH + GROUP, LANES), F32)
        for r in range(rows):
            place = row_place(r + 1, 0)
            p_ref[t, place : place + part, :] = got[r * part : (r + 1) * part, at]
        for r in range(0, rows, GROUP):
            beside = got_strip[r : r + GROUP, at]
            for column, value in (
                (-1, jnp.where(core == 1, beside, 0.0)),
                (part, jnp.where(core == 0, beside, 0.0)),
            ):
                place = row_place(r + 1, column)
                p_ref[t, pl.ds(place, GROUP, stride=PITCH), :] = value


def copy_row(from_ref, from_row, to_ref, to_row, part):
    sub = lax.broadcasted_iota(jnp.int32, (GROUP, LANES), 0)
    for t in range(from_ref.shape[0]):
        for place in range(0, FIRST + part + GROUP, GROUP):
            source = pl.ds(pl.multiple_of(from_row * PITCH + place, GROUP), GROUP)
            target = pl.ds(pl.multiple_of(to_row * PITCH + place, GROUP), GROUP)
            value = from_ref[t, source, :]
            if place < FIRST:
                value = jnp.where(sub == GROUP - 1, value, to_ref[t, target, :])
            elif place >= FIRST + part:
                value = jnp.where(sub == 0, value, to_ref[t, target, :])
            to_ref[t, target, :] = value


def prep_kernel(
    own_hbm, w_in_hbm, w_out_hbm, fwd_hbm, bwd_hbm, spec_hbm, filt_hbm, gain_hbm, kernel_hbm, bias_hbm,
    p_ref, w_in_ref, w_out_ref, fwd_ref, bwd_ref, taps_ref, h_ref, outer_ref,
    own_ref, spec_ref, filt_ref, gain_ref, kernel_ref, bias_ref, sems,
):
    core = lax.axis_index("row")
    rows, cols, width = own_ref.shape
    part = cols // 2
    moves = [
        (own_hbm, own_ref),
        (w_in_hbm, w_in_ref),
        (spec_hbm, spec_ref),
        (filt_hbm, filt_ref),
        (gain_hbm, gain_ref),
        (kernel_hbm, kernel_ref),
        (bias_hbm, bias_ref),
        (fwd_hbm, fwd_ref),
        (bwd_hbm, bwd_ref),
        (w_out_hbm, w_out_ref),
    ]
    copies = [pltpu.make_async_copy(src, dst, sems.at[i]) for i, (src, dst) in enumerate(moves)]
    for copy in copies:
        copy.start()
    copies[0].wait()
    start = pl.multiple_of(core * part, part)
    far = pl.multiple_of((1 - core) * part, part)
    inner_edge = core * (part - 1)
    outer_ref[...] = pick_column(own_ref[:, pl.ds(start, part), :], inner_edge)
    beside = pick_column(own_ref[:, pl.ds(far, part), :], inner_edge)
    for copy in copies[1:7]:
        copy.wait()
    project(own_ref[:, pl.ds(start, part), :], beside, core, w_in_ref, p_ref)
    filt = filt_ref[...]
    gain = gain_ref[...]
    spectrum = jnp.dot(spec_ref[0], filt, preferred_element_type=F32) + jnp.dot(
        spec_ref[1], filt, preferred_element_type=F32
    )
    for j in range(6):
        part_j = spectrum[j * rows : (j + 1) * rows]
        h_ref[j * rows : (j + 1) * rows, :] = part_j + gain if j in (0, 2) else part_j
    for a in range(3):
        taps_ref[3 * a : 3 * a + 3, :] = kernel_ref[a].astype(F32)
    taps_ref[9, :] = bias_ref[...]
    for copy in copies[7:]:
        copy.wait()


def add_edge_terms(first, second, core, taps, edge_ref, mixed_ref, column):
    rows, channels = first.shape
    for t in range(channels // LANES):
        at = slice(t * LANES, (t + 1) * LANES)
        edge_ref[t, 0:8, :] = jnp.zeros((8, LANES), F32)
        edge_ref[t, 4 * rows : 4 * rows + 8, :] = jnp.zeros((8, LANES), F32)
        for r in range(0, rows, 8):
            for row, half in ((core * rows, first), ((1 - core) * rows, second)):
                place = pl.ds(2 * (row + r + 1), 8, stride=2)
                edge_ref[t, place, :] = half[r : r + 8, at]
        for r in range(0, 2 * rows, 8):
            place = pl.ds(r * GROUP + column, 8, stride=GROUP)
            total = mixed_ref[t, place, :]
            for a in range(3):
                total = total + edge_ref[t, pl.ds(2 * (r + a), 8, stride=2), :] * taps[a][:, at]
            mixed_ref[t, place, :] = total


def column_taps(taps_ref, core, on_core0):
    first, second = on_core0, 2 - on_core0
    return [
        jnp.where(
            core == 0,
            taps_ref[3 * a + first : 3 * a + first + 1, :],
            taps_ref[3 * a + second : 3 * a + second + 1, :],
        )
        for a in range(3)
    ]


def depthwise_steps(p_ref, first, taps_ref, chunk, store, bases):
    for base in bases:
        at = slice(base, base + LANES)
        tap = [
            jnp.broadcast_to(taps_ref[k : k + 1, at], (GROUP, LANES)) for k in range(10)
        ]
        loaded = [
            [
                p_ref[
                    base // LANES,
                    pl.ds(row_place(chunk * CHUNK + r, first + b - 1), GROUP, stride=2),
                    :,
                ]
                for b in range(3)
            ]
            for r in range(CHUNK + 2)
        ]
        for r in range(CHUNK):
            value = tap[9]
            for a in range(3):
                row = loaded[r + a]
                value = value + (
                    row[0] * tap[3 * a] + row[1] * tap[3 * a + 1] + row[2] * tap[3 * a + 2]
                )
            store(chunk * CHUNK + r, at, value)
        yield


def interleave(out_ref, final, first):
    _, rows, _, width = final.shape
    for h in range(2):
        for t in range(width // LANES):
            for r in range(rows):
                out_ref[h, t, pl.ds(r * 2 * GROUP + first, GROUP, stride=2), :] = final[
                    h, r, :, t * LANES : (t + 1) * LANES
                ]


def tall_dot(left, right, pieces):
    size = left.shape[0] // pieces
    return jnp.concatenate(
        [
            jnp.dot(left[i * size : (i + 1) * size], right, preferred_element_type=F32)
            for i in range(pieces)
        ],
        0,
    )


def conv_steps(mixed, fwd_ref, bwd_ref, w_out_ref, h_ref, prod_ref, z_ref, put):
    streams, block, lanes = prod_ref.shape
    lanes = lanes // 2
    rows = block // GROUP
    width = streams * lanes

    def products(n):
        for row in range(0, rows, 2):
            for h in range(2):
                for base in range(n * lanes, (n + 1) * lanes, LANES):
                    two = [
                        mixed(h * rows + r, width + base) * mixed(h * rows + r, 2 * width + base)
                        for r in (row, row + 1)
                    ]
                    at = h * lanes + base - n * lanes
                    prod_ref[n, row * GROUP : (row + 2) * GROUP, at : at + LANES] = (
                        jnp.concatenate(two, 0).astype(BF16)
                    )
        return tall_dot(fwd_ref, prod_ref[n], 2 * streams)

    def filtered(n, spectra):
        channels = slice(n * lanes, (n + 1) * lanes)
        low, high = spectra[:, :lanes], spectra[:, lanes:]

        def response(j, s):
            place = j * rows + s
            return jnp.broadcast_to(h_ref[place : place + 1, channels], (GROUP, lanes))

        for k in range(0, rows, 2):
            parts = [[], [], [], []]
            for s in (k, k + 1):
                near_r, near_i = response(0, s), response(1, s)
                all_r, all_i = response(3, s), response(4, s)
                near_2, all_2 = (response(2, s), response(5, s)) if s == 0 else (near_r, all_r)
                re = slice(s * GROUP, (s + 1) * GROUP)
                im = slice(block + s * GROUP, block + (s + 1) * GROUP)
                lr, li, hr, hi = low[re], low[im], high[re], high[im]
                parts[0].append(lr * near_r - li * near_i)
                parts[1].append(lr * near_i + li * near_2)
                parts[2].append(lr * all_r - li * all_i + hr * near_r - hi * near_i)
                parts[3].append(lr * all_i + li * all_2 + hr * near_i + hi * near_2)
            for j in range(4):
                at, lane = (j % 2) * block + k * GROUP, (j // 2) * lanes
                z_ref[n, at : at + 2 * GROUP, lane : lane + lanes] = jnp.concatenate(
                    parts[j], 0
                ).astype(BF16)
        return tall_dot(bwd_ref, z_ref[n], 2)

    def gated(n, conv):
        columns = []
        for base in range(0, lanes, LANES):
            line = [
                mixed(h * rows + r, n * lanes + base)
                * conv[r * GROUP : (r + 1) * GROUP, h * lanes + base : h * lanes + base + LANES]
                for h in range(2)
                for r in range(rows)
            ]
            columns.append(jnp.concatenate(line, 0).astype(BF16))
        return columns

    spectra = []
    for n in range(streams):
        spectra.append(products(n))
        yield
    convs = []
    for n in range(streams):
        convs.append(filtered(n, spectra[n]))
        yield
    final = tall_dot(
        jnp.concatenate([c for n in range(streams) for c in gated(n, convs[n])], 1), w_out_ref[...], 4
    )
    yield
    put(final.reshape(2, rows, GROUP, width))


def inner_kernel(
    _, other_ref, other_strip_ref,
    w_in_ref, taps_ref, fwd_ref, bwd_ref, w_out_ref, h_ref,
    p_ref, edge_mixed_ref, out_ref,
    q_ref, mixed_ref, prod_ref, z_ref,
):
    core = lax.axis_index("row")
    rows, cols, width = other_ref.shape
    part = cols // 2
    height = 2 * rows
    start = pl.multiple_of(core * part, part)
    channels = range(0, 3 * width, LANES)
    n_chunk = rows // CHUNK

    def store_in(ref, row0):
        def store(row, at, value):
            place = pl.ds(pl.multiple_of((row0 + row) * GROUP, GROUP), GROUP)
            ref[at.start // LANES, place, :] = value

        return store

    own_at, other_at = core * rows, (1 - core) * rows

    def inner(ref, row0, chunk):
        return depthwise_steps(ref, 1 - core, taps_ref, chunk, store_in(mixed_ref, row0), channels)

    def edge(ref, row0, chunk):
        return depthwise_steps(ref, core, taps_ref, chunk, store_in(edge_mixed_ref, row0), channels)

    for i in range(n_chunk - 1):
        for _ in inner(p_ref, own_at, core + i):
            pass
    project(other_ref[:, pl.ds(start, part), :], other_strip_ref[...], core, w_in_ref, q_ref)
    copy_row(q_ref, 1 + core * (rows - 1), p_ref, (1 - core) * (rows + 1), part)
    copy_row(p_ref, rows - core * (rows - 1), q_ref, core * (rows + 1), part)
    for _ in inner(p_ref, own_at, (1 - core) * (n_chunk - 1)):
        pass

    def inner_chunk(i, carry):
        for _ in inner(q_ref, other_at, i):
            pass
        return carry

    lax.fori_loop(0, n_chunk, inner_chunk, 0)

    def put(final):
        interleave(out_ref, final, 1 - core)

    def edge_all():
        for ref, row0 in ((p_ref, own_at), (q_ref, other_at)):
            for i in range(n_chunk):
                yield from edge(ref, row0, i)

    steps = edge_all()
    conv = conv_steps(
        lambda r, base: mixed_ref[base // LANES, r * GROUP : (r + 1) * GROUP, :],
        fwd_ref, bwd_ref, w_out_ref, h_ref, prod_ref, z_ref, put,
    )
    for _ in conv:
        for _ in range(5):
            next(steps, None)
    for _ in steps:
        pass


def edge_kernel(
    _, __, halo_ref, w_in_ref, taps_ref, fwd_ref, bwd_ref, w_out_ref, h_ref,
    out_ref, mixed_ref, mine_ref, send_ref,
    strip_ref, prod_ref, z_ref,
):
    core = lax.axis_index("row")
    rows, part, width = mine_ref.shape
    got = jnp.dot(halo_ref[...], w_in_ref[...], preferred_element_type=F32)
    add_edge_terms(
        got[:rows], got[rows:], 1 - core, column_taps(taps_ref, core, 0), strip_ref,
        mixed_ref, core * (GROUP - 1),
    )

    def mixed(r, base):
        return mixed_ref[base // LANES, r * GROUP : (r + 1) * GROUP, :]

    def put(final):
        interleave(out_ref, final, core)

    for _ in conv_steps(
        mixed, fwd_ref, bwd_ref, w_out_ref, h_ref, prod_ref, z_ref, put
    ):
        pass
    for ref, half in ((mine_ref, core), (send_ref, 1 - core)):
        for t in range(width // LANES):
            ref[:, :, t * LANES : (t + 1) * LANES] = (
                out_ref[half, t].reshape(rows, part, LANES).astype(BF16)
            )


def on_device(image_tokens, w_in, conv_kernel, conv_bias, long_filter, skip_gain, w_out):
    rows, cols, width = image_tokens.shape
    part = cols // 2
    height = 2 * rows
    n_col = lax.axis_size("col")
    core = lax.axis_index("row")
    fwd, bwd, spectra = transforms(rows, GROUP)
    spec_hi = spectra.astype(BF16)
    spec_lo = (spectra - spec_hi.astype(np.float64)).astype(BF16)
    spec = np.stack([spec_hi, spec_lo])
    vmem = pl.BlockSpec(memory_space=pltpu.VMEM)
    hbm = pl.BlockSpec(memory_space=pltpu.HBM)
    shape = jax.ShapeDtypeStruct
    limit = pltpu.CompilerParams(vmem_limit_bytes=24 * 1024 * 1024)

    p_shape = shape((3 * width // LANES, (rows + 2) * PITCH + GROUP, LANES), F32)
    out_shape = shape((2, width // LANES, rows * part, LANES), F32)
    mixed_shape = shape((3 * width // LANES, height * GROUP, LANES), F32)

    swap = [(0, 1), (1, 0)]
    rowmajor = Layout((0, 1, 2))
    image_tokens = with_layout_constraint(image_tokens, rowmajor)
    other = with_layout_constraint(lax.ppermute(image_tokens, "row", swap), rowmajor)

    def keep(array):
        return pltpu.with_memory_space_constraint(array, pltpu.HBM)

    projected, w_in_v, w_out_v, fwd_v, bwd_v, taps, spectrum, outer = pl.pallas_call(
        prep_kernel,
        out_shape=(
            p_shape,
            shape(w_in.shape, BF16),
            shape(w_out.shape, BF16),
            shape(fwd.shape, BF16),
            shape(bwd.shape, BF16),
            shape((16, 3 * width), F32),
            shape((6 * rows, width), F32),
            shape((rows, width), BF16),
        ),
        in_specs=[hbm] * 10,
        out_specs=(vmem,) * 8,
        scratch_shapes=[
            pltpu.VMEM(image_tokens.shape, BF16),
            pltpu.VMEM(spec.shape, BF16),
            pltpu.VMEM(long_filter.shape, BF16),
            pltpu.VMEM((1, width), F32),
            pltpu.VMEM(conv_kernel.shape, BF16),
            pltpu.VMEM(conv_bias.shape, F32),
            pltpu.SemaphoreType.DMA((10,)),
        ],
        compiler_params=limit,
        cost_estimate=pl.CostEstimate(flops=0, bytes_accessed=3 * 1024 * 1024, transcendentals=0),
    )(
        keep(image_tokens), keep(w_in), keep(w_out), keep(fwd.astype(BF16)), keep(bwd.astype(BF16)),
        keep(spec), keep(long_filter), keep(skip_gain[None]), keep(conv_kernel), keep(conv_bias),
    )

    def by_core(low, high):
        return jnp.where(core == 0, low, high)

    def column(low):
        return by_core(other[:, low], other[:, cols - 1 - low])

    pairs = []
    for j in range(n_col - 1):
        pairs += [(n_col + j, j + 1), (j + 1, n_col + j)]
    halo = lax.ppermute(jnp.concatenate([outer, column(0)], 0), ("row", "col"), pairs)
    _, edge_mixed, inner = pl.pallas_call(
        inner_kernel,
        out_shape=(p_shape, mixed_shape, out_shape),
        in_specs=[vmem] * 9,
        out_specs=(vmem,) * 3,
        input_output_aliases={0: 0},
        scratch_shapes=[
            pltpu.VMEM(p_shape.shape, F32),
            pltpu.VMEM(mixed_shape.shape, F32),
            pltpu.VMEM((width // LANES, rows * GROUP, 2 * LANES), BF16),
            pltpu.VMEM((width // LANES, 2 * rows * GROUP, 2 * LANES), BF16),
        ],
        compiler_params=limit,
        cost_estimate=pl.CostEstimate(flops=10**9, bytes_accessed=12 * 1024 * 1024, transcendentals=0),
    )(projected, other, column(part), w_in_v, taps, fwd_v, bwd_v, w_out_v, spectrum)
    half_shape = shape((rows, part, width), BF16)
    _, _, mine, send = pl.pallas_call(
        edge_kernel,
        out_shape=(out_shape, mixed_shape, half_shape, half_shape),
        in_specs=[vmem] * 9,
        out_specs=(vmem,) * 4,
        input_output_aliases={0: 0, 1: 1},
        scratch_shapes=[
            pltpu.VMEM((3 * width // LANES, 2 * height + 8, LANES), F32),
            pltpu.VMEM((1, rows * GROUP, 2 * width), BF16),
            pltpu.VMEM((1, 2 * rows * GROUP, 2 * width), BF16),
        ],
        compiler_params=limit,
        cost_estimate=pl.CostEstimate(flops=3 * 10**8, bytes_accessed=4 * 1024 * 1024, transcendentals=0),
    )(inner, edge_mixed, halo, w_in_v, taps, fwd_v, bwd_v, w_out_v, spectrum)
    theirs = lax.ppermute(send, "row", swap)
    both = jnp.concatenate([mine, mine], 1)
    return lax.dynamic_update_slice_in_dim(both, theirs, (1 - core) * part, 1)


def solution(mesh):
    in_specs = (P("row", "col", None), P(), P(), P(), P(), P(), P())
    out_specs = P("row", "col", None)
    return jax.shard_map(
        on_device, mesh=mesh, in_specs=in_specs, out_specs=out_specs, check_vma=False
    )
```

```python
import jax
import jax.numpy as jnp
import numpy as np
from jax import lax
from jax.experimental import pallas as pl
from jax.experimental.layout import Layout, with_layout_constraint
from jax.experimental.pallas import tpu as pltpu
from jax.sharding import PartitionSpec as P

F32 = jnp.float32
BF16 = jnp.bfloat16


def transforms(half, group):
    size = 2 * half
    slot = np.arange(half)[:, None]
    pos = np.arange(half)[None, :]
    angle = 2 * np.pi * slot * pos / size
    real, imag = np.cos(angle), -np.sin(angle)
    imag[0] = (-1.0) ** np.arange(half)
    forward = np.concatenate([real, imag], 0)
    back_real = 2 * np.cos(angle.T) / size
    back_real[:, 0] = 1 / size
    back_imag = -2 * np.sin(angle.T) / size
    back_imag[:, 0] = (-1.0) ** np.arange(half) / size
    backward = np.concatenate([back_real, back_imag], 1)
    lag = np.arange(size)[None, :]
    angle = 2 * np.pi * slot * lag / size
    real, imag = np.cos(angle), -np.sin(angle)
    imag[0] = 0
    real2 = real.copy()
    real2[0] = (-1.0) ** np.arange(size)
    near = (lag < half).astype(np.float64)
    sign = (-1.0) ** slot
    sign2 = sign.copy()
    sign2[0] = 1
    spectra = np.concatenate(
        [real * near, imag * near, real2 * near, real * sign, imag * sign, real2 * sign2], 0
    )
    eye = np.eye(group)
    return np.kron(forward, eye), np.kron(backward, eye), spectra


LANES = 128
GROUP = 8
CHUNK = 16
PITCH = 24
FIRST = 8


def pick_column(block, column):
    rows, cols, width = block.shape
    shape = (rows, rows * cols)
    place = lax.broadcasted_iota(jnp.int32, shape, 1)
    wanted = lax.broadcasted_iota(jnp.int32, shape, 0) * cols + column
    return jnp.dot(
        jnp.where(place == wanted, 1.0, 0.0).astype(BF16),
        block.reshape(rows * cols, width),
        preferred_element_type=F32,
    ).astype(BF16)


def row_place(row, column):
    return row * PITCH + FIRST + column


def project(tokens, strip, core, w_in_ref, p_ref):
    rows, part, width = tokens.shape
    count = rows * part
    got = jnp.dot(tokens.reshape(count, width), w_in_ref[...], preferred_element_type=F32)
    got_strip = jnp.dot(strip, w_in_ref[...], preferred_element_type=F32)
    for t in range(3 * width // LANES):
        at = slice(t * LANES, (t + 1) * LANES)
        for row in (0, rows + 1):
            place = row * PITCH
            p_ref[t, place : place + PITCH + GROUP, :] = jnp.zeros((PITCH + GROUP, LANES), F32)
        for r in range(rows):
            place = row_place(r + 1, 0)
            p_ref[t, place : place + part, :] = got[r * part : (r + 1) * part, at]
        for r in range(0, rows, GROUP):
            beside = got_strip[r : r + GROUP, at]
            for column, value in (
                (-1, jnp.where(core == 1, beside, 0.0)),
                (part, jnp.where(core == 0, beside, 0.0)),
            ):
                place = row_place(r + 1, column)
                p_ref[t, pl.ds(place, GROUP, stride=PITCH), :] = value


def copy_row(from_ref, from_row, to_ref, to_row, part):
    sub = lax.broadcasted_iota(jnp.int32, (GROUP, LANES), 0)
    for t in range(from_ref.shape[0]):
        for place in range(0, FIRST + part + GROUP, GROUP):
            source = pl.ds(pl.multiple_of(from_row * PITCH + place, GROUP), GROUP)
            target = pl.ds(pl.multiple_of(to_row * PITCH + place, GROUP), GROUP)
            value = from_ref[t, source, :]
            if place < FIRST:
                value = jnp.where(sub == GROUP - 1, value, to_ref[t, target, :])
            elif place >= FIRST + part:
                value = jnp.where(sub == 0, value, to_ref[t, target, :])
            to_ref[t, target, :] = value


def prep_kernel(
    own_hbm, w_in_hbm, w_out_hbm, fwd_hbm, bwd_hbm, spec_hbm, filt_hbm, gain_hbm, kernel_hbm, bias_hbm,
    p_ref, w_in_ref, w_out_ref, fwd_ref, bwd_ref, taps_ref, h_ref, outer_ref,
    own_ref, spec_ref, filt_ref, gain_ref, kernel_ref, bias_ref, sems,
):
    core = lax.axis_index("row")
    rows, cols, width = own_ref.shape
    part = cols // 2
    moves = [
        (own_hbm, own_ref),
        (w_in_hbm, w_in_ref),
        (spec_hbm, spec_ref),
        (filt_hbm, filt_ref),
        (gain_hbm, gain_ref),
        (kernel_hbm, kernel_ref),
        (bias_hbm, bias_ref),
        (fwd_hbm, fwd_ref),
        (bwd_hbm, bwd_ref),
        (w_out_hbm, w_out_ref),
    ]
    copies = [pltpu.make_async_copy(src, dst, sems.at[i]) for i, (src, dst) in enumerate(moves)]
    for copy in copies:
        copy.start()
    copies[0].wait()
    start = pl.multiple_of(core * part, part)
    far = pl.multiple_of((1 - core) * part, part)
    inner_edge = core * (part - 1)
    outer_ref[...] = pick_column(own_ref[:, pl.ds(start, part), :], inner_edge)
    beside = pick_column(own_ref[:, pl.ds(far, part), :], inner_edge)
    for copy in copies[1:7]:
        copy.wait()
    project(own_ref[:, pl.ds(start, part), :], beside, core, w_in_ref, p_ref)
    filt = filt_ref[...]
    gain = gain_ref[...]
    spectrum = jnp.dot(spec_ref[0], filt, preferred_element_type=F32) + jnp.dot(
        spec_ref[1], filt, preferred_element_type=F32
    )
    for j in range(6):
        part_j = spectrum[j * rows : (j + 1) * rows]
        part_j = part_j + gain if j in (0, 2) else part_j
        h_ref[j * rows // 8 : (j + 1) * rows // 8] = part_j.reshape(rows // 8, 8, width)
    for a in range(3):
        taps_ref[3 * a : 3 * a + 3, :] = kernel_ref[a].astype(F32)
    taps_ref[9, :] = bias_ref[...]
    for copy in copies[7:]:
        copy.wait()


def add_edge_terms(first, second, core, taps, edge_ref, mixed_ref, column):
    rows, channels = first.shape
    for t in range(channels // LANES):
        at = slice(t * LANES, (t + 1) * LANES)
        edge_ref[t, 0:8, :] = jnp.zeros((8, LANES), F32)
        edge_ref[t, 4 * rows : 4 * rows + 8, :] = jnp.zeros((8, LANES), F32)
        for r in range(0, rows, 8):
            for row, half in ((core * rows, first), ((1 - core) * rows, second)):
                place = pl.ds(2 * (row + r + 1), 8, stride=2)
                edge_ref[t, place, :] = half[r : r + 8, at]
        for r in range(0, 2 * rows, 8):
            place = pl.ds(r * GROUP + column, 8, stride=GROUP)
            total = mixed_ref[t, place, :]
            for a in range(3):
                total = total + edge_ref[t, pl.ds(2 * (r + a), 8, stride=2), :] * taps[a][:, at]
            mixed_ref[t, place, :] = total


def column_taps(taps_ref, core, on_core0):
    first, second = on_core0, 2 - on_core0
    return [
        jnp.where(
            core == 0,
            taps_ref[3 * a + first : 3 * a + first + 1, :],
            taps_ref[3 * a + second : 3 * a + second + 1, :],
        )
        for a in range(3)
    ]


def depthwise_steps(p_ref, first, taps_ref, chunk, store, bases):
    for base in bases:
        at = slice(base, base + LANES)
        tap = [
            jnp.broadcast_to(taps_ref[k : k + 1, at], (GROUP, LANES)) for k in range(10)
        ]
        loaded = [
            [
                p_ref[
                    base // LANES,
                    pl.ds(row_place(chunk * CHUNK + r, first + b - 1), GROUP, stride=2),
                    :,
                ]
                for b in range(3)
            ]
            for r in range(CHUNK + 2)
        ]
        for r in range(CHUNK):
            value = tap[9]
            for a in range(3):
                row = loaded[r + a]
                value = value + (
                    row[0] * tap[3 * a] + row[1] * tap[3 * a + 1] + row[2] * tap[3 * a + 2]
                )
            store(chunk * CHUNK + r, at, value)
        yield


def interleave(out_ref, final, first):
    _, rows, _, width = final.shape
    for h in range(2):
        for t in range(width // LANES):
            for r in range(rows):
                out_ref[h, t, pl.ds(r * 2 * GROUP + first, GROUP, stride=2), :] = final[
                    h, r, :, t * LANES : (t + 1) * LANES
                ]


def conv_steps(mixed, fwd_ref, bwd_ref, w_out_ref, h_ref, prod_ref, z_ref, put):
    streams, block, lanes = prod_ref.shape
    lanes = lanes // 2
    rows = block // GROUP
    width = streams * lanes

    def products(n):
        for row in range(0, rows, 2):
            for h in range(2):
                for base in range(n * lanes, (n + 1) * lanes, LANES):
                    two = [
                        mixed(h * rows + r, width + base) * mixed(h * rows + r, 2 * width + base)
                        for r in (row, row + 1)
                    ]
                    at = h * lanes + base - n * lanes
                    prod_ref[n, row * GROUP : (row + 2) * GROUP, at : at + LANES] = (
                        jnp.concatenate(two, 0).astype(BF16)
                    )
        return jnp.dot(fwd_ref[...], prod_ref[n], preferred_element_type=F32)

    def filtered(n, spectra):
        channels = slice(n * lanes, (n + 1) * lanes)
        low, high = spectra[:, :lanes], spectra[:, lanes:]

        def response(j, s):
            place = j * rows // 8 + s // 8
            return jnp.broadcast_to(h_ref[place, s % 8 : s % 8 + 1, channels], (GROUP, lanes))

        for k in range(0, rows, 2):
            parts = [[], [], [], []]
            for s in (k, k + 1):
                near_r, near_i = response(0, s), response(1, s)
                all_r, all_i = response(3, s), response(4, s)
                near_2, all_2 = (response(2, s), response(5, s)) if s == 0 else (near_r, all_r)
                re = slice(s * GROUP, (s + 1) * GROUP)
                im = slice(block + s * GROUP, block + (s + 1) * GROUP)
                lr, li, hr, hi = low[re], low[im], high[re], high[im]
                parts[0].append(lr * near_r - li * near_i)
                parts[1].append(lr * near_i + li * near_2)
                parts[2].append(lr * all_r - li * all_i + hr * near_r - hi * near_i)
                parts[3].append(lr * all_i + li * all_2 + hr * near_i + hi * near_2)
            for j in range(4):
                at, lane = (j % 2) * block + k * GROUP, (j // 2) * lanes
                z_ref[n, at : at + 2 * GROUP, lane : lane + lanes] = jnp.concatenate(
                    parts[j], 0
                ).astype(BF16)
        return jnp.dot(bwd_ref[...], z_ref[n], preferred_element_type=F32)

    def gated(n, conv):
        columns = []
        for base in range(0, lanes, LANES):
            line = [
                mixed(h * rows + r, n * lanes + base)
                * conv[r * GROUP : (r + 1) * GROUP, h * lanes + base : h * lanes + base + LANES]
                for h in range(2)
                for r in range(rows)
            ]
            columns.append(jnp.concatenate(line, 0).astype(BF16))
        return columns

    spectra = []
    for n in range(streams):
        spectra.append(products(n))
        yield
    convs = []
    for n in range(streams):
        convs.append(filtered(n, spectra[n]))
        yield
    final = jnp.dot(
        jnp.concatenate([c for n in range(streams) for c in gated(n, convs[n])], 1),
        w_out_ref[...],
        preferred_element_type=F32,
    )
    yield
    put(final.reshape(2, rows, GROUP, width))


def conv_loops(mixed_ref, fwd_ref, bwd_ref, w_out_ref, h_ref, prod_ref, s_ref, z_ref, c_ref, g_ref):
    block, width = prod_ref.shape[0], prod_ref.shape[1] // 2
    rows = block // GROUP
    bases = range(0, width, LANES)

    def mixed(row, base):
        return mixed_ref[base // LANES, pl.ds(pl.multiple_of(row * GROUP, GROUP), GROUP), :]

    def pair_place(first, step):
        return pl.ds(pl.multiple_of((first + step) * GROUP, 2 * GROUP), 2 * GROUP)

    def products(i, carry):
        for row in range(0, 8, 2):
            for h in range(2):
                for base in bases:
                    two = [
                        mixed(h * rows + 8 * i + r, width + base)
                        * mixed(h * rows + 8 * i + r, 2 * width + base)
                        for r in (row, row + 1)
                    ]
                    at = h * width + base
                    prod_ref[pair_place(8 * i, row), at : at + LANES] = jnp.concatenate(
                        two, 0
                    ).astype(BF16)
        return carry

    lax.fori_loop(0, rows // 8, products, 0)
    s_ref[...] = jnp.dot(fwd_ref[...], prod_ref[...], preferred_element_type=F32)

    def filtered(i, carry):
        for k in range(0, 8, 2):
            parts = [[], [], [], []]
            for s in (k, k + 1):
                near_r, near_i, near_2, all_r, all_i, all_2 = (
                    jnp.broadcast_to(h_ref[j * (rows // 8) + i, s : s + 1, :], (GROUP, width))
                    for j in range(6)
                )
                re = pl.ds(pl.multiple_of((8 * i + s) * GROUP, GROUP), GROUP)
                im = pl.ds(pl.multiple_of(block + (8 * i + s) * GROUP, GROUP), GROUP)
                lr, hr = s_ref[re, :width], s_ref[re, width:]
                li, hi = s_ref[im, :width], s_ref[im, width:]
                parts[0].append(lr * near_r - li * near_i)
                parts[1].append(lr * near_i + li * near_2)
                parts[2].append(lr * all_r - li * all_i + hr * near_r - hi * near_i)
                parts[3].append(lr * all_i + li * all_2 + hr * near_i + hi * near_2)
            for j in range(4):
                lane = (j // 2) * width
                z_ref[pair_place((j % 2) * rows + 8 * i, k), lane : lane + width] = (
                    jnp.concatenate(parts[j], 0).astype(BF16)
                )
        return carry

    lax.fori_loop(0, rows // 8, filtered, 0)
    c_ref[...] = jnp.dot(bwd_ref[...], z_ref[...], preferred_element_type=F32)

    def gated(i, carry):
        for row in range(0, 8, 2):
            for h in range(2):
                for base in bases:
                    two = [
                        mixed(h * rows + 8 * i + r, base)
                        * c_ref[
                            pl.ds(pl.multiple_of((8 * i + r) * GROUP, GROUP), GROUP),
                            h * width + base : h * width + base + LANES,
                        ]
                        for r in (row, row + 1)
                    ]
                    g_ref[pair_place(h * rows + 8 * i, row), base : base + LANES] = jnp.concatenate(
                        two, 0
                    ).astype(BF16)
        return carry

    lax.fori_loop(0, rows // 8, gated, 0)
    return jnp.dot(g_ref[...], w_out_ref[...], preferred_element_type=F32)


def inner_kernel(
    _, other_ref, other_strip_ref,
    w_in_ref, taps_ref, fwd_ref, bwd_ref, w_out_ref, h_ref,
    p_ref, edge_mixed_ref, out_ref,
    q_ref, mixed_ref, prod_ref, z_ref,
):
    core = lax.axis_index("row")
    rows, cols, width = other_ref.shape
    part = cols // 2
    height = 2 * rows
    start = pl.multiple_of(core * part, part)
    channels = range(0, 3 * width, LANES)
    n_chunk = rows // CHUNK

    def store_in(ref, row0):
        def store(row, at, value):
            place = pl.ds(pl.multiple_of((row0 + row) * GROUP, GROUP), GROUP)
            ref[at.start // LANES, place, :] = value

        return store

    own_at, other_at = core * rows, (1 - core) * rows

    def inner(ref, row0, chunk):
        return depthwise_steps(ref, 1 - core, taps_ref, chunk, store_in(mixed_ref, row0), channels)

    def edge(ref, row0, chunk):
        return depthwise_steps(ref, core, taps_ref, chunk, store_in(edge_mixed_ref, row0), channels)

    for i in range(n_chunk - 1):
        for _ in inner(p_ref, own_at, core + i):
            pass
    project(other_ref[:, pl.ds(start, part), :], other_strip_ref[...], core, w_in_ref, q_ref)
    copy_row(q_ref, 1 + core * (rows - 1), p_ref, (1 - core) * (rows + 1), part)
    copy_row(p_ref, rows - core * (rows - 1), q_ref, core * (rows + 1), part)
    for _ in inner(p_ref, own_at, (1 - core) * (n_chunk - 1)):
        pass

    def inner_chunk(i, carry):
        for _ in inner(q_ref, other_at, i):
            pass
        return carry

    lax.fori_loop(0, n_chunk, inner_chunk, 0)

    def put(final):
        interleave(out_ref, final, 1 - core)

    def edge_all():
        for ref, row0 in ((p_ref, own_at), (q_ref, other_at)):
            for i in range(n_chunk):
                yield from edge(ref, row0, i)

    steps = edge_all()
    conv = conv_steps(
        lambda r, base: mixed_ref[base // LANES, r * GROUP : (r + 1) * GROUP, :],
        fwd_ref, bwd_ref, w_out_ref, h_ref, prod_ref, z_ref, put,
    )
    for _ in conv:
        for _ in range(5):
            next(steps, None)
    for _ in steps:
        pass


def edge_kernel(
    _, __, halo_ref, w_in_ref, taps_ref, fwd_ref, bwd_ref, w_out_ref, h_ref,
    out_ref, mixed_ref, mine_ref, send_ref,
    strip_ref, prod_ref, s_ref, z_ref, c_ref, g_ref,
):
    core = lax.axis_index("row")
    rows, part, width = mine_ref.shape
    got = jnp.dot(halo_ref[...], w_in_ref[...], preferred_element_type=F32)
    add_edge_terms(
        got[:rows], got[rows:], 1 - core, column_taps(taps_ref, core, 0), strip_ref,
        mixed_ref, core * (GROUP - 1),
    )

    final = conv_loops(
        mixed_ref, fwd_ref, bwd_ref, w_out_ref, h_ref, prod_ref, s_ref, z_ref, c_ref, g_ref
    )
    interleave(out_ref, final.reshape(2, rows, GROUP, width), core)

    def finish(i, carry):
        for ref, half in ((mine_ref, core), (send_ref, 1 - core)):
            for t in range(width // LANES):
                place = pl.ds(pl.multiple_of(8 * i * part, 8 * part), 8 * part)
                ref[pl.ds(8 * i, 8), :, t * LANES : (t + 1) * LANES] = (
                    out_ref[half, t, place, :].reshape(8, part, LANES).astype(BF16)
                )
        return carry

    lax.fori_loop(0, rows // 8, finish, 0)


def on_device(image_tokens, w_in, conv_kernel, conv_bias, long_filter, skip_gain, w_out):
    rows, cols, width = image_tokens.shape
    part = cols // 2
    height = 2 * rows
    n_col = lax.axis_size("col")
    core = lax.axis_index("row")
    fwd, bwd, spectra = transforms(rows, GROUP)
    spec_hi = spectra.astype(BF16)
    spec_lo = (spectra - spec_hi.astype(np.float64)).astype(BF16)
    spec = np.stack([spec_hi, spec_lo])
    vmem = pl.BlockSpec(memory_space=pltpu.VMEM)
    hbm = pl.BlockSpec(memory_space=pltpu.HBM)
    shape = jax.ShapeDtypeStruct
    limit = pltpu.CompilerParams(vmem_limit_bytes=24 * 1024 * 1024)

    p_shape = shape((3 * width // LANES, (rows + 2) * PITCH + GROUP, LANES), F32)
    out_shape = shape((2, width // LANES, rows * part, LANES), F32)
    mixed_shape = shape((3 * width // LANES, height * GROUP, LANES), F32)

    swap = [(0, 1), (1, 0)]
    rowmajor = Layout((0, 1, 2))
    image_tokens = with_layout_constraint(image_tokens, rowmajor)
    other = with_layout_constraint(lax.ppermute(image_tokens, "row", swap), rowmajor)

    def keep(array):
        return pltpu.with_memory_space_constraint(array, pltpu.HBM)

    projected, w_in_v, w_out_v, fwd_v, bwd_v, taps, spectrum, outer = pl.pallas_call(
        prep_kernel,
        out_shape=(
            p_shape,
            shape(w_in.shape, BF16),
            shape(w_out.shape, BF16),
            shape(fwd.shape, BF16),
            shape(bwd.shape, BF16),
            shape((16, 3 * width), F32),
            shape((6 * rows // 8, 8, width), F32),
            shape((rows, width), BF16),
        ),
        in_specs=[hbm] * 10,
        out_specs=(vmem,) * 8,
        scratch_shapes=[
            pltpu.VMEM(image_tokens.shape, BF16),
            pltpu.VMEM(spec.shape, BF16),
            pltpu.VMEM(long_filter.shape, BF16),
            pltpu.VMEM((1, width), F32),
            pltpu.VMEM(conv_kernel.shape, BF16),
            pltpu.VMEM(conv_bias.shape, F32),
            pltpu.SemaphoreType.DMA((10,)),
        ],
        compiler_params=limit,
        cost_estimate=pl.CostEstimate(flops=0, bytes_accessed=3 * 1024 * 1024, transcendentals=0),
    )(
        keep(image_tokens), keep(w_in), keep(w_out), keep(fwd.astype(BF16)), keep(bwd.astype(BF16)),
        keep(spec), keep(long_filter), keep(skip_gain[None]), keep(conv_kernel), keep(conv_bias),
    )

    def by_core(low, high):
        return jnp.where(core == 0, low, high)

    def column(low):
        return by_core(other[:, low], other[:, cols - 1 - low])

    pairs = []
    for j in range(n_col - 1):
        pairs += [(n_col + j, j + 1), (j + 1, n_col + j)]
    halo = lax.ppermute(jnp.concatenate([outer, column(0)], 0), ("row", "col"), pairs)
    _, edge_mixed, inner = pl.pallas_call(
        inner_kernel,
        out_shape=(p_shape, mixed_shape, out_shape),
        in_specs=[vmem] * 9,
        out_specs=(vmem,) * 3,
        input_output_aliases={0: 0},
        scratch_shapes=[
            pltpu.VMEM(p_shape.shape, F32),
            pltpu.VMEM(mixed_shape.shape, F32),
            pltpu.VMEM((width // LANES, rows * GROUP, 2 * LANES), BF16),
            pltpu.VMEM((width // LANES, 2 * rows * GROUP, 2 * LANES), BF16),
        ],
        compiler_params=limit,
        cost_estimate=pl.CostEstimate(flops=10**9, bytes_accessed=12 * 1024 * 1024, transcendentals=0),
    )(projected, other, column(part), w_in_v, taps, fwd_v, bwd_v, w_out_v, spectrum)
    half_shape = shape((rows, part, width), BF16)
    _, _, mine, send = pl.pallas_call(
        edge_kernel,
        out_shape=(out_shape, mixed_shape, half_shape, half_shape),
        in_specs=[vmem] * 9,
        out_specs=(vmem,) * 4,
        input_output_aliases={0: 0, 1: 1},
        scratch_shapes=[
            pltpu.VMEM((3 * width // LANES, 2 * height + 8, LANES), F32),
            pltpu.VMEM((rows * GROUP, 2 * width), BF16),
            pltpu.VMEM((2 * rows * GROUP, 2 * width), F32),
            pltpu.VMEM((2 * rows * GROUP, 2 * width), BF16),
            pltpu.VMEM((rows * GROUP, 2 * width), F32),
            pltpu.VMEM((2 * rows * GROUP, width), BF16),
        ],
        compiler_params=limit,
        cost_estimate=pl.CostEstimate(flops=3 * 10**8, bytes_accessed=4 * 1024 * 1024, transcendentals=0),
    )(inner, edge_mixed, halo, w_in_v, taps, fwd_v, bwd_v, w_out_v, spectrum)
    theirs = lax.ppermute(send, "row", swap)
    both = jnp.concatenate([mine, mine], 1)
    return lax.dynamic_update_slice_in_dim(both, theirs, (1 - core) * part, 1)


def solution(mesh):
    in_specs = (P("row", "col", None), P(), P(), P(), P(), P(), P())
    out_specs = P("row", "col", None)
    return jax.shard_map(
        on_device, mesh=mesh, in_specs=in_specs, out_specs=out_specs, check_vma=False
    )
```

```python
import jax
import jax.numpy as jnp
import numpy as np
from jax import lax
from jax.experimental import pallas as pl
from jax.experimental.layout import Layout, with_layout_constraint
from jax.experimental.pallas import tpu as pltpu
from jax.sharding import PartitionSpec as P

F32 = jnp.float32
BF16 = jnp.bfloat16


def transforms(half, group):
    size = 2 * half
    slot = np.arange(half)[:, None]
    pos = np.arange(half)[None, :]
    angle = 2 * np.pi * slot * pos / size
    real, imag = np.cos(angle), -np.sin(angle)
    imag[0] = (-1.0) ** np.arange(half)
    forward = np.concatenate([real, imag], 0)
    back_real = 2 * np.cos(angle.T) / size
    back_real[:, 0] = 1 / size
    back_imag = -2 * np.sin(angle.T) / size
    back_imag[:, 0] = (-1.0) ** np.arange(half) / size
    backward = np.concatenate([back_real, back_imag], 1)
    lag = np.arange(size)[None, :]
    angle = 2 * np.pi * slot * lag / size
    real, imag = np.cos(angle), -np.sin(angle)
    imag[0] = 0
    real2 = real.copy()
    real2[0] = (-1.0) ** np.arange(size)
    near = (lag < half).astype(np.float64)
    sign = (-1.0) ** slot
    sign2 = sign.copy()
    sign2[0] = 1
    spectra = np.concatenate(
        [real * near, imag * near, real2 * near, real * sign, imag * sign, real2 * sign2], 0
    )
    eye = np.eye(group)
    return np.kron(forward, eye), np.kron(backward, eye), spectra


LANES = 128
GROUP = 8
CHUNK = 16
PITCH = 24
FIRST = 8


def pick_column(block, column):
    rows, cols, width = block.shape
    shape = (rows, rows * cols)
    place = lax.broadcasted_iota(jnp.int32, shape, 1)
    wanted = lax.broadcasted_iota(jnp.int32, shape, 0) * cols + column
    return jnp.dot(
        jnp.where(place == wanted, 1.0, 0.0).astype(BF16),
        block.reshape(rows * cols, width),
        preferred_element_type=F32,
    ).astype(BF16)


def row_place(row, column):
    return row * PITCH + FIRST + column


def project(tokens, strip, core, w_in_ref, p_ref):
    rows, part, width = tokens.shape
    count = rows * part
    got = jnp.dot(tokens.reshape(count, width), w_in_ref[...], preferred_element_type=F32)
    got_strip = jnp.dot(strip, w_in_ref[...], preferred_element_type=F32)
    for t in range(3 * width // LANES):
        at = slice(t * LANES, (t + 1) * LANES)
        for row in (0, rows + 1):
            place = row * PITCH
            p_ref[t, place : place + PITCH + GROUP, :] = jnp.zeros((PITCH + GROUP, LANES), F32)
        for r in range(rows):
            place = row_place(r + 1, 0)
            p_ref[t, place : place + part, :] = got[r * part : (r + 1) * part, at]
        for r in range(0, rows, GROUP):
            beside = got_strip[r : r + GROUP, at]
            for column, value in (
                (-1, jnp.where(core == 1, beside, 0.0)),
                (part, jnp.where(core == 0, beside, 0.0)),
            ):
                place = row_place(r + 1, column)
                p_ref[t, pl.ds(place, GROUP, stride=PITCH), :] = value


def copy_row(from_ref, from_row, to_ref, to_row, part):
    sub = lax.broadcasted_iota(jnp.int32, (GROUP, LANES), 0)
    for t in range(from_ref.shape[0]):
        for place in range(0, FIRST + part + GROUP, GROUP):
            source = pl.ds(pl.multiple_of(from_row * PITCH + place, GROUP), GROUP)
            target = pl.ds(pl.multiple_of(to_row * PITCH + place, GROUP), GROUP)
            value = from_ref[t, source, :]
            if place < FIRST:
                value = jnp.where(sub == GROUP - 1, value, to_ref[t, target, :])
            elif place >= FIRST + part:
                value = jnp.where(sub == 0, value, to_ref[t, target, :])
            to_ref[t, target, :] = value


def prep_kernel(
    own_hbm, w_in_hbm, w_out_hbm, fwd_hbm, bwd_hbm, spec_hbm, filt_hbm, gain_hbm, kernel_hbm, bias_hbm,
    p_ref, w_in_ref, w_out_ref, fwd_ref, bwd_ref, taps_ref, h_ref, outer_ref,
    own_ref, spec_ref, filt_ref, gain_ref, kernel_ref, bias_ref, sems,
):
    core = lax.axis_index("row")
    rows, cols, width = own_ref.shape
    part = cols // 2
    moves = [
        (own_hbm, own_ref),
        (w_in_hbm, w_in_ref),
        (spec_hbm, spec_ref),
        (filt_hbm, filt_ref),
        (gain_hbm, gain_ref),
        (kernel_hbm, kernel_ref),
        (bias_hbm, bias_ref),
        (fwd_hbm, fwd_ref),
        (bwd_hbm, bwd_ref),
        (w_out_hbm, w_out_ref),
    ]
    copies = [pltpu.make_async_copy(src, dst, sems.at[i]) for i, (src, dst) in enumerate(moves)]
    for copy in copies:
        copy.start()
    copies[0].wait()
    start = pl.multiple_of(core * part, part)
    far = pl.multiple_of((1 - core) * part, part)
    inner_edge = core * (part - 1)
    outer_ref[...] = pick_column(own_ref[:, pl.ds(start, part), :], inner_edge)
    beside = pick_column(own_ref[:, pl.ds(far, part), :], inner_edge)
    for copy in copies[1:7]:
        copy.wait()
    project(own_ref[:, pl.ds(start, part), :], beside, core, w_in_ref, p_ref)
    filt = filt_ref[...]
    gain = gain_ref[...]
    spectrum = jnp.dot(spec_ref[0], filt, preferred_element_type=F32) + jnp.dot(
        spec_ref[1], filt, preferred_element_type=F32
    )
    pieces = [spectrum[j * rows : (j + 1) * rows] for j in range(6)]
    near = [pieces[0] + gain, pieces[1], pieces[2] + gain]
    for j in range(3):
        h_ref[0, j] = near[j]
        h_ref[0, 3 + j] = jnp.zeros((rows, width), F32)
        h_ref[1, j] = pieces[3 + j]
        h_ref[1, 3 + j] = near[j]
    for a in range(3):
        taps_ref[3 * a : 3 * a + 3, :] = kernel_ref[a].astype(F32)
    taps_ref[9, :] = bias_ref[...]
    for copy in copies[7:]:
        copy.wait()


def add_edge_terms(first, second, core, taps, edge_ref, mixed_ref, column):
    rows, channels = first.shape
    for t in range(channels // LANES):
        at = slice(t * LANES, (t + 1) * LANES)
        edge_ref[t, 0:8, :] = jnp.zeros((8, LANES), F32)
        edge_ref[t, 4 * rows : 4 * rows + 8, :] = jnp.zeros((8, LANES), F32)
        for r in range(0, rows, 8):
            for row, half in ((core * rows, first), ((1 - core) * rows, second)):
                place = pl.ds(2 * (row + r + 1), 8, stride=2)
                edge_ref[t, place, :] = half[r : r + 8, at]
        for r in range(0, 2 * rows, 8):
            place = pl.ds(r * GROUP + column, 8, stride=GROUP)
            total = mixed_ref[t, place, :]
            for a in range(3):
                total = total + edge_ref[t, pl.ds(2 * (r + a), 8, stride=2), :] * taps[a][:, at]
            mixed_ref[t, place, :] = total


def column_taps(taps_ref, core, on_core0):
    first, second = on_core0, 2 - on_core0
    return [
        jnp.where(
            core == 0,
            taps_ref[3 * a + first : 3 * a + first + 1, :],
            taps_ref[3 * a + second : 3 * a + second + 1, :],
        )
        for a in range(3)
    ]


def depthwise_steps(p_ref, first, taps_ref, chunk, store, bases):
    for base in bases:
        at = slice(base, base + LANES)
        tap = [
            jnp.broadcast_to(taps_ref[k : k + 1, at], (GROUP, LANES)) for k in range(10)
        ]
        loaded = [
            [
                p_ref[
                    base // LANES,
                    pl.ds(row_place(chunk * CHUNK + r, first + b - 1), GROUP, stride=2),
                    :,
                ]
                for b in range(3)
            ]
            for r in range(CHUNK + 2)
        ]
        for r in range(CHUNK):
            value = tap[9]
            for a in range(3):
                row = loaded[r + a]
                value = value + (
                    row[0] * tap[3 * a] + row[1] * tap[3 * a + 1] + row[2] * tap[3 * a + 2]
                )
            store(chunk * CHUNK + r, at, value)
        yield


def interleave(out_ref, final, first):
    _, rows, _, width = final.shape
    for h in range(2):
        for t in range(width // LANES):
            for r in range(rows):
                out_ref[h, t, pl.ds(r * 2 * GROUP + first, GROUP, stride=2), :] = final[
                    h, r, :, t * LANES : (t + 1) * LANES
                ]


def conv_steps(mixed, fwd_ref, bwd_ref, w_out_ref, h_ref, prod_ref, z_ref, put):
    streams, block, lanes = prod_ref.shape
    lanes = lanes // 2
    rows = block // GROUP
    width = streams * lanes

    def products(n):
        for row in range(0, rows, 2):
            for h in range(2):
                for base in range(n * lanes, (n + 1) * lanes, LANES):
                    two = [
                        mixed(h * rows + r, width + base) * mixed(h * rows + r, 2 * width + base)
                        for r in (row, row + 1)
                    ]
                    at = h * lanes + base - n * lanes
                    prod_ref[n, row * GROUP : (row + 2) * GROUP, at : at + LANES] = (
                        jnp.concatenate(two, 0).astype(BF16)
                    )
        return jnp.dot(fwd_ref[...], prod_ref[n], preferred_element_type=F32)

    def filtered(n, spectra):
        channels = slice(n * lanes, (n + 1) * lanes)
        low, high = spectra[:, :lanes], spectra[:, lanes:]

        def response(j, s):
            return jnp.broadcast_to(h_ref[j // 3, j % 3, s : s + 1, channels], (GROUP, lanes))

        for k in range(0, rows, 2):
            parts = [[], [], [], []]
            for s in (k, k + 1):
                near_r, near_i = response(0, s), response(1, s)
                all_r, all_i = response(3, s), response(4, s)
                near_2, all_2 = (response(2, s), response(5, s)) if s == 0 else (near_r, all_r)
                re = slice(s * GROUP, (s + 1) * GROUP)
                im = slice(block + s * GROUP, block + (s + 1) * GROUP)
                lr, li, hr, hi = low[re], low[im], high[re], high[im]
                parts[0].append(lr * near_r - li * near_i)
                parts[1].append(lr * near_i + li * near_2)
                parts[2].append(lr * all_r - li * all_i + hr * near_r - hi * near_i)
                parts[3].append(lr * all_i + li * all_2 + hr * near_i + hi * near_2)
            for j in range(4):
                at, lane = (j % 2) * block + k * GROUP, (j // 2) * lanes
                z_ref[n, at : at + 2 * GROUP, lane : lane + lanes] = jnp.concatenate(
                    parts[j], 0
                ).astype(BF16)
        return jnp.dot(bwd_ref[...], z_ref[n], preferred_element_type=F32)

    def gated(n, conv):
        columns = []
        for base in range(0, lanes, LANES):
            line = [
                mixed(h * rows + r, n * lanes + base)
                * conv[r * GROUP : (r + 1) * GROUP, h * lanes + base : h * lanes + base + LANES]
                for h in range(2)
                for r in range(rows)
            ]
            columns.append(jnp.concatenate(line, 0).astype(BF16))
        return columns

    spectra = []
    for n in range(streams):
        spectra.append(products(n))
        yield
    convs = []
    for n in range(streams):
        convs.append(filtered(n, spectra[n]))
        yield
    final = jnp.dot(
        jnp.concatenate([c for n in range(streams) for c in gated(n, convs[n])], 1),
        w_out_ref[...],
        preferred_element_type=F32,
    )
    yield
    put(final.reshape(2, rows, GROUP, width))


def inner_kernel(
    _, other_ref, other_strip_ref,
    w_in_ref, taps_ref, fwd_ref, bwd_ref, w_out_ref, h_ref,
    p_ref, edge_mixed_ref, out_ref,
    q_ref, mixed_ref, prod_ref, z_ref,
):
    core = lax.axis_index("row")
    rows, cols, width = other_ref.shape
    part = cols // 2
    height = 2 * rows
    start = pl.multiple_of(core * part, part)
    channels = range(0, 3 * width, LANES)
    n_chunk = rows // CHUNK

    def store_in(ref, row0):
        def store(row, at, value):
            place = pl.ds(pl.multiple_of((row0 + row) * GROUP, GROUP), GROUP)
            ref[at.start // LANES, place, :] = value

        return store

    own_at, other_at = core * rows, (1 - core) * rows

    def inner(ref, row0, chunk):
        return depthwise_steps(ref, 1 - core, taps_ref, chunk, store_in(mixed_ref, row0), channels)

    def edge(ref, row0, chunk):
        return depthwise_steps(ref, core, taps_ref, chunk, store_in(edge_mixed_ref, row0), channels)

    for i in range(n_chunk - 1):
        for _ in inner(p_ref, own_at, core + i):
            pass
    project(other_ref[:, pl.ds(start, part), :], other_strip_ref[...], core, w_in_ref, q_ref)
    copy_row(q_ref, 1 + core * (rows - 1), p_ref, (1 - core) * (rows + 1), part)
    copy_row(p_ref, rows - core * (rows - 1), q_ref, core * (rows + 1), part)
    for _ in inner(p_ref, own_at, (1 - core) * (n_chunk - 1)):
        pass

    def inner_chunk(i, carry):
        for _ in inner(q_ref, other_at, i):
            pass
        return carry

    lax.fori_loop(0, n_chunk, inner_chunk, 0)

    def put(final):
        interleave(out_ref, final, 1 - core)

    def edge_all():
        for ref, row0 in ((p_ref, own_at), (q_ref, other_at)):
            for i in range(n_chunk):
                yield from edge(ref, row0, i)

    steps = edge_all()
    conv = conv_steps(
        lambda r, base: mixed_ref[base // LANES, r * GROUP : (r + 1) * GROUP, :],
        fwd_ref, bwd_ref, w_out_ref, h_ref, prod_ref, z_ref, put,
    )
    for _ in conv:
        for _ in range(5):
            next(steps, None)
    for _ in steps:
        pass


def finish_half(half, core, s_ref, mixed_ref, bwd_ref, w_out_ref, h_ref, z_ref, out_ref, to_ref):
    rows, part, width = to_ref.shape
    block = rows * GROUP
    for k in range(0, rows, 2):
        parts = [[], []]
        for s in (k, k + 1):

            def response(j):
                return jnp.broadcast_to(h_ref[half, j, s : s + 1, :], (GROUP, width))

            upper_r, upper_i, lower_r, lower_i = (response(j) for j in (0, 1, 3, 4))
            upper_2, lower_2 = (response(2), response(5)) if s == 0 else (upper_r, lower_r)
            re = slice(s * GROUP, (s + 1) * GROUP)
            im = slice(block + s * GROUP, block + (s + 1) * GROUP)
            lr, hr = s_ref[re, :width], s_ref[re, width:]
            li, hi = s_ref[im, :width], s_ref[im, width:]
            parts[0].append(lr * upper_r - li * upper_i + hr * lower_r - hi * lower_i)
            parts[1].append(lr * upper_i + li * upper_2 + hr * lower_i + hi * lower_2)
        for j in range(2):
            at = j * block + k * GROUP
            z_ref[at : at + 2 * GROUP, :] = jnp.concatenate(parts[j], 0).astype(BF16)
    conv = jnp.dot(bwd_ref[...], z_ref[...], preferred_element_type=F32)
    columns = []
    for t in range(width // LANES):
        line = [
            mixed_ref[t, pl.ds(pl.multiple_of((half * rows + r) * GROUP, GROUP), GROUP), :]
            * conv[r * GROUP : (r + 1) * GROUP, t * LANES : (t + 1) * LANES]
            for r in range(rows)
        ]
        columns.append(jnp.concatenate(line, 0).astype(BF16))
    final = jnp.dot(jnp.concatenate(columns, 1), w_out_ref[...], preferred_element_type=F32)
    for t in range(width // LANES):
        at = slice(t * LANES, (t + 1) * LANES)
        for r in range(rows):
            out_ref[half, t, pl.ds(r * part + core, GROUP, stride=2), :] = final[
                r * GROUP : (r + 1) * GROUP, at
            ]
        to_ref[:, :, at] = out_ref[half, t].reshape(rows, part, LANES).astype(BF16)


def edge_kernel(
    _, __, halo_ref, w_in_ref, taps_ref, fwd_ref, bwd_ref, w_out_ref, h_ref,
    out_ref, mixed_ref, s_ref, send_ref,
    strip_ref, prod_ref, z_ref,
):
    core = lax.axis_index("row")
    rows, part, width = send_ref.shape
    got = jnp.dot(halo_ref[...], w_in_ref[...], preferred_element_type=F32)
    add_edge_terms(
        got[:rows], got[rows:], 1 - core, column_taps(taps_ref, core, 0), strip_ref,
        mixed_ref, core * (GROUP - 1),
    )

    def mixed(r, base):
        return mixed_ref[base // LANES, r * GROUP : (r + 1) * GROUP, :]

    for row in range(0, rows, 2):
        for h in range(2):
            for base in range(0, width, LANES):
                two = [
                    mixed(h * rows + r, width + base) * mixed(h * rows + r, 2 * width + base)
                    for r in (row, row + 1)
                ]
                at = h * width + base
                prod_ref[row * GROUP : (row + 2) * GROUP, at : at + LANES] = jnp.concatenate(
                    two, 0
                ).astype(BF16)
    s_ref[...] = jnp.dot(fwd_ref[...], prod_ref[...], preferred_element_type=F32)
    finish_half(
        1 - core, core, s_ref, mixed_ref, bwd_ref, w_out_ref, h_ref, z_ref, out_ref, send_ref
    )


def own_kernel(
    _, mixed_ref, s_ref, bwd_ref, w_out_ref, h_ref,
    out_ref, mine_ref,
    z_ref,
):
    core = lax.axis_index("row")
    finish_half(core, core, s_ref, mixed_ref, bwd_ref, w_out_ref, h_ref, z_ref, out_ref, mine_ref)


def on_device(image_tokens, w_in, conv_kernel, conv_bias, long_filter, skip_gain, w_out):
    rows, cols, width = image_tokens.shape
    part = cols // 2
    height = 2 * rows
    n_col = lax.axis_size("col")
    core = lax.axis_index("row")
    fwd, bwd, spectra = transforms(rows, GROUP)
    spec_hi = spectra.astype(BF16)
    spec_lo = (spectra - spec_hi.astype(np.float64)).astype(BF16)
    spec = np.stack([spec_hi, spec_lo])
    vmem = pl.BlockSpec(memory_space=pltpu.VMEM)
    hbm = pl.BlockSpec(memory_space=pltpu.HBM)
    shape = jax.ShapeDtypeStruct
    limit = pltpu.CompilerParams(vmem_limit_bytes=24 * 1024 * 1024)

    p_shape = shape((3 * width // LANES, (rows + 2) * PITCH + GROUP, LANES), F32)
    out_shape = shape((2, width // LANES, rows * part, LANES), F32)
    mixed_shape = shape((3 * width // LANES, height * GROUP, LANES), F32)

    swap = [(0, 1), (1, 0)]
    rowmajor = Layout((0, 1, 2))
    image_tokens = with_layout_constraint(image_tokens, rowmajor)
    other = with_layout_constraint(lax.ppermute(image_tokens, "row", swap), rowmajor)

    def keep(array):
        return pltpu.with_memory_space_constraint(array, pltpu.HBM)

    projected, w_in_v, w_out_v, fwd_v, bwd_v, taps, spectrum, outer = pl.pallas_call(
        prep_kernel,
        out_shape=(
            p_shape,
            shape(w_in.shape, BF16),
            shape(w_out.shape, BF16),
            shape(fwd.shape, BF16),
            shape(bwd.shape, BF16),
            shape((16, 3 * width), F32),
            shape((2, 6, rows, width), F32),
            shape((rows, width), BF16),
        ),
        in_specs=[hbm] * 10,
        out_specs=(vmem,) * 8,
        scratch_shapes=[
            pltpu.VMEM(image_tokens.shape, BF16),
            pltpu.VMEM(spec.shape, BF16),
            pltpu.VMEM(long_filter.shape, BF16),
            pltpu.VMEM((1, width), F32),
            pltpu.VMEM(conv_kernel.shape, BF16),
            pltpu.VMEM(conv_bias.shape, F32),
            pltpu.SemaphoreType.DMA((10,)),
        ],
        compiler_params=limit,
        cost_estimate=pl.CostEstimate(flops=0, bytes_accessed=3 * 1024 * 1024, transcendentals=0),
    )(
        keep(image_tokens), keep(w_in), keep(w_out), keep(fwd.astype(BF16)), keep(bwd.astype(BF16)),
        keep(spec), keep(long_filter), keep(skip_gain[None]), keep(conv_kernel), keep(conv_bias),
    )

    def by_core(low, high):
        return jnp.where(core == 0, low, high)

    def column(low):
        return by_core(other[:, low], other[:, cols - 1 - low])

    pairs = []
    for j in range(n_col - 1):
        pairs += [(n_col + j, j + 1), (j + 1, n_col + j)]
    halo = lax.ppermute(jnp.concatenate([outer, column(0)], 0), ("row", "col"), pairs)
    _, edge_mixed, inner = pl.pallas_call(
        inner_kernel,
        out_shape=(p_shape, mixed_shape, out_shape),
        in_specs=[vmem] * 9,
        out_specs=(vmem,) * 3,
        input_output_aliases={0: 0},
        scratch_shapes=[
            pltpu.VMEM(p_shape.shape, F32),
            pltpu.VMEM(mixed_shape.shape, F32),
            pltpu.VMEM((width // LANES, rows * GROUP, 2 * LANES), BF16),
            pltpu.VMEM((width // LANES, 2 * rows * GROUP, 2 * LANES), BF16),
        ],
        compiler_params=limit,
        cost_estimate=pl.CostEstimate(flops=10**9, bytes_accessed=12 * 1024 * 1024, transcendentals=0),
    )(projected, other, column(part), w_in_v, taps, fwd_v, bwd_v, w_out_v, spectrum)
    half_shape = shape((rows, part, width), BF16)
    s_shape = shape((2 * rows * GROUP, 2 * width), F32)
    z_scratch = pltpu.VMEM((2 * rows * GROUP, width), BF16)
    out, edge_mixed, transforms_edge, send = pl.pallas_call(
        edge_kernel,
        out_shape=(out_shape, mixed_shape, s_shape, half_shape),
        in_specs=[vmem] * 9,
        out_specs=(vmem,) * 4,
        input_output_aliases={0: 0, 1: 1},
        scratch_shapes=[
            pltpu.VMEM((3 * width // LANES, 2 * height + 8, LANES), F32),
            pltpu.VMEM((rows * GROUP, 2 * width), BF16),
            z_scratch,
        ],
        compiler_params=limit,
        cost_estimate=pl.CostEstimate(flops=3 * 10**8, bytes_accessed=4 * 1024 * 1024, transcendentals=0),
    )(inner, edge_mixed, halo, w_in_v, taps, fwd_v, bwd_v, w_out_v, spectrum)
    theirs = lax.ppermute(send, "row", swap)
    _, mine = pl.pallas_call(
        own_kernel,
        out_shape=(out_shape, half_shape),
        in_specs=[vmem] * 6,
        out_specs=(vmem,) * 2,
        input_output_aliases={0: 0},
        scratch_shapes=[z_scratch],
        compiler_params=limit,
        cost_estimate=pl.CostEstimate(flops=10**8, bytes_accessed=2 * 1024 * 1024, transcendentals=0),
    )(out, edge_mixed, transforms_edge, bwd_v, w_out_v, spectrum)
    both = jnp.concatenate([mine, mine], 1)
    return lax.dynamic_update_slice_in_dim(both, theirs, (1 - core) * part, 1)


def solution(mesh):
    in_specs = (P("row", "col", None), P(), P(), P(), P(), P(), P())
    out_specs = P("row", "col", None)
    return jax.shard_map(
        on_device, mesh=mesh, in_specs=in_specs, out_specs=out_specs, check_vma=False
    )
```

```python
import jax
import jax.numpy as jnp
import numpy as np
from jax import lax
from jax.experimental import pallas as pl
from jax.experimental.layout import Layout, with_layout_constraint
from jax.experimental.pallas import tpu as pltpu
from jax.sharding import PartitionSpec as P

F32 = jnp.float32
BF16 = jnp.bfloat16


def transforms(half, group):
    size = 2 * half
    slot = np.arange(half)[:, None]
    pos = np.arange(half)[None, :]
    angle = 2 * np.pi * slot * pos / size
    real, imag = np.cos(angle), -np.sin(angle)
    imag[0] = (-1.0) ** np.arange(half)
    forward = np.concatenate([real, imag], 0)
    back_real = 2 * np.cos(angle.T) / size
    back_real[:, 0] = 1 / size
    back_imag = -2 * np.sin(angle.T) / size
    back_imag[:, 0] = (-1.0) ** np.arange(half) / size
    backward = np.concatenate([back_real, back_imag], 1)
    lag = np.arange(size)[None, :]
    angle = 2 * np.pi * slot * lag / size
    real, imag = np.cos(angle), -np.sin(angle)
    imag[0] = 0
    real2 = real.copy()
    real2[0] = (-1.0) ** np.arange(size)
    near = (lag < half).astype(np.float64)
    sign = (-1.0) ** slot
    sign2 = sign.copy()
    sign2[0] = 1
    spectra = np.concatenate(
        [real * near, imag * near, real2 * near, real * sign, imag * sign, real2 * sign2], 0
    )
    eye = np.eye(group)
    return np.kron(forward, eye), np.kron(backward, eye), spectra


LANES = 128
GROUP = 8
CHUNK = 16
PITCH = 24
FIRST = 8


def pick_column(block, column):
    rows, cols, width = block.shape
    shape = (rows, rows * cols)
    place = lax.broadcasted_iota(jnp.int32, shape, 1)
    wanted = lax.broadcasted_iota(jnp.int32, shape, 0) * cols + column
    return jnp.dot(
        jnp.where(place == wanted, 1.0, 0.0).astype(BF16),
        block.reshape(rows * cols, width),
        preferred_element_type=F32,
    ).astype(BF16)


def row_place(row, column):
    return row * PITCH + FIRST + column


def project(tokens, strip, core, w_in_ref, p_ref):
    rows, part, width = tokens.shape
    count = rows * part
    got = jnp.dot(tokens.reshape(count, width), w_in_ref[...], preferred_element_type=F32)
    got_strip = jnp.dot(strip, w_in_ref[...], preferred_element_type=F32)
    for t in range(3 * width // LANES):
        at = slice(t * LANES, (t + 1) * LANES)
        for row in (0, rows + 1):
            place = row * PITCH
            p_ref[t, place : place + PITCH + GROUP, :] = jnp.zeros((PITCH + GROUP, LANES), F32)
        for r in range(rows):
            place = row_place(r + 1, 0)
            p_ref[t, place : place + part, :] = got[r * part : (r + 1) * part, at]
        for r in range(0, rows, GROUP):
            beside = got_strip[r : r + GROUP, at]
            for column, value in (
                (-1, jnp.where(core == 1, beside, 0.0)),
                (part, jnp.where(core == 0, beside, 0.0)),
            ):
                place = row_place(r + 1, column)
                p_ref[t, pl.ds(place, GROUP, stride=PITCH), :] = value


def copy_row(from_ref, from_row, to_ref, to_row, part):
    sub = lax.broadcasted_iota(jnp.int32, (GROUP, LANES), 0)
    for t in range(from_ref.shape[0]):
        for place in range(0, FIRST + part + GROUP, GROUP):
            source = pl.ds(pl.multiple_of(from_row * PITCH + place, GROUP), GROUP)
            target = pl.ds(pl.multiple_of(to_row * PITCH + place, GROUP), GROUP)
            value = from_ref[t, source, :]
            if place < FIRST:
                value = jnp.where(sub == GROUP - 1, value, to_ref[t, target, :])
            elif place >= FIRST + part:
                value = jnp.where(sub == 0, value, to_ref[t, target, :])
            to_ref[t, target, :] = value


def prep_kernel(
    own_hbm, w_in_hbm, w_out_hbm, fwd_hbm, bwd_hbm, spec_hbm, filt_hbm, gain_hbm, kernel_hbm, bias_hbm,
    p_ref, w_in_ref, w_out_ref, fwd_ref, bwd_ref, taps_ref, h_ref, outer_ref,
    own_ref, spec_ref, filt_ref, gain_ref, kernel_ref, bias_ref, sems,
):
    core = lax.axis_index("row")
    rows, cols, width = own_ref.shape
    part = cols // 2
    moves = [
        (own_hbm, own_ref),
        (w_in_hbm, w_in_ref),
        (spec_hbm, spec_ref),
        (filt_hbm, filt_ref),
        (gain_hbm, gain_ref),
        (kernel_hbm, kernel_ref),
        (bias_hbm, bias_ref),
        (fwd_hbm, fwd_ref),
        (bwd_hbm, bwd_ref),
        (w_out_hbm, w_out_ref),
    ]
    copies = [pltpu.make_async_copy(src, dst, sems.at[i]) for i, (src, dst) in enumerate(moves)]
    for copy in copies:
        copy.start()
    copies[0].wait()
    start = pl.multiple_of(core * part, part)
    far = pl.multiple_of((1 - core) * part, part)
    inner_edge = core * (part - 1)
    outer_ref[...] = pick_column(own_ref[:, pl.ds(start, part), :], inner_edge)
    beside = pick_column(own_ref[:, pl.ds(far, part), :], inner_edge)
    for copy in copies[1:7]:
        copy.wait()
    project(own_ref[:, pl.ds(start, part), :], beside, core, w_in_ref, p_ref)
    filt = filt_ref[...]
    gain = gain_ref[...]
    spectrum = jnp.dot(spec_ref[0], filt, preferred_element_type=F32) + jnp.dot(
        spec_ref[1], filt, preferred_element_type=F32
    )
    pieces = [spectrum[j * rows : (j + 1) * rows] for j in range(6)]
    near = [pieces[0] + gain, pieces[1], pieces[2] + gain]
    for j in range(3):
        h_ref[0, j] = near[j]
        h_ref[0, 3 + j] = jnp.zeros((rows, width), F32)
        h_ref[1, j] = pieces[3 + j]
        h_ref[1, 3 + j] = near[j]
    for a in range(3):
        taps_ref[3 * a : 3 * a + 3, :] = kernel_ref[a].astype(F32)
    taps_ref[9, :] = bias_ref[...]
    for copy in copies[7:]:
        copy.wait()


def add_edge_terms(first, second, core, taps, edge_ref, mixed_ref, column):
    rows, channels = first.shape
    for t in range(channels // LANES):
        at = slice(t * LANES, (t + 1) * LANES)
        edge_ref[t, 0:8, :] = jnp.zeros((8, LANES), F32)
        edge_ref[t, 4 * rows : 4 * rows + 8, :] = jnp.zeros((8, LANES), F32)
        for r in range(0, rows, 8):
            for row, half in ((core * rows, first), ((1 - core) * rows, second)):
                place = pl.ds(2 * (row + r + 1), 8, stride=2)
                edge_ref[t, place, :] = half[r : r + 8, at]
        for r in range(0, 2 * rows, 8):
            place = pl.ds(r * GROUP + column, 8, stride=GROUP)
            total = mixed_ref[t, place, :]
            for a in range(3):
                total = total + edge_ref[t, pl.ds(2 * (r + a), 8, stride=2), :] * taps[a][:, at]
            mixed_ref[t, place, :] = total


def column_taps(taps_ref, core, on_core0):
    first, second = on_core0, 2 - on_core0
    return [
        jnp.where(
            core == 0,
            taps_ref[3 * a + first : 3 * a + first + 1, :],
            taps_ref[3 * a + second : 3 * a + second + 1, :],
        )
        for a in range(3)
    ]


def depthwise_steps(p_ref, first, taps_ref, chunk, store, bases):
    for base in bases:
        at = slice(base, base + LANES)
        tap = [
            jnp.broadcast_to(taps_ref[k : k + 1, at], (GROUP, LANES)) for k in range(10)
        ]
        loaded = [
            [
                p_ref[
                    base // LANES,
                    pl.ds(row_place(chunk * CHUNK + r, first + b - 1), GROUP, stride=2),
                    :,
                ]
                for b in range(3)
            ]
            for r in range(CHUNK + 2)
        ]
        for r in range(CHUNK):
            value = tap[9]
            for a in range(3):
                row = loaded[r + a]
                value = value + (
                    row[0] * tap[3 * a] + row[1] * tap[3 * a + 1] + row[2] * tap[3 * a + 2]
                )
            store(chunk * CHUNK + r, at, value)
        yield


def interleave(out_ref, final, first):
    _, rows, _, width = final.shape
    for h in range(2):
        for t in range(width // LANES):
            for r in range(rows):
                out_ref[h, t, pl.ds(r * 2 * GROUP + first, GROUP, stride=2), :] = final[
                    h, r, :, t * LANES : (t + 1) * LANES
                ]


def conv_steps(mixed, fwd_ref, bwd_ref, w_out_ref, h_ref, prod_ref, z_ref, put):
    streams, block, lanes = prod_ref.shape
    lanes = lanes // 2
    rows = block // GROUP
    width = streams * lanes

    def products(n):
        for row in range(0, rows, 2):
            for h in range(2):
                for base in range(n * lanes, (n + 1) * lanes, LANES):
                    two = [
                        mixed(h * rows + r, width + base) * mixed(h * rows + r, 2 * width + base)
                        for r in (row, row + 1)
                    ]
                    at = h * lanes + base - n * lanes
                    prod_ref[n, row * GROUP : (row + 2) * GROUP, at : at + LANES] = (
                        jnp.concatenate(two, 0).astype(BF16)
                    )
        return jnp.dot(fwd_ref[...], prod_ref[n], preferred_element_type=F32)

    def filtered(n, spectra):
        channels = slice(n * lanes, (n + 1) * lanes)
        low, high = spectra[:, :lanes], spectra[:, lanes:]

        def response(j, s):
            return jnp.broadcast_to(h_ref[j // 3, j % 3, s : s + 1, channels], (GROUP, lanes))

        for k in range(0, rows, 2):
            parts = [[], [], [], []]
            for s in (k, k + 1):
                near_r, near_i = response(0, s), response(1, s)
                all_r, all_i = response(3, s), response(4, s)
                near_2, all_2 = (response(2, s), response(5, s)) if s == 0 else (near_r, all_r)
                re = slice(s * GROUP, (s + 1) * GROUP)
                im = slice(block + s * GROUP, block + (s + 1) * GROUP)
                lr, li, hr, hi = low[re], low[im], high[re], high[im]
                parts[0].append(lr * near_r - li * near_i)
                parts[1].append(lr * near_i + li * near_2)
                parts[2].append(lr * all_r - li * all_i + hr * near_r - hi * near_i)
                parts[3].append(lr * all_i + li * all_2 + hr * near_i + hi * near_2)
            for j in range(4):
                at, lane = (j % 2) * block + k * GROUP, (j // 2) * lanes
                z_ref[n, at : at + 2 * GROUP, lane : lane + lanes] = jnp.concatenate(
                    parts[j], 0
                ).astype(BF16)
        return jnp.dot(bwd_ref[...], z_ref[n], preferred_element_type=F32)

    def gated(n, conv):
        columns = []
        for base in range(0, lanes, LANES):
            line = [
                mixed(h * rows + r, n * lanes + base)
                * conv[r * GROUP : (r + 1) * GROUP, h * lanes + base : h * lanes + base + LANES]
                for h in range(2)
                for r in range(rows)
            ]
            columns.append(jnp.concatenate(line, 0).astype(BF16))
        return columns

    spectra = []
    for n in range(streams):
        spectra.append(products(n))
        yield
    convs = []
    for n in range(streams):
        convs.append(filtered(n, spectra[n]))
        yield
    final = jnp.dot(
        jnp.concatenate([c for n in range(streams) for c in gated(n, convs[n])], 1),
        w_out_ref[...],
        preferred_element_type=F32,
    )
    yield
    put(final.reshape(2, rows, GROUP, width))


def inner_kernel(
    _, other_ref, other_strip_ref,
    w_in_ref, taps_ref, fwd_ref, bwd_ref, w_out_ref, h_ref,
    p_ref, edge_mixed_ref, out_ref,
    q_ref, mixed_ref, prod_ref, z_ref,
):
    core = lax.axis_index("row")
    rows, cols, width = other_ref.shape
    part = cols // 2
    height = 2 * rows
    start = pl.multiple_of(core * part, part)
    channels = range(0, 3 * width, LANES)
    n_chunk = rows // CHUNK

    def store_in(ref, row0):
        def store(row, at, value):
            place = pl.ds(pl.multiple_of((row0 + row) * GROUP, GROUP), GROUP)
            ref[at.start // LANES, place, :] = value

        return store

    own_at, other_at = core * rows, (1 - core) * rows

    def inner(ref, row0, chunk):
        return depthwise_steps(ref, 1 - core, taps_ref, chunk, store_in(mixed_ref, row0), channels)

    def edge(ref, row0, chunk):
        return depthwise_steps(ref, core, taps_ref, chunk, store_in(edge_mixed_ref, row0), channels)

    for i in range(n_chunk - 1):
        for _ in inner(p_ref, own_at, core + i):
            pass
    project(other_ref[:, pl.ds(start, part), :], other_strip_ref[...], core, w_in_ref, q_ref)
    copy_row(q_ref, 1 + core * (rows - 1), p_ref, (1 - core) * (rows + 1), part)
    copy_row(p_ref, rows - core * (rows - 1), q_ref, core * (rows + 1), part)
    for _ in inner(p_ref, own_at, (1 - core) * (n_chunk - 1)):
        pass

    def inner_chunk(i, carry):
        for _ in inner(q_ref, other_at, i):
            pass
        return carry

    lax.fori_loop(0, n_chunk, inner_chunk, 0)

    def put(final):
        interleave(out_ref, final, 1 - core)

    def edge_all():
        for ref, row0 in ((p_ref, own_at), (q_ref, other_at)):
            for i in range(n_chunk):
                yield from edge(ref, row0, i)

    steps = edge_all()
    conv = conv_steps(
        lambda r, base: mixed_ref[base // LANES, r * GROUP : (r + 1) * GROUP, :],
        fwd_ref, bwd_ref, w_out_ref, h_ref, prod_ref, z_ref, put,
    )
    for _ in conv:
        for _ in range(5):
            next(steps, None)
    for _ in steps:
        pass


def finish_half(half, core, s_ref, mixed_ref, bwd_ref, w_out_ref, h_ref, z_ref, out_ref, to_ref):
    rows, part, width = to_ref.shape
    block = rows * GROUP
    for k in range(0, rows, 2):
        parts = [[], []]
        for s in (k, k + 1):

            def response(j):
                return jnp.broadcast_to(h_ref[half, j, s : s + 1, :], (GROUP, width))

            upper_r, upper_i, lower_r, lower_i = (response(j) for j in (0, 1, 3, 4))
            upper_2, lower_2 = (response(2), response(5)) if s == 0 else (upper_r, lower_r)
            re = slice(s * GROUP, (s + 1) * GROUP)
            im = slice(block + s * GROUP, block + (s + 1) * GROUP)
            lr, hr = s_ref[re, :width], s_ref[re, width:]
            li, hi = s_ref[im, :width], s_ref[im, width:]
            parts[0].append(lr * upper_r - li * upper_i + hr * lower_r - hi * lower_i)
            parts[1].append(lr * upper_i + li * upper_2 + hr * lower_i + hi * lower_2)
        for j in range(2):
            at = j * block + k * GROUP
            z_ref[at : at + 2 * GROUP, :] = jnp.concatenate(parts[j], 0).astype(BF16)
    conv = jnp.dot(bwd_ref[...], z_ref[...], preferred_element_type=F32)
    columns = []
    for t in range(width // LANES):
        line = [
            mixed_ref[t, pl.ds(pl.multiple_of((half * rows + r) * GROUP, GROUP), GROUP), :]
            * conv[r * GROUP : (r + 1) * GROUP, t * LANES : (t + 1) * LANES]
            for r in range(rows)
        ]
        columns.append(jnp.concatenate(line, 0).astype(BF16))
    final = jnp.dot(jnp.concatenate(columns, 1), w_out_ref[...], preferred_element_type=F32)
    for t in range(width // LANES):
        at = slice(t * LANES, (t + 1) * LANES)
        for r in range(rows):
            out_ref[half, t, pl.ds(r * part + core, GROUP, stride=2), :] = final[
                r * GROUP : (r + 1) * GROUP, at
            ]
        to_ref[:, :, at] = out_ref[half, t].reshape(rows, part, LANES).astype(BF16)


def edge_kernel(
    _, __, halo_ref, w_in_ref, taps_ref, fwd_ref, bwd_ref, w_out_ref, h_ref,
    out_ref, mixed_ref, s_ref, send_ref,
    strip_ref, prod_ref, z_ref,
):
    core = lax.axis_index("row")
    rows, part, width = send_ref.shape
    got = jnp.dot(halo_ref[...], w_in_ref[...], preferred_element_type=F32)
    add_edge_terms(
        got[:rows], got[rows:], 1 - core, column_taps(taps_ref, core, 0), strip_ref,
        mixed_ref, core * (GROUP - 1),
    )

    def mixed(r, base):
        return mixed_ref[base // LANES, r * GROUP : (r + 1) * GROUP, :]

    for row in range(0, rows, 2):
        for h in range(2):
            for base in range(0, width, LANES):
                two = [
                    mixed(h * rows + r, width + base) * mixed(h * rows + r, 2 * width + base)
                    for r in (row, row + 1)
                ]
                at = h * width + base
                prod_ref[row * GROUP : (row + 2) * GROUP, at : at + LANES] = jnp.concatenate(
                    two, 0
                ).astype(BF16)
    s_ref[...] = jnp.dot(fwd_ref[...], prod_ref[...], preferred_element_type=F32)
    finish_half(
        1 - core, core, s_ref, mixed_ref, bwd_ref, w_out_ref, h_ref, z_ref, out_ref, send_ref
    )


def own_kernel(
    _, mixed_ref, s_ref, bwd_ref, w_out_ref, h_ref,
    out_ref, mine_ref,
    z_ref,
):
    core = lax.axis_index("row")
    finish_half(core, core, s_ref, mixed_ref, bwd_ref, w_out_ref, h_ref, z_ref, out_ref, mine_ref)


def on_device(image_tokens, w_in, conv_kernel, conv_bias, long_filter, skip_gain, w_out):
    rows, cols, width = image_tokens.shape
    part = cols // 2
    height = 2 * rows
    n_col = lax.axis_size("col")
    core = lax.axis_index("row")
    fwd, bwd, spectra = transforms(rows, GROUP)
    spec_hi = spectra.astype(BF16)
    spec_lo = (spectra - spec_hi.astype(np.float64)).astype(BF16)
    spec = np.stack([spec_hi, spec_lo])
    vmem = pl.BlockSpec(memory_space=pltpu.VMEM)
    hbm = pl.BlockSpec(memory_space=pltpu.HBM)
    shape = jax.ShapeDtypeStruct
    limit = pltpu.CompilerParams(vmem_limit_bytes=24 * 1024 * 1024)

    p_shape = shape((3 * width // LANES, (rows + 2) * PITCH + GROUP, LANES), F32)
    out_shape = shape((2, width // LANES, rows * part, LANES), F32)
    mixed_shape = shape((3 * width // LANES, height * GROUP, LANES), F32)

    swap = [(0, 1), (1, 0)]
    rowmajor = Layout((0, 1, 2))
    on_first = core == 0
    offset = ((1 - core) * part).astype(jnp.uint32)
    image_tokens, on_first, offset = lax.optimization_barrier((image_tokens, on_first, offset))
    image_tokens = with_layout_constraint(image_tokens, rowmajor)
    other = with_layout_constraint(lax.ppermute(image_tokens, "row", swap), rowmajor)

    def keep(array):
        return pltpu.with_memory_space_constraint(array, pltpu.HBM)

    projected, w_in_v, w_out_v, fwd_v, bwd_v, taps, spectrum, outer = pl.pallas_call(
        prep_kernel,
        out_shape=(
            p_shape,
            shape(w_in.shape, BF16),
            shape(w_out.shape, BF16),
            shape(fwd.shape, BF16),
            shape(bwd.shape, BF16),
            shape((16, 3 * width), F32),
            shape((2, 6, rows, width), F32),
            shape((rows, width), BF16),
        ),
        in_specs=[hbm] * 10,
        out_specs=(vmem,) * 8,
        scratch_shapes=[
            pltpu.VMEM(image_tokens.shape, BF16),
            pltpu.VMEM(spec.shape, BF16),
            pltpu.VMEM(long_filter.shape, BF16),
            pltpu.VMEM((1, width), F32),
            pltpu.VMEM(conv_kernel.shape, BF16),
            pltpu.VMEM(conv_bias.shape, F32),
            pltpu.SemaphoreType.DMA((10,)),
        ],
        compiler_params=limit,
        cost_estimate=pl.CostEstimate(flops=0, bytes_accessed=3 * 1024 * 1024, transcendentals=0),
    )(
        keep(image_tokens), keep(w_in), keep(w_out), keep(fwd.astype(BF16)), keep(bwd.astype(BF16)),
        keep(spec), keep(long_filter), keep(skip_gain[None]), keep(conv_kernel), keep(conv_bias),
    )

    def by_core(low, high):
        return jnp.where(on_first, low, high)

    def column(low):
        return by_core(other[:, low], other[:, cols - 1 - low])

    pairs = []
    for j in range(n_col - 1):
        pairs += [(n_col + j, j + 1), (j + 1, n_col + j)]
    halo = lax.ppermute(jnp.concatenate([outer, column(0)], 0), ("row", "col"), pairs)
    _, edge_mixed, inner = pl.pallas_call(
        inner_kernel,
        out_shape=(p_shape, mixed_shape, out_shape),
        in_specs=[vmem] * 9,
        out_specs=(vmem,) * 3,
        input_output_aliases={0: 0},
        scratch_shapes=[
            pltpu.VMEM(p_shape.shape, F32),
            pltpu.VMEM(mixed_shape.shape, F32),
            pltpu.VMEM((width // LANES, rows * GROUP, 2 * LANES), BF16),
            pltpu.VMEM((width // LANES, 2 * rows * GROUP, 2 * LANES), BF16),
        ],
        compiler_params=limit,
        cost_estimate=pl.CostEstimate(flops=10**9, bytes_accessed=12 * 1024 * 1024, transcendentals=0),
    )(projected, other, column(part), w_in_v, taps, fwd_v, bwd_v, w_out_v, spectrum)
    half_shape = shape((rows, part, width), BF16)
    s_shape = shape((2 * rows * GROUP, 2 * width), F32)
    z_scratch = pltpu.VMEM((2 * rows * GROUP, width), BF16)
    out, edge_mixed, transforms_edge, send = pl.pallas_call(
        edge_kernel,
        out_shape=(out_shape, mixed_shape, s_shape, half_shape),
        in_specs=[vmem] * 9,
        out_specs=(vmem,) * 4,
        input_output_aliases={0: 0, 1: 1},
        scratch_shapes=[
            pltpu.VMEM((3 * width // LANES, 2 * height + 8, LANES), F32),
            pltpu.VMEM((rows * GROUP, 2 * width), BF16),
            z_scratch,
        ],
        compiler_params=limit,
        cost_estimate=pl.CostEstimate(flops=3 * 10**8, bytes_accessed=4 * 1024 * 1024, transcendentals=0),
    )(inner, edge_mixed, halo, w_in_v, taps, fwd_v, bwd_v, w_out_v, spectrum)
    theirs = lax.ppermute(send, "row", swap)
    _, mine = pl.pallas_call(
        own_kernel,
        out_shape=(out_shape, half_shape),
        in_specs=[vmem] * 6,
        out_specs=(vmem,) * 2,
        input_output_aliases={0: 0},
        scratch_shapes=[z_scratch],
        compiler_params=limit,
        cost_estimate=pl.CostEstimate(flops=10**8, bytes_accessed=2 * 1024 * 1024, transcendentals=0),
    )(out, edge_mixed, transforms_edge, bwd_v, w_out_v, spectrum)
    both = jnp.concatenate([mine, mine], 1)
    zero = jnp.uint32(0)
    return lax.dynamic_update_slice(both, theirs, (zero, offset, zero))


def solution(mesh):
    in_specs = (P("row", "col", None), P(), P(), P(), P(), P(), P())
    out_specs = P("row", "col", None)
    return jax.shard_map(
        on_device, mesh=mesh, in_specs=in_specs, out_specs=out_specs, check_vma=False
    )
```

```python
import jax
import jax.numpy as jnp
import numpy as np
from jax import lax
from jax.experimental import pallas as pl
from jax.experimental.layout import Layout, with_layout_constraint
from jax.experimental.pallas import tpu as pltpu
from jax.sharding import PartitionSpec as P

F32 = jnp.float32
BF16 = jnp.bfloat16


def transforms(half, group):
    size = 2 * half
    slot = np.arange(half)[:, None]
    pos = np.arange(half)[None, :]
    angle = 2 * np.pi * slot * pos / size
    real, imag = np.cos(angle), -np.sin(angle)
    imag[0] = (-1.0) ** np.arange(half)
    forward = np.concatenate([real, imag], 0)
    back_real = 2 * np.cos(angle.T) / size
    back_real[:, 0] = 1 / size
    back_imag = -2 * np.sin(angle.T) / size
    back_imag[:, 0] = (-1.0) ** np.arange(half) / size
    backward = np.concatenate([back_real, back_imag], 1)
    lag = np.arange(size)[None, :]
    angle = 2 * np.pi * slot * lag / size
    real, imag = np.cos(angle), -np.sin(angle)
    imag[0] = 0
    real2 = real.copy()
    real2[0] = (-1.0) ** np.arange(size)
    near = (lag < half).astype(np.float64)
    sign = (-1.0) ** slot
    sign2 = sign.copy()
    sign2[0] = 1
    spectra = np.concatenate(
        [real * near, imag * near, real2 * near, real * sign, imag * sign, real2 * sign2], 0
    )
    eye = np.eye(group)
    return np.kron(forward, eye), np.kron(backward, eye), spectra


LANES = 128
GROUP = 8
CHUNK = 16
PITCH = 24
FIRST = 8


def pick_column(block, column):
    rows, cols, width = block.shape
    shape = (rows, rows * cols)
    place = lax.broadcasted_iota(jnp.int32, shape, 1)
    wanted = lax.broadcasted_iota(jnp.int32, shape, 0) * cols + column
    return jnp.dot(
        jnp.where(place == wanted, 1.0, 0.0).astype(BF16),
        block.reshape(rows * cols, width),
        preferred_element_type=F32,
    ).astype(BF16)


def row_place(row, column):
    return row * PITCH + FIRST + column


def project(tokens, strip, core, w_in_ref, p_ref):
    rows, part, width = tokens.shape
    count = rows * part
    got = jnp.dot(tokens.reshape(count, width), w_in_ref[...], preferred_element_type=F32)
    got_strip = jnp.dot(strip, w_in_ref[...], preferred_element_type=F32)
    for t in range(3 * width // LANES):
        at = slice(t * LANES, (t + 1) * LANES)
        for row in (0, rows + 1):
            place = row * PITCH
            p_ref[t, place : place + PITCH + GROUP, :] = jnp.zeros((PITCH + GROUP, LANES), F32)
        for r in range(rows):
            place = row_place(r + 1, 0)
            p_ref[t, place : place + part, :] = got[r * part : (r + 1) * part, at]
        for r in range(0, rows, GROUP):
            beside = got_strip[r : r + GROUP, at]
            for column, value in (
                (-1, jnp.where(core == 1, beside, 0.0)),
                (part, jnp.where(core == 0, beside, 0.0)),
            ):
                place = row_place(r + 1, column)
                p_ref[t, pl.ds(place, GROUP, stride=PITCH), :] = value


def copy_row(from_ref, from_row, to_ref, to_row, part):
    sub = lax.broadcasted_iota(jnp.int32, (GROUP, LANES), 0)
    for t in range(from_ref.shape[0]):
        for place in range(0, FIRST + part + GROUP, GROUP):
            source = pl.ds(pl.multiple_of(from_row * PITCH + place, GROUP), GROUP)
            target = pl.ds(pl.multiple_of(to_row * PITCH + place, GROUP), GROUP)
            value = from_ref[t, source, :]
            if place < FIRST:
                value = jnp.where(sub == GROUP - 1, value, to_ref[t, target, :])
            elif place >= FIRST + part:
                value = jnp.where(sub == 0, value, to_ref[t, target, :])
            to_ref[t, target, :] = value


def prep_kernel(
    own_hbm, w_in_hbm, w_out_hbm, fwd_hbm, bwd_hbm, spec_hbm, filt_hbm, gain_hbm, kernel_hbm, bias_hbm,
    p_ref, w_in_ref, w_out_ref, fwd_ref, bwd_ref, taps_ref, h_ref, outer_ref,
    own_ref, spec_ref, filt_ref, gain_ref, kernel_ref, bias_ref, sems,
):
    core = lax.axis_index("row")
    rows, cols, width = own_ref.shape
    part = cols // 2
    moves = [
        (own_hbm, own_ref),
        (w_in_hbm, w_in_ref),
        (spec_hbm, spec_ref),
        (filt_hbm, filt_ref),
        (gain_hbm, gain_ref),
        (kernel_hbm, kernel_ref),
        (bias_hbm, bias_ref),
        (fwd_hbm, fwd_ref),
        (bwd_hbm, bwd_ref),
        (w_out_hbm, w_out_ref),
    ]
    copies = [pltpu.make_async_copy(src, dst, sems.at[i]) for i, (src, dst) in enumerate(moves)]
    for copy in copies:
        copy.start()
    copies[0].wait()
    start = pl.multiple_of(core * part, part)
    far = pl.multiple_of((1 - core) * part, part)
    inner_edge = core * (part - 1)
    outer_ref[...] = pick_column(own_ref[:, pl.ds(start, part), :], inner_edge)
    beside = pick_column(own_ref[:, pl.ds(far, part), :], inner_edge)
    for copy in copies[1:7]:
        copy.wait()
    project(own_ref[:, pl.ds(start, part), :], beside, core, w_in_ref, p_ref)
    filt = filt_ref[...]
    gain = gain_ref[...]
    spectrum = jnp.dot(spec_ref[0], filt, preferred_element_type=F32) + jnp.dot(
        spec_ref[1], filt, preferred_element_type=F32
    )
    pieces = [spectrum[j * rows : (j + 1) * rows] for j in range(6)]
    near = [pieces[0] + gain, pieces[1], pieces[2] + gain]
    for j in range(3):
        h_ref[0, j] = near[j]
        h_ref[0, 3 + j] = jnp.zeros((rows, width), F32)
        h_ref[1, j] = pieces[3 + j]
        h_ref[1, 3 + j] = near[j]
    for a in range(3):
        taps_ref[3 * a : 3 * a + 3, :] = kernel_ref[a].astype(F32)
    taps_ref[9, :] = bias_ref[...]
    for copy in copies[7:]:
        copy.wait()


def add_edge_terms(first, second, core, taps, edge_ref, mixed_ref, column):
    rows, channels = first.shape
    for t in range(channels // LANES):
        at = slice(t * LANES, (t + 1) * LANES)
        edge_ref[t, 0:8, :] = jnp.zeros((8, LANES), F32)
        edge_ref[t, 4 * rows : 4 * rows + 8, :] = jnp.zeros((8, LANES), F32)
        for r in range(0, rows, 8):
            for row, half in ((core * rows, first), ((1 - core) * rows, second)):
                place = pl.ds(2 * (row + r + 1), 8, stride=2)
                edge_ref[t, place, :] = half[r : r + 8, at]
        for r in range(0, 2 * rows, 8):
            place = pl.ds(r * GROUP + column, 8, stride=GROUP)
            total = mixed_ref[t, place, :]
            for a in range(3):
                total = total + edge_ref[t, pl.ds(2 * (r + a), 8, stride=2), :] * taps[a][:, at]
            mixed_ref[t, place, :] = total


def column_taps(taps_ref, core, on_core0):
    first, second = on_core0, 2 - on_core0
    return [
        jnp.where(
            core == 0,
            taps_ref[3 * a + first : 3 * a + first + 1, :],
            taps_ref[3 * a + second : 3 * a + second + 1, :],
        )
        for a in range(3)
    ]


def depthwise_steps(p_ref, first, taps_ref, chunk, store, bases):
    for base in bases:
        at = slice(base, base + LANES)
        tap = [
            jnp.broadcast_to(taps_ref[k : k + 1, at], (GROUP, LANES)) for k in range(10)
        ]
        loaded = [
            [
                p_ref[
                    base // LANES,
                    pl.ds(row_place(chunk * CHUNK + r, first + b - 1), GROUP, stride=2),
                    :,
                ]
                for b in range(3)
            ]
            for r in range(CHUNK + 2)
        ]
        for r in range(CHUNK):
            value = tap[9]
            for a in range(3):
                row = loaded[r + a]
                value = value + (
                    row[0] * tap[3 * a] + row[1] * tap[3 * a + 1] + row[2] * tap[3 * a + 2]
                )
            store(chunk * CHUNK + r, at, value)
        yield


def interleave(out_ref, final, first):
    _, rows, _, width = final.shape
    for h in range(2):
        for t in range(width // LANES):
            for r in range(rows):
                out_ref[h, t, pl.ds(r * 2 * GROUP + first, GROUP, stride=2), :] = final[
                    h, r, :, t * LANES : (t + 1) * LANES
                ]


def conv_steps(mixed, fwd_ref, bwd_ref, w_out_ref, h_ref, prod_ref, z_ref, put):
    streams, block, lanes = prod_ref.shape
    lanes = lanes // 2
    rows = block // GROUP
    width = streams * lanes

    def products(n):
        for row in range(0, rows, 2):
            for h in range(2):
                for base in range(n * lanes, (n + 1) * lanes, LANES):
                    two = [
                        mixed(h * rows + r, width + base) * mixed(h * rows + r, 2 * width + base)
                        for r in (row, row + 1)
                    ]
                    at = h * lanes + base - n * lanes
                    prod_ref[n, row * GROUP : (row + 2) * GROUP, at : at + LANES] = (
                        jnp.concatenate(two, 0).astype(BF16)
                    )
        return jnp.dot(fwd_ref[...], prod_ref[n], preferred_element_type=F32)

    def filtered(n, spectra):
        channels = slice(n * lanes, (n + 1) * lanes)
        low, high = spectra[:, :lanes], spectra[:, lanes:]

        def response(j, s):
            return jnp.broadcast_to(h_ref[j // 3, j % 3, s : s + 1, channels], (GROUP, lanes))

        for k in range(0, rows, 2):
            parts = [[], [], [], []]
            for s in (k, k + 1):
                near_r, near_i = response(0, s), response(1, s)
                all_r, all_i = response(3, s), response(4, s)
                near_2, all_2 = (response(2, s), response(5, s)) if s == 0 else (near_r, all_r)
                re = slice(s * GROUP, (s + 1) * GROUP)
                im = slice(block + s * GROUP, block + (s + 1) * GROUP)
                lr, li, hr, hi = low[re], low[im], high[re], high[im]
                parts[0].append(lr * near_r - li * near_i)
                parts[1].append(lr * near_i + li * near_2)
                parts[2].append(lr * all_r - li * all_i + hr * near_r - hi * near_i)
                parts[3].append(lr * all_i + li * all_2 + hr * near_i + hi * near_2)
            for j in range(4):
                at, lane = (j % 2) * block + k * GROUP, (j // 2) * lanes
                z_ref[n, at : at + 2 * GROUP, lane : lane + lanes] = jnp.concatenate(
                    parts[j], 0
                ).astype(BF16)
        return jnp.dot(bwd_ref[...], z_ref[n], preferred_element_type=F32)

    def gated(n, conv):
        columns = []
        for base in range(0, lanes, LANES):
            line = [
                mixed(h * rows + r, n * lanes + base)
                * conv[r * GROUP : (r + 1) * GROUP, h * lanes + base : h * lanes + base + LANES]
                for h in range(2)
                for r in range(rows)
            ]
            columns.append(jnp.concatenate(line, 0).astype(BF16))
        return columns

    spectra = []
    for n in range(streams):
        spectra.append(products(n))
        yield
    convs = []
    for n in range(streams):
        convs.append(filtered(n, spectra[n]))
        yield
    final = jnp.dot(
        jnp.concatenate([c for n in range(streams) for c in gated(n, convs[n])], 1),
        w_out_ref[...],
        preferred_element_type=F32,
    )
    yield
    put(final.reshape(2, rows, GROUP, width))


def inner_kernel(
    _, other_ref, other_strip_ref,
    w_in_ref, taps_ref, fwd_ref, bwd_ref, w_out_ref, h_ref,
    p_ref, edge_mixed_ref, out_ref,
    q_ref, mixed_ref, prod_ref, z_ref,
):
    core = lax.axis_index("row")
    rows, cols, width = other_ref.shape
    part = cols // 2
    height = 2 * rows
    start = pl.multiple_of(core * part, part)
    channels = range(0, 3 * width, LANES)
    n_chunk = rows // CHUNK

    def store_in(ref, row0):
        def store(row, at, value):
            place = pl.ds(pl.multiple_of((row0 + row) * GROUP, GROUP), GROUP)
            ref[at.start // LANES, place, :] = value

        return store

    own_at, other_at = core * rows, (1 - core) * rows

    def inner(ref, row0, chunk):
        return depthwise_steps(ref, 1 - core, taps_ref, chunk, store_in(mixed_ref, row0), channels)

    def edge(ref, row0, chunk):
        return depthwise_steps(ref, core, taps_ref, chunk, store_in(edge_mixed_ref, row0), channels)

    for i in range(n_chunk - 1):
        for _ in inner(p_ref, own_at, core + i):
            pass
    project(other_ref[:, pl.ds(start, part), :], other_strip_ref[...], core, w_in_ref, q_ref)
    copy_row(q_ref, 1 + core * (rows - 1), p_ref, (1 - core) * (rows + 1), part)
    copy_row(p_ref, rows - core * (rows - 1), q_ref, core * (rows + 1), part)
    for _ in inner(p_ref, own_at, (1 - core) * (n_chunk - 1)):
        pass

    def inner_chunk(i, carry):
        for _ in inner(q_ref, other_at, i):
            pass
        return carry

    lax.fori_loop(0, n_chunk, inner_chunk, 0)

    def put(final):
        interleave(out_ref, final, 1 - core)

    def edge_all():
        for ref, row0 in ((p_ref, own_at), (q_ref, other_at)):
            for i in range(n_chunk):
                yield from edge(ref, row0, i)

    steps = edge_all()
    conv = conv_steps(
        lambda r, base: mixed_ref[base // LANES, r * GROUP : (r + 1) * GROUP, :],
        fwd_ref, bwd_ref, w_out_ref, h_ref, prod_ref, z_ref, put,
    )
    for _ in conv:
        for _ in range(5):
            next(steps, None)
    for _ in steps:
        pass


def finish_half(half, core, s_ref, mixed_ref, bwd_ref, w_out_ref, h_ref, z_ref, out_ref, to_ref):
    rows, part, width = to_ref.shape
    block = rows * GROUP
    for k in range(0, rows, 2):
        parts = [[], []]
        for s in (k, k + 1):

            def response(j):
                return jnp.broadcast_to(h_ref[half, j, s : s + 1, :], (GROUP, width))

            upper_r, upper_i, lower_r, lower_i = (response(j) for j in (0, 1, 3, 4))
            upper_2, lower_2 = (response(2), response(5)) if s == 0 else (upper_r, lower_r)
            re = slice(s * GROUP, (s + 1) * GROUP)
            im = slice(block + s * GROUP, block + (s + 1) * GROUP)
            lr, hr = s_ref[re, :width], s_ref[re, width:]
            li, hi = s_ref[im, :width], s_ref[im, width:]
            parts[0].append(lr * upper_r - li * upper_i + hr * lower_r - hi * lower_i)
            parts[1].append(lr * upper_i + li * upper_2 + hr * lower_i + hi * lower_2)
        for j in range(2):
            at = j * block + k * GROUP
            z_ref[at : at + 2 * GROUP, :] = jnp.concatenate(parts[j], 0).astype(BF16)
    conv = jnp.dot(bwd_ref[...], z_ref[...], preferred_element_type=F32)
    columns = []
    for t in range(width // LANES):
        line = [
            mixed_ref[t, pl.ds(pl.multiple_of((half * rows + r) * GROUP, GROUP), GROUP), :]
            * conv[r * GROUP : (r + 1) * GROUP, t * LANES : (t + 1) * LANES]
            for r in range(rows)
        ]
        columns.append(jnp.concatenate(line, 0).astype(BF16))
    final = jnp.dot(jnp.concatenate(columns, 1), w_out_ref[...], preferred_element_type=F32)
    for t in range(width // LANES):
        at = slice(t * LANES, (t + 1) * LANES)
        for r in range(rows):
            out_ref[half, t, pl.ds(r * part + core, GROUP, stride=2), :] = final[
                r * GROUP : (r + 1) * GROUP, at
            ]
        to_ref[:, :, at] = out_ref[half, t].reshape(rows, part, LANES).astype(BF16)


def edge_kernel(
    _, __, halo_ref, w_in_ref, taps_ref, fwd_ref, bwd_ref, w_out_ref, h_ref,
    out_ref, mixed_ref, s_ref, send_ref,
    strip_ref, prod_ref, z_ref,
):
    core = lax.axis_index("row")
    rows, part, width = send_ref.shape
    got = jnp.dot(halo_ref[...], w_in_ref[...], preferred_element_type=F32)
    add_edge_terms(
        got[:rows], got[rows:], 1 - core, column_taps(taps_ref, core, 0), strip_ref,
        mixed_ref, core * (GROUP - 1),
    )

    def mixed(r, base):
        return mixed_ref[base // LANES, r * GROUP : (r + 1) * GROUP, :]

    for row in range(0, rows, 2):
        for h in range(2):
            for base in range(0, width, LANES):
                two = [
                    mixed(h * rows + r, width + base) * mixed(h * rows + r, 2 * width + base)
                    for r in (row, row + 1)
                ]
                at = h * width + base
                prod_ref[row * GROUP : (row + 2) * GROUP, at : at + LANES] = jnp.concatenate(
                    two, 0
                ).astype(BF16)
    s_ref[...] = jnp.dot(fwd_ref[...], prod_ref[...], preferred_element_type=F32)
    finish_half(
        1 - core, core, s_ref, mixed_ref, bwd_ref, w_out_ref, h_ref, z_ref, out_ref, send_ref
    )


def own_kernel(
    _, mixed_ref, s_ref, bwd_ref, w_out_ref, h_ref,
    out_ref, mine_ref,
    z_ref,
):
    core = lax.axis_index("row")
    finish_half(core, core, s_ref, mixed_ref, bwd_ref, w_out_ref, h_ref, z_ref, out_ref, mine_ref)


def on_device(image_tokens, w_in, conv_kernel, conv_bias, long_filter, skip_gain, w_out):
    rows, cols, width = image_tokens.shape
    part = cols // 2
    height = 2 * rows
    n_col = lax.axis_size("col")
    core = lax.axis_index("row")
    fwd, bwd, spectra = transforms(rows, GROUP)
    spec_hi = spectra.astype(BF16)
    spec_lo = (spectra - spec_hi.astype(np.float64)).astype(BF16)
    spec = np.stack([spec_hi, spec_lo])
    vmem = pl.BlockSpec(memory_space=pltpu.VMEM)
    hbm = pl.BlockSpec(memory_space=pltpu.HBM)
    shape = jax.ShapeDtypeStruct
    limit = pltpu.CompilerParams(vmem_limit_bytes=24 * 1024 * 1024)

    p_shape = shape((3 * width // LANES, (rows + 2) * PITCH + GROUP, LANES), F32)
    out_shape = shape((2, width // LANES, rows * part, LANES), F32)
    mixed_shape = shape((3 * width // LANES, height * GROUP, LANES), F32)

    swap = [(0, 1), (1, 0)]
    rowmajor = Layout((0, 1, 2))
    on_first = core == 0
    image_tokens, on_first = lax.optimization_barrier((image_tokens, on_first))
    image_tokens = with_layout_constraint(image_tokens, rowmajor)
    other = with_layout_constraint(lax.ppermute(image_tokens, "row", swap), rowmajor)

    def keep(array):
        return pltpu.with_memory_space_constraint(array, pltpu.HBM)

    projected, w_in_v, w_out_v, fwd_v, bwd_v, taps, spectrum, outer = pl.pallas_call(
        prep_kernel,
        out_shape=(
            p_shape,
            shape(w_in.shape, BF16),
            shape(w_out.shape, BF16),
            shape(fwd.shape, BF16),
            shape(bwd.shape, BF16),
            shape((16, 3 * width), F32),
            shape((2, 6, rows, width), F32),
            shape((rows, width), BF16),
        ),
        in_specs=[hbm] * 10,
        out_specs=(vmem,) * 8,
        scratch_shapes=[
            pltpu.VMEM(image_tokens.shape, BF16),
            pltpu.VMEM(spec.shape, BF16),
            pltpu.VMEM(long_filter.shape, BF16),
            pltpu.VMEM((1, width), F32),
            pltpu.VMEM(conv_kernel.shape, BF16),
            pltpu.VMEM(conv_bias.shape, F32),
            pltpu.SemaphoreType.DMA((10,)),
        ],
        compiler_params=limit,
        cost_estimate=pl.CostEstimate(flops=0, bytes_accessed=3 * 1024 * 1024, transcendentals=0),
    )(
        keep(image_tokens), keep(w_in), keep(w_out), keep(fwd.astype(BF16)), keep(bwd.astype(BF16)),
        keep(spec), keep(long_filter), keep(skip_gain[None]), keep(conv_kernel), keep(conv_bias),
    )

    def by_core(low, high):
        return jnp.where(on_first, low, high)

    def column(low):
        return by_core(other[:, low], other[:, cols - 1 - low])

    pairs = []
    for j in range(n_col - 1):
        pairs += [(n_col + j, j + 1), (j + 1, n_col + j)]
    halo = lax.ppermute(jnp.concatenate([outer, column(0)], 0), ("row", "col"), pairs)
    _, edge_mixed, inner = pl.pallas_call(
        inner_kernel,
        out_shape=(p_shape, mixed_shape, out_shape),
        in_specs=[vmem] * 9,
        out_specs=(vmem,) * 3,
        input_output_aliases={0: 0},
        scratch_shapes=[
            pltpu.VMEM(p_shape.shape, F32),
            pltpu.VMEM(mixed_shape.shape, F32),
            pltpu.VMEM((width // LANES, rows * GROUP, 2 * LANES), BF16),
            pltpu.VMEM((width // LANES, 2 * rows * GROUP, 2 * LANES), BF16),
        ],
        compiler_params=limit,
        cost_estimate=pl.CostEstimate(flops=10**9, bytes_accessed=12 * 1024 * 1024, transcendentals=0),
    )(projected, other, column(part), w_in_v, taps, fwd_v, bwd_v, w_out_v, spectrum)
    half_shape = shape((rows, part, width), BF16)
    s_shape = shape((2 * rows * GROUP, 2 * width), F32)
    z_scratch = pltpu.VMEM((2 * rows * GROUP, width), BF16)
    out, edge_mixed, transforms_edge, send = pl.pallas_call(
        edge_kernel,
        out_shape=(out_shape, mixed_shape, s_shape, half_shape),
        in_specs=[vmem] * 9,
        out_specs=(vmem,) * 4,
        input_output_aliases={0: 0, 1: 1},
        scratch_shapes=[
            pltpu.VMEM((3 * width // LANES, 2 * height + 8, LANES), F32),
            pltpu.VMEM((rows * GROUP, 2 * width), BF16),
            z_scratch,
        ],
        compiler_params=limit,
        cost_estimate=pl.CostEstimate(flops=3 * 10**8, bytes_accessed=4 * 1024 * 1024, transcendentals=0),
    )(inner, edge_mixed, halo, w_in_v, taps, fwd_v, bwd_v, w_out_v, spectrum)
    theirs = lax.ppermute(send, "row", swap)
    _, mine = pl.pallas_call(
        own_kernel,
        out_shape=(out_shape, half_shape),
        in_specs=[vmem] * 6,
        out_specs=(vmem,) * 2,
        input_output_aliases={0: 0},
        scratch_shapes=[z_scratch],
        compiler_params=limit,
        cost_estimate=pl.CostEstimate(flops=10**8, bytes_accessed=2 * 1024 * 1024, transcendentals=0),
    )(out, edge_mixed, transforms_edge, bwd_v, w_out_v, spectrum)
    mine, late_core = lax.optimization_barrier((mine, core))
    offset = (1 - late_core) * part
    both = jnp.concatenate([mine, mine], 1)
    zero = jnp.int32(0)
    return lax.dynamic_update_slice_p.bind(both, theirs, zero, offset, zero)


def solution(mesh):
    in_specs = (P("row", "col", None), P(), P(), P(), P(), P(), P())
    out_specs = P("row", "col", None)
    return jax.shard_map(
        on_device, mesh=mesh, in_specs=in_specs, out_specs=out_specs, check_vma=False
    )
```

```python
import jax
import jax.numpy as jnp
import numpy as np
from jax import lax
from jax.experimental import pallas as pl
from jax.experimental.layout import Layout, with_layout_constraint
from jax.experimental.pallas import tpu as pltpu
from jax.sharding import PartitionSpec as P

F32 = jnp.float32
BF16 = jnp.bfloat16


def transforms(half, group):
    size = 2 * half
    slot = np.arange(half)[:, None]
    pos = np.arange(half)[None, :]
    angle = 2 * np.pi * slot * pos / size
    real, imag = np.cos(angle), -np.sin(angle)
    imag[0] = (-1.0) ** np.arange(half)
    forward = np.concatenate([real, imag], 0)
    back_real = 2 * np.cos(angle.T) / size
    back_real[:, 0] = 1 / size
    back_imag = -2 * np.sin(angle.T) / size
    back_imag[:, 0] = (-1.0) ** np.arange(half) / size
    backward = np.concatenate([back_real, back_imag], 1)
    lag = np.arange(size)[None, :]
    angle = 2 * np.pi * slot * lag / size
    real, imag = np.cos(angle), -np.sin(angle)
    imag[0] = 0
    real2 = real.copy()
    real2[0] = (-1.0) ** np.arange(size)
    near = (lag < half).astype(np.float64)
    sign = (-1.0) ** slot
    sign2 = sign.copy()
    sign2[0] = 1
    spectra = np.concatenate(
        [real * near, imag * near, real2 * near, real * sign, imag * sign, real2 * sign2], 0
    )
    eye = np.eye(group)
    return np.kron(forward, eye), np.kron(backward, eye), spectra


LANES = 128
GROUP = 8
CHUNK = 16
PITCH = 24
FIRST = 8


def pick_column(block, column):
    rows, cols, width = block.shape
    shape = (rows, rows * cols)
    place = lax.broadcasted_iota(jnp.int32, shape, 1)
    wanted = lax.broadcasted_iota(jnp.int32, shape, 0) * cols + column
    return jnp.dot(
        jnp.where(place == wanted, 1.0, 0.0).astype(BF16),
        block.reshape(rows * cols, width),
        preferred_element_type=F32,
    ).astype(BF16)


def row_place(row, column):
    return row * PITCH + FIRST + column


def project(tokens, strip, core, w_in_ref, p_ref):
    rows, part, width = tokens.shape
    count = rows * part
    got = jnp.dot(tokens.reshape(count, width), w_in_ref[...], preferred_element_type=F32)
    got_strip = jnp.dot(strip, w_in_ref[...], preferred_element_type=F32)
    for t in range(3 * width // LANES):
        at = slice(t * LANES, (t + 1) * LANES)
        for row in (0, rows + 1):
            place = row * PITCH
            p_ref[t, place : place + PITCH + GROUP, :] = jnp.zeros((PITCH + GROUP, LANES), F32)
        for r in range(rows):
            place = row_place(r + 1, 0)
            p_ref[t, place : place + part, :] = got[r * part : (r + 1) * part, at]
        for r in range(0, rows, GROUP):
            beside = got_strip[r : r + GROUP, at]
            for column, value in (
                (-1, jnp.where(core == 1, beside, 0.0)),
                (part, jnp.where(core == 0, beside, 0.0)),
            ):
                place = row_place(r + 1, column)
                p_ref[t, pl.ds(place, GROUP, stride=PITCH), :] = value


def copy_row(from_ref, from_row, to_ref, to_row, part):
    sub = lax.broadcasted_iota(jnp.int32, (GROUP, LANES), 0)
    for t in range(from_ref.shape[0]):
        for place in range(0, FIRST + part + GROUP, GROUP):
            source = pl.ds(pl.multiple_of(from_row * PITCH + place, GROUP), GROUP)
            target = pl.ds(pl.multiple_of(to_row * PITCH + place, GROUP), GROUP)
            value = from_ref[t, source, :]
            if place < FIRST:
                value = jnp.where(sub == GROUP - 1, value, to_ref[t, target, :])
            elif place >= FIRST + part:
                value = jnp.where(sub == 0, value, to_ref[t, target, :])
            to_ref[t, target, :] = value


def prep_kernel(
    own_hbm, w_in_hbm, w_out_hbm, fwd_hbm, bwd_hbm, spec_hbm, filt_hbm, gain_hbm, kernel_hbm, bias_hbm,
    p_ref, w_in_ref, w_out_ref, fwd_ref, bwd_ref, taps_ref, h_ref, outer_ref,
    own_ref, spec_ref, filt_ref, gain_ref, kernel_ref, bias_ref, sems,
):
    core = lax.axis_index("row")
    rows, cols, width = own_ref.shape
    part = cols // 2
    moves = [
        (own_hbm, own_ref),
        (w_in_hbm, w_in_ref),
        (spec_hbm, spec_ref),
        (filt_hbm, filt_ref),
        (gain_hbm, gain_ref),
        (kernel_hbm, kernel_ref),
        (bias_hbm, bias_ref),
        (fwd_hbm, fwd_ref),
        (bwd_hbm, bwd_ref),
        (w_out_hbm, w_out_ref),
    ]
    copies = [pltpu.make_async_copy(src, dst, sems.at[i]) for i, (src, dst) in enumerate(moves)]
    for copy in copies:
        copy.start()
    copies[0].wait()
    start = pl.multiple_of(core * part, part)
    far = pl.multiple_of((1 - core) * part, part)
    inner_edge = core * (part - 1)
    outer_ref[...] = pick_column(own_ref[:, pl.ds(start, part), :], inner_edge)
    beside = pick_column(own_ref[:, pl.ds(far, part), :], inner_edge)
    for copy in copies[1:7]:
        copy.wait()
    project(own_ref[:, pl.ds(start, part), :], beside, core, w_in_ref, p_ref)
    filt = filt_ref[...]
    gain = gain_ref[...]
    spectrum = jnp.dot(spec_ref[0], filt, preferred_element_type=F32) + jnp.dot(
        spec_ref[1], filt, preferred_element_type=F32
    )
    pieces = [spectrum[j * rows : (j + 1) * rows] for j in range(6)]
    near = [pieces[0] + gain, pieces[1], pieces[2] + gain]
    for j in range(3):
        h_ref[0, j] = near[j]
        h_ref[0, 3 + j] = jnp.zeros((rows, width), F32)
        h_ref[1, j] = pieces[3 + j]
        h_ref[1, 3 + j] = near[j]
    for a in range(3):
        taps_ref[3 * a : 3 * a + 3, :] = kernel_ref[a].astype(F32)
    taps_ref[9, :] = bias_ref[...]
    for copy in copies[7:]:
        copy.wait()


def add_edge_terms(first, second, core, taps, edge_ref, mixed_ref, column):
    rows, channels = first.shape
    for t in range(channels // LANES):
        at = slice(t * LANES, (t + 1) * LANES)
        edge_ref[t, 0:8, :] = jnp.zeros((8, LANES), F32)
        edge_ref[t, 4 * rows : 4 * rows + 8, :] = jnp.zeros((8, LANES), F32)
        for r in range(0, rows, 8):
            for row, half in ((core * rows, first), ((1 - core) * rows, second)):
                place = pl.ds(2 * (row + r + 1), 8, stride=2)
                edge_ref[t, place, :] = half[r : r + 8, at]
        for r in range(0, 2 * rows, 8):
            place = pl.ds(r * GROUP + column, 8, stride=GROUP)
            total = mixed_ref[t, place, :]
            for a in range(3):
                total = total + edge_ref[t, pl.ds(2 * (r + a), 8, stride=2), :] * taps[a][:, at]
            mixed_ref[t, place, :] = total


def column_taps(taps_ref, core, on_core0):
    first, second = on_core0, 2 - on_core0
    return [
        jnp.where(
            core == 0,
            taps_ref[3 * a + first : 3 * a + first + 1, :],
            taps_ref[3 * a + second : 3 * a + second + 1, :],
        )
        for a in range(3)
    ]


def depthwise_steps(p_ref, first, taps_ref, chunk, store, bases):
    for base in bases:
        at = slice(base, base + LANES)
        tap = [
            jnp.broadcast_to(taps_ref[k : k + 1, at], (GROUP, LANES)) for k in range(10)
        ]
        loaded = [
            [
                p_ref[
                    base // LANES,
                    pl.ds(row_place(chunk * CHUNK + r, first + b - 1), GROUP, stride=2),
                    :,
                ]
                for b in range(3)
            ]
            for r in range(CHUNK + 2)
        ]
        for r in range(CHUNK):
            value = tap[9]
            for a in range(3):
                row = loaded[r + a]
                value = value + (
                    row[0] * tap[3 * a] + row[1] * tap[3 * a + 1] + row[2] * tap[3 * a + 2]
                )
            store(chunk * CHUNK + r, at, value)
        yield


def interleave(out_ref, final, first):
    _, rows, _, width = final.shape
    for h in range(2):
        for t in range(width // LANES):
            for r in range(rows):
                out_ref[h, t, pl.ds(r * 2 * GROUP + first, GROUP, stride=2), :] = final[
                    h, r, :, t * LANES : (t + 1) * LANES
                ]


def conv_steps(mixed, fwd_ref, bwd_ref, w_out_ref, h_ref, prod_ref, z_ref, put):
    streams, block, lanes = prod_ref.shape
    lanes = lanes // 2
    rows = block // GROUP
    width = streams * lanes

    def products(n):
        for row in range(0, rows, 2):
            for h in range(2):
                for base in range(n * lanes, (n + 1) * lanes, LANES):
                    two = [
                        mixed(h * rows + r, width + base) * mixed(h * rows + r, 2 * width + base)
                        for r in (row, row + 1)
                    ]
                    at = h * lanes + base - n * lanes
                    prod_ref[n, row * GROUP : (row + 2) * GROUP, at : at + LANES] = (
                        jnp.concatenate(two, 0).astype(BF16)
                    )
        return jnp.dot(fwd_ref[...], prod_ref[n], preferred_element_type=F32)

    def filtered(n, spectra):
        channels = slice(n * lanes, (n + 1) * lanes)
        low, high = spectra[:, :lanes], spectra[:, lanes:]

        def response(j, s):
            return jnp.broadcast_to(h_ref[j // 3, j % 3, s : s + 1, channels], (GROUP, lanes))

        for k in range(0, rows, 2):
            parts = [[], [], [], []]
            for s in (k, k + 1):
                near_r, near_i = response(0, s), response(1, s)
                all_r, all_i = response(3, s), response(4, s)
                near_2, all_2 = (response(2, s), response(5, s)) if s == 0 else (near_r, all_r)
                re = slice(s * GROUP, (s + 1) * GROUP)
                im = slice(block + s * GROUP, block + (s + 1) * GROUP)
                lr, li, hr, hi = low[re], low[im], high[re], high[im]
                parts[0].append(lr * near_r - li * near_i)
                parts[1].append(lr * near_i + li * near_2)
                parts[2].append(lr * all_r - li * all_i + hr * near_r - hi * near_i)
                parts[3].append(lr * all_i + li * all_2 + hr * near_i + hi * near_2)
            for j in range(4):
                at, lane = (j % 2) * block + k * GROUP, (j // 2) * lanes
                z_ref[n, at : at + 2 * GROUP, lane : lane + lanes] = jnp.concatenate(
                    parts[j], 0
                ).astype(BF16)
        return jnp.dot(bwd_ref[...], z_ref[n], preferred_element_type=F32)

    def gated(n, conv):
        columns = []
        for base in range(0, lanes, LANES):
            line = [
                mixed(h * rows + r, n * lanes + base)
                * conv[r * GROUP : (r + 1) * GROUP, h * lanes + base : h * lanes + base + LANES]
                for h in range(2)
                for r in range(rows)
            ]
            columns.append(jnp.concatenate(line, 0).astype(BF16))
        return columns

    spectra = []
    for n in range(streams):
        spectra.append(products(n))
        yield
    convs = []
    for n in range(streams):
        convs.append(filtered(n, spectra[n]))
        yield
    final = jnp.dot(
        jnp.concatenate([c for n in range(streams) for c in gated(n, convs[n])], 1),
        w_out_ref[...],
        preferred_element_type=F32,
    )
    yield
    put(final.reshape(2, rows, GROUP, width))


def inner_kernel(
    _, other_ref, other_strip_ref,
    w_in_ref, taps_ref, fwd_ref, bwd_ref, w_out_ref, h_ref,
    p_ref, edge_mixed_ref, out_ref,
    q_ref, mixed_ref, prod_ref, z_ref,
):
    core = lax.axis_index("row")
    rows, cols, width = other_ref.shape
    part = cols // 2
    height = 2 * rows
    start = pl.multiple_of(core * part, part)
    channels = range(0, 3 * width, LANES)
    n_chunk = rows // CHUNK

    def store_in(ref, row0):
        def store(row, at, value):
            place = pl.ds(pl.multiple_of((row0 + row) * GROUP, GROUP), GROUP)
            ref[at.start // LANES, place, :] = value

        return store

    own_at, other_at = core * rows, (1 - core) * rows

    def inner(ref, row0, chunk):
        return depthwise_steps(ref, 1 - core, taps_ref, chunk, store_in(mixed_ref, row0), channels)

    def edge(ref, row0, chunk):
        return depthwise_steps(ref, core, taps_ref, chunk, store_in(edge_mixed_ref, row0), channels)

    for i in range(n_chunk - 1):
        for _ in inner(p_ref, own_at, core + i):
            pass
    project(other_ref[:, pl.ds(start, part), :], other_strip_ref[...], core, w_in_ref, q_ref)
    copy_row(q_ref, 1 + core * (rows - 1), p_ref, (1 - core) * (rows + 1), part)
    copy_row(p_ref, rows - core * (rows - 1), q_ref, core * (rows + 1), part)
    for _ in inner(p_ref, own_at, (1 - core) * (n_chunk - 1)):
        pass

    def inner_chunk(i, carry):
        for _ in inner(q_ref, other_at, i):
            pass
        return carry

    lax.fori_loop(0, n_chunk, inner_chunk, 0)

    def put(final):
        interleave(out_ref, final, 1 - core)

    def edge_all():
        for ref, row0 in ((p_ref, own_at), (q_ref, other_at)):
            for i in range(n_chunk):
                yield from edge(ref, row0, i)

    steps = edge_all()
    conv = conv_steps(
        lambda r, base: mixed_ref[base // LANES, r * GROUP : (r + 1) * GROUP, :],
        fwd_ref, bwd_ref, w_out_ref, h_ref, prod_ref, z_ref, put,
    )
    for _ in conv:
        for _ in range(5):
            next(steps, None)
    for _ in steps:
        pass


def finish_half(half, core, s_ref, mixed_ref, bwd_ref, w_out_ref, h_ref, z_ref, out_ref, to_ref):
    rows, part, width = to_ref.shape
    block = rows * GROUP
    for k in range(0, rows, 2):
        parts = [[], []]
        for s in (k, k + 1):

            def response(j):
                return jnp.broadcast_to(h_ref[half, j, s : s + 1, :], (GROUP, width))

            upper_r, upper_i, lower_r, lower_i = (response(j) for j in (0, 1, 3, 4))
            upper_2, lower_2 = (response(2), response(5)) if s == 0 else (upper_r, lower_r)
            re = slice(s * GROUP, (s + 1) * GROUP)
            im = slice(block + s * GROUP, block + (s + 1) * GROUP)
            lr, hr = s_ref[re, :width], s_ref[re, width:]
            li, hi = s_ref[im, :width], s_ref[im, width:]
            parts[0].append(lr * upper_r - li * upper_i + hr * lower_r - hi * lower_i)
            parts[1].append(lr * upper_i + li * upper_2 + hr * lower_i + hi * lower_2)
        for j in range(2):
            at = j * block + k * GROUP
            z_ref[at : at + 2 * GROUP, :] = jnp.concatenate(parts[j], 0).astype(BF16)
    conv = jnp.dot(bwd_ref[...], z_ref[...], preferred_element_type=F32)
    columns = []
    for t in range(width // LANES):
        line = [
            mixed_ref[t, pl.ds(pl.multiple_of((half * rows + r) * GROUP, GROUP), GROUP), :]
            * conv[r * GROUP : (r + 1) * GROUP, t * LANES : (t + 1) * LANES]
            for r in range(rows)
        ]
        columns.append(jnp.concatenate(line, 0).astype(BF16))
    final = jnp.dot(jnp.concatenate(columns, 1), w_out_ref[...], preferred_element_type=F32)
    for t in range(width // LANES):
        at = slice(t * LANES, (t + 1) * LANES)
        for r in range(rows):
            out_ref[half, t, pl.ds(r * part + core, GROUP, stride=2), :] = final[
                r * GROUP : (r + 1) * GROUP, at
            ]
        to_ref[:, :, at] = out_ref[half, t].reshape(rows, part, LANES).astype(BF16)


def edge_kernel(
    _, __, halo_ref, w_in_ref, taps_ref, fwd_ref, bwd_ref, w_out_ref, h_ref,
    out_ref, mixed_ref, s_ref, send_ref,
    strip_ref, prod_ref, z_ref,
):
    core = lax.axis_index("row")
    rows, part, width = send_ref.shape
    got = jnp.dot(halo_ref[...], w_in_ref[...], preferred_element_type=F32)
    add_edge_terms(
        got[:rows], got[rows:], 1 - core, column_taps(taps_ref, core, 0), strip_ref,
        mixed_ref, core * (GROUP - 1),
    )

    def mixed(r, base):
        return mixed_ref[base // LANES, r * GROUP : (r + 1) * GROUP, :]

    for row in range(0, rows, 2):
        for h in range(2):
            for base in range(0, width, LANES):
                two = [
                    mixed(h * rows + r, width + base) * mixed(h * rows + r, 2 * width + base)
                    for r in (row, row + 1)
                ]
                at = h * width + base
                prod_ref[row * GROUP : (row + 2) * GROUP, at : at + LANES] = jnp.concatenate(
                    two, 0
                ).astype(BF16)
    s_ref[...] = jnp.dot(fwd_ref[...], prod_ref[...], preferred_element_type=F32)
    finish_half(
        1 - core, core, s_ref, mixed_ref, bwd_ref, w_out_ref, h_ref, z_ref, out_ref, send_ref
    )


def own_kernel(
    _, mixed_ref, s_ref, bwd_ref, w_out_ref, h_ref,
    out_ref, mine_ref,
    z_ref,
):
    core = lax.axis_index("row")
    finish_half(core, core, s_ref, mixed_ref, bwd_ref, w_out_ref, h_ref, z_ref, out_ref, mine_ref)


def on_device(image_tokens, w_in, conv_kernel, conv_bias, long_filter, skip_gain, w_out):
    rows, cols, width = image_tokens.shape
    part = cols // 2
    height = 2 * rows
    n_col = lax.axis_size("col")
    core = lax.axis_index("row")
    fwd, bwd, spectra = transforms(rows, GROUP)
    spec_hi = spectra.astype(BF16)
    spec_lo = (spectra - spec_hi.astype(np.float64)).astype(BF16)
    spec = np.stack([spec_hi, spec_lo])
    vmem = pl.BlockSpec(memory_space=pltpu.VMEM)
    hbm = pl.BlockSpec(memory_space=pltpu.HBM)
    shape = jax.ShapeDtypeStruct
    limit = pltpu.CompilerParams(vmem_limit_bytes=24 * 1024 * 1024)

    p_shape = shape((3 * width // LANES, (rows + 2) * PITCH + GROUP, LANES), F32)
    out_shape = shape((2, width // LANES, rows * part, LANES), F32)
    mixed_shape = shape((3 * width // LANES, height * GROUP, LANES), F32)

    swap = [(0, 1), (1, 0)]
    rowmajor = Layout((0, 1, 2))
    on_first = core == 0
    image_tokens, on_first = lax.optimization_barrier((image_tokens, on_first))
    image_tokens = with_layout_constraint(image_tokens, rowmajor)
    other = with_layout_constraint(lax.ppermute(image_tokens, "row", swap), rowmajor)

    def keep(array):
        return pltpu.with_memory_space_constraint(array, pltpu.HBM)

    projected, w_in_v, w_out_v, fwd_v, bwd_v, taps, spectrum, outer = pl.pallas_call(
        prep_kernel,
        out_shape=(
            p_shape,
            shape(w_in.shape, BF16),
            shape(w_out.shape, BF16),
            shape(fwd.shape, BF16),
            shape(bwd.shape, BF16),
            shape((16, 3 * width), F32),
            shape((2, 6, rows, width), F32),
            shape((rows, width), BF16),
        ),
        in_specs=[hbm] * 10,
        out_specs=(vmem,) * 8,
        scratch_shapes=[
            pltpu.VMEM(image_tokens.shape, BF16),
            pltpu.VMEM(spec.shape, BF16),
            pltpu.VMEM(long_filter.shape, BF16),
            pltpu.VMEM((1, width), F32),
            pltpu.VMEM(conv_kernel.shape, BF16),
            pltpu.VMEM(conv_bias.shape, F32),
            pltpu.SemaphoreType.DMA((10,)),
        ],
        compiler_params=limit,
        cost_estimate=pl.CostEstimate(flops=0, bytes_accessed=3 * 1024 * 1024, transcendentals=0),
    )(
        keep(image_tokens), keep(w_in), keep(w_out), keep(fwd.astype(BF16)), keep(bwd.astype(BF16)),
        keep(spec), keep(long_filter), keep(skip_gain[None]), keep(conv_kernel), keep(conv_bias),
    )

    def by_core(low, high):
        return jnp.where(on_first, low, high)

    def column(low):
        return by_core(other[:, low], other[:, cols - 1 - low])

    pairs = []
    for j in range(n_col - 1):
        pairs += [(n_col + j, j + 1), (j + 1, n_col + j)]
    halo = lax.ppermute(jnp.concatenate([outer, column(0)], 0), ("row", "col"), pairs)
    _, edge_mixed, inner = pl.pallas_call(
        inner_kernel,
        out_shape=(p_shape, mixed_shape, out_shape),
        in_specs=[vmem] * 9,
        out_specs=(vmem,) * 3,
        input_output_aliases={0: 0},
        scratch_shapes=[
            pltpu.VMEM(p_shape.shape, F32),
            pltpu.VMEM(mixed_shape.shape, F32),
            pltpu.VMEM((width // LANES, rows * GROUP, 2 * LANES), BF16),
            pltpu.VMEM((width // LANES, 2 * rows * GROUP, 2 * LANES), BF16),
        ],
        compiler_params=limit,
        cost_estimate=pl.CostEstimate(flops=10**9, bytes_accessed=12 * 1024 * 1024, transcendentals=0),
    )(projected, other, column(part), w_in_v, taps, fwd_v, bwd_v, w_out_v, spectrum)
    half_shape = shape((rows, part, width), BF16)
    s_shape = shape((2 * rows * GROUP, 2 * width), F32)
    z_scratch = pltpu.VMEM((2 * rows * GROUP, width), BF16)
    out, edge_mixed, transforms_edge, send = pl.pallas_call(
        edge_kernel,
        out_shape=(out_shape, mixed_shape, s_shape, half_shape),
        in_specs=[vmem] * 9,
        out_specs=(vmem,) * 4,
        input_output_aliases={0: 0, 1: 1},
        scratch_shapes=[
            pltpu.VMEM((3 * width // LANES, 2 * height + 8, LANES), F32),
            pltpu.VMEM((rows * GROUP, 2 * width), BF16),
            z_scratch,
        ],
        compiler_params=limit,
        cost_estimate=pl.CostEstimate(flops=3 * 10**8, bytes_accessed=4 * 1024 * 1024, transcendentals=0),
    )(inner, edge_mixed, halo, w_in_v, taps, fwd_v, bwd_v, w_out_v, spectrum)
    theirs = lax.ppermute(send, "row", swap)
    _, mine = pl.pallas_call(
        own_kernel,
        out_shape=(out_shape, half_shape),
        in_specs=[vmem] * 6,
        out_specs=(vmem,) * 2,
        input_output_aliases={0: 0},
        scratch_shapes=[z_scratch],
        compiler_params=limit,
        cost_estimate=pl.CostEstimate(flops=10**8, bytes_accessed=2 * 1024 * 1024, transcendentals=0),
    )(out, edge_mixed, transforms_edge, bwd_v, w_out_v, spectrum)
    mine, late_core = lax.optimization_barrier((mine, core))
    offset = (1 - late_core) * part
    both = jnp.broadcast_to(mine[:, None], (rows, 2, part, width)).reshape(rows, cols, width)
    zero = jnp.int32(0)
    return lax.dynamic_update_slice_p.bind(both, theirs, zero, offset, zero)


def solution(mesh):
    in_specs = (P("row", "col", None), P(), P(), P(), P(), P(), P())
    out_specs = P("row", "col", None)
    return jax.shard_map(
        on_device, mesh=mesh, in_specs=in_specs, out_specs=out_specs, check_vma=False
    )
```

```python
import jax
import jax.numpy as jnp
import numpy as np
from jax import lax
from jax.experimental import pallas as pl
from jax.experimental.layout import Layout, with_layout_constraint
from jax.experimental.pallas import tpu as pltpu
from jax.sharding import PartitionSpec as P

F32 = jnp.float32
BF16 = jnp.bfloat16


def transforms(half, group):
    size = 2 * half
    slot = np.arange(half)[:, None]
    pos = np.arange(half)[None, :]
    angle = 2 * np.pi * slot * pos / size
    real, imag = np.cos(angle), -np.sin(angle)
    imag[0] = (-1.0) ** np.arange(half)
    forward = np.concatenate([real, imag], 0)
    back_real = 2 * np.cos(angle.T) / size
    back_real[:, 0] = 1 / size
    back_imag = -2 * np.sin(angle.T) / size
    back_imag[:, 0] = (-1.0) ** np.arange(half) / size
    backward = np.concatenate([back_real, back_imag], 1)
    lag = np.arange(size)[None, :]
    angle = 2 * np.pi * slot * lag / size
    real, imag = np.cos(angle), -np.sin(angle)
    imag[0] = 0
    real2 = real.copy()
    real2[0] = (-1.0) ** np.arange(size)
    near = (lag < half).astype(np.float64)
    sign = (-1.0) ** slot
    sign2 = sign.copy()
    sign2[0] = 1
    spectra = np.concatenate(
        [real * near, imag * near, real2 * near, real * sign, imag * sign, real2 * sign2], 0
    )
    eye = np.eye(group)
    return np.kron(forward, eye), np.kron(backward, eye), spectra


LANES = 128
GROUP = 8
CHUNK = 16
PITCH = 24
FIRST = 8


def pick_column(block, column):
    rows, cols, width = block.shape
    shape = (rows, rows * cols)
    place = lax.broadcasted_iota(jnp.int32, shape, 1)
    wanted = lax.broadcasted_iota(jnp.int32, shape, 0) * cols + column
    return jnp.dot(
        jnp.where(place == wanted, 1.0, 0.0).astype(BF16),
        block.reshape(rows * cols, width),
        preferred_element_type=F32,
    ).astype(BF16)


def row_place(row, column):
    return row * PITCH + FIRST + column


def project(tokens, strip, core, w_in_ref, p_ref):
    rows, part, width = tokens.shape
    count = rows * part
    got = jnp.dot(tokens.reshape(count, width), w_in_ref[...], preferred_element_type=F32)
    got_strip = jnp.dot(strip, w_in_ref[...], preferred_element_type=F32)
    for t in range(3 * width // LANES):
        at = slice(t * LANES, (t + 1) * LANES)
        for row in (0, rows + 1):
            place = row * PITCH
            p_ref[t, place : place + PITCH + GROUP, :] = jnp.zeros((PITCH + GROUP, LANES), F32)
        for r in range(rows):
            place = row_place(r + 1, 0)
            p_ref[t, place : place + part, :] = got[r * part : (r + 1) * part, at]
        for r in range(0, rows, GROUP):
            beside = got_strip[r : r + GROUP, at]
            for column, value in (
                (-1, jnp.where(core == 1, beside, 0.0)),
                (part, jnp.where(core == 0, beside, 0.0)),
            ):
                place = row_place(r + 1, column)
                p_ref[t, pl.ds(place, GROUP, stride=PITCH), :] = value


def copy_row(from_ref, from_row, to_ref, to_row, part):
    sub = lax.broadcasted_iota(jnp.int32, (GROUP, LANES), 0)
    for t in range(from_ref.shape[0]):
        for place in range(0, FIRST + part + GROUP, GROUP):
            source = pl.ds(pl.multiple_of(from_row * PITCH + place, GROUP), GROUP)
            target = pl.ds(pl.multiple_of(to_row * PITCH + place, GROUP), GROUP)
            value = from_ref[t, source, :]
            if place < FIRST:
                value = jnp.where(sub == GROUP - 1, value, to_ref[t, target, :])
            elif place >= FIRST + part:
                value = jnp.where(sub == 0, value, to_ref[t, target, :])
            to_ref[t, target, :] = value


def prep_kernel(
    own_hbm, w_in_hbm, w_out_hbm, fwd_hbm, bwd_hbm, spec_hbm, filt_hbm, gain_hbm, kernel_hbm, bias_hbm,
    p_ref, w_in_ref, w_out_ref, fwd_ref, bwd_ref, taps_ref, h_ref, outer_ref,
    own_ref, spec_ref, filt_ref, gain_ref, kernel_ref, bias_ref, sems,
):
    core = lax.axis_index("row")
    rows, cols, width = own_ref.shape
    part = cols // 2
    moves = [
        (own_hbm, own_ref),
        (w_in_hbm, w_in_ref),
        (spec_hbm, spec_ref),
        (filt_hbm, filt_ref),
        (gain_hbm, gain_ref),
        (kernel_hbm, kernel_ref),
        (bias_hbm, bias_ref),
        (fwd_hbm, fwd_ref),
        (bwd_hbm, bwd_ref),
        (w_out_hbm, w_out_ref),
    ]
    copies = [pltpu.make_async_copy(src, dst, sems.at[i]) for i, (src, dst) in enumerate(moves)]
    for copy in copies:
        copy.start()
    copies[0].wait()
    start = pl.multiple_of(core * part, part)
    far = pl.multiple_of((1 - core) * part, part)
    inner_edge = core * (part - 1)
    outer_ref[...] = pick_column(own_ref[:, pl.ds(start, part), :], inner_edge)
    beside = pick_column(own_ref[:, pl.ds(far, part), :], inner_edge)
    for copy in copies[1:7]:
        copy.wait()
    project(own_ref[:, pl.ds(start, part), :], beside, core, w_in_ref, p_ref)
    filt = filt_ref[...]
    gain = gain_ref[...]
    spectrum = jnp.dot(spec_ref[0], filt, preferred_element_type=F32) + jnp.dot(
        spec_ref[1], filt, preferred_element_type=F32
    )
    pieces = [spectrum[j * rows : (j + 1) * rows] for j in range(6)]
    near = [pieces[0] + gain, pieces[1], pieces[2] + gain]
    for j in range(3):
        h_ref[0, j] = near[j]
        h_ref[0, 3 + j] = jnp.zeros((rows, width), F32)
        h_ref[1, j] = pieces[3 + j]
        h_ref[1, 3 + j] = near[j]
    for a in range(3):
        taps_ref[3 * a : 3 * a + 3, :] = kernel_ref[a].astype(F32)
    taps_ref[9, :] = bias_ref[...]
    for copy in copies[7:]:
        copy.wait()


def add_edge_terms(first, second, core, taps, edge_ref, mixed_ref, column):
    rows, channels = first.shape
    for t in range(channels // LANES):
        at = slice(t * LANES, (t + 1) * LANES)
        edge_ref[t, 0:8, :] = jnp.zeros((8, LANES), F32)
        edge_ref[t, 4 * rows : 4 * rows + 8, :] = jnp.zeros((8, LANES), F32)
        for r in range(0, rows, 8):
            for row, half in ((core * rows, first), ((1 - core) * rows, second)):
                place = pl.ds(2 * (row + r + 1), 8, stride=2)
                edge_ref[t, place, :] = half[r : r + 8, at]
        for r in range(0, 2 * rows, 8):
            place = pl.ds(r * GROUP + column, 8, stride=GROUP)
            total = mixed_ref[t, place, :]
            for a in range(3):
                total = total + edge_ref[t, pl.ds(2 * (r + a), 8, stride=2), :] * taps[a][:, at]
            mixed_ref[t, place, :] = total


def column_taps(taps_ref, core, on_core0):
    first, second = on_core0, 2 - on_core0
    return [
        jnp.where(
            core == 0,
            taps_ref[3 * a + first : 3 * a + first + 1, :],
            taps_ref[3 * a + second : 3 * a + second + 1, :],
        )
        for a in range(3)
    ]


def depthwise_steps(p_ref, first, taps_ref, chunk, store, bases):
    for base in bases:
        at = slice(base, base + LANES)
        tap = [
            jnp.broadcast_to(taps_ref[k : k + 1, at], (GROUP, LANES)) for k in range(10)
        ]
        loaded = [
            [
                p_ref[
                    base // LANES,
                    pl.ds(row_place(chunk * CHUNK + r, first + b - 1), GROUP, stride=2),
                    :,
                ]
                for b in range(3)
            ]
            for r in range(CHUNK + 2)
        ]
        for r in range(CHUNK):
            value = tap[9]
            for a in range(3):
                row = loaded[r + a]
                value = value + (
                    row[0] * tap[3 * a] + row[1] * tap[3 * a + 1] + row[2] * tap[3 * a + 2]
                )
            store(chunk * CHUNK + r, at, value)
        yield


def interleave(out_ref, final, first):
    _, rows, _, width = final.shape
    for h in range(2):
        for t in range(width // LANES):
            for r in range(rows):
                out_ref[h, t, pl.ds(r * 2 * GROUP + first, GROUP, stride=2), :] = final[
                    h, r, :, t * LANES : (t + 1) * LANES
                ]


def conv_steps(mixed, fwd_ref, bwd_ref, w_out_ref, h_ref, prod_ref, z_ref, put):
    streams, block, lanes = prod_ref.shape
    lanes = lanes // 2
    rows = block // GROUP
    width = streams * lanes

    def products(n):
        for row in range(0, rows, 2):
            for h in range(2):
                for base in range(n * lanes, (n + 1) * lanes, LANES):
                    two = [
                        mixed(h * rows + r, width + base) * mixed(h * rows + r, 2 * width + base)
                        for r in (row, row + 1)
                    ]
                    at = h * lanes + base - n * lanes
                    prod_ref[n, row * GROUP : (row + 2) * GROUP, at : at + LANES] = (
                        jnp.concatenate(two, 0).astype(BF16)
                    )
        return jnp.dot(fwd_ref[...], prod_ref[n], preferred_element_type=F32)

    def filtered(n, spectra):
        channels = slice(n * lanes, (n + 1) * lanes)
        low, high = spectra[:, :lanes], spectra[:, lanes:]

        def response(j, s):
            return jnp.broadcast_to(h_ref[j // 3, j % 3, s : s + 1, channels], (GROUP, lanes))

        for k in range(0, rows, 2):
            parts = [[], [], [], []]
            for s in (k, k + 1):
                near_r, near_i = response(0, s), response(1, s)
                all_r, all_i = response(3, s), response(4, s)
                near_2, all_2 = (response(2, s), response(5, s)) if s == 0 else (near_r, all_r)
                re = slice(s * GROUP, (s + 1) * GROUP)
                im = slice(block + s * GROUP, block + (s + 1) * GROUP)
                lr, li, hr, hi = low[re], low[im], high[re], high[im]
                parts[0].append(lr * near_r - li * near_i)
                parts[1].append(lr * near_i + li * near_2)
                parts[2].append(lr * all_r - li * all_i + hr * near_r - hi * near_i)
                parts[3].append(lr * all_i + li * all_2 + hr * near_i + hi * near_2)
            for j in range(4):
                at, lane = (j % 2) * block + k * GROUP, (j // 2) * lanes
                z_ref[n, at : at + 2 * GROUP, lane : lane + lanes] = jnp.concatenate(
                    parts[j], 0
                ).astype(BF16)
        return jnp.dot(bwd_ref[...], z_ref[n], preferred_element_type=F32)

    def gated(n, conv):
        columns = []
        for base in range(0, lanes, LANES):
            line = [
                mixed(h * rows + r, n * lanes + base)
                * conv[r * GROUP : (r + 1) * GROUP, h * lanes + base : h * lanes + base + LANES]
                for h in range(2)
                for r in range(rows)
            ]
            columns.append(jnp.concatenate(line, 0).astype(BF16))
        return columns

    spectra = []
    for n in range(streams):
        spectra.append(products(n))
        yield
    convs = []
    for n in range(streams):
        convs.append(filtered(n, spectra[n]))
        yield
    final = jnp.dot(
        jnp.concatenate([c for n in range(streams) for c in gated(n, convs[n])], 1),
        w_out_ref[...],
        preferred_element_type=F32,
    )
    yield
    put(final.reshape(2, rows, GROUP, width))


def inner_kernel(
    _, other_ref, other_strip_ref,
    w_in_ref, taps_ref, fwd_ref, bwd_ref, w_out_ref, h_ref,
    p_ref, edge_mixed_ref, out_ref,
    q_ref, mixed_ref, prod_ref, z_ref,
):
    core = lax.axis_index("row")
    rows, cols, width = other_ref.shape
    part = cols // 2
    height = 2 * rows
    start = pl.multiple_of(core * part, part)
    channels = range(0, 3 * width, LANES)
    n_chunk = rows // CHUNK

    def store_in(ref, row0):
        def store(row, at, value):
            place = pl.ds(pl.multiple_of((row0 + row) * GROUP, GROUP), GROUP)
            ref[at.start // LANES, place, :] = value

        return store

    own_at, other_at = core * rows, (1 - core) * rows

    def inner(ref, row0, chunk):
        return depthwise_steps(ref, 1 - core, taps_ref, chunk, store_in(mixed_ref, row0), channels)

    def edge(ref, row0, chunk):
        return depthwise_steps(ref, core, taps_ref, chunk, store_in(edge_mixed_ref, row0), channels)

    for i in range(n_chunk - 1):
        for _ in inner(p_ref, own_at, core + i):
            pass
    project(other_ref[:, pl.ds(start, part), :], other_strip_ref[...], core, w_in_ref, q_ref)
    copy_row(q_ref, 1 + core * (rows - 1), p_ref, (1 - core) * (rows + 1), part)
    copy_row(p_ref, rows - core * (rows - 1), q_ref, core * (rows + 1), part)
    for _ in inner(p_ref, own_at, (1 - core) * (n_chunk - 1)):
        pass

    def inner_chunk(i, carry):
        for _ in inner(q_ref, other_at, i):
            pass
        return carry

    lax.fori_loop(0, n_chunk, inner_chunk, 0)

    def put(final):
        interleave(out_ref, final, 1 - core)

    def edge_all():
        for ref, row0 in ((p_ref, own_at), (q_ref, other_at)):
            for i in range(n_chunk):
                yield from edge(ref, row0, i)

    steps = edge_all()
    conv = conv_steps(
        lambda r, base: mixed_ref[base // LANES, r * GROUP : (r + 1) * GROUP, :],
        fwd_ref, bwd_ref, w_out_ref, h_ref, prod_ref, z_ref, put,
    )
    for _ in conv:
        for _ in range(5):
            next(steps, None)
    for _ in steps:
        pass


def inverse_half(half, s_ref, bwd_ref, h_ref, z_ref):
    rows, width = h_ref.shape[2:]
    block = rows * GROUP
    for k in range(0, rows, 2):
        parts = [[], []]
        for s in (k, k + 1):

            def response(j):
                return jnp.broadcast_to(h_ref[half, j, s : s + 1, :], (GROUP, width))

            upper_r, upper_i, lower_r, lower_i = (response(j) for j in (0, 1, 3, 4))
            upper_2, lower_2 = (response(2), response(5)) if s == 0 else (upper_r, lower_r)
            re = slice(s * GROUP, (s + 1) * GROUP)
            im = slice(block + s * GROUP, block + (s + 1) * GROUP)
            lr, hr = s_ref[re, :width], s_ref[re, width:]
            li, hi = s_ref[im, :width], s_ref[im, width:]
            parts[0].append(lr * upper_r - li * upper_i + hr * lower_r - hi * lower_i)
            parts[1].append(lr * upper_i + li * upper_2 + hr * lower_i + hi * lower_2)
        for j in range(2):
            at = j * block + k * GROUP
            z_ref[at : at + 2 * GROUP, :] = jnp.concatenate(parts[j], 0).astype(BF16)
    return jnp.dot(bwd_ref[...], z_ref[...], preferred_element_type=F32)


def finish_half(half, core, conv, mixed_ref, w_out_ref, out_ref, to_ref):
    rows, part, width = to_ref.shape
    columns = []
    for t in range(width // LANES):
        line = [
            mixed_ref[t, pl.ds(pl.multiple_of((half * rows + r) * GROUP, GROUP), GROUP), :]
            * conv[r * GROUP : (r + 1) * GROUP, t * LANES : (t + 1) * LANES]
            for r in range(rows)
        ]
        columns.append(jnp.concatenate(line, 0).astype(BF16))
    final = jnp.dot(jnp.concatenate(columns, 1), w_out_ref[...], preferred_element_type=F32)
    for t in range(width // LANES):
        at = slice(t * LANES, (t + 1) * LANES)
        for r in range(rows):
            out_ref[half, t, pl.ds(r * part + core, GROUP, stride=2), :] = final[
                r * GROUP : (r + 1) * GROUP, at
            ]
        to_ref[:, :, at] = out_ref[half, t].reshape(rows, part, LANES).astype(BF16)


def edge_kernel(
    _, __, halo_ref, w_in_ref, taps_ref, fwd_ref, bwd_ref, w_out_ref, h_ref,
    out_ref, mixed_ref, own_conv_ref, send_ref,
    strip_ref, prod_ref, s_ref, z_ref, own_z_ref,
):
    core = lax.axis_index("row")
    rows, part, width = send_ref.shape
    got = jnp.dot(halo_ref[...], w_in_ref[...], preferred_element_type=F32)
    add_edge_terms(
        got[:rows], got[rows:], 1 - core, column_taps(taps_ref, core, 0), strip_ref,
        mixed_ref, core * (GROUP - 1),
    )

    def mixed(r, base):
        return mixed_ref[base // LANES, r * GROUP : (r + 1) * GROUP, :]

    for row in range(0, rows, 2):
        for h in range(2):
            for base in range(0, width, LANES):
                two = [
                    mixed(h * rows + r, width + base) * mixed(h * rows + r, 2 * width + base)
                    for r in (row, row + 1)
                ]
                at = h * width + base
                prod_ref[row * GROUP : (row + 2) * GROUP, at : at + LANES] = jnp.concatenate(
                    two, 0
                ).astype(BF16)
    s_ref[...] = jnp.dot(fwd_ref[...], prod_ref[...], preferred_element_type=F32)
    conv = inverse_half(1 - core, s_ref, bwd_ref, h_ref, z_ref)
    own_conv_ref[...] = inverse_half(core, s_ref, bwd_ref, h_ref, own_z_ref)
    finish_half(1 - core, core, conv, mixed_ref, w_out_ref, out_ref, send_ref)


def own_kernel(_, mixed_ref, conv_ref, w_out_ref, out_ref, mine_ref):
    core = lax.axis_index("row")
    finish_half(core, core, conv_ref, mixed_ref, w_out_ref, out_ref, mine_ref)


def on_device(image_tokens, w_in, conv_kernel, conv_bias, long_filter, skip_gain, w_out):
    rows, cols, width = image_tokens.shape
    part = cols // 2
    height = 2 * rows
    n_col = lax.axis_size("col")
    core = lax.axis_index("row")
    fwd, bwd, spectra = transforms(rows, GROUP)
    spec_hi = spectra.astype(BF16)
    spec_lo = (spectra - spec_hi.astype(np.float64)).astype(BF16)
    spec = np.stack([spec_hi, spec_lo])
    vmem = pl.BlockSpec(memory_space=pltpu.VMEM)
    hbm = pl.BlockSpec(memory_space=pltpu.HBM)
    shape = jax.ShapeDtypeStruct
    limit = pltpu.CompilerParams(vmem_limit_bytes=24 * 1024 * 1024)

    p_shape = shape((3 * width // LANES, (rows + 2) * PITCH + GROUP, LANES), F32)
    out_shape = shape((2, width // LANES, rows * part, LANES), F32)
    mixed_shape = shape((3 * width // LANES, height * GROUP, LANES), F32)

    swap = [(0, 1), (1, 0)]
    rowmajor = Layout((0, 1, 2))
    on_first = core == 0
    image_tokens, on_first = lax.optimization_barrier((image_tokens, on_first))
    image_tokens = with_layout_constraint(image_tokens, rowmajor)
    other = with_layout_constraint(lax.ppermute(image_tokens, "row", swap), rowmajor)

    def keep(array):
        return pltpu.with_memory_space_constraint(array, pltpu.HBM)

    projected, w_in_v, w_out_v, fwd_v, bwd_v, taps, spectrum, outer = pl.pallas_call(
        prep_kernel,
        out_shape=(
            p_shape,
            shape(w_in.shape, BF16),
            shape(w_out.shape, BF16),
            shape(fwd.shape, BF16),
            shape(bwd.shape, BF16),
            shape((16, 3 * width), F32),
            shape((2, 6, rows, width), F32),
            shape((rows, width), BF16),
        ),
        in_specs=[hbm] * 10,
        out_specs=(vmem,) * 8,
        scratch_shapes=[
            pltpu.VMEM(image_tokens.shape, BF16),
            pltpu.VMEM(spec.shape, BF16),
            pltpu.VMEM(long_filter.shape, BF16),
            pltpu.VMEM((1, width), F32),
            pltpu.VMEM(conv_kernel.shape, BF16),
            pltpu.VMEM(conv_bias.shape, F32),
            pltpu.SemaphoreType.DMA((10,)),
        ],
        compiler_params=limit,
        cost_estimate=pl.CostEstimate(flops=0, bytes_accessed=3 * 1024 * 1024, transcendentals=0),
    )(
        keep(image_tokens), keep(w_in), keep(w_out), keep(fwd.astype(BF16)), keep(bwd.astype(BF16)),
        keep(spec), keep(long_filter), keep(skip_gain[None]), keep(conv_kernel), keep(conv_bias),
    )

    def by_core(low, high):
        return jnp.where(on_first, low, high)

    def column(low):
        return by_core(other[:, low], other[:, cols - 1 - low])

    pairs = []
    for j in range(n_col - 1):
        pairs += [(n_col + j, j + 1), (j + 1, n_col + j)]
    halo = lax.ppermute(jnp.concatenate([outer, column(0)], 0), ("row", "col"), pairs)
    _, edge_mixed, inner = pl.pallas_call(
        inner_kernel,
        out_shape=(p_shape, mixed_shape, out_shape),
        in_specs=[vmem] * 9,
        out_specs=(vmem,) * 3,
        input_output_aliases={0: 0},
        scratch_shapes=[
            pltpu.VMEM(p_shape.shape, F32),
            pltpu.VMEM(mixed_shape.shape, F32),
            pltpu.VMEM((width // LANES, rows * GROUP, 2 * LANES), BF16),
            pltpu.VMEM((width // LANES, 2 * rows * GROUP, 2 * LANES), BF16),
        ],
        compiler_params=limit,
        cost_estimate=pl.CostEstimate(flops=10**9, bytes_accessed=12 * 1024 * 1024, transcendentals=0),
    )(projected, other, column(part), w_in_v, taps, fwd_v, bwd_v, w_out_v, spectrum)
    half_shape = shape((rows, part, width), BF16)
    conv_shape = shape((rows * GROUP, width), F32)
    z_scratch = pltpu.VMEM((2 * rows * GROUP, width), BF16)
    out, edge_mixed, own_conv, send = pl.pallas_call(
        edge_kernel,
        out_shape=(out_shape, mixed_shape, conv_shape, half_shape),
        in_specs=[vmem] * 9,
        out_specs=(vmem,) * 4,
        input_output_aliases={0: 0, 1: 1},
        scratch_shapes=[
            pltpu.VMEM((3 * width // LANES, 2 * height + 8, LANES), F32),
            pltpu.VMEM((rows * GROUP, 2 * width), BF16),
            pltpu.VMEM((2 * rows * GROUP, 2 * width), F32),
            z_scratch,
            z_scratch,
        ],
        compiler_params=limit,
        cost_estimate=pl.CostEstimate(flops=3 * 10**8, bytes_accessed=4 * 1024 * 1024, transcendentals=0),
    )(inner, edge_mixed, halo, w_in_v, taps, fwd_v, bwd_v, w_out_v, spectrum)
    theirs = lax.ppermute(send, "row", swap)
    _, mine = pl.pallas_call(
        own_kernel,
        out_shape=(out_shape, half_shape),
        in_specs=[vmem] * 4,
        out_specs=(vmem,) * 2,
        input_output_aliases={0: 0},
        compiler_params=limit,
        cost_estimate=pl.CostEstimate(flops=10**8, bytes_accessed=2 * 1024 * 1024, transcendentals=0),
    )(out, edge_mixed, own_conv, w_out_v)
    mine, late_core = lax.optimization_barrier((mine, core))
    offset = (1 - late_core) * part
    both = jnp.concatenate([mine, mine], 1)
    zero = jnp.int32(0)
    return lax.dynamic_update_slice_p.bind(both, theirs, zero, offset, zero)


def solution(mesh):
    in_specs = (P("row", "col", None), P(), P(), P(), P(), P(), P())
    out_specs = P("row", "col", None)
    return jax.shard_map(
        on_device, mesh=mesh, in_specs=in_specs, out_specs=out_specs, check_vma=False
    )
```

```python
import jax
import jax.numpy as jnp
import numpy as np
from jax import lax
from jax.experimental import pallas as pl
from jax.experimental.layout import Layout, with_layout_constraint
from jax.experimental.pallas import tpu as pltpu
from jax.sharding import PartitionSpec as P

F32 = jnp.float32
BF16 = jnp.bfloat16


def transforms(half, group):
    size = 2 * half
    slot = np.arange(half)[:, None]
    pos = np.arange(half)[None, :]
    angle = 2 * np.pi * slot * pos / size
    real, imag = np.cos(angle), -np.sin(angle)
    imag[0] = (-1.0) ** np.arange(half)
    forward = np.concatenate([real, imag], 0)
    back_real = 2 * np.cos(angle.T) / size
    back_real[:, 0] = 1 / size
    back_imag = -2 * np.sin(angle.T) / size
    back_imag[:, 0] = (-1.0) ** np.arange(half) / size
    backward = np.concatenate([back_real, back_imag], 1)
    lag = np.arange(size)[None, :]
    angle = 2 * np.pi * slot * lag / size
    real, imag = np.cos(angle), -np.sin(angle)
    imag[0] = 0
    real2 = real.copy()
    real2[0] = (-1.0) ** np.arange(size)
    near = (lag < half).astype(np.float64)
    sign = (-1.0) ** slot
    sign2 = sign.copy()
    sign2[0] = 1
    spectra = np.concatenate(
        [real * near, imag * near, real2 * near, real * sign, imag * sign, real2 * sign2], 0
    )
    eye = np.eye(group)
    return np.kron(forward, eye), np.kron(backward, eye), spectra


LANES = 128
GROUP = 8
CHUNK = 16
PITCH = 24
FIRST = 8


def pick_column(block, column):
    rows, cols, width = block.shape
    shape = (rows, rows * cols)
    place = lax.broadcasted_iota(jnp.int32, shape, 1)
    wanted = lax.broadcasted_iota(jnp.int32, shape, 0) * cols + column
    return jnp.dot(
        jnp.where(place == wanted, 1.0, 0.0).astype(BF16),
        block.reshape(rows * cols, width),
        preferred_element_type=F32,
    ).astype(BF16)


def row_place(row, column):
    return row * PITCH + FIRST + column


def project(tokens, strip, core, w_in_ref, p_ref):
    rows, part, width = tokens.shape
    count = rows * part
    got = jnp.dot(tokens.reshape(count, width), w_in_ref[...], preferred_element_type=F32)
    got_strip = jnp.dot(strip, w_in_ref[...], preferred_element_type=F32)
    for t in range(3 * width // LANES):
        at = slice(t * LANES, (t + 1) * LANES)
        for row in (0, rows + 1):
            place = row * PITCH
            p_ref[t, place : place + PITCH + GROUP, :] = jnp.zeros((PITCH + GROUP, LANES), F32)
        for r in range(rows):
            place = row_place(r + 1, 0)
            p_ref[t, place : place + part, :] = got[r * part : (r + 1) * part, at]
        for r in range(0, rows, GROUP):
            beside = got_strip[r : r + GROUP, at]
            for column, value in (
                (-1, jnp.where(core == 1, beside, 0.0)),
                (part, jnp.where(core == 0, beside, 0.0)),
            ):
                place = row_place(r + 1, column)
                p_ref[t, pl.ds(place, GROUP, stride=PITCH), :] = value


def copy_row(from_ref, from_row, to_ref, to_row, part):
    sub = lax.broadcasted_iota(jnp.int32, (GROUP, LANES), 0)
    for t in range(from_ref.shape[0]):
        for place in range(0, FIRST + part + GROUP, GROUP):
            source = pl.ds(pl.multiple_of(from_row * PITCH + place, GROUP), GROUP)
            target = pl.ds(pl.multiple_of(to_row * PITCH + place, GROUP), GROUP)
            value = from_ref[t, source, :]
            if place < FIRST:
                value = jnp.where(sub == GROUP - 1, value, to_ref[t, target, :])
            elif place >= FIRST + part:
                value = jnp.where(sub == 0, value, to_ref[t, target, :])
            to_ref[t, target, :] = value


def prep_kernel(
    own_hbm, w_in_hbm, w_out_hbm, fwd_hbm, bwd_hbm, spec_hbm, filt_hbm, gain_hbm, kernel_hbm, bias_hbm,
    p_ref, w_in_ref, w_out_ref, fwd_ref, bwd_ref, taps_ref, h_ref, outer_ref,
    own_ref, spec_ref, filt_ref, gain_ref, kernel_ref, bias_ref, sems,
):
    core = lax.axis_index("row")
    rows, cols, width = own_ref.shape
    part = cols // 2
    moves = [
        (own_hbm, own_ref),
        (w_in_hbm, w_in_ref),
        (spec_hbm, spec_ref),
        (filt_hbm, filt_ref),
        (gain_hbm, gain_ref),
        (kernel_hbm, kernel_ref),
        (bias_hbm, bias_ref),
        (fwd_hbm, fwd_ref),
        (bwd_hbm, bwd_ref),
        (w_out_hbm, w_out_ref),
    ]
    copies = [pltpu.make_async_copy(src, dst, sems.at[i]) for i, (src, dst) in enumerate(moves)]
    for copy in copies:
        copy.start()
    copies[0].wait()
    start = pl.multiple_of(core * part, part)
    far = pl.multiple_of((1 - core) * part, part)
    inner_edge = core * (part - 1)
    outer_ref[...] = pick_column(own_ref[:, pl.ds(start, part), :], inner_edge)
    beside = pick_column(own_ref[:, pl.ds(far, part), :], inner_edge)
    for copy in copies[1:7]:
        copy.wait()
    project(own_ref[:, pl.ds(start, part), :], beside, core, w_in_ref, p_ref)
    filt = filt_ref[...]
    gain = gain_ref[...]
    spectrum = jnp.dot(spec_ref[0], filt, preferred_element_type=F32) + jnp.dot(
        spec_ref[1], filt, preferred_element_type=F32
    )
    for j in range(6):
        part_j = spectrum[j * rows : (j + 1) * rows]
        h_ref[j * rows : (j + 1) * rows, :] = part_j + gain if j in (0, 2) else part_j
    for a in range(3):
        taps_ref[3 * a : 3 * a + 3, :] = kernel_ref[a].astype(F32)
    taps_ref[9, :] = bias_ref[...]
    for copy in copies[7:]:
        copy.wait()


def add_edge_terms(first, second, core, taps, edge_ref, mixed_ref, column):
    rows, channels = first.shape
    for t in range(channels // LANES):
        at = slice(t * LANES, (t + 1) * LANES)
        edge_ref[t, 0:8, :] = jnp.zeros((8, LANES), F32)
        edge_ref[t, 4 * rows : 4 * rows + 8, :] = jnp.zeros((8, LANES), F32)
        for r in range(0, rows, 8):
            for row, half in ((core * rows, first), ((1 - core) * rows, second)):
                place = pl.ds(2 * (row + r + 1), 8, stride=2)
                edge_ref[t, place, :] = half[r : r + 8, at]
        for r in range(0, 2 * rows, 8):
            place = pl.ds(r * GROUP + column, 8, stride=GROUP)
            total = mixed_ref[t, place, :]
            for a in range(3):
                total = total + edge_ref[t, pl.ds(2 * (r + a), 8, stride=2), :] * taps[a][:, at]
            mixed_ref[t, place, :] = total


def column_taps(taps_ref, core, on_core0):
    first, second = on_core0, 2 - on_core0
    return [
        jnp.where(
            core == 0,
            taps_ref[3 * a + first : 3 * a + first + 1, :],
            taps_ref[3 * a + second : 3 * a + second + 1, :],
        )
        for a in range(3)
    ]


def depthwise_steps(p_ref, first, taps_ref, chunk, store, bases):
    for base in bases:
        at = slice(base, base + LANES)
        tap = [
            jnp.broadcast_to(taps_ref[k : k + 1, at], (GROUP, LANES)) for k in range(10)
        ]
        loaded = [
            [
                p_ref[
                    base // LANES,
                    pl.ds(row_place(chunk * CHUNK + r, first + b - 1), GROUP, stride=2),
                    :,
                ]
                for b in range(3)
            ]
            for r in range(CHUNK + 2)
        ]
        for r in range(CHUNK):
            value = tap[9]
            for a in range(3):
                row = loaded[r + a]
                value = value + (
                    row[0] * tap[3 * a] + row[1] * tap[3 * a + 1] + row[2] * tap[3 * a + 2]
                )
            store(chunk * CHUNK + r, at, value)
        yield


def interleave(out_ref, final, first):
    _, rows, _, width = final.shape
    for h in range(2):
        for t in range(width // LANES):
            for r in range(rows):
                out_ref[h, t, pl.ds(r * 2 * GROUP + first, GROUP, stride=2), :] = final[
                    h, r, :, t * LANES : (t + 1) * LANES
                ]


def conv_steps(mixed, fwd_ref, bwd_ref, w_out_ref, h_ref, prod_ref, z_ref, put):
    streams, block, lanes = prod_ref.shape
    lanes = lanes // 2
    rows = block // GROUP
    width = streams * lanes

    def products(n):
        for row in range(0, rows, 2):
            for h in range(2):
                for base in range(n * lanes, (n + 1) * lanes, LANES):
                    two = [
                        mixed(h * rows + r, width + base) * mixed(h * rows + r, 2 * width + base)
                        for r in (row, row + 1)
                    ]
                    at = h * lanes + base - n * lanes
                    prod_ref[n, row * GROUP : (row + 2) * GROUP, at : at + LANES] = (
                        jnp.concatenate(two, 0).astype(BF16)
                    )
        return jnp.dot(fwd_ref[...], prod_ref[n], preferred_element_type=F32)

    def filtered(n, spectra):
        channels = slice(n * lanes, (n + 1) * lanes)
        low, high = spectra[:, :lanes], spectra[:, lanes:]

        def response(j, s):
            place = j * rows + s
            return jnp.broadcast_to(h_ref[place : place + 1, channels], (GROUP, lanes))

        for k in range(0, rows, 2):
            parts = [[], [], [], []]
            for s in (k, k + 1):
                near_r, near_i = response(0, s), response(1, s)
                all_r, all_i = response(3, s), response(4, s)
                near_2, all_2 = (response(2, s), response(5, s)) if s == 0 else (near_r, all_r)
                re = slice(s * GROUP, (s + 1) * GROUP)
                im = slice(block + s * GROUP, block + (s + 1) * GROUP)
                lr, li, hr, hi = low[re], low[im], high[re], high[im]
                parts[0].append(lr * near_r - li * near_i)
                parts[1].append(lr * near_i + li * near_2)
                parts[2].append(lr * all_r - li * all_i + hr * near_r - hi * near_i)
                parts[3].append(lr * all_i + li * all_2 + hr * near_i + hi * near_2)
            for j in range(4):
                at, lane = (j % 2) * block + k * GROUP, (j // 2) * lanes
                z_ref[n, at : at + 2 * GROUP, lane : lane + lanes] = jnp.concatenate(
                    parts[j], 0
                ).astype(BF16)
        return jnp.dot(bwd_ref[...], z_ref[n], preferred_element_type=F32)

    def gated(n, conv):
        columns = []
        for base in range(0, lanes, LANES):
            line = [
                mixed(h * rows + r, n * lanes + base)
                * conv[r * GROUP : (r + 1) * GROUP, h * lanes + base : h * lanes + base + LANES]
                for h in range(2)
                for r in range(rows)
            ]
            columns.append(jnp.concatenate(line, 0).astype(BF16))
        return columns

    spectra = []
    for n in range(streams):
        spectra.append(products(n))
        yield
    convs = []
    for n in range(streams):
        convs.append(filtered(n, spectra[n]))
        yield
    final = jnp.dot(
        jnp.concatenate([c for n in range(streams) for c in gated(n, convs[n])], 1),
        w_out_ref[...],
        preferred_element_type=F32,
    )
    yield
    put(final.reshape(2, rows, GROUP, width))


def inner_kernel(
    _, other_ref, other_strip_ref,
    w_in_ref, taps_ref, fwd_ref, bwd_ref, w_out_ref, h_ref,
    p_ref, edge_mixed_ref, out_ref,
    q_ref, mixed_ref, prod_ref, z_ref,
):
    core = lax.axis_index("row")
    rows, cols, width = other_ref.shape
    part = cols // 2
    height = 2 * rows
    start = pl.multiple_of(core * part, part)
    channels = range(0, 3 * width, LANES)
    n_chunk = rows // CHUNK

    def store_in(ref, row0):
        def store(row, at, value):
            place = pl.ds(pl.multiple_of((row0 + row) * GROUP, GROUP), GROUP)
            ref[at.start // LANES, place, :] = value

        return store

    own_at, other_at = core * rows, (1 - core) * rows

    def inner(ref, row0, chunk):
        return depthwise_steps(ref, 1 - core, taps_ref, chunk, store_in(mixed_ref, row0), channels)

    def edge(ref, row0, chunk):
        return depthwise_steps(ref, core, taps_ref, chunk, store_in(edge_mixed_ref, row0), channels)

    for i in range(n_chunk - 1):
        for _ in inner(p_ref, own_at, core + i):
            pass
    project(other_ref[:, pl.ds(start, part), :], other_strip_ref[...], core, w_in_ref, q_ref)
    copy_row(q_ref, 1 + core * (rows - 1), p_ref, (1 - core) * (rows + 1), part)
    copy_row(p_ref, rows - core * (rows - 1), q_ref, core * (rows + 1), part)
    for _ in inner(p_ref, own_at, (1 - core) * (n_chunk - 1)):
        pass

    def inner_chunk(i, carry):
        for _ in inner(q_ref, other_at, i):
            pass
        return carry

    lax.fori_loop(0, n_chunk, inner_chunk, 0)

    def put(final):
        interleave(out_ref, final, 1 - core)

    def edge_all():
        for ref, row0 in ((p_ref, own_at), (q_ref, other_at)):
            for i in range(n_chunk):
                yield from edge(ref, row0, i)

    steps = edge_all()
    conv = conv_steps(
        lambda r, base: mixed_ref[base // LANES, r * GROUP : (r + 1) * GROUP, :],
        fwd_ref, bwd_ref, w_out_ref, h_ref, prod_ref, z_ref, put,
    )
    for _ in conv:
        for _ in range(8):
            next(steps, None)
    for _ in steps:
        pass


def edge_kernel(
    _, __, halo_ref, w_in_ref, taps_ref, fwd_ref, bwd_ref, w_out_ref, h_ref,
    out_ref, mixed_ref, mine_ref, send_ref,
    strip_ref, prod_ref, z_ref,
):
    core = lax.axis_index("row")
    rows, part, width = mine_ref.shape
    got = jnp.dot(halo_ref[...], w_in_ref[...], preferred_element_type=F32)
    add_edge_terms(
        got[:rows], got[rows:], 1 - core, column_taps(taps_ref, core, 0), strip_ref,
        mixed_ref, core * (GROUP - 1),
    )

    def mixed(r, base):
        return mixed_ref[base // LANES, r * GROUP : (r + 1) * GROUP, :]

    def put(final):
        interleave(out_ref, final, core)

    for _ in conv_steps(
        mixed, fwd_ref, bwd_ref, w_out_ref, h_ref, prod_ref, z_ref, put
    ):
        pass
    for ref, half in ((mine_ref, core), (send_ref, 1 - core)):
        for t in range(width // LANES):
            ref[:, :, t * LANES : (t + 1) * LANES] = (
                out_ref[half, t].reshape(rows, part, LANES).astype(BF16)
            )


def on_device(image_tokens, w_in, conv_kernel, conv_bias, long_filter, skip_gain, w_out):
    rows, cols, width = image_tokens.shape
    part = cols // 2
    height = 2 * rows
    n_col = lax.axis_size("col")
    core = lax.axis_index("row")
    fwd, bwd, spectra = transforms(rows, GROUP)
    spec_hi = spectra.astype(BF16)
    spec_lo = (spectra - spec_hi.astype(np.float64)).astype(BF16)
    spec = np.stack([spec_hi, spec_lo])
    vmem = pl.BlockSpec(memory_space=pltpu.VMEM)
    hbm = pl.BlockSpec(memory_space=pltpu.HBM)
    shape = jax.ShapeDtypeStruct
    limit = pltpu.CompilerParams(vmem_limit_bytes=24 * 1024 * 1024)

    p_shape = shape((3 * width // LANES, (rows + 2) * PITCH + GROUP, LANES), F32)
    out_shape = shape((2, width // LANES, rows * part, LANES), F32)
    mixed_shape = shape((3 * width // LANES, height * GROUP, LANES), F32)

    swap = [(0, 1), (1, 0)]
    rowmajor = Layout((0, 1, 2))
    image_tokens = with_layout_constraint(image_tokens, rowmajor)
    other = with_layout_constraint(lax.ppermute(image_tokens, "row", swap), rowmajor)

    def keep(array):
        return pltpu.with_memory_space_constraint(array, pltpu.HBM)

    projected, w_in_v, w_out_v, fwd_v, bwd_v, taps, spectrum, outer = pl.pallas_call(
        prep_kernel,
        out_shape=(
            p_shape,
            shape(w_in.shape, BF16),
            shape(w_out.shape, BF16),
            shape(fwd.shape, BF16),
            shape(bwd.shape, BF16),
            shape((16, 3 * width), F32),
            shape((6 * rows, width), F32),
            shape((rows, width), BF16),
        ),
        in_specs=[hbm] * 10,
        out_specs=(vmem,) * 8,
        scratch_shapes=[
            pltpu.VMEM(image_tokens.shape, BF16),
            pltpu.VMEM(spec.shape, BF16),
            pltpu.VMEM(long_filter.shape, BF16),
            pltpu.VMEM((1, width), F32),
            pltpu.VMEM(conv_kernel.shape, BF16),
            pltpu.VMEM(conv_bias.shape, F32),
            pltpu.SemaphoreType.DMA((10,)),
        ],
        compiler_params=limit,
        cost_estimate=pl.CostEstimate(flops=0, bytes_accessed=3 * 1024 * 1024, transcendentals=0),
    )(
        keep(image_tokens), keep(w_in), keep(w_out), keep(fwd.astype(BF16)), keep(bwd.astype(BF16)),
        keep(spec), keep(long_filter), keep(skip_gain[None]), keep(conv_kernel), keep(conv_bias),
    )

    def by_core(low, high):
        return jnp.where(core == 0, low, high)

    def column(low):
        return by_core(other[:, low], other[:, cols - 1 - low])

    pairs = []
    for j in range(n_col - 1):
        pairs += [(n_col + j, j + 1), (j + 1, n_col + j)]
    halo = lax.ppermute(jnp.concatenate([outer, column(0)], 0), ("row", "col"), pairs)
    _, edge_mixed, inner = pl.pallas_call(
        inner_kernel,
        out_shape=(p_shape, mixed_shape, out_shape),
        in_specs=[vmem] * 9,
        out_specs=(vmem,) * 3,
        input_output_aliases={0: 0},
        scratch_shapes=[
            pltpu.VMEM(p_shape.shape, F32),
            pltpu.VMEM(mixed_shape.shape, F32),
            pltpu.VMEM((1, rows * GROUP, 2 * width), BF16),
            pltpu.VMEM((1, 2 * rows * GROUP, 2 * width), BF16),
        ],
        compiler_params=limit,
        cost_estimate=pl.CostEstimate(flops=10**9, bytes_accessed=12 * 1024 * 1024, transcendentals=0),
    )(projected, other, column(part), w_in_v, taps, fwd_v, bwd_v, w_out_v, spectrum)
    half_shape = shape((rows, part, width), BF16)
    _, _, mine, send = pl.pallas_call(
        edge_kernel,
        out_shape=(out_shape, mixed_shape, half_shape, half_shape),
        in_specs=[vmem] * 9,
        out_specs=(vmem,) * 4,
        input_output_aliases={0: 0, 1: 1},
        scratch_shapes=[
            pltpu.VMEM((3 * width // LANES, 2 * height + 8, LANES), F32),
            pltpu.VMEM((1, rows * GROUP, 2 * width), BF16),
            pltpu.VMEM((1, 2 * rows * GROUP, 2 * width), BF16),
        ],
        compiler_params=limit,
        cost_estimate=pl.CostEstimate(flops=3 * 10**8, bytes_accessed=4 * 1024 * 1024, transcendentals=0),
    )(inner, edge_mixed, halo, w_in_v, taps, fwd_v, bwd_v, w_out_v, spectrum)
    theirs = lax.ppermute(send, "row", swap)
    both = jnp.concatenate([mine, mine], 1)
    return lax.dynamic_update_slice_in_dim(both, theirs, (1 - core) * part, 1)


def solution(mesh):
    in_specs = (P("row", "col", None), P(), P(), P(), P(), P(), P())
    out_specs = P("row", "col", None)
    return jax.shard_map(
        on_device, mesh=mesh, in_specs=in_specs, out_specs=out_specs, check_vma=False
    )
```

```python
import jax
import jax.numpy as jnp
import numpy as np
from jax import lax
from jax.experimental import pallas as pl
from jax.experimental.layout import Layout, with_layout_constraint
from jax.experimental.pallas import tpu as pltpu
from jax.sharding import PartitionSpec as P

F32 = jnp.float32
BF16 = jnp.bfloat16


def transforms(half, group):
    size = 2 * half
    slot = np.arange(half)[:, None]
    pos = np.arange(half)[None, :]
    angle = 2 * np.pi * slot * pos / size
    real, imag = np.cos(angle), -np.sin(angle)
    imag[0] = (-1.0) ** np.arange(half)
    forward = np.concatenate([real, imag], 0)
    back_real = 2 * np.cos(angle.T) / size
    back_real[:, 0] = 1 / size
    back_imag = -2 * np.sin(angle.T) / size
    back_imag[:, 0] = (-1.0) ** np.arange(half) / size
    backward = np.concatenate([back_real, back_imag], 1)
    lag = np.arange(size)[None, :]
    angle = 2 * np.pi * slot * lag / size
    real, imag = np.cos(angle), -np.sin(angle)
    imag[0] = 0
    real2 = real.copy()
    real2[0] = (-1.0) ** np.arange(size)
    near = (lag < half).astype(np.float64)
    sign = (-1.0) ** slot
    sign2 = sign.copy()
    sign2[0] = 1
    spectra = np.concatenate(
        [real * near, imag * near, real2 * near, real * sign, imag * sign, real2 * sign2], 0
    )
    eye = np.eye(group)
    return np.kron(forward, eye), np.kron(backward, eye), spectra


LANES = 128
GROUP = 8
CHUNK = 16
PITCH = 24
FIRST = 8


def pick_column(block, column):
    rows, cols, width = block.shape
    shape = (rows, rows * cols)
    place = lax.broadcasted_iota(jnp.int32, shape, 1)
    wanted = lax.broadcasted_iota(jnp.int32, shape, 0) * cols + column
    return jnp.dot(
        jnp.where(place == wanted, 1.0, 0.0).astype(BF16),
        block.reshape(rows * cols, width),
        preferred_element_type=F32,
    ).astype(BF16)


def row_place(row, column):
    return row * PITCH + FIRST + column


def project(tokens, strip, core, w_in_ref, p_ref):
    rows, part, width = tokens.shape
    count = rows * part
    got = jnp.dot(tokens.reshape(count, width), w_in_ref[...], preferred_element_type=F32)
    got_strip = jnp.dot(strip, w_in_ref[...], preferred_element_type=F32)
    for t in range(3 * width // LANES):
        at = slice(t * LANES, (t + 1) * LANES)
        for row in (0, rows + 1):
            place = row * PITCH
            p_ref[t, place : place + PITCH + GROUP, :] = jnp.zeros((PITCH + GROUP, LANES), F32)
        for r in range(rows):
            place = row_place(r + 1, 0)
            p_ref[t, place : place + part, :] = got[r * part : (r + 1) * part, at]
        for r in range(0, rows, GROUP):
            beside = got_strip[r : r + GROUP, at]
            for column, value in (
                (-1, jnp.where(core == 1, beside, 0.0)),
                (part, jnp.where(core == 0, beside, 0.0)),
            ):
                place = row_place(r + 1, column)
                p_ref[t, pl.ds(place, GROUP, stride=PITCH), :] = value


def copy_row(from_ref, from_row, to_ref, to_row, part):
    sub = lax.broadcasted_iota(jnp.int32, (GROUP, LANES), 0)
    for t in range(from_ref.shape[0]):
        for place in range(0, FIRST + part + GROUP, GROUP):
            source = pl.ds(pl.multiple_of(from_row * PITCH + place, GROUP), GROUP)
            target = pl.ds(pl.multiple_of(to_row * PITCH + place, GROUP), GROUP)
            value = from_ref[t, source, :]
            if place < FIRST:
                value = jnp.where(sub == GROUP - 1, value, to_ref[t, target, :])
            elif place >= FIRST + part:
                value = jnp.where(sub == 0, value, to_ref[t, target, :])
            to_ref[t, target, :] = value


def prep_kernel(
    own_hbm, w_in_hbm, w_out_hbm, fwd_hbm, bwd_hbm, spec_hbm, filt_hbm, gain_hbm, kernel_hbm, bias_hbm,
    p_ref, w_in_ref, w_out_ref, fwd_ref, bwd_ref, taps_ref, h_ref, outer_ref,
    own_ref, spec_ref, filt_ref, gain_ref, kernel_ref, bias_ref, sems,
):
    core = lax.axis_index("row")
    rows, cols, width = own_ref.shape
    part = cols // 2
    moves = [
        (own_hbm, own_ref),
        (w_in_hbm, w_in_ref),
        (spec_hbm, spec_ref),
        (filt_hbm, filt_ref),
        (gain_hbm, gain_ref),
        (kernel_hbm, kernel_ref),
        (bias_hbm, bias_ref),
        (fwd_hbm, fwd_ref),
        (bwd_hbm, bwd_ref),
        (w_out_hbm, w_out_ref),
    ]
    copies = [pltpu.make_async_copy(src, dst, sems.at[i]) for i, (src, dst) in enumerate(moves)]
    for copy in copies:
        copy.start()
    copies[0].wait()
    start = pl.multiple_of(core * part, part)
    far = pl.multiple_of((1 - core) * part, part)
    inner_edge = core * (part - 1)
    outer_ref[...] = pick_column(own_ref[:, pl.ds(start, part), :], inner_edge)
    beside = pick_column(own_ref[:, pl.ds(far, part), :], inner_edge)
    for copy in copies[1:7]:
        copy.wait()
    project(own_ref[:, pl.ds(start, part), :], beside, core, w_in_ref, p_ref)
    filt = filt_ref[...]
    gain = gain_ref[...]
    spectrum = jnp.dot(spec_ref[0], filt, preferred_element_type=F32) + jnp.dot(
        spec_ref[1], filt, preferred_element_type=F32
    )
    for j in range(6):
        part_j = spectrum[j * rows : (j + 1) * rows]
        h_ref[j * rows : (j + 1) * rows, :] = part_j + gain if j in (0, 2) else part_j
    for a in range(3):
        taps_ref[3 * a : 3 * a + 3, :] = kernel_ref[a].astype(F32)
    taps_ref[9, :] = bias_ref[...]
    for copy in copies[7:]:
        copy.wait()


def add_edge_terms(first, second, core, taps, edge_ref, mixed_ref, column):
    rows, channels = first.shape
    for t in range(channels // LANES):
        at = slice(t * LANES, (t + 1) * LANES)
        edge_ref[t, 0:8, :] = jnp.zeros((8, LANES), F32)
        edge_ref[t, 4 * rows : 4 * rows + 8, :] = jnp.zeros((8, LANES), F32)
        for r in range(0, rows, 8):
            for row, half in ((core * rows, first), ((1 - core) * rows, second)):
                place = pl.ds(2 * (row + r + 1), 8, stride=2)
                edge_ref[t, place, :] = half[r : r + 8, at]
        for r in range(0, 2 * rows, 8):
            place = pl.ds(r * GROUP + column, 8, stride=GROUP)
            total = mixed_ref[t, place, :]
            for a in range(3):
                total = total + edge_ref[t, pl.ds(2 * (r + a), 8, stride=2), :] * taps[a][:, at]
            mixed_ref[t, place, :] = total


def column_taps(taps_ref, core, on_core0):
    first, second = on_core0, 2 - on_core0
    return [
        jnp.where(
            core == 0,
            taps_ref[3 * a + first : 3 * a + first + 1, :],
            taps_ref[3 * a + second : 3 * a + second + 1, :],
        )
        for a in range(3)
    ]


def depthwise_steps(p_ref, first, taps_ref, chunk, store, bases):
    for base in bases:
        at = slice(base, base + LANES)
        tap = [
            jnp.broadcast_to(taps_ref[k : k + 1, at], (GROUP, LANES)) for k in range(10)
        ]
        loaded = [
            [
                p_ref[
                    base // LANES,
                    pl.ds(row_place(chunk * CHUNK + r, first + b - 1), GROUP, stride=2),
                    :,
                ]
                for b in range(3)
            ]
            for r in range(CHUNK + 2)
        ]
        for r in range(CHUNK):
            value = tap[9]
            for a in range(3):
                row = loaded[r + a]
                value = value + (
                    row[0] * tap[3 * a] + row[1] * tap[3 * a + 1] + row[2] * tap[3 * a + 2]
                )
            store(chunk * CHUNK + r, at, value)
        yield


def interleave(out_ref, final, first):
    _, rows, _, width = final.shape
    for h in range(2):
        for t in range(width // LANES):
            for r in range(rows):
                out_ref[h, t, pl.ds(r * 2 * GROUP + first, GROUP, stride=2), :] = final[
                    h, r, :, t * LANES : (t + 1) * LANES
                ]


def conv_steps(mixed, fwd_ref, bwd_ref, w_out_ref, h_ref, prod_ref, z_ref, put):
    streams, block, lanes = prod_ref.shape
    lanes = lanes // 2
    rows = block // GROUP
    width = streams * lanes

    def products(n):
        for row in range(0, rows, 2):
            for h in range(2):
                for base in range(n * lanes, (n + 1) * lanes, LANES):
                    two = [
                        mixed(h * rows + r, width + base) * mixed(h * rows + r, 2 * width + base)
                        for r in (row, row + 1)
                    ]
                    at = h * lanes + base - n * lanes
                    prod_ref[n, row * GROUP : (row + 2) * GROUP, at : at + LANES] = (
                        jnp.concatenate(two, 0).astype(BF16)
                    )
        return jnp.dot(fwd_ref[...], prod_ref[n], preferred_element_type=F32)

    def filtered(n, spectra):
        channels = slice(n * lanes, (n + 1) * lanes)
        low, high = spectra[:, :lanes], spectra[:, lanes:]

        def response(j, s):
            place = j * rows + s
            return jnp.broadcast_to(h_ref[place : place + 1, channels], (GROUP, lanes))

        for k in range(0, rows, 2):
            parts = [[], [], [], []]
            for s in (k, k + 1):
                near_r, near_i = response(0, s), response(1, s)
                all_r, all_i = response(3, s), response(4, s)
                near_2, all_2 = (response(2, s), response(5, s)) if s == 0 else (near_r, all_r)
                re = slice(s * GROUP, (s + 1) * GROUP)
                im = slice(block + s * GROUP, block + (s + 1) * GROUP)
                lr, li, hr, hi = low[re], low[im], high[re], high[im]
                parts[0].append(lr * near_r - li * near_i)
                parts[1].append(lr * near_i + li * near_2)
                parts[2].append(lr * all_r - li * all_i + hr * near_r - hi * near_i)
                parts[3].append(lr * all_i + li * all_2 + hr * near_i + hi * near_2)
            for j in range(4):
                at, lane = (j % 2) * block + k * GROUP, (j // 2) * lanes
                z_ref[n, at : at + 2 * GROUP, lane : lane + lanes] = jnp.concatenate(
                    parts[j], 0
                ).astype(BF16)
        return jnp.dot(bwd_ref[...], z_ref[n], preferred_element_type=F32)

    def gated(n, conv):
        columns = []
        for base in range(0, lanes, LANES):
            line = [
                mixed(h * rows + r, n * lanes + base)
                * conv[r * GROUP : (r + 1) * GROUP, h * lanes + base : h * lanes + base + LANES]
                for h in range(2)
                for r in range(rows)
            ]
            columns.append(jnp.concatenate(line, 0).astype(BF16))
        return columns

    spectra = []
    for n in range(streams):
        spectra.append(products(n))
        yield
    convs = []
    for n in range(streams):
        convs.append(filtered(n, spectra[n]))
        yield
    final = jnp.dot(
        jnp.concatenate([c for n in range(streams) for c in gated(n, convs[n])], 1),
        w_out_ref[...],
        preferred_element_type=F32,
    )
    yield
    put(final.reshape(2, rows, GROUP, width))


def inner_kernel(
    _, other_ref, other_strip_ref,
    w_in_ref, taps_ref, fwd_ref, bwd_ref, w_out_ref, h_ref,
    p_ref, edge_mixed_ref, out_ref,
    q_ref, mixed_ref, prod_ref, z_ref,
):
    core = lax.axis_index("row")
    rows, cols, width = other_ref.shape
    part = cols // 2
    height = 2 * rows
    start = pl.multiple_of(core * part, part)
    channels = range(0, 3 * width, LANES)
    n_chunk = rows // CHUNK

    def store_in(ref, row0):
        def store(row, at, value):
            place = pl.ds(pl.multiple_of((row0 + row) * GROUP, GROUP), GROUP)
            ref[at.start // LANES, place, :] = value

        return store

    own_at, other_at = core * rows, (1 - core) * rows

    def inner(ref, row0, chunk):
        return depthwise_steps(ref, 1 - core, taps_ref, chunk, store_in(mixed_ref, row0), channels)

    def edge(ref, row0, chunk):
        return depthwise_steps(ref, core, taps_ref, chunk, store_in(edge_mixed_ref, row0), channels)

    for i in range(n_chunk - 1):
        for _ in inner(p_ref, own_at, core + i):
            pass
    project(other_ref[:, pl.ds(start, part), :], other_strip_ref[...], core, w_in_ref, q_ref)
    copy_row(q_ref, 1 + core * (rows - 1), p_ref, (1 - core) * (rows + 1), part)
    copy_row(p_ref, rows - core * (rows - 1), q_ref, core * (rows + 1), part)
    for _ in inner(p_ref, own_at, (1 - core) * (n_chunk - 1)):
        pass

    for i in range(n_chunk):
        for _ in inner(q_ref, other_at, i):
            pass

    def put(final):
        interleave(out_ref, final, 1 - core)

    def edge_all():
        for ref, row0 in ((p_ref, own_at), (q_ref, other_at)):
            for i in range(n_chunk):
                yield from edge(ref, row0, i)

    steps = edge_all()
    conv = conv_steps(
        lambda r, base: mixed_ref[base // LANES, r * GROUP : (r + 1) * GROUP, :],
        fwd_ref, bwd_ref, w_out_ref, h_ref, prod_ref, z_ref, put,
    )
    for _ in conv:
        for _ in range(5):
            next(steps, None)
    for _ in steps:
        pass


def edge_kernel(
    _, __, halo_ref, w_in_ref, taps_ref, fwd_ref, bwd_ref, w_out_ref, h_ref,
    out_ref, mixed_ref, mine_ref, send_ref,
    strip_ref, prod_ref, z_ref,
):
    core = lax.axis_index("row")
    rows, part, width = mine_ref.shape
    got = jnp.dot(halo_ref[...], w_in_ref[...], preferred_element_type=F32)
    add_edge_terms(
        got[:rows], got[rows:], 1 - core, column_taps(taps_ref, core, 0), strip_ref,
        mixed_ref, core * (GROUP - 1),
    )

    def mixed(r, base):
        return mixed_ref[base // LANES, r * GROUP : (r + 1) * GROUP, :]

    def put(final):
        interleave(out_ref, final, core)

    for _ in conv_steps(
        mixed, fwd_ref, bwd_ref, w_out_ref, h_ref, prod_ref, z_ref, put
    ):
        pass
    for ref, half in ((mine_ref, core), (send_ref, 1 - core)):
        for t in range(width // LANES):
            ref[:, :, t * LANES : (t + 1) * LANES] = (
                out_ref[half, t].reshape(rows, part, LANES).astype(BF16)
            )


def on_device(image_tokens, w_in, conv_kernel, conv_bias, long_filter, skip_gain, w_out):
    rows, cols, width = image_tokens.shape
    part = cols // 2
    height = 2 * rows
    n_col = lax.axis_size("col")
    core = lax.axis_index("row")
    fwd, bwd, spectra = transforms(rows, GROUP)
    spec_hi = spectra.astype(BF16)
    spec_lo = (spectra - spec_hi.astype(np.float64)).astype(BF16)
    spec = np.stack([spec_hi, spec_lo])
    vmem = pl.BlockSpec(memory_space=pltpu.VMEM)
    hbm = pl.BlockSpec(memory_space=pltpu.HBM)
    shape = jax.ShapeDtypeStruct
    limit = pltpu.CompilerParams(vmem_limit_bytes=24 * 1024 * 1024)

    p_shape = shape((3 * width // LANES, (rows + 2) * PITCH + GROUP, LANES), F32)
    out_shape = shape((2, width // LANES, rows * part, LANES), F32)
    mixed_shape = shape((3 * width // LANES, height * GROUP, LANES), F32)

    swap = [(0, 1), (1, 0)]
    rowmajor = Layout((0, 1, 2))
    image_tokens = with_layout_constraint(image_tokens, rowmajor)
    other = with_layout_constraint(lax.ppermute(image_tokens, "row", swap), rowmajor)

    def keep(array):
        return pltpu.with_memory_space_constraint(array, pltpu.HBM)

    projected, w_in_v, w_out_v, fwd_v, bwd_v, taps, spectrum, outer = pl.pallas_call(
        prep_kernel,
        out_shape=(
            p_shape,
            shape(w_in.shape, BF16),
            shape(w_out.shape, BF16),
            shape(fwd.shape, BF16),
            shape(bwd.shape, BF16),
            shape((16, 3 * width), F32),
            shape((6 * rows, width), F32),
            shape((rows, width), BF16),
        ),
        in_specs=[hbm] * 10,
        out_specs=(vmem,) * 8,
        scratch_shapes=[
            pltpu.VMEM(image_tokens.shape, BF16),
            pltpu.VMEM(spec.shape, BF16),
            pltpu.VMEM(long_filter.shape, BF16),
            pltpu.VMEM((1, width), F32),
            pltpu.VMEM(conv_kernel.shape, BF16),
            pltpu.VMEM(conv_bias.shape, F32),
            pltpu.SemaphoreType.DMA((10,)),
        ],
        compiler_params=limit,
        cost_estimate=pl.CostEstimate(flops=0, bytes_accessed=3 * 1024 * 1024, transcendentals=0),
    )(
        keep(image_tokens), keep(w_in), keep(w_out), keep(fwd.astype(BF16)), keep(bwd.astype(BF16)),
        keep(spec), keep(long_filter), keep(skip_gain[None]), keep(conv_kernel), keep(conv_bias),
    )

    def by_core(low, high):
        return jnp.where(core == 0, low, high)

    def column(low):
        return by_core(other[:, low], other[:, cols - 1 - low])

    pairs = []
    for j in range(n_col - 1):
        pairs += [(n_col + j, j + 1), (j + 1, n_col + j)]
    halo = lax.ppermute(jnp.concatenate([outer, column(0)], 0), ("row", "col"), pairs)
    _, edge_mixed, inner = pl.pallas_call(
        inner_kernel,
        out_shape=(p_shape, mixed_shape, out_shape),
        in_specs=[vmem] * 9,
        out_specs=(vmem,) * 3,
        input_output_aliases={0: 0},
        scratch_shapes=[
            pltpu.VMEM(p_shape.shape, F32),
            pltpu.VMEM(mixed_shape.shape, F32),
            pltpu.VMEM((width // LANES, rows * GROUP, 2 * LANES), BF16),
            pltpu.VMEM((width // LANES, 2 * rows * GROUP, 2 * LANES), BF16),
        ],
        compiler_params=limit,
        cost_estimate=pl.CostEstimate(flops=10**9, bytes_accessed=12 * 1024 * 1024, transcendentals=0),
    )(projected, other, column(part), w_in_v, taps, fwd_v, bwd_v, w_out_v, spectrum)
    half_shape = shape((rows, part, width), BF16)
    _, _, mine, send = pl.pallas_call(
        edge_kernel,
        out_shape=(out_shape, mixed_shape, half_shape, half_shape),
        in_specs=[vmem] * 9,
        out_specs=(vmem,) * 4,
        input_output_aliases={0: 0, 1: 1},
        scratch_shapes=[
            pltpu.VMEM((3 * width // LANES, 2 * height + 8, LANES), F32),
            pltpu.VMEM((1, rows * GROUP, 2 * width), BF16),
            pltpu.VMEM((1, 2 * rows * GROUP, 2 * width), BF16),
        ],
        compiler_params=limit,
        cost_estimate=pl.CostEstimate(flops=3 * 10**8, bytes_accessed=4 * 1024 * 1024, transcendentals=0),
    )(inner, edge_mixed, halo, w_in_v, taps, fwd_v, bwd_v, w_out_v, spectrum)
    theirs = lax.ppermute(send, "row", swap)
    both = jnp.concatenate([mine, mine], 1)
    return lax.dynamic_update_slice_in_dim(both, theirs, (1 - core) * part, 1)


def solution(mesh):
    in_specs = (P("row", "col", None), P(), P(), P(), P(), P(), P())
    out_specs = P("row", "col", None)
    return jax.shard_map(
        on_device, mesh=mesh, in_specs=in_specs, out_specs=out_specs, check_vma=False
    )
```

```python
import jax
import jax.numpy as jnp
import numpy as np
from jax import lax
from jax.experimental import pallas as pl
from jax.experimental.layout import Layout, with_layout_constraint
from jax.experimental.pallas import tpu as pltpu
from jax.sharding import PartitionSpec as P

F32 = jnp.float32
BF16 = jnp.bfloat16


def transforms(half, group):
    size = 2 * half
    slot = np.arange(half)[:, None]
    pos = np.arange(half)[None, :]
    angle = 2 * np.pi * slot * pos / size
    real, imag = np.cos(angle), -np.sin(angle)
    imag[0] = (-1.0) ** np.arange(half)
    forward = np.concatenate([real, imag], 0)
    back_real = 2 * np.cos(angle.T) / size
    back_real[:, 0] = 1 / size
    back_imag = -2 * np.sin(angle.T) / size
    back_imag[:, 0] = (-1.0) ** np.arange(half) / size
    backward = np.concatenate([back_real, back_imag], 1)
    lag = np.arange(size)[None, :]
    angle = 2 * np.pi * slot * lag / size
    real, imag = np.cos(angle), -np.sin(angle)
    imag[0] = 0
    real2 = real.copy()
    real2[0] = (-1.0) ** np.arange(size)
    near = (lag < half).astype(np.float64)
    sign = (-1.0) ** slot
    sign2 = sign.copy()
    sign2[0] = 1
    spectra = np.concatenate(
        [real * near, imag * near, real2 * near, real * sign, imag * sign, real2 * sign2], 0
    )
    eye = np.eye(group)
    return np.kron(forward, eye), np.kron(backward, eye), spectra


LANES = 128
GROUP = 8
CHUNK = 16
PITCH = 24
FIRST = 8


def pick_column(block, column):
    rows, cols, width = block.shape
    shape = (rows, rows * cols)
    place = lax.broadcasted_iota(jnp.int32, shape, 1)
    wanted = lax.broadcasted_iota(jnp.int32, shape, 0) * cols + column
    return jnp.dot(
        jnp.where(place == wanted, 1.0, 0.0).astype(BF16),
        block.reshape(rows * cols, width),
        preferred_element_type=F32,
    ).astype(BF16)


def row_place(row, column):
    return row * PITCH + FIRST + column


def project(tokens, strip, core, w_in_ref, p_ref):
    rows, part, width = tokens.shape
    count = rows * part
    got = jnp.dot(tokens.reshape(count, width), w_in_ref[...], preferred_element_type=F32)
    got_strip = jnp.dot(strip, w_in_ref[...], preferred_element_type=F32)
    for t in range(3 * width // LANES):
        at = slice(t * LANES, (t + 1) * LANES)
        for row in (0, rows + 1):
            place = row * PITCH
            p_ref[t, place : place + PITCH + GROUP, :] = jnp.zeros((PITCH + GROUP, LANES), F32)
        for r in range(rows):
            place = row_place(r + 1, 0)
            p_ref[t, place : place + part, :] = got[r * part : (r + 1) * part, at]
        for r in range(0, rows, GROUP):
            beside = got_strip[r : r + GROUP, at]
            for column, value in (
                (-1, jnp.where(core == 1, beside, 0.0)),
                (part, jnp.where(core == 0, beside, 0.0)),
            ):
                place = row_place(r + 1, column)
                p_ref[t, pl.ds(place, GROUP, stride=PITCH), :] = value


def copy_row(from_ref, from_row, to_ref, to_row, part):
    sub = lax.broadcasted_iota(jnp.int32, (GROUP, LANES), 0)
    for t in range(from_ref.shape[0]):
        for place in range(0, FIRST + part + GROUP, GROUP):
            source = pl.ds(pl.multiple_of(from_row * PITCH + place, GROUP), GROUP)
            target = pl.ds(pl.multiple_of(to_row * PITCH + place, GROUP), GROUP)
            value = from_ref[t, source, :]
            if place < FIRST:
                value = jnp.where(sub == GROUP - 1, value, to_ref[t, target, :])
            elif place >= FIRST + part:
                value = jnp.where(sub == 0, value, to_ref[t, target, :])
            to_ref[t, target, :] = value


def prep_kernel(
    own_hbm, w_in_hbm, w_out_hbm, fwd_hbm, bwd_hbm, spec_hbm, filt_hbm, gain_hbm, kernel_hbm, bias_hbm,
    p_ref, w_in_ref, w_out_ref, fwd_ref, bwd_ref, taps_ref, h_ref, outer_ref,
    own_ref, spec_ref, filt_ref, gain_ref, kernel_ref, bias_ref, sems,
):
    core = lax.axis_index("row")
    rows, cols, width = own_ref.shape
    part = cols // 2
    moves = [
        (own_hbm, own_ref),
        (w_in_hbm, w_in_ref),
        (spec_hbm, spec_ref),
        (filt_hbm, filt_ref),
        (gain_hbm, gain_ref),
        (kernel_hbm, kernel_ref),
        (bias_hbm, bias_ref),
        (fwd_hbm, fwd_ref),
        (bwd_hbm, bwd_ref),
        (w_out_hbm, w_out_ref),
    ]
    copies = [pltpu.make_async_copy(src, dst, sems.at[i]) for i, (src, dst) in enumerate(moves)]
    for copy in copies:
        copy.start()
    copies[0].wait()
    start = pl.multiple_of(core * part, part)
    far = pl.multiple_of((1 - core) * part, part)
    inner_edge = core * (part - 1)
    outer_ref[...] = pick_column(own_ref[:, pl.ds(start, part), :], inner_edge)
    beside = pick_column(own_ref[:, pl.ds(far, part), :], inner_edge)
    for copy in copies[1:7]:
        copy.wait()
    project(own_ref[:, pl.ds(start, part), :], beside, core, w_in_ref, p_ref)
    filt = filt_ref[...]
    gain = gain_ref[...]
    spectrum = jnp.dot(spec_ref[0], filt, preferred_element_type=F32) + jnp.dot(
        spec_ref[1], filt, preferred_element_type=F32
    )
    for j in range(6):
        part_j = spectrum[j * rows : (j + 1) * rows]
        h_ref[j * rows : (j + 1) * rows, :] = part_j + gain if j in (0, 2) else part_j
    for a in range(3):
        taps_ref[3 * a : 3 * a + 3, :] = kernel_ref[a].astype(F32)
    taps_ref[9, :] = bias_ref[...]
    for copy in copies[7:]:
        copy.wait()


def add_edge_terms(first, second, core, taps, edge_ref, mixed_ref, column):
    rows, channels = first.shape
    for t in range(channels // LANES):
        at = slice(t * LANES, (t + 1) * LANES)
        edge_ref[t, 0:8, :] = jnp.zeros((8, LANES), F32)
        edge_ref[t, 4 * rows : 4 * rows + 8, :] = jnp.zeros((8, LANES), F32)
        for r in range(0, rows, 8):
            for row, half in ((core * rows, first), ((1 - core) * rows, second)):
                place = pl.ds(2 * (row + r + 1), 8, stride=2)
                edge_ref[t, place, :] = half[r : r + 8, at]
        for r in range(0, 2 * rows, 8):
            place = pl.ds(r * GROUP + column, 8, stride=GROUP)
            total = mixed_ref[t, place, :]
            for a in range(3):
                total = total + edge_ref[t, pl.ds(2 * (r + a), 8, stride=2), :] * taps[a][:, at]
            mixed_ref[t, place, :] = total


def column_taps(taps_ref, core, on_core0):
    first, second = on_core0, 2 - on_core0
    return [
        jnp.where(
            core == 0,
            taps_ref[3 * a + first : 3 * a + first + 1, :],
            taps_ref[3 * a + second : 3 * a + second + 1, :],
        )
        for a in range(3)
    ]


def depthwise_steps(p_ref, first, taps_ref, chunk, store, bases):
    for base in bases:
        at = slice(base, base + LANES)
        tap = [
            jnp.broadcast_to(taps_ref[k : k + 1, at], (GROUP, LANES)) for k in range(10)
        ]
        loaded = [
            [
                p_ref[
                    base // LANES,
                    pl.ds(row_place(chunk * CHUNK + r, first + b - 1), GROUP, stride=2),
                    :,
                ]
                for b in range(3)
            ]
            for r in range(CHUNK + 2)
        ]
        for r in range(CHUNK):
            value = tap[9]
            for a in range(3):
                row = loaded[r + a]
                value = value + (
                    row[0] * tap[3 * a] + row[1] * tap[3 * a + 1] + row[2] * tap[3 * a + 2]
                )
            store(chunk * CHUNK + r, at, value)
        yield


def interleave(out_ref, final, first):
    _, rows, _, width = final.shape
    for h in range(2):
        for t in range(width // LANES):
            for r in range(rows):
                out_ref[h, t, pl.ds(r * 2 * GROUP + first, GROUP, stride=2), :] = final[
                    h, r, :, t * LANES : (t + 1) * LANES
                ]


def conv_steps(mixed, fwd_ref, bwd_ref, w_out_ref, h_ref, prod_ref, z_ref, put):
    streams, block, lanes = prod_ref.shape
    lanes = lanes // 2
    rows = block // GROUP
    width = streams * lanes

    def products(n):
        for row in range(0, rows, 2):
            for h in range(2):
                for base in range(n * lanes, (n + 1) * lanes, LANES):
                    two = [
                        mixed(h * rows + r, width + base) * mixed(h * rows + r, 2 * width + base)
                        for r in (row, row + 1)
                    ]
                    at = h * lanes + base - n * lanes
                    prod_ref[n, row * GROUP : (row + 2) * GROUP, at : at + LANES] = (
                        jnp.concatenate(two, 0).astype(BF16)
                    )
        return jnp.dot(fwd_ref[...], prod_ref[n], preferred_element_type=F32)

    def filtered(n, spectra):
        channels = slice(n * lanes, (n + 1) * lanes)
        low, high = spectra[:, :lanes], spectra[:, lanes:]

        def response(j, s):
            place = j * rows + s
            return jnp.broadcast_to(h_ref[place : place + 1, channels], (GROUP, lanes))

        for k in range(0, rows, 2):
            parts = [[], [], [], []]
            for s in (k, k + 1):
                near_r, near_i = response(0, s), response(1, s)
                all_r, all_i = response(3, s), response(4, s)
                near_2, all_2 = (response(2, s), response(5, s)) if s == 0 else (near_r, all_r)
                re = slice(s * GROUP, (s + 1) * GROUP)
                im = slice(block + s * GROUP, block + (s + 1) * GROUP)
                lr, li, hr, hi = low[re], low[im], high[re], high[im]
                parts[0].append(lr * near_r - li * near_i)
                parts[1].append(lr * near_i + li * near_2)
                parts[2].append(lr * all_r - li * all_i + hr * near_r - hi * near_i)
                parts[3].append(lr * all_i + li * all_2 + hr * near_i + hi * near_2)
            for j in range(4):
                at, lane = (j % 2) * block + k * GROUP, (j // 2) * lanes
                z_ref[n, at : at + 2 * GROUP, lane : lane + lanes] = jnp.concatenate(
                    parts[j], 0
                ).astype(BF16)
        return jnp.dot(bwd_ref[...], z_ref[n], preferred_element_type=F32)

    def gated(n, conv):
        columns = []
        for base in range(0, lanes, LANES):
            line = [
                mixed(h * rows + r, n * lanes + base)
                * conv[r * GROUP : (r + 1) * GROUP, h * lanes + base : h * lanes + base + LANES]
                for h in range(2)
                for r in range(rows)
            ]
            columns.append(jnp.concatenate(line, 0).astype(BF16))
        return columns

    spectra = []
    for n in range(streams):
        spectra.append(products(n))
        yield
    convs = []
    for n in range(streams):
        convs.append(filtered(n, spectra[n]))
        yield
    final = jnp.dot(
        jnp.concatenate([c for n in range(streams) for c in gated(n, convs[n])], 1),
        w_out_ref[...],
        preferred_element_type=F32,
    )
    yield
    put(final.reshape(2, rows, GROUP, width))


def inner_kernel(
    _, other_ref, other_strip_ref,
    w_in_ref, taps_ref, fwd_ref, bwd_ref, w_out_ref, h_ref,
    p_ref, edge_mixed_ref, out_ref,
    q_ref, mixed_ref, prod_ref, z_ref,
):
    core = lax.axis_index("row")
    rows, cols, width = other_ref.shape
    part = cols // 2
    height = 2 * rows
    start = pl.multiple_of(core * part, part)
    channels = range(0, 3 * width, LANES)
    n_chunk = rows // CHUNK

    def store_in(ref, row0):
        def store(row, at, value):
            place = pl.ds(pl.multiple_of((row0 + row) * GROUP, GROUP), GROUP)
            ref[at.start // LANES, place, :] = value

        return store

    own_at, other_at = core * rows, (1 - core) * rows

    def inner(ref, row0, chunk):
        return depthwise_steps(ref, 1 - core, taps_ref, chunk, store_in(mixed_ref, row0), channels)

    def edge(ref, row0, chunk):
        return depthwise_steps(ref, core, taps_ref, chunk, store_in(edge_mixed_ref, row0), channels)

    for i in range(n_chunk - 1):
        for _ in inner(p_ref, own_at, core + i):
            pass
    project(other_ref[:, pl.ds(start, part), :], other_strip_ref[...], core, w_in_ref, q_ref)
    copy_row(q_ref, 1 + core * (rows - 1), p_ref, (1 - core) * (rows + 1), part)
    copy_row(p_ref, rows - core * (rows - 1), q_ref, core * (rows + 1), part)
    for _ in inner(p_ref, own_at, (1 - core) * (n_chunk - 1)):
        pass

    def inner_chunk(i, carry):
        for _ in inner(q_ref, other_at, i):
            pass
        return carry

    lax.fori_loop(0, n_chunk, inner_chunk, 0)

    def put(final):
        interleave(out_ref, final, 1 - core)

    for ref, row0 in ((p_ref, own_at), (q_ref, other_at)):

        def edge_chunk(i, carry, ref=ref, row0=row0):
            for _ in edge(ref, row0, i):
                pass
            return carry

        lax.fori_loop(0, n_chunk, edge_chunk, 0)

    conv = conv_steps(
        lambda r, base: mixed_ref[base // LANES, r * GROUP : (r + 1) * GROUP, :],
        fwd_ref, bwd_ref, w_out_ref, h_ref, prod_ref, z_ref, put,
    )
    for _ in conv:
        pass


def edge_kernel(
    _, __, halo_ref, w_in_ref, taps_ref, fwd_ref, bwd_ref, w_out_ref, h_ref,
    out_ref, mixed_ref, mine_ref, send_ref,
    strip_ref, prod_ref, z_ref,
):
    core = lax.axis_index("row")
    rows, part, width = mine_ref.shape
    got = jnp.dot(halo_ref[...], w_in_ref[...], preferred_element_type=F32)
    add_edge_terms(
        got[:rows], got[rows:], 1 - core, column_taps(taps_ref, core, 0), strip_ref,
        mixed_ref, core * (GROUP - 1),
    )

    def mixed(r, base):
        return mixed_ref[base // LANES, r * GROUP : (r + 1) * GROUP, :]

    def put(final):
        interleave(out_ref, final, core)

    for _ in conv_steps(
        mixed, fwd_ref, bwd_ref, w_out_ref, h_ref, prod_ref, z_ref, put
    ):
        pass
    for ref, half in ((mine_ref, core), (send_ref, 1 - core)):
        for t in range(width // LANES):
            ref[:, :, t * LANES : (t + 1) * LANES] = (
                out_ref[half, t].reshape(rows, part, LANES).astype(BF16)
            )


def on_device(image_tokens, w_in, conv_kernel, conv_bias, long_filter, skip_gain, w_out):
    rows, cols, width = image_tokens.shape
    part = cols // 2
    height = 2 * rows
    n_col = lax.axis_size("col")
    core = lax.axis_index("row")
    fwd, bwd, spectra = transforms(rows, GROUP)
    spec_hi = spectra.astype(BF16)
    spec_lo = (spectra - spec_hi.astype(np.float64)).astype(BF16)
    spec = np.stack([spec_hi, spec_lo])
    vmem = pl.BlockSpec(memory_space=pltpu.VMEM)
    hbm = pl.BlockSpec(memory_space=pltpu.HBM)
    shape = jax.ShapeDtypeStruct
    limit = pltpu.CompilerParams(vmem_limit_bytes=24 * 1024 * 1024)

    p_shape = shape((3 * width // LANES, (rows + 2) * PITCH + GROUP, LANES), F32)
    out_shape = shape((2, width // LANES, rows * part, LANES), F32)
    mixed_shape = shape((3 * width // LANES, height * GROUP, LANES), F32)

    swap = [(0, 1), (1, 0)]
    rowmajor = Layout((0, 1, 2))
    image_tokens = with_layout_constraint(image_tokens, rowmajor)
    other = with_layout_constraint(lax.ppermute(image_tokens, "row", swap), rowmajor)

    def keep(array):
        return pltpu.with_memory_space_constraint(array, pltpu.HBM)

    projected, w_in_v, w_out_v, fwd_v, bwd_v, taps, spectrum, outer = pl.pallas_call(
        prep_kernel,
        out_shape=(
            p_shape,
            shape(w_in.shape, BF16),
            shape(w_out.shape, BF16),
            shape(fwd.shape, BF16),
            shape(bwd.shape, BF16),
            shape((16, 3 * width), F32),
            shape((6 * rows, width), F32),
            shape((rows, width), BF16),
        ),
        in_specs=[hbm] * 10,
        out_specs=(vmem,) * 8,
        scratch_shapes=[
            pltpu.VMEM(image_tokens.shape, BF16),
            pltpu.VMEM(spec.shape, BF16),
            pltpu.VMEM(long_filter.shape, BF16),
            pltpu.VMEM((1, width), F32),
            pltpu.VMEM(conv_kernel.shape, BF16),
            pltpu.VMEM(conv_bias.shape, F32),
            pltpu.SemaphoreType.DMA((10,)),
        ],
        compiler_params=limit,
        cost_estimate=pl.CostEstimate(flops=0, bytes_accessed=3 * 1024 * 1024, transcendentals=0),
    )(
        keep(image_tokens), keep(w_in), keep(w_out), keep(fwd.astype(BF16)), keep(bwd.astype(BF16)),
        keep(spec), keep(long_filter), keep(skip_gain[None]), keep(conv_kernel), keep(conv_bias),
    )

    def by_core(low, high):
        return jnp.where(core == 0, low, high)

    def column(low):
        return by_core(other[:, low], other[:, cols - 1 - low])

    pairs = []
    for j in range(n_col - 1):
        pairs += [(n_col + j, j + 1), (j + 1, n_col + j)]
    halo = lax.ppermute(jnp.concatenate([outer, column(0)], 0), ("row", "col"), pairs)
    _, edge_mixed, inner = pl.pallas_call(
        inner_kernel,
        out_shape=(p_shape, mixed_shape, out_shape),
        in_specs=[vmem] * 9,
        out_specs=(vmem,) * 3,
        input_output_aliases={0: 0},
        scratch_shapes=[
            pltpu.VMEM(p_shape.shape, F32),
            pltpu.VMEM(mixed_shape.shape, F32),
            pltpu.VMEM((width // LANES, rows * GROUP, 2 * LANES), BF16),
            pltpu.VMEM((width // LANES, 2 * rows * GROUP, 2 * LANES), BF16),
        ],
        compiler_params=limit,
        cost_estimate=pl.CostEstimate(flops=10**9, bytes_accessed=12 * 1024 * 1024, transcendentals=0),
    )(projected, other, column(part), w_in_v, taps, fwd_v, bwd_v, w_out_v, spectrum)
    half_shape = shape((rows, part, width), BF16)
    _, _, mine, send = pl.pallas_call(
        edge_kernel,
        out_shape=(out_shape, mixed_shape, half_shape, half_shape),
        in_specs=[vmem] * 9,
        out_specs=(vmem,) * 4,
        input_output_aliases={0: 0, 1: 1},
        scratch_shapes=[
            pltpu.VMEM((3 * width // LANES, 2 * height + 8, LANES), F32),
            pltpu.VMEM((1, rows * GROUP, 2 * width), BF16),
            pltpu.VMEM((1, 2 * rows * GROUP, 2 * width), BF16),
        ],
        compiler_params=limit,
        cost_estimate=pl.CostEstimate(flops=3 * 10**8, bytes_accessed=4 * 1024 * 1024, transcendentals=0),
    )(inner, edge_mixed, halo, w_in_v, taps, fwd_v, bwd_v, w_out_v, spectrum)
    theirs = lax.ppermute(send, "row", swap)
    both = jnp.concatenate([mine, mine], 1)
    return lax.dynamic_update_slice_in_dim(both, theirs, (1 - core) * part, 1)


def solution(mesh):
    in_specs = (P("row", "col", None), P(), P(), P(), P(), P(), P())
    out_specs = P("row", "col", None)
    return jax.shard_map(
        on_device, mesh=mesh, in_specs=in_specs, out_specs=out_specs, check_vma=False
    )
```
